32 devices in a mesh: segment: 2 (over core), dp: 16 (over z, y, x).
Axes of the slice: x: 2, y: 2, z: 4, core: 2. Of those that a mesh axis runs over, the one named last changes fastest.
Arguments:
- latent: bfloat16 [2, 16, 6, 6, 1024], P(None, 'dp')
- noise: float32 [2, 16, 144], P(None, 'dp'), may hold values from -6 to 6
- real_bank: bfloat16 [64, 144, 512], P('dp'), may hold values from -6 to 6
- real_index: int32 [2, 16], P(None, 'dp'), may hold values from 0 to 3
- frozen_feat: bfloat16 [512, 320], replicated, may hold values from -0.25 to 0.25
- frozen_proj: bfloat16 [320, 512], replicated, may hold values from -0.3125 to 0.3125
- power_vec: float32 [512], replicated, may hold values from -6 to 6
- conv_w: float32 [9216, 1024], P('dp'), may hold values from -0.0625 to 0.0625
- conv_mom: float32 [9216, 1024], P('dp')
- squeeze_w: float32 [1024, 512], P('dp'), may hold values from -1 to 1
- squeeze_mom: float32 [1024, 512], P('dp')
- excite_w: float32 [512, 512], P('dp'), may hold values from -0.5 to 0.5
- excite_mom: float32 [512, 512], P('dp')
- critic_w: float32 [512, 512], P('dp'), may hold values from -0.25 to 0.25
- critic_mom: float32 [512, 512], P('dp')
- vectors: float32 [3585], replicated
- vec_m: float32 [3585], replicated
- vec_v: float32 [3585], replicated
Outputs:
- loss_sum: float32 [], replicated
- conv_mom_new: float32 [9216, 1024], P('dp')
- conv_new: float32 [9216, 1024], P('dp')
- squeeze_mom_new: float32 [1024, 512], P('dp')
- squeeze_new: float32 [1024, 512], P('dp')
- excite_mom_new: float32 [512, 512], P('dp')
- excite_new: float32 [512, 512], P('dp')
- critic_mom_new: float32 [512, 512], P('dp')
- critic_new: float32 [512, 512], P('dp')
- vec_m_new: float32 [3585], replicated
- vec_v_new: float32 [3585], replicated
- vectors_new: float32 [3585], replicated
The draws below stay inside these ranges and needn't reach their ends.
Inputs may be any that keep to these rules, and one draw needn't show every extreme that they name: real_index[m, b] picks one of the 4 real maps stored in the dp block that holds image b.
All inputs are finite; a program needn't handle non-finite values.
Results may differ from the reference program's by a relative error of at most 0.0023.
The reference program's roundings to bfloat16 on the way count: a program that leaves them out, or rounds other values in their place, can miss the bound.
Values may be sent and summed in bfloat16 or wider, within the bound.
A program may use at most 384 MiB of HBM per device.

```python
import math
import jax
import jax.numpy as jnp
from jax import lax

CIN = 1024
OUTC = 512
GLU2 = 1024
FEAT = 320
PROJ = 512
SIDE = 6
PIX = 144
IMGS = 1
MICRO = 2
BANK = 4
NS_STEPS = 5
STEP = 10
BATCH = 16
BANK_ALL = 64
ROWS_CONV = 9216
VEC = 3585
NPATCH = 4608


def grad_scale():
    return 0.02 / math.sqrt(MICRO * BATCH * PIX)


def vector_scales():
    generator_part = jnp.full((3 * GLU2,), grad_scale(), jnp.float32)
    head_part = jnp.full((PROJ,), 25.0 * grad_scale(), jnp.float32)
    return jnp.concatenate([generator_part, head_part, jnp.full((1,), 0.2, jnp.float32)])


def momentum_draw(key, rows_count, cols_count):
    return jax.random.normal(key, (rows_count, cols_count), jnp.float32) * grad_scale()


def draw_latent(key, part):
    key = jax.random.fold_in(key, 1)
    shape = (MICRO, BATCH, SIDE, SIDE, CIN)
    place = jnp.arange(BATCH, dtype=jnp.float32) / max(BATCH - 1, 1)
    base = jax.random.normal(key, shape, jnp.float32)
    rising = 1.0 + 2.0 * place
    return (base * rising[None, :, None, None, None]).astype(jnp.bfloat16)


def draw_vectors(key, part):
    key = jax.random.fold_in(key, 2)
    keys = jax.random.split(key, 5)
    noise_gain = jax.random.uniform(keys[0], (GLU2,), jnp.float32, 0.2, 0.6)
    bn_gain = jax.random.uniform(keys[1], (GLU2,), jnp.float32, 0.7, 1.3)
    bn_bias = 0.2 * jax.random.normal(keys[2], (GLU2,), jnp.float32)
    head = jax.random.normal(keys[3], (PROJ,), jnp.float32) * (2.0 / math.sqrt(PROJ))
    offset = jax.random.uniform(keys[4], (1,), jnp.float32, 0.1, 0.5)
    return jnp.concatenate([noise_gain, bn_gain, bn_bias, head, offset])


def draw_vec_m(key, part):
    key = jax.random.fold_in(key, 3)
    return 0.111 * vector_scales() * jax.random.normal(key, (VEC,), jnp.float32)


def draw_vec_v(key, part):
    key = jax.random.fold_in(key, 4)
    factor = jax.random.uniform(key, (VEC,), jnp.float32, 1.0, 4.0)
    scales = vector_scales()
    return 0.0526 * scales * scales * factor


def draw_conv_mom(key, part):
    key = jax.random.fold_in(key, 5)
    return momentum_draw(key, ROWS_CONV, GLU2)


def draw_squeeze_mom(key, part):
    key = jax.random.fold_in(key, 6)
    return momentum_draw(key, CIN, OUTC)


def draw_excite_mom(key, part):
    key = jax.random.fold_in(key, 7)
    return momentum_draw(key, OUTC, OUTC)


def draw_critic_mom(key, part):
    key = jax.random.fold_in(key, 8)
    return momentum_draw(key, PROJ, PROJ)


def with_ends(values, stream_key, low, high):
    extent = values.shape
    index_at = [jax.random.randint(jax.random.fold_in(stream_key, axis), (), 0, extent[axis]) for axis in range(len(extent))]
    values = values.at[tuple(index_at)].set(low)
    longest = extent.index(max(extent))
    index_at[longest] = (index_at[longest] + 1) % extent[longest]
    return values.at[tuple(index_at)].set(high)


def levels(own_key, shape, cuts, smallest, high):
    loudness, own = 1.0, jax.random.fold_in(own_key, 6)
    for axis_at, blocks in cuts:
        draws = jnp.exp(jax.random.uniform(jax.random.fold_in(own, axis_at), (blocks,), jnp.float32, smallest / len(cuts), high / len(cuts)))
        loudness = loudness * jnp.repeat(draws, shape[axis_at] // blocks).reshape([-1 if axis == axis_at else 1 for axis in range(len(shape))])
    return loudness


def bell_draw(rng, dims, spread, most, cuts=(), kind=jnp.bfloat16):
    array = spread * jax.random.normal(rng, dims, jnp.float32)
    if cuts:
        array = array * levels(rng, dims, cuts, -0.22, 0.18)
    return jnp.clip(array, -most, most).astype(kind)


def setup_inputs(seed: int = 0) -> dict:
    streams_of = jax.random.split(jax.random.key(seed), 19)
    return {
        "latent": draw_latent(jax.random.fold_in(streams_of[18], 71), 0),
        "noise": bell_draw(streams_of[1], (MICRO, BATCH, PIX), 1.0, 6.0, ((1, 16),), jnp.float32),
        "real_bank": bell_draw(streams_of[2], (BANK_ALL, PIX, OUTC), 1.0, 6.0, ((0, 16),)),
        "real_index": with_ends(jax.random.randint(streams_of[3], (MICRO, BATCH), 0, BANK), jax.random.fold_in(streams_of[3], 1), 0, BANK - 1).astype(jnp.int32),
        "frozen_feat": bell_draw(streams_of[4], (OUTC, FEAT), OUTC ** -0.5, 0.25),
        "frozen_proj": bell_draw(streams_of[5], (FEAT, PROJ), FEAT ** -0.5, 0.3125),
        "power_vec": bell_draw(streams_of[6], (PROJ,), 1.0, 6.0, (), jnp.float32),
        "conv_w": bell_draw(streams_of[7], (ROWS_CONV, GLU2), ROWS_CONV ** -0.5, 0.0625, ((0, 16),), jnp.float32),
        "conv_mom": draw_conv_mom(jax.random.fold_in(streams_of[18], 71), 0),
        "squeeze_w": bell_draw(streams_of[9], (CIN, OUTC), (CIN // (SIDE * SIDE)) ** -0.5, 1.0, ((0, 16),), jnp.float32),
        "squeeze_mom": draw_squeeze_mom(jax.random.fold_in(streams_of[18], 71), 0),
        "excite_w": bell_draw(streams_of[11], (OUTC, OUTC), (OUTC // 4) ** -0.5, 0.5, ((0, 16),), jnp.float32),
        "excite_mom": draw_excite_mom(jax.random.fold_in(streams_of[18], 71), 0),
        "critic_w": bell_draw(streams_of[13], (PROJ, PROJ), PROJ ** -0.5, 0.25, ((0, 16),), jnp.float32),
        "critic_mom": draw_critic_mom(jax.random.fold_in(streams_of[18], 71), 0),
        "vectors": draw_vectors(jax.random.fold_in(streams_of[18], 71), 0),
        "vec_m": draw_vec_m(jax.random.fold_in(streams_of[18], 71), 0),
        "vec_v": draw_vec_v(jax.random.fold_in(streams_of[18], 71), 0),
    }


HIGHEST_PREC = lax.Precision.HIGHEST
NORM_EPS = 1e-05
NEWTON_A = 3.4445
NEWTON_B = -4.775
NEWTON_C = 2.0315
MOMENTUM = 0.95
MUON_RATE = 0.5
DECAY = 0.01
ADAM_RATE = 0.2
ADAM_BETA1 = 0.9
ADAM_BETA2 = 0.95
ADAM_EPS = 1e-08

@jax.custom_vjp
def low(v):
    return lax.optimization_barrier(v.astype(jnp.bfloat16)).astype(jnp.float32)

@jax.custom_vjp
def low_back(v):
    return v

def low_keep(v):
    return (low(v), None)

def low_pass(kept, grad):
    return (grad,)

def back_keep(v):
    return (v, None)

def back_low(kept, grad):
    return (low(grad),)
low.defvjp(low_keep, low_pass)
low_back.defvjp(back_keep, back_low)

def matmul(left, right):
    return jnp.dot(left, right, precision=HIGHEST_PREC, preferred_element_type=jnp.float32)

def spectral_norm(weight, power):
    vector = matmul(weight, power)
    vector = vector * lax.rsqrt(jnp.sum(vector * vector))
    product_one = matmul(vector, weight)
    return weight / jnp.sqrt(jnp.sum(product_one * product_one))

def excite(pooled, squeeze_w, excite_w):
    return jax.nn.sigmoid(matmul(jax.nn.silu(matmul(pooled, squeeze_w)), excite_w))

def generate(latent_now, noise_now, conv_low, squeeze_low, excite_low, vectors):
    upsampled = jnp.repeat(jnp.repeat(latent_now, 2, axis=1), 2, axis=2)
    kernel = conv_low.reshape(3, 3, CIN, GLU2)
    hidden = lax.conv_general_dilated(upsampled, kernel, (1, 1), ((1, 1), (1, 1)), dimension_numbers=('NHWC', 'HWIO', 'NHWC'), precision=HIGHEST_PREC)
    hidden = low_back(hidden).reshape(BATCH, PIX, GLU2)
    shifted = hidden + noise_now[:, :, None] * vectors[:GLU2]
    mean_vec = lax.optimization_barrier(jnp.mean(shifted, axis=(0, 1)))
    square_vec = lax.optimization_barrier(jnp.mean(shifted * shifted, axis=(0, 1)))
    centred = (shifted - mean_vec) * lax.rsqrt(square_vec - mean_vec * mean_vec + NORM_EPS)
    normed = centred * vectors[GLU2:2 * GLU2] + vectors[2 * GLU2:3 * GLU2]
    gated = normed[..., :OUTC] * jax.nn.sigmoid(normed[..., OUTC:])
    pooled = lax.optimization_barrier(jnp.mean(latent_now, axis=(1, 2)))
    excitation = excite(pooled, squeeze_low, excite_low)
    fake_map = gated * excitation[:, None, :]
    return low_back(low(fake_map))

def critic_logits(inputs, frozen_feat, frozen_proj, spectral, out_weight, out_bias):
    pre_act = low_back(matmul(inputs, frozen_feat))
    features = low(jax.nn.silu(pre_act))
    projected = low(low_back(matmul(features, frozen_proj)))
    critic_act = low_back(matmul(projected, spectral))
    return matmul(jax.nn.silu(critic_act), out_weight) + out_bias

def orthogonalize(momentum_now):
    iterate = momentum_now / (jnp.sqrt(jnp.sum(momentum_now * momentum_now)) + 1e-07)
    for iteration in range(NS_STEPS):
        gram = matmul(iterate.T, iterate)
        product_one = matmul(iterate, gram)
        iterate = NEWTON_A * iterate + NEWTON_B * product_one + NEWTON_C * matmul(product_one, gram)
    return iterate

def muon_update(weight, momentum_now, gradient):
    new_mom = MOMENTUM * momentum_now + gradient
    return (new_mom, weight * (1.0 - MUON_RATE * DECAY) - MUON_RATE * orthogonalize(new_mom))

def reference(latent, noise, real_bank, real_index, frozen_feat, frozen_proj, power_vec, conv_w, conv_mom, squeeze_w, squeeze_mom, excite_w, excite_mom, critic_w, critic_mom, vectors, vec_m, vec_v):
    latent_f = latent.astype(jnp.float32)
    feat_f = frozen_feat.astype(jnp.float32)
    proj_f = frozen_proj.astype(jnp.float32)
    owner_dev = jnp.arange(BATCH, dtype=jnp.int32) // IMGS
    bank_rows = (owner_dev[None, :] * BANK + real_index).astype(jnp.int32)
    real_maps = real_bank.astype(jnp.float32)[bank_rows]

    def objective(conv_p, squeeze_p, excite_p, critic_p, vector_p):
        conv_low = low(conv_p)
        squeeze_low = low(squeeze_p)
        excite_low = low(excite_p)
        spectral = low(spectral_norm(low(critic_p), power_vec))
        out_weight = vector_p[3 * GLU2:3 * GLU2 + PROJ]
        out_bias = vector_p[3 * GLU2 + PROJ]

        def micro_loss(inputs):
            latent_now, noise_now, real_now = inputs
            fake_map = generate(latent_now, noise_now, conv_low, squeeze_low, excite_low, vector_p)
            fake_logit = critic_logits(fake_map.reshape(BATCH * PIX, OUTC), feat_f, proj_f, spectral, out_weight, out_bias)
            real_logit = critic_logits(real_now.reshape(BATCH * PIX, OUTC), feat_f, proj_f, spectral, out_weight, out_bias)
            return jnp.sum(jax.nn.softplus(1.0 - real_logit)) + jnp.sum(jax.nn.softplus(1.0 + fake_logit))

        def accumulate(running, inputs):
            return (running + jax.checkpoint(micro_loss)(inputs), None)
        running, unused = lax.scan(accumulate, jnp.zeros((), jnp.float32), (latent_f, noise, real_maps))
        return (running / NPATCH, running)
    mean_loss, backward, loss_sum = jax.vjp(objective, conv_w, squeeze_w, excite_w, critic_w, vectors, has_aux=True)
    grad_conv, grad_squeeze, grad_excite, grad_critic, grad_vec = backward(jnp.ones_like(mean_loss))
    grad_vec = jnp.concatenate([-grad_vec[:3 * GLU2], grad_vec[3 * GLU2:]])
    conv_mom_new, conv_new = muon_update(conv_w, conv_mom, -grad_conv)
    squeeze_mom_new, squeeze_new = muon_update(squeeze_w, squeeze_mom, -grad_squeeze)
    excite_mom_new, excite_new = muon_update(excite_w, excite_mom, -grad_excite)
    critic_mom_new, critic_new = muon_update(critic_w, critic_mom, grad_critic)
    vec_m_new = ADAM_BETA1 * vec_m + (1.0 - ADAM_BETA1) * grad_vec
    vec_v_new = ADAM_BETA2 * vec_v + (1.0 - ADAM_BETA2) * grad_vec * grad_vec
    first_hat = vec_m_new / (1.0 - ADAM_BETA1 ** STEP)
    second_hat = vec_v_new / (1.0 - ADAM_BETA2 ** STEP)
    vectors_new = vectors * (1.0 - ADAM_RATE * DECAY) - ADAM_RATE * first_hat / (jnp.sqrt(second_hat) + ADAM_EPS)
    return (loss_sum, conv_mom_new, conv_new, squeeze_mom_new, squeeze_new, excite_mom_new, excite_new, critic_mom_new, critic_new, vec_m_new, vec_v_new, vectors_new)
```

```python
from functools import partial

import jax
import jax.numpy as jnp
from jax import lax
from jax.experimental import pallas as pl
from jax.experimental.pallas import tpu as pltpu
from jax.sharding import PartitionSpec as P

NS_STEPS = 5
STEP = 10


HIGHEST_PREC = lax.Precision.HIGHEST
HIGH_PREC = lax.Precision.HIGH
MESH = pl.DeviceIdType.MESH
NORM_EPS = 1e-05
NEWTON_A = 3.4445
NEWTON_B = -4.775
NEWTON_C = 2.0315
MOMENTUM = 0.95
MUON_RATE = 0.5
DECAY = 0.01
ADAM_RATE = 0.2
ADAM_BETA1 = 0.9
ADAM_BETA2 = 0.95
ADAM_EPS = 1e-08
LANES = 128
SUBLANES = 8
VMEM_BYTES = 56 * 1024 * 1024


def low_dot(left, right):
    return jnp.dot(left, right, preferred_element_type=jnp.float32)


def high_dot(left, right):
    return jnp.dot(left, right, precision=HIGHEST_PREC, preferred_element_type=jnp.float32)


def mid_dot(left, right):
    return jnp.dot(left, right, precision=HIGH_PREC, preferred_element_type=jnp.float32)


def silu_slope(value):
    opened = jax.nn.sigmoid(value)
    return opened * (1.0 + value * (1.0 - opened))


def adam(vectors, vec_m, vec_v, vector_grad):
    vec_m_new = ADAM_BETA1 * vec_m + (1.0 - ADAM_BETA1) * vector_grad
    vec_v_new = ADAM_BETA2 * vec_v + (1.0 - ADAM_BETA2) * vector_grad * vector_grad
    first_hat = vec_m_new / (1.0 - ADAM_BETA1**STEP)
    second_hat = vec_v_new / (1.0 - ADAM_BETA2**STEP)
    vectors_new = vectors * (1.0 - ADAM_RATE * DECAY) - ADAM_RATE * first_hat / (
        jnp.sqrt(second_hat) + ADAM_EPS
    )
    return vec_m_new, vec_v_new, vectors_new


def exchange(n, ident, plans, arrays):
    count = len(plans)

    def shape(kind, paired, x):
        if kind == "sib":
            return jax.ShapeDtypeStruct(x.shape, x.dtype)
        block = x.shape if kind == "gather" else x.shape[1:]
        return jax.ShapeDtypeStruct(((n, 2) if paired else (n,)) + block, x.dtype)

    outs = [shape(kind, paired, x) for (kind, paired), x in zip(plans, arrays)]
    spread = [a for a in range(count) if plans[a][0] != "sib"]
    single = [a for a in range(count) if plans[a][0] == "sib"]
    passing = [a for a in spread if plans[a][1]]

    def body(*refs):
        ins, results = refs[:count], refs[count : 2 * count]
        send, recv, pass_send, pass_recv, here = refs[2 * count :]
        me, side = lax.axis_index("dp"), lax.axis_index("segment")
        other = 1 - side
        barrier = pltpu.get_barrier_semaphore()
        greeted = 0
        if spread:

            @pl.loop(1, n)
            def _(k):
                pl.semaphore_signal(
                    barrier, inc=1, device_id={"dp": lax.rem(me + k, n)}, device_id_type=MESH
                )

            greeted += n - 1
        if passing or single:
            pl.semaphore_signal(
                barrier, inc=1, device_id={"segment": other}, device_id_type=MESH
            )
            greeted += 1
        pl.semaphore_wait(barrier, greeted)

        def source(a, peer):
            return ins[a] if plans[a][0] == "gather" else ins[a].at[peer]

        def slot(a, owner, of_side):
            return results[a].at[owner, of_side] if plans[a][1] else results[a].at[owner]

        def outgoing(a, k):
            peer = lax.rem(me + k, n)
            return pltpu.make_async_remote_copy(
                src_ref=source(a, peer),
                dst_ref=slot(a, me, side),
                send_sem=send.at[a, k],
                recv_sem=recv.at[a, me],
                device_id={"dp": peer},
                device_id_type=MESH,
            )

        def incoming(a, owner):
            return pltpu.make_async_remote_copy(
                src_ref=source(a, owner),
                dst_ref=slot(a, owner, side),
                send_sem=send.at[a, 0],
                recv_sem=recv.at[a, owner],
                device_id={"dp": owner},
                device_id_type=MESH,
            )

        def passed(a, src, owner, of_side):
            return pltpu.make_async_remote_copy(
                src_ref=src,
                dst_ref=slot(a, owner, of_side),
                send_sem=pass_send.at[a, owner],
                recv_sem=pass_recv.at[a, owner],
                device_id={"segment": other},
                device_id_type=MESH,
            )

        def sibling(a):
            return pltpu.make_async_remote_copy(
                src_ref=ins[a],
                dst_ref=results[a],
                send_sem=pass_send.at[a, 0],
                recv_sem=pass_recv.at[a, 0],
                device_id={"segment": other},
                device_id_type=MESH,
            )

        def own(a):
            return pltpu.make_async_copy(source(a, me), slot(a, me, side), here.at[a])

        for a in single:
            sibling(a).start()
        if spread:

            @pl.loop(1, n)
            def _(k):
                for a in spread:
                    outgoing(a, k).start()

            for a in spread:
                own(a).start()
            for a in passing:
                passed(a, source(a, me), me, side).start()

            @pl.loop(1, n)
            def _(k):
                owner = lax.rem(me + n - k, n)
                for a in spread:
                    incoming(a, owner).wait_recv()
                    if plans[a][1]:
                        passed(a, slot(a, owner, side), owner, side).start()

            for a in spread:
                own(a).wait()

            @pl.loop(1, n)
            def _(k):
                for a in spread:
                    outgoing(a, k).wait_send()

        if passing:

            @pl.loop(0, n)
            def _(k):
                for a in passing:
                    passed(a, slot(a, k, side), k, side).wait_send()
                    passed(a, slot(a, k, other), k, other).wait_recv()

        for a in single:
            sibling(a).wait()

    anywhere = pl.BlockSpec(memory_space=pl.ANY)
    return pl.pallas_call(
        body,
        out_shape=outs,
        in_specs=[anywhere] * count,
        out_specs=[anywhere] * count,
        scratch_shapes=[pltpu.SemaphoreType.DMA((count, n))] * 4
        + [pltpu.SemaphoreType.DMA((count,))],
        compiler_params=pltpu.CompilerParams(collective_id=ident, has_side_effects=True),
        name=f"exchange_{ident}",
    )(*arrays)


def split_three(value):
    top = value.astype(jnp.bfloat16)
    rest = value - top.astype(jnp.float32)
    middle = rest.astype(jnp.bfloat16)
    bottom = (rest - middle.astype(jnp.float32)).astype(jnp.bfloat16)
    return top, middle, bottom


def exact_dot(value, low):
    rows = value.shape[0]
    product = low_dot(jnp.concatenate(split_three(value), axis=0), low)
    return product[:rows] + product[rows : 2 * rows] + product[2 * rows :]


def lane_of(shape):
    return lax.broadcasted_iota(jnp.int32, shape, len(shape) - 1)


def fold(value):
    axis = value.ndim - 1
    value = value + pltpu.roll(value, 64, axis)
    return value + pltpu.roll(value, 32, axis)


def row_pieces(rows, groups, taps_rows):
    depth = rows // groups
    pieces = []
    for chip in range(taps_rows[0] * taps_rows[1] // rows):
        for group in range(groups):
            first = chip * rows + group * depth
            at = first
            while at < first + depth:
                tap, channel = divmod(at, taps_rows[1])
                take = min(first + depth - at, taps_rows[1] - channel)
                pieces.append((chip, group, at - first, tap, channel, take))
                at += take
    return pieces


def shift_rows(value, side, steps):
    parts = []
    empty = jnp.zeros((1,) + value.shape[1:], value.dtype)
    for first in range(0, value.shape[0], side):
        block = value[first : first + side]
        parts += [empty, block[:-1]] if steps > 0 else [block[1:], empty]
    return jnp.concatenate(parts, axis=0)


def per_micro(values, side):
    return jnp.concatenate(
        [jnp.broadcast_to(v[None], (side, SUBLANES, LANES)) for v in values], axis=0
    )


def front_kernel(side, micros, pixel_count, lat, conv, noise, consts, squeeze, excite_cols,
                 fake, xn, stats, opened_out, z1_out, pooled_out, weight, z, h, gate8):
    images = lat.shape[0]
    half_in = lat.shape[3]
    channels = 2 * half_in
    depth = conv.shape[1]
    taps = weight.shape[1] // LANES
    bf16 = jnp.bfloat16
    group = lane_of((depth, LANES)) // 32
    masks = [(group == g).astype(jnp.float32).astype(bf16) for g in range(4)]
    for chip, g, first, tap, channel, take in row_pieces(4 * depth, 4, (taps, channels)):
        weight[channel : channel + take, tap * LANES : (tap + 1) * LANES] = (
            conv[chip, first : first + take, :] * masks[g][:take]
        )
    rows_image = lat.shape[2]
    lines = micros * side
    step = 4

    @pl.loop(0, images // step)
    def _(k):
        here = pl.ds(k * step, step)
        left = lat[here, 0].reshape(step * rows_image, half_in)
        right = lat[here, 1].reshape(step * rows_image, half_in)
        for tap in range(taps):
            cols = slice(tap * LANES, (tap + 1) * LANES)
            product = low_dot(left, weight[:half_in, cols]) + low_dot(right, weight[half_in:, cols])
            z[tap, here] = fold(product).reshape(step, lines, SUBLANES, LANES)

    shape3 = (lines, SUBLANES, LANES)
    lane = lane_of(shape3)
    row_first = (lane // 64) == 0
    col_first = ((lane // 32) % 2) == 0
    inside = lax.broadcasted_iota(jnp.int32, shape3, 1) < side
    first_half = (lane % 32) < 16
    gain_noise = consts[0:1, :][None]
    gain = consts[1:2, :][None]
    bias = consts[2:3, :][None]
    zero = jnp.zeros((SUBLANES, LANES), jnp.float32)

    def place(img, carry):
        lines_of = []
        for ky in range(3):
            z0, z1, z2 = z[3 * ky, img], z[3 * ky + 1, img], z[3 * ky + 2, img]
            lines_of.append(
                z1
                + jnp.where(col_first, pltpu.roll(z0, 1, 1), z0)
                + jnp.where(col_first, z2, pltpu.roll(z2, SUBLANES - 1, 1))
            )
        x0, x1, x2 = lines_of
        value = (
            x1
            + jnp.where(row_first, shift_rows(x0, side, 1), x0)
            + jnp.where(row_first, x2, shift_rows(x2, side, -1))
        )
        value = value + noise[img] * gain_noise
        value = jnp.where(inside, value, 0.0)
        h[img] = value
        new = []
        for m in range(micros):
            part = value[m * side : (m + 1) * side]
            new.append(carry[2 * m] + jnp.sum(part, axis=0))
            new.append(carry[2 * m + 1] + jnp.sum(part * part, axis=0))
        return tuple(new)

    sums = lax.fori_loop(0, images, place, (zero,) * (2 * micros))
    means, stds = [], []
    for m in range(micros):
        mean_now = jnp.sum(fold(sums[2 * m]), axis=0, keepdims=True) / pixel_count
        square = jnp.sum(fold(sums[2 * m + 1]), axis=0, keepdims=True) / pixel_count
        means.append(mean_now)
        stds.append(lax.rsqrt(square - mean_now * mean_now + NORM_EPS))
        stats[m : m + 1, :] = stds[m]
    mean12, std12 = per_micro(means, side), per_micro(stds, side)

    count = images * micros
    owner = lax.broadcasted_iota(jnp.int32, (count, count * (rows_image // micros)), 1) // (rows_image // micros)
    pool = (owner == lax.broadcasted_iota(jnp.int32, owner.shape, 0)).astype(jnp.float32).astype(bf16)
    area = 1.0 / (side * side)
    pooled = [low_dot(pool, lat[:, p].reshape(images * rows_image, half_in)) * area for p in range(2)]
    z1 = exact_dot(pooled[0], squeeze[:half_in]) + exact_dot(pooled[1], squeeze[half_in:])
    z1_out[...] = z1
    pooled_out[:, :half_in] = pooled[0]
    pooled_out[:, half_in:] = pooled[1]
    opened = jax.nn.sigmoid(exact_dot(z1 * jax.nn.sigmoid(z1), excite_cols[...]))
    opened_out[...] = opened
    gate8[...] = jnp.broadcast_to(opened[:, None, :], gate8.shape)

    @pl.loop(0, images)
    def _(img):
        centred = (h[img] - mean12) * std12
        xn[img] = centred
        y = centred * gain + bias
        gated = y * pltpu.roll(jax.nn.sigmoid(y), LANES - 16, 2)
        pieces = []
        for m in range(micros):
            pieces.append(gated[m * side : (m + 1) * side] * gate8[img * micros + m][None])
        packed = jnp.where(first_half[:side], pieces[0], pltpu.roll(pieces[1], 16, 2))
        fake[img] = packed.reshape(side * SUBLANES, LANES).astype(bf16)


def front(side, pixel_count, lat, conv, noise, consts, squeeze, excite_cols):
    images, _, rows_image, half_in = lat.shape
    micros = rows_image // (side * SUBLANES)
    lines = micros * side
    count = images * micros
    f32 = jnp.float32
    return pl.pallas_call(
        partial(front_kernel, side, micros, pixel_count),
        out_shape=[
            jax.ShapeDtypeStruct((images, side * SUBLANES, LANES), jnp.bfloat16),
            jax.ShapeDtypeStruct((images, lines, SUBLANES, LANES), f32),
            jax.ShapeDtypeStruct((SUBLANES, LANES), f32),
            jax.ShapeDtypeStruct((count, LANES), f32),
            jax.ShapeDtypeStruct((count, squeeze.shape[1]), f32),
            jax.ShapeDtypeStruct((count, 2 * half_in), f32),
        ],
        scratch_shapes=[
            pltpu.VMEM((2 * half_in, 9 * LANES), jnp.bfloat16),
            pltpu.VMEM((9, images, lines, SUBLANES, LANES), f32),
            pltpu.VMEM((images, lines, SUBLANES, LANES), f32),
            pltpu.VMEM((count, SUBLANES, LANES), f32),
        ],
        compiler_params=pltpu.CompilerParams(vmem_limit_bytes=VMEM_BYTES),
        name="front",
    )(lat, conv, noise, consts, squeeze, excite_cols)


def critic_kernel(side, patches, fake, real, feat, proj, critic, power, head, offset,
                  dfake, dspec, tail, column_v, column_t, row_w):
    bf16 = jnp.bfloat16
    weight = critic[...].astype(jnp.float32)
    product = jnp.sum(weight * power[...], axis=1, keepdims=True)
    length = lax.rsqrt(jnp.sum(product * product))
    vec = product * length
    back = jnp.sum(weight * vec, axis=0, keepdims=True)
    sigma = jnp.sqrt(jnp.sum(back * back))
    unit = back / sigma
    turned = jnp.sum(weight * unit, axis=1, keepdims=True)
    turned = (turned - vec * jnp.sum(turned * vec)) * length
    column_v[...] = vec
    column_t[...] = turned
    row_w[...] = jnp.broadcast_to(unit, row_w.shape)
    spectral = (weight / sigma).astype(bf16)

    fakes = fake.shape[0]
    rows = fakes + real.shape[0]
    inputs = jnp.concatenate([fake[...], real[...]], axis=0)
    pre_act = low_dot(inputs, feat[...])
    features = (pre_act * jax.nn.sigmoid(pre_act)).astype(bf16)
    projected = low_dot(features, proj[...]).astype(bf16)
    critic_act = low_dot(projected, spectral)
    opened = jax.nn.sigmoid(critic_act)
    activated = critic_act * opened
    logits = jnp.sum(activated * head[...], axis=1, keepdims=True) + offset[0]
    row = lax.broadcasted_iota(jnp.int32, (rows, 1), 0)
    sign = jnp.where(row < fakes, 1.0, -1.0)
    valid = jnp.logical_or(row >= fakes, (row % SUBLANES) < side)
    margin = 1.0 + sign * logits
    soft = jnp.maximum(margin, 0.0) + jnp.log1p(jnp.exp(-jnp.abs(margin)))
    loss = jnp.sum(jnp.where(valid, soft, 0.0))
    dlogit = jnp.where(valid, sign * jax.nn.sigmoid(margin), 0.0) / patches
    slope = opened * (1.0 + critic_act * (1.0 - opened))
    dact = (dlogit * head[...] * slope).astype(bf16)
    dspec[...] = lax.dot_general(
        projected, dact, (((0,), (0,)), ((), ())), preferred_element_type=jnp.float32
    )
    dhead = jnp.sum(dlogit * activated, axis=0, keepdims=True)
    wide = dhead.shape[1] // LANES
    lane = lane_of((1, LANES))
    last = jnp.where(lane == 0, jnp.sum(dlogit), jnp.where(lane == 1, loss, 0.0))
    pieces = [dhead[:, k * LANES : (k + 1) * LANES] for k in range(wide)] + [last]
    tail[...] = jnp.concatenate(
        pieces + [jnp.zeros((SUBLANES - len(pieces), LANES), jnp.float32)], axis=0
    )
    turn = (((1,), (1,)), ((), ()))
    dproj = lax.dot_general(
        dact[:fakes], spectral, turn, preferred_element_type=jnp.float32
    ).astype(bf16)
    dpre = lax.dot_general(dproj, proj[...], turn, preferred_element_type=jnp.float32)
    before = pre_act[:fakes]
    dpre = (dpre * silu_slope(before)).astype(bf16)
    dfake[...] = lax.dot_general(
        dpre, feat[...], turn, preferred_element_type=jnp.float32
    ).astype(bf16)


def critic_step(side, patches, fake, real, feat, proj, critic, power, head, offset):
    f32 = jnp.float32
    size = critic.shape[0]
    vmem = pl.BlockSpec(memory_space=pltpu.VMEM)
    return pl.pallas_call(
        partial(critic_kernel, side, patches),
        out_shape=[
            jax.ShapeDtypeStruct(fake.shape, jnp.bfloat16),
            jax.ShapeDtypeStruct(critic.shape, f32),
            jax.ShapeDtypeStruct((SUBLANES, LANES), f32),
            jax.ShapeDtypeStruct((size, 1), f32),
            jax.ShapeDtypeStruct((size, 1), f32),
            jax.ShapeDtypeStruct((SUBLANES, size), f32),
        ],
        in_specs=[vmem] * 7 + [pl.BlockSpec(memory_space=pltpu.SMEM)],
        compiler_params=pltpu.CompilerParams(vmem_limit_bytes=VMEM_BYTES),
        name="critic_step",
    )(fake, real, feat, proj, critic, power, head, offset)


def back_kernel(side, micros, pixel_count, grads, xn, lat, noise, consts, stats, opened, tail,
                dconv, block, dy, packed, product, gate8):
    images = lat.shape[0]
    half_in = lat.shape[3]
    channels = 2 * half_in
    rows_image = lat.shape[2]
    lines = micros * side
    bf16 = jnp.bfloat16
    shape3 = (lines, SUBLANES, LANES)
    lane = lane_of(shape3)
    row_first = (lane // 64) == 0
    col_first = ((lane // 32) % 2) == 0
    first_half = (lane % 32) < 16
    inside = lax.broadcasted_iota(jnp.int32, shape3, 1) < side
    gain_noise = consts[0:1, :][None]
    gain = consts[1:2, :][None]
    bias = consts[2:3, :][None]
    zero = jnp.zeros((SUBLANES, LANES), jnp.float32)
    second = lax.axis_index("segment") == 1
    gate8[...] = jnp.broadcast_to(opened[...][:, None, :], gate8.shape)

    def through_gate(img, carry):
        ascent = -grads[img].astype(jnp.float32).reshape(shape3)
        ascent = jnp.where(second, pltpu.roll(ascent, LANES - 16, 2), ascent)
        ascent = jnp.where(first_half, ascent, 0.0)
        centred = xn[img]
        y = centred * gain + bias
        gate = pltpu.roll(jax.nn.sigmoid(y), LANES - 16, 2)
        dopened = ascent * (y * gate)
        scale = jnp.concatenate(
            [jnp.broadcast_to(gate8[img * micros + m][None], (side, SUBLANES, LANES)) for m in range(micros)],
            axis=0,
        )
        dgated = ascent * scale
        dnormed = jnp.where(
            first_half, dgated * gate, pltpu.roll(dgated * y * gate * (1.0 - gate), 16, 2)
        )
        dy[img] = dnormed
        new = []
        for m in range(micros):
            part = slice(m * side, (m + 1) * side)
            total = jnp.sum(fold(jnp.sum(dopened[part], axis=0)), axis=0, keepdims=True)
            gate_now = gate8[img * micros + m][0:1]
            block[pl.ds(img * micros + m, 1), :] = total * gate_now * (1.0 - gate_now)
            new.append(carry[2 * m] + jnp.sum(dnormed[part] * centred[part], axis=0))
            new.append(carry[2 * m + 1] + jnp.sum(dnormed[part], axis=0))
        return tuple(new)

    sums = lax.fori_loop(0, images, through_gate, (zero,) * (2 * micros))
    sums = [jnp.sum(fold(s), axis=0, keepdims=True) for s in sums]
    gain_row = consts[1:2, :]
    mean_back = per_micro([gain_row * sums[2 * m + 1] / pixel_count for m in range(micros)], side)
    cross_back = per_micro([gain_row * sums[2 * m] / pixel_count for m in range(micros)], side)
    std12 = per_micro([stats[m : m + 1, :] for m in range(micros)], side)
    taps = 9
    groups = (taps + 3) // 4
    lane48 = lane_of((lines * SUBLANES, LANES)) // 32

    def through_norm(img, carry):
        centred = xn[img]
        dshift = (dy[img] * gain - mean_back - centred * cross_back) * std12
        dshift = jnp.where(inside, dshift, 0.0)
        carry = carry + jnp.sum(dshift * noise[img], axis=0)
        dh = dshift.astype(bf16).astype(jnp.float32)
        swapped = jnp.where(col_first, pltpu.roll(dh, LANES - 32, 2), pltpu.roll(dh, 32, 2))
        col0 = jnp.where(col_first, dh, swapped)
        col1 = jnp.where(col_first, swapped, dh)
        by_col = [
            col1 + pltpu.roll(col0, SUBLANES - 1, 1),
            col0 + col1,
            col0 + pltpu.roll(col1, 1, 1),
        ]
        found = [None] * taps
        for kx in range(3):
            value = by_col[kx]
            turned = pltpu.roll(value, 64, 2)
            row0 = jnp.where(row_first, value, turned)
            row1 = jnp.where(row_first, turned, value)
            found[kx] = row1 + shift_rows(row0, side, -1)
            found[3 + kx] = row0 + row1
            found[6 + kx] = row0 + shift_rows(row1, side, 1)
        for g in range(groups):
            members = found[4 * g : 4 * g + 4]
            value = members[0].reshape(lines * SUBLANES, LANES)
            for k in range(1, len(members)):
                value = jnp.where(lane48 == k, members[k].reshape(lines * SUBLANES, LANES), value)
            top = value.astype(bf16)
            packed[img, :, g * LANES : (g + 1) * LANES] = top
            packed[img, :, (groups + g) * LANES : (groups + g + 1) * LANES] = (
                value - top.astype(jnp.float32)
            ).astype(bf16)
        return carry

    dgain_noise = lax.fori_loop(0, images, through_norm, zero)
    count = images * micros
    block[count : count + 1, :] = jnp.sum(fold(dgain_noise), axis=0, keepdims=True)
    block[count + 1 : count + 2, :] = sum(sums[2 * m] for m in range(micros))
    block[count + 2 : count + 3, :] = sum(sums[2 * m + 1] for m in range(micros))
    block[count + 3 : count + 8, :] = jnp.zeros((5, LANES), jnp.float32)
    block[count + 8 : count + 16, :] = tail[...]

    width = groups * LANES
    flat = packed[...].reshape(images * rows_image, 2 * width)
    for p in range(2):
        side_rows = lat[:, p].reshape(images * rows_image, half_in)
        both = lax.dot_general(
            side_rows, flat, (((0,), (0,)), ((), ())), preferred_element_type=jnp.float32
        )
        product[p * half_in : (p + 1) * half_in, :] = both[:, :width] + both[:, width:]
    depth = dconv.shape[1]
    unit = 16
    place = lane_of((unit, LANES)) // 32
    for chip in range(dconv.shape[0]):
        for at in range(0, depth, unit):
            value = None
            for g in range(4):
                tap, channel = divmod((chip * 4 + g) * depth + at, channels)
                piece = product[channel : channel + unit, (tap // 4) * LANES : (tap // 4 + 1) * LANES]
                turn = (32 * (g - tap % 4)) % LANES
                if turn:
                    piece = pltpu.roll(piece, turn, 1)
                value = piece if value is None else jnp.where(place == g, piece, value)
            dconv[chip, at : at + unit, :] = value.astype(bf16)


def back(side, pixel_count, chips, depth, grads, xn, lat, noise, consts, stats, opened, tail):
    images, _, rows_image, half_in = lat.shape
    micros = rows_image // (side * SUBLANES)
    lines = micros * side
    count = images * micros
    f32 = jnp.float32
    return pl.pallas_call(
        partial(back_kernel, side, micros, pixel_count),
        out_shape=[
            jax.ShapeDtypeStruct((chips, depth, LANES), jnp.bfloat16),
            jax.ShapeDtypeStruct((count + 16, LANES), f32),
        ],
        scratch_shapes=[
            pltpu.VMEM((images, lines, SUBLANES, LANES), f32),
            pltpu.VMEM((images, rows_image, 6 * LANES), jnp.bfloat16),
            pltpu.VMEM((2 * half_in, 3 * LANES), f32),
            pltpu.VMEM((count, SUBLANES, LANES), f32),
        ],
        compiler_params=pltpu.CompilerParams(vmem_limit_bytes=VMEM_BYTES),
        name="back",
    )(grads, xn, lat, noise, consts, stats, opened, tail)


def ortho_by_gram(momentum, gram):
    norm = jnp.sqrt(jnp.trace(gram)) + 1e-07
    x = momentum / norm
    gram = gram / (norm * norm)
    for step in range(NS_STEPS):
        square = mid_dot(gram, gram)
        poly = NEWTON_B * gram + NEWTON_C * square
        x = NEWTON_A * x + mid_dot(x, poly)
        if step < NS_STEPS - 1:
            once = NEWTON_A * gram + mid_dot(poly, gram)
            gram = NEWTON_A * once + mid_dot(once, poly)
    return x


def ortho_whole(momentum):
    x = momentum / (jnp.sqrt(jnp.sum(momentum * momentum)) + 1e-07)
    for _ in range(NS_STEPS):
        gram = high_dot(x.T, x)
        once = high_dot(x, gram)
        x = NEWTON_A * x + NEWTON_B * once + NEWTON_C * high_dot(once, gram)
    return x


def by_channels(
    latent,
    noise,
    real_bank,
    real_index,
    frozen_feat,
    frozen_proj,
    power_vec,
    conv_w,
    conv_mom,
    squeeze_w,
    squeeze_mom,
    excite_w,
    excite_mom,
    critic_w,
    critic_mom,
    vectors,
    vec_m,
    vec_v,
):
    n = lax.axis_size("dp")
    chip, side = lax.axis_index("dp"), lax.axis_index("segment")
    bf16, f32 = jnp.bfloat16, jnp.float32
    micros, _, edge, _, channels = latent.shape
    pixels = noise.shape[2]
    rows, widths = conv_w.shape
    half = widths // 2
    own = half // n // 2
    depth = rows // 4
    proj_width = critic_w.shape[1]
    pixel_count = pixels * n
    patches = micros * pixel_count

    def half_of(value, axis):
        size = value.shape[axis] // 2
        return lax.dynamic_slice_in_dim(value, side * size, size, axis)

    lat_own = jnp.pad(latent[:, 0], ((0, 0), (0, 0), (0, SUBLANES - edge), (0, 0)))
    lat_own = half_of(lat_own.reshape(micros * edge * SUBLANES, channels), 1)
    conv_own = conv_w.astype(bf16).reshape(4, depth, 2, n, 2, own)
    conv_own = lax.dynamic_index_in_dim(conv_own, side, 4, keepdims=False)
    conv_own = conv_own.transpose(3, 1, 0, 2, 4).reshape(n, depth, LANES)
    noise_own = jnp.pad(noise.reshape(-1), (0, SUBLANES * LANES - micros * pixels))
    noise_own = noise_own.reshape(SUBLANES, LANES)
    lat, conv, noise_all, squeeze_low, excite_low, critic_low = exchange(
        n,
        1,
        [("gather", True), ("a2a", False), ("gather", False)] + [("gather", True)] * 3,
        [
            lat_own,
            conv_own,
            noise_own,
            half_of(squeeze_w.astype(bf16), 0),
            half_of(excite_w.astype(bf16), 0),
            half_of(critic_w.astype(bf16), 0),
        ],
    )
    squeeze_low = squeeze_low.reshape(channels, half)
    excite_low = excite_low.reshape(half, half)
    critic_low = critic_low.reshape(proj_width, proj_width)

    noise_map = noise_all.reshape(n, -1)[:, : micros * pixels]
    noise_map = noise_map.reshape(n, micros, edge, 2, edge, 2).transpose(0, 1, 2, 4, 3, 5)
    noise_map = jnp.pad(noise_map, ((0, 0),) * 3 + ((0, SUBLANES - edge),) + ((0, 0),) * 2)
    noise_map = jnp.repeat(noise_map.reshape(n, micros * edge, SUBLANES, 4), LANES // 4, axis=3)
    consts = vectors[: 3 * widths].reshape(3, 2, n, 2, own)
    consts = lax.dynamic_slice(consts, (0, 0, chip, side, 0), (3, 2, 1, 1, own)).reshape(3, 2 * own)
    consts = jnp.pad(jnp.tile(consts, (1, 4)), ((0, SUBLANES - 3), (0, 0)))
    excite_cols = lax.dynamic_slice_in_dim(excite_low, (2 * chip + side) * own, own, 1)
    excite_cols = jnp.tile(excite_cols, (1, LANES // own))
    fake, xn, stats, opened, z1, pooled = front(
        edge, pixel_count, lat, conv, noise_map, consts, squeeze_low, excite_cols
    )

    (arrived,) = exchange(n, 2, [("a2a", True)], [fake])
    lines = edge * SUBLANES
    maps = arrived.reshape(n, 2, lines, 4, micros, own)
    maps = lax.dynamic_index_in_dim(maps, side, 4, keepdims=False)
    maps = maps.transpose(3, 2, 0, 1, 4).reshape(4 * lines, half)
    real_map = real_bank[lax.dynamic_index_in_dim(real_index, side, 0, keepdims=False)[0]]
    head = vectors[3 * widths : 3 * widths + proj_width].reshape(1, proj_width)
    offset = vectors[3 * widths + proj_width :].reshape(1)
    dfake, dspec, tail, column_v, column_t, row_w = critic_step(
        edge,
        patches,
        maps,
        real_map,
        frozen_feat,
        frozen_proj,
        critic_low,
        power_vec.reshape(1, -1),
        head,
        offset,
    )

    dfake = dfake.reshape(4, lines, n, LANES // 4).transpose(2, 1, 0, 3).reshape(n, lines, LANES)
    dspec = dspec.reshape(n, 2, proj_width // n // 2, proj_width)
    mine = lax.dynamic_index_in_dim(dspec, side, 1, keepdims=False)
    theirs = lax.dynamic_index_in_dim(dspec, 1 - side, 1, keepdims=False)
    returned, added = exchange(n, 3, [("a2a", True), ("sib", False)], [dfake, theirs])
    dspec = mine + added
    dconv, block = back(
        edge, pixel_count, n, depth, returned, xn, lat, noise_map, consts, stats, opened, tail
    )

    dconv, blocks, dspec = exchange(
        n, 4, [("a2a", True), ("gather", True), ("a2a", False)], [dconv, block, dspec]
    )
    dspec = jnp.sum(dspec, axis=0)
    count = n * micros
    conv_grad = dconv.astype(f32).reshape(n, 2, depth, 4, 2, own).transpose(3, 2, 4, 0, 1, 5)
    conv_mom_new = MOMENTUM * conv_mom + conv_grad.reshape(rows, widths)
    mine = lax.dynamic_index_in_dim(
        conv_mom_new.reshape(rows, n, 2, own * 2), side, 2, keepdims=False
    )
    part = mid_dot(mine.reshape(rows, half).T, conv_mom_new)
    parts, dspec, squeeze_mom_all, excite_mom_all, critic_mom_all = exchange(
        n,
        5,
        [("a2a", False)] + [("gather", True)] * 4,
        [
            part.reshape(n, widths // n // 2, widths),
            dspec,
            half_of(squeeze_mom, 0),
            half_of(excite_mom, 0),
            half_of(critic_mom, 0),
        ],
    )
    (gram,) = exchange(n, 6, [("gather", True)], [jnp.sum(parts, axis=0)])
    gram = gram.reshape(widths, widths)

    dspec = dspec.reshape(proj_width, proj_width)
    critic_f = critic_low.astype(f32)
    sigma = jnp.sqrt(jnp.sum(jnp.square(low_norm(critic_f, column_v))))
    along = jnp.sum(dspec * critic_f) / (sigma * sigma)
    direction = column_v * row_w[0:1] + column_t * power_vec[None, :]
    critic_grad = dspec / sigma - along * direction
    dze = blocks[:, :, :count, :own].transpose(2, 0, 1, 3).reshape(count, half)
    squeezed = z1 * jax.nn.sigmoid(z1)
    excite_grad = high_dot(squeezed.T, dze)
    dz1 = high_dot(dze, excite_low.astype(f32).T) * silu_slope(z1)
    squeeze_grad = high_dot(pooled.T, dz1)

    gains = blocks[:, :, count : count + 3, : 2 * own].reshape(n, 2, 3, 2, own)
    gains = gains.transpose(2, 3, 0, 1, 4).reshape(3 * widths)
    tails = jnp.sum(blocks[:, :, count + 8 :, :], axis=(0, 1))
    last = proj_width // LANES
    vector_grad = jnp.concatenate([gains, tails[:last].reshape(-1), tails[last, :1]])
    loss_sum = tails[last, 1]
    vec_m_new, vec_v_new, vectors_new = adam(vectors, vec_m, vec_v, vector_grad)

    whole = [
        MOMENTUM * mom.reshape(grad.shape) + grad
        for mom, grad in (
            (squeeze_mom_all, squeeze_grad),
            (excite_mom_all, excite_grad),
            (critic_mom_all, critic_grad),
        )
    ]

    def rows_of(value):
        size = value.shape[0] // n
        return lax.dynamic_slice_in_dim(value, chip * size, size, 0)

    small_moms = [rows_of(value) for value in whole]

    def on_first():
        return ortho_by_gram(conv_mom_new, gram), *[jnp.zeros_like(value) for value in small_moms]

    def on_second():
        return jnp.zeros_like(conv_mom_new), *[rows_of(ortho_whole(value)) for value in whole]

    steps = lax.cond(side == 0, on_first, on_second)
    others = exchange(n, 7, [("sib", False)] * 4, list(steps))
    conv_step = jnp.where(side == 0, steps[0], others[0])
    small_steps = [jnp.where(side == 0, b, a) for a, b in zip(steps[1:], others[1:])]
    keep = 1.0 - MUON_RATE * DECAY
    conv_new = conv_w * keep - MUON_RATE * conv_step
    small_new = [
        weight * keep - MUON_RATE * step
        for weight, step in zip((squeeze_w, excite_w, critic_w), small_steps)
    ]
    return (
        loss_sum,
        conv_mom_new,
        conv_new,
        small_moms[0],
        small_new[0],
        small_moms[1],
        small_new[1],
        small_moms[2],
        small_new[2],
        vec_m_new,
        vec_v_new,
        vectors_new,
    )


def low_norm(weight, vector):
    return jnp.sum(weight * vector, axis=0)


def shifted_2(value, axis, steps):
    count = lax.axis_size(axis)
    leading, last = (max(0, -steps), min(count, count - steps))
    return lax.ppermute(value, axis, [(source, source + steps) for source in range(leading, last)])


def for_sending(x):
    return jax.tree.map(lambda a: a.astype(jnp.bfloat16) if a.dtype == jnp.float32 else a, x)


def only_if(flag, compute):

    def empty_branch():
        return jax.tree.map(jnp.zeros_like, compute())

    return lax.cond(flag, compute, empty_branch)


def columns(latent_now):
    upsampled = jnp.repeat(jnp.repeat(latent_now, 2, axis=1), 2, axis=2)
    side_now = upsampled.shape[1]
    padded = jnp.pad(upsampled, ((0, 0), (1, 1), (1, 1), (0, 0)))
    taps = [
        padded[:, row_tap : row_tap + side_now, col_tap : col_tap + side_now, :]
        for row_tap in range(3)
        for col_tap in range(3)
    ]
    return jnp.concatenate(taps, axis=-1).reshape(-1, 9 * upsampled.shape[3])


def spectral_norm(weight, power):
    vector = high_dot(weight, power)
    vector = vector * lax.rsqrt(jnp.sum(vector * vector))
    product_one = high_dot(vector, weight)
    return weight / jnp.sqrt(jnp.sum(product_one * product_one))


def excite(pooled, squeeze_w, excite_w):
    return jax.nn.sigmoid(high_dot(jax.nn.silu(high_dot(pooled, squeeze_w)), excite_w))


def normalize(shifted, moments, pixel_count, bn_gain, bn_bias):
    mean_vec = moments[0] / pixel_count
    inv_std = lax.rsqrt(moments[1] / pixel_count - mean_vec * mean_vec + NORM_EPS)
    centred = (shifted - mean_vec) * inv_std
    return (centred, inv_std, centred * bn_gain + bn_bias)


def critic_pass(
    inputs, sign, patches, frozen_feat, frozen_proj, spectral, out_weight, out_bias, want_input
):
    pre_act = low_dot(inputs, frozen_feat)
    features = jax.nn.silu(pre_act).astype(jnp.bfloat16)
    projected = low_dot(features, frozen_proj).astype(jnp.bfloat16)
    critic_act = low_dot(projected, spectral)
    activated = jax.nn.silu(critic_act)
    logits = high_dot(activated, out_weight) + out_bias
    loss_part = jnp.sum(jax.nn.softplus(1.0 + sign * logits))
    dlogit = sign * jax.nn.sigmoid(1.0 + sign * logits) / patches
    dact = (dlogit[:, None] * out_weight * silu_slope(critic_act)).astype(jnp.bfloat16)
    result = [loss_part, low_dot(projected.T, dact), high_dot(dlogit, activated), jnp.sum(dlogit)]
    if want_input:
        dproj = low_dot(dact, spectral.T).astype(jnp.bfloat16)
        dpre = (low_dot(dproj, frozen_proj.T) * silu_slope(pre_act)).astype(jnp.bfloat16)
        result.append(low_dot(dpre, frozen_feat.T).astype(jnp.bfloat16))
    return result


def orthogonalize(momenta):
    squares = lax.psum(
        (
            jnp.sum(momenta[0] * momenta[0]),
            jnp.sum(momenta[1] * momenta[1]),
            jnp.sum(momenta[2] * momenta[2]),
            jnp.sum(momenta[3] * momenta[3]),
        ),
        "dp",
    )
    current = [
        matrix_now / (jnp.sqrt(square_now) + 1e-07)
        for matrix_now, square_now in zip(momenta, squares)
    ]

    def iterate(_, current):
        partials = [
            lax.psum_scatter(
                high_dot(matrix_now.T, matrix_now), "dp", scatter_dimension=0, tiled=True
            )
            for matrix_now in current
        ]
        full_grams = [lax.all_gather(part, "dp", axis=0, tiled=True) for part in partials]
        updated = []
        for matrix_now, gram in zip(current, full_grams):
            product_one = high_dot(matrix_now, gram)
            updated.append(
                NEWTON_A * matrix_now
                + NEWTON_B * product_one
                + NEWTON_C * high_dot(product_one, gram)
            )
        return updated

    return lax.fori_loop(0, NS_STEPS, iterate, current)


def by_images(
    latent,
    noise,
    real_bank,
    real_index,
    frozen_feat,
    frozen_proj,
    power_vec,
    conv_w,
    conv_mom,
    squeeze_w,
    squeeze_mom,
    excite_w,
    excite_mom,
    critic_w,
    critic_mom,
    vectors,
    vec_m,
    vec_v,
):
    gathered = (
        lax.all_gather(conv_w.astype(jnp.bfloat16), "dp", axis=0, tiled=True),
        lax.all_gather(squeeze_w.astype(jnp.bfloat16), "dp", axis=0, tiled=True),
        lax.all_gather(excite_w.astype(jnp.bfloat16), "dp", axis=0, tiled=True),
        lax.all_gather(critic_w.astype(jnp.bfloat16), "dp", axis=0, tiled=True),
    )
    conv_low, squeeze_low, excite_low, critic_low = gathered
    squeeze_full = squeeze_low.astype(jnp.float32)
    excite_full = excite_low.astype(jnp.float32)
    spectral_full, spectral_back = jax.vjp(
        partial(spectral_norm, power=power_vec), critic_low.astype(jnp.float32)
    )
    spectral = spectral_full.astype(jnp.bfloat16)
    micro_count, images, pixels = (noise.shape[0], noise.shape[1], noise.shape[2])
    widths = conv_low.shape[1]
    half_width = widths // 2
    proj_width = critic_low.shape[0]
    tokens = images * pixels
    pixel_count = tokens * lax.axis_size("dp")
    patches = micro_count * pixel_count
    noise_gain = vectors[:widths]
    bn_gain = vectors[widths : 2 * widths]
    bn_bias = vectors[2 * widths : 3 * widths]
    out_weight = vectors[3 * widths : 3 * widths + proj_width]
    out_bias = vectors[3 * widths + proj_width]
    generator = lax.axis_index("segment") == 0
    critic_side = jnp.logical_not(generator)
    pooled = jnp.mean(latent.astype(jnp.float32), axis=(2, 3))
    conv_acc = jnp.zeros(conv_low.shape, jnp.float32)
    squeeze_acc = jnp.zeros(squeeze_low.shape, jnp.float32)
    excite_acc = jnp.zeros(excite_low.shape, jnp.float32)
    spectral_acc = jnp.zeros(critic_low.shape, jnp.float32)
    vector_acc = jnp.zeros(vectors.shape, jnp.float32)
    loss_acc = jnp.zeros((), jnp.float32)
    for micro_step in range(micro_count):
        noise_now = noise[micro_step].reshape(-1)
        excitation, excite_back = jax.vjp(excite, pooled[micro_step], squeeze_full, excite_full)

        def gen_front():
            patches_in = columns(latent[micro_step])
            return (patches_in, low_dot(patches_in, conv_low) + noise_now[:, None] * noise_gain)

        patches_in, shifted = only_if(generator, gen_front)
        moments = lax.psum((jnp.sum(shifted, axis=0), jnp.sum(shifted * shifted, axis=0)), "dp")

        def gen_mid():
            centred, inv_std, normed = normalize(shifted, moments, pixel_count, bn_gain, bn_bias)
            gated = normed[:, :half_width] * jax.nn.sigmoid(normed[:, half_width:])
            fake_map = gated.reshape(images, pixels, half_width) * excitation[:, None, :]
            return fake_map.reshape(tokens, half_width).astype(jnp.bfloat16)

        fake_map = only_if(generator, gen_mid)
        arrived = shifted_2(fake_map, "segment", 1)

        def critic_work():
            real_map = real_bank[real_index[micro_step]].reshape(tokens, half_width)
            real_out = critic_pass(
                real_map,
                -1.0,
                patches,
                frozen_feat,
                frozen_proj,
                spectral,
                out_weight,
                out_bias,
                False,
            )
            fake_out = critic_pass(
                arrived,
                1.0,
                patches,
                frozen_feat,
                frozen_proj,
                spectral,
                out_weight,
                out_bias,
                True,
            )
            return (
                real_out[0] + fake_out[0],
                real_out[1] + fake_out[1],
                real_out[2] + fake_out[2],
                real_out[3] + fake_out[3],
                fake_out[4],
            )

        loss_part, dspec_part, dout_part, dbias_part, input_grad = only_if(critic_side, critic_work)
        returned = jax.tree.map(
            lambda part, own: part.astype(own.dtype),
            shifted_2(for_sending(input_grad), "segment", -1),
            input_grad,
        )

        def gen_back():
            dfake = -returned.astype(jnp.float32).reshape(images, pixels, half_width)
            centred, inv_std, normed = normalize(shifted, moments, pixel_count, bn_gain, bn_bias)
            opened = jax.nn.sigmoid(normed[:, half_width:])
            first_half = normed[:, :half_width]
            gated = (first_half * opened).reshape(images, pixels, half_width)
            unused, dsqueeze, dexcite = excite_back(jnp.sum(dfake * gated, axis=1))
            dgated = (dfake * excitation[:, None, :]).reshape(tokens, half_width)
            dnormed = jnp.concatenate(
                [dgated * opened, dgated * first_half * opened * (1.0 - opened)], axis=1
            )
            return (
                dnormed * bn_gain,
                centred,
                inv_std,
                dsqueeze,
                dexcite,
                jnp.sum(dnormed * centred, axis=0),
                jnp.sum(dnormed, axis=0),
            )

        dcentred, centred, inv_std, dsqueeze, dexcite, dgain, dbias = only_if(generator, gen_back)
        back_sums = lax.psum((jnp.sum(dcentred, axis=0), jnp.sum(dcentred * centred, axis=0)), "dp")

        def gen_grad():
            dshifted = inv_std * (
                dcentred - back_sums[0] / pixel_count - centred * back_sums[1] / pixel_count
            )
            return (dshifted.astype(jnp.bfloat16), jnp.sum(dshifted * noise_now[:, None], axis=0))

        dhidden, dnoise = only_if(generator, gen_grad)
        conv_acc = conv_acc + only_if(generator, lambda: low_dot(patches_in.T, dhidden))
        squeeze_acc = squeeze_acc + dsqueeze
        excite_acc = excite_acc + dexcite
        spectral_acc = spectral_acc + dspec_part
        vector_acc = vector_acc + jnp.concatenate(
            [dnoise, dgain, dbias, dout_part, dbias_part[None]]
        )
        loss_acc = loss_acc + loss_part
    critic_grad = spectral_back(spectral_acc)[0]
    conv_rows_sum, squeeze_rows, excite_rows, critic_rows = (
        lax.psum_scatter(conv_acc, "dp", scatter_dimension=0, tiled=True),
        lax.psum_scatter(squeeze_acc, "dp", scatter_dimension=0, tiled=True),
        lax.psum_scatter(excite_acc, "dp", scatter_dimension=0, tiled=True),
        lax.psum_scatter(critic_grad, "dp", scatter_dimension=0, tiled=True),
    )
    gradients = lax.psum((conv_rows_sum, squeeze_rows, excite_rows, critic_rows), "segment")
    vector_grad, loss_sum = lax.psum((vector_acc, loss_acc), ("segment", "dp"))
    weights = (conv_w, squeeze_w, excite_w, critic_w)
    new_moms = [
        MOMENTUM * old_mom + grad_now
        for old_mom, grad_now in zip((conv_mom, squeeze_mom, excite_mom, critic_mom), gradients)
    ]
    ortho = orthogonalize(new_moms)
    new_weights = [
        weight * (1.0 - MUON_RATE * DECAY) - MUON_RATE * step_dir
        for weight, step_dir in zip(weights, ortho)
    ]
    vec_m_new, vec_v_new, vectors_new = adam(vectors, vec_m, vec_v, vector_grad)
    return (
        loss_sum,
        new_moms[0],
        new_weights[0],
        new_moms[1],
        new_weights[1],
        new_moms[2],
        new_weights[2],
        new_moms[3],
        new_weights[3],
        vec_m_new,
        vec_v_new,
        vectors_new,
    )


def solution(mesh):
    placed = (
        P(None, "dp", None, None, None),
        P(None, "dp", None),
        P("dp", None, None),
        P(None, "dp"),
        P(),
        P(),
        P(),
        P("dp", None),
        P("dp", None),
        P("dp", None),
        P("dp", None),
        P("dp", None),
        P("dp", None),
        P("dp", None),
        P("dp", None),
        P(),
        P(),
        P(),
    )
    given = (
        P(),
        P("dp", None),
        P("dp", None),
        P("dp", None),
        P("dp", None),
        P("dp", None),
        P("dp", None),
        P("dp", None),
        P("dp", None),
        P(),
        P(),
        P(),
    )

    def step(latent, noise, *rest):
        n, sides = mesh.shape["dp"], mesh.shape["segment"]
        micros, images, edge = latent.shape[:3]
        fits = (
            n == 16
            and sides == 2
            and images == n
            and micros == 2
            and edge <= SUBLANES - 1
            and rest[5].shape[1] == 2 * n * sides * 16
        )
        plan = by_channels if fits else by_images
        return jax.shard_map(
            plan, mesh=mesh, in_specs=placed, out_specs=given, check_vma=False
        )(latent, noise, *rest)

    return step
```

```python
from functools import partial

import jax
import jax.numpy as jnp
from jax import lax
from jax.experimental import pallas as pl
from jax.experimental.pallas import tpu as pltpu
from jax.sharding import PartitionSpec as P

NS_STEPS = 5
STEP = 10


HIGHEST_PREC = lax.Precision.HIGHEST
HIGH_PREC = lax.Precision.HIGH
MESH = pl.DeviceIdType.MESH
NORM_EPS = 1e-05
NEWTON_A = 3.4445
NEWTON_B = -4.775
NEWTON_C = 2.0315
MOMENTUM = 0.95
MUON_RATE = 0.5
DECAY = 0.01
ADAM_RATE = 0.2
ADAM_BETA1 = 0.9
ADAM_BETA2 = 0.95
ADAM_EPS = 1e-08
LANES = 128
SUBLANES = 8
PLANE = 4
BLOCK = 256
VMEM_BYTES = 56 * 1024 * 1024


def low_dot(left, right):
    return jnp.dot(left, right, preferred_element_type=jnp.float32)


def high_dot(left, right):
    return jnp.dot(left, right, precision=HIGHEST_PREC, preferred_element_type=jnp.float32)


def mid_dot(left, right):
    return jnp.dot(left, right, precision=HIGH_PREC, preferred_element_type=jnp.float32)


def silu_slope(value):
    opened = jax.nn.sigmoid(value)
    return opened * (1.0 + value * (1.0 - opened))


def adam(vectors, vec_m, vec_v, vector_grad):
    vec_m_new = ADAM_BETA1 * vec_m + (1.0 - ADAM_BETA1) * vector_grad
    vec_v_new = ADAM_BETA2 * vec_v + (1.0 - ADAM_BETA2) * vector_grad * vector_grad
    first_hat = vec_m_new / (1.0 - ADAM_BETA1**STEP)
    second_hat = vec_v_new / (1.0 - ADAM_BETA2**STEP)
    vectors_new = vectors * (1.0 - ADAM_RATE * DECAY) - ADAM_RATE * first_hat / (
        jnp.sqrt(second_hat) + ADAM_EPS
    )
    return vec_m_new, vec_v_new, vectors_new


def exchange(n, ident, plans, arrays):
    count = len(plans)
    kinds = [kind for kind, _ in plans]

    def shape(kind, paired, x):
        if kind == "sib":
            return jax.ShapeDtypeStruct(x.shape, x.dtype)
        if kind == "cross":
            return jax.ShapeDtypeStruct((x.shape[0],) + x.shape[2:], x.dtype)
        block = x.shape if kind == "relay" else x.shape[1:]
        return jax.ShapeDtypeStruct(((n, 2) if paired else (n,)) + block, x.dtype)

    outs = [shape(kind, paired, x) for (kind, paired), x in zip(plans, arrays)]
    direct = [a for a in range(count) if kinds[a] == "a2a"]
    single = [a for a in range(count) if kinds[a] in ("sib", "cross")]
    passing = [a for a in direct if plans[a][1]]
    parts = []
    for a in range(count):
        if kinds[a] == "relay":
            rows = arrays[a].shape[0]
            unit = 16 if arrays[a].dtype == jnp.bfloat16 else 8
            if rows % (2 * unit) == 0:
                parts += [(a, 0, rows // 2, 0), (a, rows // 2, rows // 2, 1)]
            else:
                parts.append((a, 0, rows, 0))
    planes = n // PLANE

    def body(*refs):
        ins, results = refs[:count], refs[count : 2 * count]
        (send, recv, pass_send, pass_recv, here, part_recv, up_send, down_send, first_send,
         second_send, core_send, core_recv, part_here) = refs[2 * count :]
        me, side = lax.axis_index("dp"), lax.axis_index("segment")
        other = 1 - side
        z, spot = me // PLANE, me % PLANE
        beside = (spot + 1 - 2 * (spot % 2), (spot + 2) % PLANE)
        across = PLANE - 1 - spot
        barrier = pltpu.get_barrier_semaphore()

        def greet(where):
            pl.semaphore_signal(barrier, inc=1, device_id=where, device_id_type=MESH)

        greeted = 0
        if direct:

            @pl.loop(1, n)
            def _(k):
                greet({"dp": lax.rem(me + k, n)})

            greeted += n - 1
        elif parts:

            @pl.loop(1, planes)
            def _(k):
                greet({"dp": lax.rem(me + k * PLANE, n)})

            for spot_now in beside:
                greet({"dp": z * PLANE + spot_now})
            greeted += planes + 1
        if passing or single or parts:
            greet({"segment": other})
            greeted += 1
        pl.semaphore_wait(barrier, greeted)

        def remote(src, dst, send_sem, recv_sem, where):
            return pltpu.make_async_remote_copy(
                src_ref=src,
                dst_ref=dst,
                send_sem=send_sem,
                recv_sem=recv_sem,
                device_id=where,
                device_id_type=MESH,
            )

        def place(p, owner, of_side):
            a, first, rows, _ = parts[p]
            return results[a].at[owner, of_side, pl.ds(first, rows)]

        def mine(p):
            a, first, rows, _ = parts[p]
            return ins[a].at[pl.ds(first, rows)]

        def hop(p, sems, owner, chip, src=None):
            held = place(p, owner, side)
            return remote(
                held if src is None else src, held, sems.at[p, owner], part_recv.at[p, owner], {"dp": chip}
            )

        def to_core(p, owner, of_side, src=None):
            held = place(p, owner, of_side)
            return remote(
                held if src is None else src,
                held,
                core_send.at[p, owner],
                core_recv.at[p, owner],
                {"segment": other},
            )

        def arrived(p, owner):
            hop(p, first_send, owner, owner).wait_recv()

        def next_to(p, order):
            return z * PLANE + beside[parts[p][3] if order == 0 else 1 - parts[p][3]]

        def spread(p, owner, stage, src=None):
            if stage < 1:
                hop(p, first_send, owner, next_to(p, 0), src).start()
            if stage < 2:
                hop(p, second_send, owner, next_to(p, 1), src).start()
            to_core(p, owner, side, src).start()

        every = range(len(parts))
        for p in every:

            @pl.when(z < planes - 1)
            def _():
                hop(p, up_send, me, me + PLANE, mine(p)).start()

            @pl.when(z > 0)
            def _():
                hop(p, down_send, me, me - PLANE, mine(p)).start()

            spread(p, me, 0, mine(p))
            pltpu.make_async_copy(mine(p), place(p, me, side), part_here.at[p]).start()

        def source(a, peer):
            return ins[a].at[peer]

        def slot(a, owner, of_side):
            return results[a].at[owner, of_side] if plans[a][1] else results[a].at[owner]

        def outgoing(a, k):
            peer = lax.rem(me + k, n)
            return remote(source(a, peer), slot(a, me, side), send.at[a, k], recv.at[a, me], {"dp": peer})

        def incoming(a, owner):
            return remote(
                source(a, owner), slot(a, owner, side), send.at[a, 0], recv.at[a, owner], {"dp": owner}
            )

        def passed(a, src, owner, of_side):
            return remote(
                src,
                slot(a, owner, of_side),
                pass_send.at[a, owner],
                pass_recv.at[a, owner],
                {"segment": other},
            )

        def sibling(a):
            src = ins[a].at[:, other] if kinds[a] == "cross" else ins[a]
            return remote(
                src, results[a], pass_send.at[a, 0], pass_recv.at[a, 0], {"segment": other}
            )

        def own(a):
            return pltpu.make_async_copy(source(a, me), slot(a, me, side), here.at[a])

        if direct:

            @pl.loop(1, n)
            def _(k):
                for a in direct:
                    outgoing(a, k).start()

            for a in direct:
                own(a).start()
            for a in passing:
                passed(a, source(a, me), me, side).start()
        for a in single:
            sibling(a).start()

        if parts:
            for d in range(1, planes):
                for p in every:

                    @pl.when(z - d >= 0)
                    def _():
                        owner = me - d * PLANE
                        arrived(p, owner)

                        @pl.when(z < planes - 1)
                        def _():
                            hop(p, up_send, owner, me + PLANE).start()

                        spread(p, owner, 0)

                    @pl.when(z + d < planes)
                    def _():
                        owner = me + d * PLANE
                        arrived(p, owner)

                        @pl.when(z > 0)
                        def _():
                            hop(p, down_send, owner, me - PLANE).start()

                        spread(p, owner, 0)

            @pl.loop(0, planes)
            def _(k):
                line = lax.rem(z + k, planes) * PLANE
                for p in every:
                    owner = line + beside[parts[p][3]]
                    arrived(p, owner)
                    spread(p, owner, 1)

            @pl.loop(0, planes)
            def _(k):
                line = lax.rem(z + k, planes) * PLANE
                for p in every:
                    for spot_now in (beside[1 - parts[p][3]], across):
                        owner = line + spot_now
                        arrived(p, owner)
                        spread(p, owner, 2)

        if direct:

            @pl.loop(1, n)
            def _(k):
                owner = lax.rem(me + n - k, n)
                for a in direct:
                    incoming(a, owner).wait_recv()
                    if plans[a][1]:
                        passed(a, slot(a, owner, side), owner, side).start()

            for a in direct:
                own(a).wait()

            @pl.loop(1, n)
            def _(k):
                for a in direct:
                    outgoing(a, k).wait_send()

        if passing:

            @pl.loop(0, n)
            def _(k):
                for a in passing:
                    passed(a, slot(a, k, side), k, side).wait_send()
                    passed(a, slot(a, k, other), k, other).wait_recv()

        for a in single:
            sibling(a).wait()

        if parts:
            for p in every:
                pltpu.make_async_copy(mine(p), place(p, me, side), part_here.at[p]).wait()
                for d in range(0, planes):

                    @pl.when(jnp.logical_and(z - d >= 0, z < planes - 1))
                    def _():
                        hop(p, up_send, me - d * PLANE, me + PLANE).wait_send()

                    @pl.when(jnp.logical_and(z + d < planes, z > 0))
                    def _():
                        hop(p, down_send, me + d * PLANE, me - PLANE).wait_send()

            @pl.loop(0, planes)
            def _(k):
                for p in every:
                    hop(p, first_send, k * PLANE + spot, next_to(p, 0)).wait_send()
                    hop(p, second_send, k * PLANE + spot, next_to(p, 1)).wait_send()
                    hop(p, second_send, k * PLANE + beside[parts[p][3]], next_to(p, 1)).wait_send()

            @pl.loop(0, n)
            def _(k):
                for p in every:
                    to_core(p, k, side).wait_send()
                    to_core(p, k, other).wait_recv()

    anywhere = pl.BlockSpec(memory_space=pl.ANY)
    relays = max(len(parts), 1)
    return pl.pallas_call(
        body,
        out_shape=outs,
        in_specs=[anywhere] * count,
        out_specs=[anywhere] * count,
        scratch_shapes=[pltpu.SemaphoreType.DMA((count, n))] * 4
        + [pltpu.SemaphoreType.DMA((count,))]
        + [pltpu.SemaphoreType.DMA((relays, n))] * 7
        + [pltpu.SemaphoreType.DMA((relays,))],
        compiler_params=pltpu.CompilerParams(collective_id=ident, has_side_effects=True),
        name=f"exchange_{ident}",
    )(*arrays)


def share(ident, of_first, of_second):
    def body(first, second, first_out, second_out, send, recv):
        side = lax.axis_index("segment")
        other = 1 - side
        barrier = pltpu.get_barrier_semaphore()
        pl.semaphore_signal(barrier, inc=1, device_id={"segment": other}, device_id_type=MESH)
        pl.semaphore_wait(barrier, 1)
        pairs = ((first, first_out), (second, second_out))

        def over(k):
            return pltpu.make_async_remote_copy(
                src_ref=pairs[k][0],
                dst_ref=pairs[k][1],
                send_sem=send.at[k],
                recv_sem=recv.at[k],
                device_id={"segment": other},
                device_id_type=MESH,
            )

        for k in range(2):

            @pl.when(side == k)
            def _():
                over(k).start()
                over(1 - k).wait_recv()
                over(k).wait_send()

    anywhere = pl.BlockSpec(memory_space=pl.ANY)
    arrived = pl.pallas_call(
        body,
        out_shape=[jax.ShapeDtypeStruct(x.shape, x.dtype) for x in (of_first, of_second)],
        in_specs=[anywhere] * 2,
        out_specs=[anywhere] * 2,
        scratch_shapes=[pltpu.SemaphoreType.DMA((2,))] * 2,
        compiler_params=pltpu.CompilerParams(collective_id=ident, has_side_effects=True),
        name="share",
    )(of_first, of_second)
    is_first = lax.axis_index("segment") == 0
    return jnp.where(is_first, of_first, arrived[0]), jnp.where(is_first, arrived[1], of_second)


def local_call(kernel, name, out_shape, scratch, arguments, specs=None):
    return pl.pallas_call(
        kernel,
        out_shape=out_shape,
        in_specs=specs or [pl.BlockSpec(memory_space=pltpu.VMEM)] * len(arguments),
        scratch_shapes=scratch,
        compiler_params=pltpu.CompilerParams(vmem_limit_bytes=VMEM_BYTES),
        name=name,
    )(*arguments)


def split_two(value):
    top = value.astype(jnp.bfloat16)
    return top, (value - top.astype(jnp.float32)).astype(jnp.bfloat16)


def split_three(value):
    top = value.astype(jnp.bfloat16)
    rest = value - top.astype(jnp.float32)
    middle = rest.astype(jnp.bfloat16)
    bottom = (rest - middle.astype(jnp.float32)).astype(jnp.bfloat16)
    return top, middle, bottom


def exact_dot(value, low):
    rows = value.shape[0]
    product = low_dot(jnp.concatenate(split_three(value), axis=0), low)
    return product[:rows] + product[rows : 2 * rows] + product[2 * rows :]


def lane_of(shape):
    return lax.broadcasted_iota(jnp.int32, shape, len(shape) - 1)


def fold(value):
    axis = value.ndim - 1
    value = value + pltpu.roll(value, 64, axis)
    return value + pltpu.roll(value, 32, axis)


def turn(value, steps):
    steps = steps % LANES
    return pltpu.roll(value, steps, value.ndim - 1) if steps else value


def turn_back(value, steps):
    return pltpu.roll(value, lax.rem(LANES - steps, LANES), value.ndim - 1)


def row_pieces(rows, groups, taps, channels):
    depth = rows // groups
    pieces = []
    for chip in range(taps * channels // rows):
        for group in range(groups):
            first = chip * rows + group * depth
            at = first
            while at < first + depth:
                tap, channel = divmod(at, channels)
                take = min(first + depth - at, channels - channel)
                pieces.append((chip, group, at - first, tap, channel, take))
                at += take
    return pieces


def shift_rows(value, side, steps):
    parts = []
    empty = jnp.zeros((1,) + value.shape[1:], value.dtype)
    for first in range(0, value.shape[0], side):
        block = value[first : first + side]
        parts += [empty, block[:-1]] if steps > 0 else [block[1:], empty]
    return jnp.concatenate(parts, axis=0)


def per_micro(values, side):
    return jnp.concatenate(
        [jnp.broadcast_to(v[None], (side, SUBLANES, LANES)) for v in values], axis=0
    )


def pack_kernel(latent, noise, conv, squeeze, excite, critic, block, conv_out, noise_out, rows_f):
    side = lax.axis_index("segment")
    bf16 = jnp.bfloat16
    micros, _, edge, _, channels = latent.shape
    half_in = channels // 2
    rows_f[...] = jnp.zeros(rows_f.shape, jnp.float32)
    for m in range(micros):
        for i in range(edge):
            at = (m * edge + i) * SUBLANES
            rows_f[at : at + edge, :] = latent[m, 0, i].astype(jnp.float32)
    spread = rows_f.shape[0]
    block[:spread, :] = jnp.where(side == 0, rows_f[:, :half_in], rows_f[:, half_in:]).astype(bf16)
    at = spread
    for weight in (squeeze, excite, critic):
        rows = weight.shape[0] // 2
        block[at : at + rows, :] = jnp.where(side == 0, weight[:rows], weight[rows:]).astype(bf16)
        at += rows

    chips, depth, _ = conv_out.shape
    widths = conv.shape[1]
    half = widths // 2
    group = half // chips
    lane = lane_of((depth, LANES))
    for b in range(half // LANES):
        for c in range(LANES // group):
            value = jnp.zeros((depth, LANES), jnp.float32)
            for q in range(4):
                rows = slice(q * depth, (q + 1) * depth)
                first = conv[rows, b * LANES : (b + 1) * LANES]
                second = conv[rows, half + b * LANES : half + (b + 1) * LANES]
                to = q * group
                first = turn(first, to - c * group)
                second = turn(second, to - c * group)
                low = jnp.where(side == 0, first, turn(first, -group // 2))
                high = jnp.where(side == 0, turn(second, group // 2), second)
                both = jnp.where(lane % group < group // 2, low, high)
                value = jnp.where(lane // group == q, both, value)
            conv_out[b * (LANES // group) + c] = value.astype(bf16)

    pixels = noise.shape[2]
    parts = jnp.concatenate(
        [p.astype(jnp.float32) for p in split_three(noise[:, 0])]
        + [jnp.zeros((SUBLANES - 3 * micros, pixels), jnp.float32)],
        axis=0,
    ).astype(bf16)
    pixel = lax.broadcasted_iota(jnp.int32, (pixels, LANES), 0)
    spot = lane_of((pixels, LANES))
    within = spot % (4 * edge)
    lane_row = lane_of((1, LANES))
    lines = []
    for j in range(edge):
        wanted = 4 * edge * (within // 4) + 2 * edge * ((within % 4) // 2) + 2 * j + within % 2
        chosen = (pixel == wanted).astype(jnp.float32).astype(bf16)
        found = low_dot(parts, chosen)
        line = jnp.zeros((1, LANES), jnp.float32)
        for m in range(micros):
            total = found[m : m + 1] + found[micros + m : micros + m + 1]
            total = total + found[2 * micros + m : 2 * micros + m + 1]
            line = jnp.where(lane_row // (4 * edge) == m, total, line)
        lines.append(line)
    noise_out[...] = jnp.concatenate(
        lines + [jnp.zeros((SUBLANES - edge, LANES), jnp.float32)], axis=0
    )


def pack(n, latent, noise, conv_w, squeeze_w, excite_w, critic_w):
    micros, _, edge, _, channels = latent.shape
    spread = micros * edge * SUBLANES
    rows = spread + (squeeze_w.shape[0] + excite_w.shape[0] + critic_w.shape[0]) // 2
    return local_call(
        pack_kernel,
        "pack",
        [
            jax.ShapeDtypeStruct((rows, channels // 2), jnp.bfloat16),
            jax.ShapeDtypeStruct((n, conv_w.shape[0] // 4, LANES), jnp.bfloat16),
            jax.ShapeDtypeStruct((SUBLANES, LANES), jnp.float32),
        ],
        [pltpu.VMEM((spread, channels), jnp.float32)],
        [latent, noise, conv_w, squeeze_w, excite_w, critic_w],
    )


def own_columns(row_low, row_high, at, own):
    lane = lane_of((1, LANES))
    low = turn_back(row_low, at)
    high = turn(turn_back(row_high, at), own)
    value = jnp.where(lane < own, low, jnp.where(lane < 2 * own, high, 0.0))
    value = value + turn(value, 2 * own)
    return value + turn(value, 4 * own)


def front_kernel(side, micros, pixel_count, all_lat, conv, noise, vectors,
                 fake, xn, stats, opened_out, z1_out, pooled_out, consts, noise_rows,
                 weight, z, h, gate8):
    images = all_lat.shape[0]
    half_in = all_lat.shape[3]
    channels = 2 * half_in
    spread = micros * side * SUBLANES
    depth = conv.shape[1]
    taps = weight.shape[1] // LANES
    bf16, f32 = jnp.bfloat16, jnp.float32
    chip, core = lax.axis_index("dp"), lax.axis_index("segment")
    own = 16
    widths_rows = vectors.shape[0] // 3
    at = 2 * own * lax.rem(chip, PLANE) + own * core
    base = chip // PLANE
    for k in range(3):
        consts[k : k + 1, :] = own_columns(
            vectors[pl.ds(k * widths_rows + base, 1), :],
            vectors[pl.ds(k * widths_rows + widths_rows // 2 + base, 1), :],
            at,
            own,
        )
    consts[3:, :] = jnp.zeros((SUBLANES - 3, LANES), f32)

    group = lane_of((depth, LANES)) // 32
    masks = [(group == g).astype(f32).astype(bf16) for g in range(4)]
    for owner, g, first, tap, channel, take in row_pieces(4 * depth, 4, taps, channels):
        weight[channel : channel + take, tap * LANES : (tap + 1) * LANES] = (
            conv[owner, first : first + take, :] * masks[g][:take]
        )
    lines = micros * side
    step = 4

    @pl.loop(0, images // step)
    def _(k):
        here = pl.ds(k * step, step)
        left = all_lat[here, 0, :spread].reshape(step * spread, half_in)
        right = all_lat[here, 1, :spread].reshape(step * spread, half_in)
        for tap in range(taps):
            cols = slice(tap * LANES, (tap + 1) * LANES)
            product = low_dot(left, weight[:half_in, cols]) + low_dot(right, weight[half_in:, cols])
            z[tap, here] = fold(product).reshape(step, lines, SUBLANES, LANES)

    from_lane = lax.broadcasted_iota(jnp.int32, (LANES, lines * LANES), 0)
    to_lane = lane_of((LANES, lines * LANES))
    chosen = from_lane == 4 * (to_lane // LANES) + (to_lane % LANES) // 32
    wide = exact_dot(
        noise[...].reshape(images * SUBLANES, LANES), chosen.astype(f32).astype(bf16)
    )
    for line in range(lines):
        noise_rows[:, line] = wide[:, line * LANES : (line + 1) * LANES].reshape(images, SUBLANES, LANES)

    shape3 = (lines, SUBLANES, LANES)
    lane = lane_of(shape3)
    row_first = (lane // 64) == 0
    col_first = ((lane // 32) % 2) == 0
    inside = lax.broadcasted_iota(jnp.int32, shape3, 1) < side
    first_half = (lane % 32) < 16
    gain_noise = consts[0:1, :][None]
    gain = consts[1:2, :][None]
    bias = consts[2:3, :][None]
    zero = jnp.zeros((SUBLANES, LANES), f32)

    def place(img, carry):
        lines_of = []
        for ky in range(3):
            z0, z1, z2 = z[3 * ky, img], z[3 * ky + 1, img], z[3 * ky + 2, img]
            lines_of.append(
                z1
                + jnp.where(col_first, pltpu.roll(z0, 1, 1), z0)
                + jnp.where(col_first, z2, pltpu.roll(z2, SUBLANES - 1, 1))
            )
        x0, x1, x2 = lines_of
        value = (
            x1
            + jnp.where(row_first, shift_rows(x0, side, 1), x0)
            + jnp.where(row_first, x2, shift_rows(x2, side, -1))
        )
        value = value + noise_rows[img] * gain_noise
        value = jnp.where(inside, value, 0.0)
        h[img] = value
        new = []
        for m in range(micros):
            part = value[m * side : (m + 1) * side]
            new.append(carry[2 * m] + jnp.sum(part, axis=0))
            new.append(carry[2 * m + 1] + jnp.sum(part * part, axis=0))
        return tuple(new)

    sums = lax.fori_loop(0, images, place, (zero,) * (2 * micros))
    means, stds = [], []
    for m in range(micros):
        mean_now = jnp.sum(fold(sums[2 * m]), axis=0, keepdims=True) / pixel_count
        square = jnp.sum(fold(sums[2 * m + 1]), axis=0, keepdims=True) / pixel_count
        means.append(mean_now)
        stds.append(lax.rsqrt(square - mean_now * mean_now + NORM_EPS))
        stats[m : m + 1, :] = stds[m]
    mean12, std12 = per_micro(means, side), per_micro(stds, side)

    count = images * micros
    rows_map = side * SUBLANES
    owner = lax.broadcasted_iota(jnp.int32, (count, count * rows_map), 1) // rows_map
    pool = (owner == lax.broadcasted_iota(jnp.int32, owner.shape, 0)).astype(f32).astype(bf16)
    area = 1.0 / (side * side)
    pooled = [
        low_dot(pool, all_lat[:, p, :spread].reshape(images * spread, half_in)) * area
        for p in range(2)
    ]
    rows_squeeze = channels // images // 2
    rows_excite = half_in // images // 2
    squeeze = all_lat[:, :, spread : spread + rows_squeeze].reshape(channels, half_in)
    excite = all_lat[:, :, spread + rows_squeeze : spread + rows_squeeze + rows_excite]
    excite = excite.reshape(half_in, half_in)
    z1 = exact_dot(pooled[0], squeeze[:half_in]) + exact_dot(pooled[1], squeeze[half_in:])
    z1_out[...] = z1
    pooled_out[:, :half_in] = pooled[0]
    pooled_out[:, half_in:] = pooled[1]
    wide = jax.nn.sigmoid(exact_dot(z1 * jax.nn.sigmoid(z1), excite))
    opened = wide[:, :LANES]
    for b in range(1, half_in // LANES):
        opened = jnp.where(base == b, wide[:, b * LANES : (b + 1) * LANES], opened)
    opened = jnp.where(lane_of(opened.shape) < own, turn_back(opened, at), 0.0)
    for steps in (own, 2 * own, 4 * own):
        opened = opened + turn(opened, steps)
    opened_out[...] = opened
    gate8[...] = jnp.broadcast_to(opened[:, None, :], gate8.shape)

    @pl.loop(0, images)
    def _(img):
        centred = (h[img] - mean12) * std12
        xn[img] = centred
        y = centred * gain + bias
        gated = y * turn(jax.nn.sigmoid(y), -16)
        pieces = []
        for m in range(micros):
            pieces.append(gated[m * side : (m + 1) * side] * gate8[img * micros + m][None])
        packed = jnp.where(first_half[:side], pieces[0], turn(pieces[1], 16))
        fake[img] = packed.reshape(side * SUBLANES, LANES).astype(bf16)


def front(side, micros, pixel_count, lat, conv, noise, vectors):
    images, _, _, half_in = lat.shape
    lines = micros * side
    count = images * micros
    f32 = jnp.float32
    return local_call(
        partial(front_kernel, side, micros, pixel_count),
        "front",
        [
            jax.ShapeDtypeStruct((images, side * SUBLANES, LANES), jnp.bfloat16),
            jax.ShapeDtypeStruct((images, lines, SUBLANES, LANES), f32),
            jax.ShapeDtypeStruct((SUBLANES, LANES), f32),
            jax.ShapeDtypeStruct((count, LANES), f32),
            jax.ShapeDtypeStruct((count, half_in), f32),
            jax.ShapeDtypeStruct((count, 2 * half_in), f32),
            jax.ShapeDtypeStruct((SUBLANES, LANES), f32),
            jax.ShapeDtypeStruct((images, lines, SUBLANES, LANES), f32),
        ],
        [
            pltpu.VMEM((2 * half_in, 9 * LANES), jnp.bfloat16),
            pltpu.VMEM((9, images, lines, SUBLANES, LANES), f32),
            pltpu.VMEM((images, lines, SUBLANES, LANES), f32),
            pltpu.VMEM((count, SUBLANES, LANES), f32),
        ],
        [lat, conv, noise, vectors],
    )


def critic_kernel(side, patches, spread, arrived, lat, real_bank, feat, proj, power, head, offset, chosen,
                  dfake, dspec, tail, column_v, column_t, row_w, maps):
    bf16 = jnp.bfloat16
    core = lax.axis_index("segment")
    chips, _, rows_map, _ = arrived.shape
    size = feat.shape[0]
    rows_before = spread + size // chips + size // chips // 2
    weight = lat[:, :, rows_before : rows_before + size // chips // 2]
    weight = weight.reshape(size, size).astype(jnp.float32)
    product = jnp.sum(weight * power[...], axis=1, keepdims=True)
    length = lax.rsqrt(jnp.sum(product * product))
    vec = product * length
    back = jnp.sum(weight * vec, axis=0, keepdims=True)
    sigma = jnp.sqrt(jnp.sum(back * back))
    unit = back / sigma
    turned = jnp.sum(weight * unit, axis=1, keepdims=True)
    turned = (turned - vec * jnp.sum(turned * vec)) * length
    column_v[...] = vec
    column_t[...] = turned
    row_w[...] = jnp.broadcast_to(unit, row_w.shape)
    spectral = (weight / sigma).astype(bf16)

    lane = lane_of((rows_map, LANES))
    per_block = LANES // 32
    for b in range(size // LANES):
        for q in range(4):
            value = None
            for c in range(per_block):
                chip = b * per_block + c
                low = arrived[chip, 0].astype(jnp.float32)
                high = arrived[chip, 1].astype(jnp.float32)
                low = jnp.where(core == 0, low, turn(low, -16))
                high = jnp.where(core == 0, turn(high, 16), high)
                both = turn(jnp.where(lane % 32 < 16, low, high), 32 * (c - q))
                value = both if value is None else jnp.where(lane // 32 == c, both, value)
            maps[q * rows_map : (q + 1) * rows_map, b * LANES : (b + 1) * LANES] = value.astype(bf16)
    fakes = 4 * rows_map
    maps[fakes:, :] = real_bank[chosen[core, 0]]
    rows = maps.shape[0]
    pre_act = low_dot(maps[...], feat[...])
    features = (pre_act * jax.nn.sigmoid(pre_act)).astype(bf16)
    projected = low_dot(features, proj[...]).astype(bf16)
    critic_act = low_dot(projected, spectral)
    opened = jax.nn.sigmoid(critic_act)
    activated = critic_act * opened
    logits = jnp.sum(activated * head[...], axis=1, keepdims=True) + offset[0]
    row = lax.broadcasted_iota(jnp.int32, (rows, 1), 0)
    sign = jnp.where(row < fakes, 1.0, -1.0)
    valid = jnp.logical_or(row >= fakes, (row % SUBLANES) < side)
    margin = 1.0 + sign * logits
    soft = jnp.maximum(margin, 0.0) + jnp.log1p(jnp.exp(-jnp.abs(margin)))
    loss = jnp.sum(jnp.where(valid, soft, 0.0))
    dlogit = jnp.where(valid, sign * jax.nn.sigmoid(margin), 0.0) / patches
    slope = opened * (1.0 + critic_act * (1.0 - opened))
    dact = (dlogit * head[...] * slope).astype(bf16)
    found = lax.dot_general(
        projected, dact, (((0,), (0,)), ((), ())), preferred_element_type=jnp.float32
    )
    dspec[...] = found.reshape(dspec.shape)
    dhead = jnp.sum(dlogit * activated, axis=0, keepdims=True)
    lane_row = lane_of((1, LANES))
    last = jnp.where(lane_row == 0, jnp.sum(dlogit), jnp.where(lane_row == 1, loss, 0.0))
    pieces = [dhead[:, k * LANES : (k + 1) * LANES] for k in range(size // LANES)] + [last]
    tail[...] = jnp.concatenate(
        pieces + [jnp.zeros((SUBLANES - len(pieces), LANES), jnp.float32)], axis=0
    )
    turned_dims = (((1,), (1,)), ((), ()))
    dproj = lax.dot_general(
        dact[:fakes], spectral, turned_dims, preferred_element_type=jnp.float32
    ).astype(bf16)
    dpre = lax.dot_general(dproj, proj[...], turned_dims, preferred_element_type=jnp.float32)
    dpre = (dpre * silu_slope(pre_act[:fakes])).astype(bf16)
    dmaps = lax.dot_general(dpre, feat[...], turned_dims, preferred_element_type=jnp.float32)
    for chip in range(chips):
        b, c = divmod(chip, per_block)
        value = None
        for q in range(4):
            part = dmaps[q * rows_map : (q + 1) * rows_map, b * LANES : (b + 1) * LANES]
            part = turn(part, 32 * (q - c))
            value = part if value is None else jnp.where(lane // 32 == q, part, value)
        dfake[chip] = value.astype(bf16)


def critic_step(side, patches, spread, arrived, lat, real_bank, feat, proj, power, head, offset, chosen):
    f32 = jnp.float32
    chips, _, rows_map, _ = arrived.shape
    size = feat.shape[0]
    vmem = pl.BlockSpec(memory_space=pltpu.VMEM)
    smem = pl.BlockSpec(memory_space=pltpu.SMEM)
    return local_call(
        partial(critic_kernel, side, patches, spread),
        "critic_step",
        [
            jax.ShapeDtypeStruct((chips, rows_map, LANES), jnp.bfloat16),
            jax.ShapeDtypeStruct((chips, 2, size // chips // 2, size), f32),
            jax.ShapeDtypeStruct((SUBLANES, LANES), f32),
            jax.ShapeDtypeStruct((size, 1), f32),
            jax.ShapeDtypeStruct((size, 1), f32),
            jax.ShapeDtypeStruct((SUBLANES, size), f32),
        ],
        [pltpu.VMEM((4 * rows_map + real_bank.shape[1], size), jnp.bfloat16)],
        [arrived, lat, real_bank, feat, proj, power, head, offset, chosen],
        [vmem] * 7 + [smem] * 2,
    )


def back_kernel(side, micros, pixel_count, grads, xn, all_lat, noise_rows, consts, stats, opened, tail,
                dspec_own, dspec_other, dconv, block, dspec, dy, packed, product, gate8, dze):
    images = all_lat.shape[0]
    half_in = all_lat.shape[3]
    channels = 2 * half_in
    lines = micros * side
    spread = lines * SUBLANES
    bf16 = jnp.bfloat16
    shape3 = (lines, SUBLANES, LANES)
    lane = lane_of(shape3)
    row_first = (lane // 64) == 0
    col_first = ((lane // 32) % 2) == 0
    first_half = (lane % 32) < 16
    inside = lax.broadcasted_iota(jnp.int32, shape3, 1) < side
    gain = consts[1:2, :][None]
    bias = consts[2:3, :][None]
    zero = jnp.zeros((SUBLANES, LANES), jnp.float32)
    core = lax.axis_index("segment")
    second = core == 1
    gate8[...] = jnp.broadcast_to(opened[...][:, None, :], gate8.shape)
    dspec[...] = jnp.where(second, dspec_own[:, 1], dspec_own[:, 0]) + dspec_other[...]

    def through_gate(img, carry):
        ascent = -grads[img].astype(jnp.float32).reshape(shape3)
        ascent = jnp.where(second, turn(ascent, -16), ascent)
        ascent = jnp.where(first_half, ascent, 0.0)
        centred = xn[img]
        y = centred * gain + bias
        gate = turn(jax.nn.sigmoid(y), -16)
        dopened = ascent * (y * gate)
        scale = jnp.concatenate(
            [jnp.broadcast_to(gate8[img * micros + m][None], (side, SUBLANES, LANES)) for m in range(micros)],
            axis=0,
        )
        dgated = ascent * scale
        dnormed = jnp.where(first_half, dgated * gate, turn(dgated * y * gate * (1.0 - gate), 16))
        dy[img] = dnormed
        new = []
        for m in range(micros):
            part = slice(m * side, (m + 1) * side)
            total = fold(jnp.sum(dopened[part], axis=0))
            total = total + turn(total, 16)
            gate_now = gate8[img * micros + m]
            dze[img * micros + m] = (
                jnp.broadcast_to(jnp.sum(total, axis=0, keepdims=True), (SUBLANES, LANES))
                * gate_now
                * (1.0 - gate_now)
            )
            new.append(carry[2 * m] + jnp.sum(dnormed[part] * centred[part], axis=0))
            new.append(carry[2 * m + 1] + jnp.sum(dnormed[part], axis=0))
        return tuple(new)

    sums = lax.fori_loop(0, images, through_gate, (zero,) * (2 * micros))
    sums = [jnp.sum(fold(s), axis=0, keepdims=True) for s in sums]
    gain_row = consts[1:2, :]
    mean_back = per_micro([gain_row * sums[2 * m + 1] / pixel_count for m in range(micros)], side)
    cross_back = per_micro([gain_row * sums[2 * m] / pixel_count for m in range(micros)], side)
    std12 = per_micro([stats[m : m + 1, :] for m in range(micros)], side)
    taps = 9
    groups = (taps + 3) // 4
    lane_flat = lane_of((spread, LANES)) // 32

    def through_norm(img, carry):
        centred = xn[img]
        dshift = (dy[img] * gain - mean_back - centred * cross_back) * std12
        dshift = jnp.where(inside, dshift, 0.0)
        carry = carry + jnp.sum(dshift * noise_rows[img], axis=0)
        dh = dshift.astype(bf16).astype(jnp.float32)
        swapped = jnp.where(col_first, turn(dh, -32), turn(dh, 32))
        col0 = jnp.where(col_first, dh, swapped)
        col1 = jnp.where(col_first, swapped, dh)
        by_col = [
            col1 + pltpu.roll(col0, SUBLANES - 1, 1),
            col0 + col1,
            col0 + pltpu.roll(col1, 1, 1),
        ]
        found = [None] * taps
        for kx in range(3):
            value = by_col[kx]
            turned = turn(value, 64)
            row0 = jnp.where(row_first, value, turned)
            row1 = jnp.where(row_first, turned, value)
            found[kx] = row1 + shift_rows(row0, side, -1)
            found[3 + kx] = row0 + row1
            found[6 + kx] = row0 + shift_rows(row1, side, 1)
        for g in range(groups):
            members = [f.reshape(spread, LANES) for f in found[4 * g : 4 * g + 4]]
            value = members[0]
            for k in range(1, len(members)):
                value = jnp.where(lane_flat == k, members[k], value)
            top, rest = split_two(value)
            packed[img, :, g * LANES : (g + 1) * LANES] = top
            packed[img, :, (groups + g) * LANES : (groups + g + 1) * LANES] = rest
        return carry

    dgain_noise = lax.fori_loop(0, images, through_norm, zero)
    dgain_noise = jnp.sum(fold(dgain_noise), axis=0, keepdims=True)
    lane_row = lane_of((1, LANES))
    for r in range(images * micros // 8):
        value = jnp.zeros((1, LANES), jnp.float32)
        for g in range(8):
            value = jnp.where(lane_row // 16 == g, dze[8 * r + g][0:1], value)
        block[r : r + 1, :] = value
    gains = jnp.where(
        lane_row // 32 == 0,
        dgain_noise,
        jnp.where(
            lane_row // 32 == 1,
            sum(sums[2 * m] for m in range(micros)),
            sum(sums[2 * m + 1] for m in range(micros)),
        ),
    )
    block[4:5, :] = gains
    block[5:8, :] = jnp.zeros((3, LANES), jnp.float32)
    block[8:16, :] = tail[...]

    width = groups * LANES
    flat = packed[...].reshape(images * spread, 2 * width)
    for p in range(2):
        side_rows = all_lat[:, p, :spread].reshape(images * spread, half_in)
        both = lax.dot_general(
            side_rows, flat, (((0,), (0,)), ((), ())), preferred_element_type=jnp.float32
        )
        product[p * half_in : (p + 1) * half_in, :] = both[:, :width] + both[:, width:]
    depth = dconv.shape[1]
    unit = 16
    lane_unit = lane_of((unit, LANES)) // 32
    for chip in range(dconv.shape[0]):
        for at in range(0, depth, unit):
            value = None
            for g in range(4):
                tap, channel = divmod((chip * 4 + g) * depth + at, channels)
                piece = product[channel : channel + unit, (tap // 4) * LANES : (tap // 4 + 1) * LANES]
                piece = turn(piece, 32 * (g - tap % 4))
                value = piece if value is None else jnp.where(lane_unit == g, piece, value)
            dconv[chip, at : at + unit, :] = value.astype(bf16)


def back(side, micros, pixel_count, depth, grads, xn, lat, noise_rows, consts, stats, opened, tail,
         dspec_own, dspec_other):
    images, _, _, half_in = lat.shape
    lines = micros * side
    count = images * micros
    f32 = jnp.float32
    return local_call(
        partial(back_kernel, side, micros, pixel_count),
        "back",
        [
            jax.ShapeDtypeStruct((images, depth, LANES), jnp.bfloat16),
            jax.ShapeDtypeStruct((2 * SUBLANES, LANES), f32),
            jax.ShapeDtypeStruct(dspec_other.shape, f32),
        ],
        [
            pltpu.VMEM((images, lines, SUBLANES, LANES), f32),
            pltpu.VMEM((images, lines * SUBLANES, 6 * LANES), jnp.bfloat16),
            pltpu.VMEM((2 * half_in, 3 * LANES), f32),
            pltpu.VMEM((count, SUBLANES, LANES), f32),
            pltpu.VMEM((count, SUBLANES, LANES), f32),
        ],
        [grads, xn, lat, noise_rows, consts, stats, opened, tail, dspec_own, dspec_other],
    )


def owner_kernel(dconv, mom, parts_in, mom_new, gram, parts, top, rest):
    chips, _, depth, _ = dconv.shape
    rows, widths = mom.shape
    half = widths // 2
    blocks = widths // LANES
    core = lax.axis_index("segment")
    lane = lane_of((depth, LANES))
    parts[...] = jnp.sum(parts_in[...], axis=0)
    for b in range(half // LANES):
        halves = []
        for c in range(PLANE):
            low = dconv[b * PLANE + c, 0].astype(jnp.float32)
            high = dconv[b * PLANE + c, 1].astype(jnp.float32)
            halves.append(
                (
                    jnp.where(lane % 32 < 16, low, turn(high, 16)),
                    jnp.where(lane % 32 < 16, turn(low, -16), high),
                )
            )
        for q in range(4):
            for k in range(2):
                value = None
                for c in range(PLANE):
                    piece = turn(halves[c][k], 32 * (c - q))
                    value = piece if value is None else jnp.where(lane // 32 == c, piece, value)
                at = (slice(q * depth, (q + 1) * depth), slice(k * half + b * LANES, k * half + (b + 1) * LANES))
                mom_new[at] = MOMENTUM * mom[at] + value
    for b in range(blocks):
        high, low = split_two(mom_new[:, b * LANES : (b + 1) * LANES])
        for at in (b, b + blocks) if b < PLANE else (b,):
            cols = slice(at * LANES, (at + 1) * LANES)
            top[:, cols] = high
            rest[:, cols] = low
    dims = (((0,), (0,)), ((), ()))
    share = LANES // 4
    span = gram.shape[2]

    @pl.loop(0, blocks)
    def _(b):
        own = pl.ds(pl.multiple_of(b * LANES, LANES), LANES)
        wide = pl.ds(pl.multiple_of(b * LANES, LANES), span)
        left_high, left_low = top[:, own], rest[:, own]
        right_high, right_low = top[:, wide], rest[:, wide]

        def times(left, right):
            return lax.dot_general(left, right, dims, preferred_element_type=jnp.float32)

        found = times(left_high, right_high) + (times(left_high, right_low) + times(left_low, right_high))
        for h in range(2):
            first = 2 * share * h
            gram[2 * b + h] = jnp.where(
                core == 0, found[first : first + share], found[first + share : first + 2 * share]
            )


def owner(dconv, mom, dspec):
    chips, _, depth, _ = dconv.shape
    rows, widths = mom.shape
    f32 = jnp.float32
    span = (widths // LANES // 2 + 1) * LANES
    return local_call(
        owner_kernel,
        "owner",
        [
            jax.ShapeDtypeStruct(mom.shape, f32),
            jax.ShapeDtypeStruct((chips, widths // chips // 2, span), f32),
            jax.ShapeDtypeStruct(dspec.shape[1:], f32),
        ],
        [pltpu.VMEM((rows, widths + PLANE * LANES), jnp.bfloat16)] * 2,
        [dconv, mom, dspec],
    )


def three(left_high, left_low, right_high, right_low, dims=(((1,), (0,)), ((), ()))):
    def times(left, right):
        return lax.dot_general(left, right, dims, preferred_element_type=jnp.float32)

    return times(left_high, right_high) + (times(left_high, right_low) + times(left_low, right_high))


def store_block(value, i, j, high, low):
    rows, cols = slice(i * BLOCK, (i + 1) * BLOCK), slice(j * BLOCK, (j + 1) * BLOCK)
    high[rows, cols], low[rows, cols] = split_two(value)
    if i < j:
        high[cols, rows], low[cols, rows] = split_two(value.T)


def polynomial(gram, gram_high, gram_low, high, low):
    for j in range(gram.shape[0] // BLOCK):
        cols, rows = slice(j * BLOCK, (j + 1) * BLOCK), slice(0, (j + 1) * BLOCK)
        found = three(gram_high[rows, :], gram_low[rows, :], gram_high[:, cols], gram_low[:, cols])
        for i in range(j + 1):
            here = slice(i * BLOCK, (i + 1) * BLOCK)
            store_block(NEWTON_B * gram[here, cols] + NEWTON_C * found[here], i, j, high, low)


def multiply(source, source_high, source_low, poly_high, poly_low, result, high, low):
    for j in range(source.shape[0] // BLOCK):
        cols, rows = slice(j * BLOCK, (j + 1) * BLOCK), slice(0, (j + 1) * BLOCK)
        found = three(source_high[rows, :], source_low[rows, :], poly_high[:, cols], poly_low[:, cols])
        for i in range(j + 1):
            here = slice(i * BLOCK, (i + 1) * BLOCK)
            value = NEWTON_A * source[here, cols] + found[here]
            result[here, cols] = value
            store_block(value, i, j, high, low)


def apply(x, x_high, x_low, poly_high, poly_low):
    for j in range(x.shape[1] // BLOCK):
        cols = slice(j * BLOCK, (j + 1) * BLOCK)
        found = three(x_high[...], x_low[...], poly_high[:, cols], poly_low[:, cols])
        x[:, cols] = NEWTON_A * x[:, cols] + found


def resplit(x, x_high, x_low):
    for j in range(x.shape[1] // BLOCK):
        cols = slice(j * BLOCK, (j + 1) * BLOCK)
        x_high[:, cols], x_low[:, cols] = split_two(x[:, cols])


def conv_ortho_kernel(packed, mom, weight, weight_new, gram, other, g_high, g_low, p_high, p_low,
                      t_high, t_low, x, x_high, x_low):
    size = gram.shape[0]
    blocks = size // LANES
    span = packed.shape[1] // LANES
    eye = lax.broadcasted_iota(jnp.int32, (LANES, LANES), 0) == lane_of((LANES, LANES))
    total = jnp.zeros((LANES, LANES), jnp.float32)
    for b in range(blocks):
        total = total + jnp.where(eye, packed[b * LANES : (b + 1) * LANES, :LANES], 0.0)
    norm = jnp.sqrt(jnp.sum(total)) + 1e-07
    scale = 1.0 / norm
    for r in range(blocks):
        rows = slice(r * LANES, (r + 1) * LANES)
        for c in range(blocks):
            cols = slice(c * LANES, (c + 1) * LANES)
            ahead = (c - r) % blocks
            if ahead < span and (2 * ahead < blocks or r < c):
                value = packed[rows, ahead * LANES : (ahead + 1) * LANES]
            else:
                behind = (r - c) % blocks
                value = packed[cols, behind * LANES : (behind + 1) * LANES].T
            value = (value * scale) * scale
            if (r * LANES) // BLOCK <= (c * LANES) // BLOCK:
                gram[rows, cols] = value
            g_high[rows, cols], g_low[rows, cols] = split_two(value)
    x[...] = mom[...] * scale
    resplit(x, x_high, x_low)

    @pl.loop(0, NS_STEPS)
    def _(step):
        polynomial(gram, g_high, g_low, p_high, p_low)
        apply(x, x_high, x_low, p_high, p_low)

        @pl.when(step < NS_STEPS - 1)
        def _():
            resplit(x, x_high, x_low)
            multiply(gram, g_high, g_low, p_high, p_low, other, t_high, t_low)
            multiply(other, t_high, t_low, p_high, p_low, gram, g_high, g_low)

    weight_new[...] = weight[...] * (1.0 - MUON_RATE * DECAY) - MUON_RATE * x[...]


def conv_ortho(packed, mom, weight):
    size = packed.shape[0]
    f32, bf16 = jnp.float32, jnp.bfloat16
    return local_call(
        conv_ortho_kernel,
        "conv_ortho",
        jax.ShapeDtypeStruct(weight.shape, f32),
        [pltpu.VMEM((size, size), f32)] * 2
        + [pltpu.VMEM((size, size), bf16)] * 6
        + [pltpu.VMEM(mom.shape, f32)]
        + [pltpu.VMEM(mom.shape, bf16)] * 2,
        [packed, mom, weight],
    )


def whole_ortho_kernel(chips, mom, weight, weight_new, x, x_high, x_low, gram, g_high, g_low, p_high, p_low):
    size = gram.shape[0]
    x[...] = mom[...]
    norm = jnp.sqrt(jnp.sum(x[...] * x[...])) + 1e-07
    x[...] = x[...] / norm
    resplit(x, x_high, x_low)

    @pl.loop(0, NS_STEPS)
    def _(_):
        for j in range(size // BLOCK):
            cols, rows = slice(j * BLOCK, (j + 1) * BLOCK), slice(0, (j + 1) * BLOCK)
            found = three(
                x_high[:, rows], x_low[:, rows], x_high[:, cols], x_low[:, cols], (((0,), (0,)), ((), ()))
            )
            for i in range(j + 1):
                here = slice(i * BLOCK, (i + 1) * BLOCK)
                gram[here, cols] = found[here]
                store_block(found[here], i, j, g_high, g_low)
        polynomial(gram, g_high, g_low, p_high, p_low)
        apply(x, x_high, x_low, p_high, p_low)
        resplit(x, x_high, x_low)

    rows = weight.shape[0]
    mine = pl.ds(pl.multiple_of(lax.axis_index("dp") * rows, rows), rows)
    weight_new[...] = weight[...] * (1.0 - MUON_RATE * DECAY) - MUON_RATE * x[mine, :]


def whole_ortho(chips, mom, weight):
    size = mom.shape[1]
    f32, bf16 = jnp.float32, jnp.bfloat16
    return local_call(
        partial(whole_ortho_kernel, chips),
        "whole_ortho",
        jax.ShapeDtypeStruct(weight.shape, f32),
        [pltpu.VMEM(mom.shape, f32)]
        + [pltpu.VMEM(mom.shape, bf16)] * 2
        + [pltpu.VMEM((size, size), f32)]
        + [pltpu.VMEM((size, size), bf16)] * 4,
        [mom, weight],
    )


def by_channels(
    latent,
    noise,
    real_bank,
    real_index,
    frozen_feat,
    frozen_proj,
    power_vec,
    conv_w,
    conv_mom,
    squeeze_w,
    squeeze_mom,
    excite_w,
    excite_mom,
    critic_w,
    critic_mom,
    vectors,
    vec_m,
    vec_v,
):
    n = lax.axis_size("dp")
    chip, side = lax.axis_index("dp"), lax.axis_index("segment")
    f32 = jnp.float32
    micros, _, edge, _, channels = latent.shape
    pixels = noise.shape[2]
    rows, widths = conv_w.shape
    half = widths // 2
    own = half // n // 2
    depth = rows // 4
    proj_width = critic_w.shape[1]
    pixel_count = pixels * n
    patches = micros * pixel_count
    spread = micros * edge * SUBLANES

    block, conv_own, noise_own = pack(n, latent, noise, conv_w, squeeze_w, excite_w, critic_w)
    lat, conv, noise_all = exchange(
        n, 1, [("relay", True), ("a2a", False), ("relay", True)], [block, conv_own, noise_own]
    )

    gains = vectors[: 3 * widths].reshape(3 * widths // LANES, LANES)
    fake, xn, stats, opened, z1, pooled, consts, noise_rows = front(
        edge, micros, pixel_count, lat, conv, noise_all[:, 0], gains
    )
    (arrived,) = exchange(n, 2, [("a2a", True)], [fake])
    head = vectors[3 * widths : 3 * widths + proj_width].reshape(1, proj_width)
    offset = vectors[3 * widths + proj_width :].reshape(1)
    dfake, dspec, tail, column_v, column_t, row_w = critic_step(
        edge,
        patches,
        spread,
        arrived,
        lat,
        real_bank,
        frozen_feat,
        frozen_proj,
        power_vec.reshape(1, -1),
        head,
        offset,
        real_index,
    )

    returned, added = exchange(n, 3, [("a2a", True), ("cross", False)], [dfake, dspec])
    dconv, block, dspec = back(
        edge, micros, pixel_count, depth, returned, xn, lat, noise_rows, consts, stats, opened, tail,
        dspec, added,
    )

    def half_of(value):
        size = value.shape[0] // 2
        return lax.dynamic_slice_in_dim(value, side * size, size, 0)

    moms = jnp.concatenate([half_of(squeeze_mom), half_of(excite_mom), half_of(critic_mom)], axis=0)
    dconv, blocks, dspec, moms = exchange(
        n,
        4,
        [("a2a", True), ("relay", True), ("a2a", False), ("relay", True)],
        [dconv, block, dspec, moms],
    )
    conv_mom_new, gram, dspec = owner(dconv, conv_mom, dspec)
    grams, dspec = exchange(n, 5, [("a2a", False), ("relay", True)], [gram, dspec])
    (gram,) = exchange(n, 6, [("relay", True)], [jnp.sum(grams, axis=0)])
    gram = gram.reshape(widths, -1)

    def rows_of(value):
        size = value.shape[0] // n
        return lax.dynamic_slice_in_dim(value, chip * size, size, 0)

    width_small = squeeze_w.shape[1]
    vec_rows = -(-(3 * vectors.shape[0] + 1) // width_small)
    vec_rows += -vec_rows % SUBLANES
    small_rows = 2 * (squeeze_w.shape[0] + excite_w.shape[0] + critic_w.shape[0]) + vec_rows

    def on_first():
        return conv_ortho(gram, conv_mom_new, conv_w), jnp.zeros((small_rows, width_small), f32)

    def on_second():
        first = spread
        low = []
        for count in (squeeze_w.shape[0], excite_w.shape[0], critic_w.shape[0]):
            low.append(lat[:, :, first : first + count // 2].reshape(n * count, -1).astype(f32))
            first += count // 2
        _, excite_full, critic_full = low
        dspec_full = dspec.reshape(proj_width, proj_width)
        sigma = jnp.sqrt(jnp.sum(jnp.square(jnp.sum(critic_full * column_v, axis=0))))
        along = jnp.sum(dspec_full * critic_full) / (sigma * sigma)
        direction = column_v * row_w[0:1] + column_t * power_vec[None, :]
        critic_grad = dspec_full / sigma - along * direction
        dze = blocks[:, :, :4].reshape(n, 2, n * micros, own)
        dze = dze.transpose(2, 0, 1, 3).reshape(n * micros, half)
        squeezed = z1 * jax.nn.sigmoid(z1)
        excite_grad = high_dot(squeezed.T, dze)
        dz1 = high_dot(dze, excite_full.T) * silu_slope(z1)
        squeeze_grad = high_dot(pooled.T, dz1)
        first = 0
        moms_new, weights_new = [], []
        for weight, grad in ((squeeze_w, squeeze_grad), (excite_w, excite_grad), (critic_w, critic_grad)):
            count = weight.shape[0]
            old = moms[:, :, first : first + count // 2].reshape(n * count, -1)
            first += count // 2
            new = MOMENTUM * old + grad
            moms_new.append(rows_of(new))
            weights_new.append(whole_ortho(n, new, weight))
        changes = blocks[:, :, 4, : 3 * 2 * own].reshape(n, 2, 3, 2, own)
        changes = changes.transpose(2, 3, 0, 1, 4).reshape(3 * widths)
        tails = jnp.sum(blocks[:, :, 8:], axis=(0, 1))
        last = proj_width // LANES
        vector_grad = jnp.concatenate([changes, tails[:last].reshape(-1), tails[last, :1]])
        flat = jnp.concatenate([*adam(vectors, vec_m, vec_v, vector_grad), tails[last, 1:2]])
        flat = jnp.pad(flat, (0, vec_rows * width_small - flat.shape[0]))
        small = jnp.concatenate([*moms_new, *weights_new, flat.reshape(vec_rows, width_small)], axis=0)
        return jnp.zeros_like(conv_w), small

    conv_new, small = share(7, *lax.cond(side == 0, on_first, on_second))
    pieces = []
    first = 0
    for weight in (squeeze_w, excite_w, critic_w) * 2:
        pieces.append(small[first : first + weight.shape[0]])
        first += weight.shape[0]
    flat = small[first:].reshape(-1)
    size = vectors.shape[0]
    return (
        flat[3 * size],
        conv_mom_new,
        conv_new,
        pieces[0],
        pieces[3],
        pieces[1],
        pieces[4],
        pieces[2],
        pieces[5],
        flat[:size],
        flat[size : 2 * size],
        flat[2 * size : 3 * size],
    )


def shifted_2(value, axis, steps):
    count = lax.axis_size(axis)
    leading, last = (max(0, -steps), min(count, count - steps))
    return lax.ppermute(value, axis, [(source, source + steps) for source in range(leading, last)])


def for_sending(x):
    return jax.tree.map(lambda a: a.astype(jnp.bfloat16) if a.dtype == jnp.float32 else a, x)


def only_if(flag, compute):

    def empty_branch():
        return jax.tree.map(jnp.zeros_like, compute())

    return lax.cond(flag, compute, empty_branch)


def columns(latent_now):
    upsampled = jnp.repeat(jnp.repeat(latent_now, 2, axis=1), 2, axis=2)
    side_now = upsampled.shape[1]
    padded = jnp.pad(upsampled, ((0, 0), (1, 1), (1, 1), (0, 0)))
    taps = [
        padded[:, row_tap : row_tap + side_now, col_tap : col_tap + side_now, :]
        for row_tap in range(3)
        for col_tap in range(3)
    ]
    return jnp.concatenate(taps, axis=-1).reshape(-1, 9 * upsampled.shape[3])


def spectral_norm(weight, power):
    vector = high_dot(weight, power)
    vector = vector * lax.rsqrt(jnp.sum(vector * vector))
    product_one = high_dot(vector, weight)
    return weight / jnp.sqrt(jnp.sum(product_one * product_one))


def excite(pooled, squeeze_w, excite_w):
    return jax.nn.sigmoid(high_dot(jax.nn.silu(high_dot(pooled, squeeze_w)), excite_w))


def normalize(shifted, moments, pixel_count, bn_gain, bn_bias):
    mean_vec = moments[0] / pixel_count
    inv_std = lax.rsqrt(moments[1] / pixel_count - mean_vec * mean_vec + NORM_EPS)
    centred = (shifted - mean_vec) * inv_std
    return (centred, inv_std, centred * bn_gain + bn_bias)


def critic_pass(
    inputs, sign, patches, frozen_feat, frozen_proj, spectral, out_weight, out_bias, want_input
):
    pre_act = low_dot(inputs, frozen_feat)
    features = jax.nn.silu(pre_act).astype(jnp.bfloat16)
    projected = low_dot(features, frozen_proj).astype(jnp.bfloat16)
    critic_act = low_dot(projected, spectral)
    activated = jax.nn.silu(critic_act)
    logits = high_dot(activated, out_weight) + out_bias
    loss_part = jnp.sum(jax.nn.softplus(1.0 + sign * logits))
    dlogit = sign * jax.nn.sigmoid(1.0 + sign * logits) / patches
    dact = (dlogit[:, None] * out_weight * silu_slope(critic_act)).astype(jnp.bfloat16)
    result = [loss_part, low_dot(projected.T, dact), high_dot(dlogit, activated), jnp.sum(dlogit)]
    if want_input:
        dproj = low_dot(dact, spectral.T).astype(jnp.bfloat16)
        dpre = (low_dot(dproj, frozen_proj.T) * silu_slope(pre_act)).astype(jnp.bfloat16)
        result.append(low_dot(dpre, frozen_feat.T).astype(jnp.bfloat16))
    return result


def orthogonalize(momenta):
    squares = lax.psum(
        (
            jnp.sum(momenta[0] * momenta[0]),
            jnp.sum(momenta[1] * momenta[1]),
            jnp.sum(momenta[2] * momenta[2]),
            jnp.sum(momenta[3] * momenta[3]),
        ),
        "dp",
    )
    current = [
        matrix_now / (jnp.sqrt(square_now) + 1e-07)
        for matrix_now, square_now in zip(momenta, squares)
    ]

    def iterate(_, current):
        partials = [
            lax.psum_scatter(
                high_dot(matrix_now.T, matrix_now), "dp", scatter_dimension=0, tiled=True
            )
            for matrix_now in current
        ]
        full_grams = [lax.all_gather(part, "dp", axis=0, tiled=True) for part in partials]
        updated = []
        for matrix_now, gram in zip(current, full_grams):
            product_one = high_dot(matrix_now, gram)
            updated.append(
                NEWTON_A * matrix_now
                + NEWTON_B * product_one
                + NEWTON_C * high_dot(product_one, gram)
            )
        return updated

    return lax.fori_loop(0, NS_STEPS, iterate, current)


def by_images(
    latent,
    noise,
    real_bank,
    real_index,
    frozen_feat,
    frozen_proj,
    power_vec,
    conv_w,
    conv_mom,
    squeeze_w,
    squeeze_mom,
    excite_w,
    excite_mom,
    critic_w,
    critic_mom,
    vectors,
    vec_m,
    vec_v,
):
    gathered = (
        lax.all_gather(conv_w.astype(jnp.bfloat16), "dp", axis=0, tiled=True),
        lax.all_gather(squeeze_w.astype(jnp.bfloat16), "dp", axis=0, tiled=True),
        lax.all_gather(excite_w.astype(jnp.bfloat16), "dp", axis=0, tiled=True),
        lax.all_gather(critic_w.astype(jnp.bfloat16), "dp", axis=0, tiled=True),
    )
    conv_low, squeeze_low, excite_low, critic_low = gathered
    squeeze_full = squeeze_low.astype(jnp.float32)
    excite_full = excite_low.astype(jnp.float32)
    spectral_full, spectral_back = jax.vjp(
        partial(spectral_norm, power=power_vec), critic_low.astype(jnp.float32)
    )
    spectral = spectral_full.astype(jnp.bfloat16)
    micro_count, images, pixels = (noise.shape[0], noise.shape[1], noise.shape[2])
    widths = conv_low.shape[1]
    half_width = widths // 2
    proj_width = critic_low.shape[0]
    tokens = images * pixels
    pixel_count = tokens * lax.axis_size("dp")
    patches = micro_count * pixel_count
    noise_gain = vectors[:widths]
    bn_gain = vectors[widths : 2 * widths]
    bn_bias = vectors[2 * widths : 3 * widths]
    out_weight = vectors[3 * widths : 3 * widths + proj_width]
    out_bias = vectors[3 * widths + proj_width]
    generator = lax.axis_index("segment") == 0
    critic_side = jnp.logical_not(generator)
    pooled = jnp.mean(latent.astype(jnp.float32), axis=(2, 3))
    conv_acc = jnp.zeros(conv_low.shape, jnp.float32)
    squeeze_acc = jnp.zeros(squeeze_low.shape, jnp.float32)
    excite_acc = jnp.zeros(excite_low.shape, jnp.float32)
    spectral_acc = jnp.zeros(critic_low.shape, jnp.float32)
    vector_acc = jnp.zeros(vectors.shape, jnp.float32)
    loss_acc = jnp.zeros((), jnp.float32)
    for micro_step in range(micro_count):
        noise_now = noise[micro_step].reshape(-1)
        excitation, excite_back = jax.vjp(excite, pooled[micro_step], squeeze_full, excite_full)

        def gen_front():
            patches_in = columns(latent[micro_step])
            return (patches_in, low_dot(patches_in, conv_low) + noise_now[:, None] * noise_gain)

        patches_in, shifted = only_if(generator, gen_front)
        moments = lax.psum((jnp.sum(shifted, axis=0), jnp.sum(shifted * shifted, axis=0)), "dp")

        def gen_mid():
            centred, inv_std, normed = normalize(shifted, moments, pixel_count, bn_gain, bn_bias)
            gated = normed[:, :half_width] * jax.nn.sigmoid(normed[:, half_width:])
            fake_map = gated.reshape(images, pixels, half_width) * excitation[:, None, :]
            return fake_map.reshape(tokens, half_width).astype(jnp.bfloat16)

        fake_map = only_if(generator, gen_mid)
        arrived = shifted_2(fake_map, "segment", 1)

        def critic_work():
            real_map = real_bank[real_index[micro_step]].reshape(tokens, half_width)
            real_out = critic_pass(
                real_map,
                -1.0,
                patches,
                frozen_feat,
                frozen_proj,
                spectral,
                out_weight,
                out_bias,
                False,
            )
            fake_out = critic_pass(
                arrived,
                1.0,
                patches,
                frozen_feat,
                frozen_proj,
                spectral,
                out_weight,
                out_bias,
                True,
            )
            return (
                real_out[0] + fake_out[0],
                real_out[1] + fake_out[1],
                real_out[2] + fake_out[2],
                real_out[3] + fake_out[3],
                fake_out[4],
            )

        loss_part, dspec_part, dout_part, dbias_part, input_grad = only_if(critic_side, critic_work)
        returned = jax.tree.map(
            lambda part, own: part.astype(own.dtype),
            shifted_2(for_sending(input_grad), "segment", -1),
            input_grad,
        )

        def gen_back():
            dfake = -returned.astype(jnp.float32).reshape(images, pixels, half_width)
            centred, inv_std, normed = normalize(shifted, moments, pixel_count, bn_gain, bn_bias)
            opened = jax.nn.sigmoid(normed[:, half_width:])
            first_half = normed[:, :half_width]
            gated = (first_half * opened).reshape(images, pixels, half_width)
            unused, dsqueeze, dexcite = excite_back(jnp.sum(dfake * gated, axis=1))
            dgated = (dfake * excitation[:, None, :]).reshape(tokens, half_width)
            dnormed = jnp.concatenate(
                [dgated * opened, dgated * first_half * opened * (1.0 - opened)], axis=1
            )
            return (
                dnormed * bn_gain,
                centred,
                inv_std,
                dsqueeze,
                dexcite,
                jnp.sum(dnormed * centred, axis=0),
                jnp.sum(dnormed, axis=0),
            )

        dcentred, centred, inv_std, dsqueeze, dexcite, dgain, dbias = only_if(generator, gen_back)
        back_sums = lax.psum((jnp.sum(dcentred, axis=0), jnp.sum(dcentred * centred, axis=0)), "dp")

        def gen_grad():
            dshifted = inv_std * (
                dcentred - back_sums[0] / pixel_count - centred * back_sums[1] / pixel_count
            )
            return (dshifted.astype(jnp.bfloat16), jnp.sum(dshifted * noise_now[:, None], axis=0))

        dhidden, dnoise = only_if(generator, gen_grad)
        conv_acc = conv_acc + only_if(generator, lambda: low_dot(patches_in.T, dhidden))
        squeeze_acc = squeeze_acc + dsqueeze
        excite_acc = excite_acc + dexcite
        spectral_acc = spectral_acc + dspec_part
        vector_acc = vector_acc + jnp.concatenate(
            [dnoise, dgain, dbias, dout_part, dbias_part[None]]
        )
        loss_acc = loss_acc + loss_part
    critic_grad = spectral_back(spectral_acc)[0]
    conv_rows_sum, squeeze_rows, excite_rows, critic_rows = (
        lax.psum_scatter(conv_acc, "dp", scatter_dimension=0, tiled=True),
        lax.psum_scatter(squeeze_acc, "dp", scatter_dimension=0, tiled=True),
        lax.psum_scatter(excite_acc, "dp", scatter_dimension=0, tiled=True),
        lax.psum_scatter(critic_grad, "dp", scatter_dimension=0, tiled=True),
    )
    gradients = lax.psum((conv_rows_sum, squeeze_rows, excite_rows, critic_rows), "segment")
    vector_grad, loss_sum = lax.psum((vector_acc, loss_acc), ("segment", "dp"))
    weights = (conv_w, squeeze_w, excite_w, critic_w)
    new_moms = [
        MOMENTUM * old_mom + grad_now
        for old_mom, grad_now in zip((conv_mom, squeeze_mom, excite_mom, critic_mom), gradients)
    ]
    ortho = orthogonalize(new_moms)
    new_weights = [
        weight * (1.0 - MUON_RATE * DECAY) - MUON_RATE * step_dir
        for weight, step_dir in zip(weights, ortho)
    ]
    vec_m_new, vec_v_new, vectors_new = adam(vectors, vec_m, vec_v, vector_grad)
    return (
        loss_sum,
        new_moms[0],
        new_weights[0],
        new_moms[1],
        new_weights[1],
        new_moms[2],
        new_weights[2],
        new_moms[3],
        new_weights[3],
        vec_m_new,
        vec_v_new,
        vectors_new,
    )


def solution(mesh):
    placed = (
        P(None, "dp", None, None, None),
        P(None, "dp", None),
        P("dp", None, None),
        P(None, "dp"),
        P(),
        P(),
        P(),
        P("dp", None),
        P("dp", None),
        P("dp", None),
        P("dp", None),
        P("dp", None),
        P("dp", None),
        P("dp", None),
        P("dp", None),
        P(),
        P(),
        P(),
    )
    given = (
        P(),
        P("dp", None),
        P("dp", None),
        P("dp", None),
        P("dp", None),
        P("dp", None),
        P("dp", None),
        P("dp", None),
        P("dp", None),
        P(),
        P(),
        P(),
    )

    def step(latent, noise, *rest):
        n, sides = mesh.shape["dp"], mesh.shape["segment"]
        micros, images, edge = latent.shape[:3]
        fits = (
            n == 16
            and sides == 2
            and images == n
            and micros == 2
            and edge <= SUBLANES - 1
            and rest[5].shape[1] == 2 * n * sides * 16
        )
        plan = by_channels if fits else by_images
        return jax.shard_map(
            plan, mesh=mesh, in_specs=placed, out_specs=given, check_vma=False
        )(latent, noise, *rest)

    return step
```

```python
from functools import partial

import jax
import jax.numpy as jnp
from jax import lax
from jax.experimental import pallas as pl
from jax.experimental.pallas import tpu as pltpu
from jax.sharding import PartitionSpec as P

NS_STEPS = 5
STEP = 10


HIGHEST_PREC = lax.Precision.HIGHEST
HIGH_PREC = lax.Precision.HIGH
MESH = pl.DeviceIdType.MESH
NORM_EPS = 1e-05
NEWTON_A = 3.4445
NEWTON_B = -4.775
NEWTON_C = 2.0315
MOMENTUM = 0.95
MUON_RATE = 0.5
DECAY = 0.01
ADAM_RATE = 0.2
ADAM_BETA1 = 0.9
ADAM_BETA2 = 0.95
ADAM_EPS = 1e-08
LANES = 128
SUBLANES = 8
PLANE = 4
BLOCK = 256
FINE_BYTES = 64 * 1024
NO_COST = pl.CostEstimate(flops=0, bytes_accessed=0, transcendentals=0)
VMEM_BYTES = 56 * 1024 * 1024


def low_dot(left, right):
    return jnp.dot(left, right, preferred_element_type=jnp.float32)


def high_dot(left, right):
    return jnp.dot(left, right, precision=HIGHEST_PREC, preferred_element_type=jnp.float32)


def mid_dot(left, right):
    return jnp.dot(left, right, precision=HIGH_PREC, preferred_element_type=jnp.float32)


def silu_slope(value):
    opened = jax.nn.sigmoid(value)
    return opened * (1.0 + value * (1.0 - opened))


def adam(vectors, vec_m, vec_v, vector_grad):
    vec_m_new = ADAM_BETA1 * vec_m + (1.0 - ADAM_BETA1) * vector_grad
    vec_v_new = ADAM_BETA2 * vec_v + (1.0 - ADAM_BETA2) * vector_grad * vector_grad
    first_hat = vec_m_new / (1.0 - ADAM_BETA1**STEP)
    second_hat = vec_v_new / (1.0 - ADAM_BETA2**STEP)
    vectors_new = vectors * (1.0 - ADAM_RATE * DECAY) - ADAM_RATE * first_hat / (
        jnp.sqrt(second_hat) + ADAM_EPS
    )
    return vec_m_new, vec_v_new, vectors_new


def exchange(n, ident, plans, arrays):
    count = len(plans)
    kinds = [kind for kind, _ in plans]
    planes = n // PLANE

    def shape(kind, paired, x):
        if kind == "relay":
            lead, block = (planes, PLANE, 2), x.shape
        elif kind == "a2a":
            lead, block = ((n, 2) if paired else (n,)), x.shape[1:]
        elif kind == "plane":
            lead, block = (PLANE,), x.shape[1:]
        elif kind == "line":
            lead, block = (planes,), x.shape[1:]
        else:
            lead, block = (), x.shape[:1] + x.shape[2:]
        return jax.ShapeDtypeStruct(lead + block, x.dtype)

    outs = [shape(kind, paired, x) for (kind, paired), x in zip(plans, arrays)]
    direct = [a for a in range(count) if kinds[a] == "a2a"]
    near = [a for a in range(count) if kinds[a] in ("plane", "line")]
    single = [a for a in range(count) if kinds[a] == "cross"]
    passing = [a for a in direct if plans[a][1]]
    parts = []
    for a in range(count):
        if kinds[a] == "relay":
            rows = arrays[a].shape[0]
            unit = 16 if arrays[a].dtype == jnp.bfloat16 else 8
            cut = -(-rows // (2 * unit)) * unit
            fine = arrays[a].size * arrays[a].dtype.itemsize > FINE_BYTES
            parts.append((a, 0, cut, 0, fine))
            if cut < rows:
                parts.append((a, cut, rows - cut, 1, fine))
    small = [p for p in range(len(parts)) if not parts[p][4]]
    large = [p for p in range(len(parts)) if parts[p][4]]

    def body(*refs):
        ins, results = refs[:count], refs[count : 2 * count]
        (send, recv, pass_send, pass_recv, here, up_send, z_send, z_recv, first_send, first_recv,
         second_send, second_recv, core_send, core_recv, part_here) = refs[2 * count :]
        me, side = lax.axis_index("dp"), lax.axis_index("segment")
        other = 1 - side
        z, spot = me // PLANE, me % PLANE
        beside = (spot + 1 - 2 * (spot % 2), (spot + 2) % PLANE)
        across = PLANE - 1 - spot
        barrier = pltpu.get_barrier_semaphore()

        def greet(where):
            pl.semaphore_signal(barrier, inc=1, device_id=where, device_id_type=MESH)

        greeted = 0
        if direct or near:

            @pl.loop(1, n)
            def _(k):
                greet({"dp": lax.rem(me + k, n)})

            greeted += n - 1
        elif parts:

            @pl.loop(1, planes)
            def _(k):
                greet({"dp": lax.rem(me + k * PLANE, n)})

            for spot_now in beside:
                greet({"dp": z * PLANE + spot_now})
            greeted += planes + 1
        if passing or single or parts:
            greet({"segment": other})
            greeted += 1
        pl.semaphore_wait(barrier, greeted)

        def remote(src, dst, send_sem, recv_sem, where):
            return pltpu.make_async_remote_copy(
                src_ref=src,
                dst_ref=dst,
                send_sem=send_sem,
                recv_sem=recv_sem,
                device_id=where,
                device_id_type=MESH,
            )

        every = range(len(parts))

        def cell(p, plane, spot_now):
            a, first, rows = parts[p][:3]
            return results[a].at[plane, spot_now, side, pl.ds(first, rows)]

        def column(p, spot_now, of_side):
            a, first, rows = parts[p][:3]
            return results[a].at[:, spot_now, of_side, pl.ds(first, rows)]

        def mine(p):
            a, first, rows = parts[p][:3]
            return ins[a].at[pl.ds(first, rows)]

        def first_spot(p):
            return beside[parts[p][3]]

        def second_spot(p):
            return beside[1 - parts[p][3]]

        def along(p, k):
            chip = lax.rem(z + k, planes) * PLANE + spot
            return remote(mine(p), cell(p, z, spot), z_send.at[p, k], z_recv.at[p, z], {"dp": chip})

        def chain(p, plane, up, src=None):
            held = cell(p, plane, spot)
            return remote(
                held if src is None else src,
                held,
                (up_send if up else z_send).at[p, plane],
                z_recv.at[p, plane],
                {"dp": me + PLANE if up else me - PLANE},
            )

        def from_plane(p, plane):
            held = cell(p, plane, spot)
            return remote(held, held, z_send.at[p, 0], z_recv.at[p, plane], {"dp": me})

        def to_first(p, plane, src=None, of_spot=None):
            held = cell(p, plane, spot if of_spot is None else of_spot)
            return remote(
                held if src is None else src,
                held,
                first_send.at[p, plane],
                first_recv.at[p, plane],
                {"dp": z * PLANE + first_spot(p)},
            )

        def to_second(p, plane, src=None, of_spot=None, shift=0):
            held = cell(p, plane, spot if of_spot is None else of_spot)
            return remote(
                held if src is None else src,
                held,
                second_send.at[p, plane + shift],
                second_recv.at[p, plane + shift],
                {"dp": z * PLANE + second_spot(p)},
            )

        def column_to_second(p, spot_now):
            held = column(p, spot_now, side)
            return remote(
                held,
                held,
                second_send.at[p, planes],
                second_recv.at[p, planes],
                {"dp": z * PLANE + second_spot(p)},
            )

        def to_core(p, spot_now, of_side):
            held = column(p, spot_now, of_side)
            return remote(
                held, held, core_send.at[p, spot_now], core_recv.at[p, spot_now], {"segment": other}
            )

        def keep(p):
            return pltpu.make_async_copy(mine(p), cell(p, z, spot), part_here.at[p])

        for p in every:
            to_first(p, z, mine(p)).start()
            to_second(p, z, mine(p)).start()
            if p in small:
                for k in range(1, planes):
                    along(p, k).start()
            else:

                @pl.when(z < planes - 1)
                def _():
                    chain(p, z, True, mine(p)).start()

                @pl.when(z > 0)
                def _():
                    chain(p, z, False, mine(p)).start()

            keep(p).start()

        def peer_of(a, k):
            if kinds[a] == "plane":
                return z * PLANE + lax.rem(spot + k, PLANE)
            if kinds[a] == "line":
                return lax.rem(z + k, planes) * PLANE + spot
            return lax.rem(me + k, n)

        def number(a, chip):
            if kinds[a] == "plane":
                return chip % PLANE
            if kinds[a] == "line":
                return chip // PLANE
            return chip

        def source(a, chip):
            return ins[a].at[number(a, chip)]

        def slot(a, chip, of_side):
            if plans[a][1]:
                return results[a].at[chip, of_side]
            return results[a].at[number(a, chip)]

        def outgoing(a, k):
            peer = peer_of(a, k)
            return remote(
                source(a, peer),
                slot(a, me, side),
                send.at[a, k],
                recv.at[a, number(a, me)],
                {"dp": peer},
            )

        def incoming(a, chip):
            return remote(
                source(a, chip), slot(a, chip, side), send.at[a, 0], recv.at[a, number(a, chip)], {"dp": chip}
            )

        def passed(a, src, chip, of_side):
            return remote(
                src,
                slot(a, chip, of_side),
                pass_send.at[a, chip],
                pass_recv.at[a, chip],
                {"segment": other},
            )

        def crossing(a):
            return remote(
                ins[a].at[:, other],
                results[a],
                pass_send.at[a, 0],
                pass_recv.at[a, 0],
                {"segment": other},
            )

        def own(a):
            return pltpu.make_async_copy(source(a, me), slot(a, me, side), here.at[a])

        def spread(p, plane):
            from_plane(p, plane).wait_recv()
            to_first(p, plane).start()
            to_second(p, plane).start()

        if small:

            @pl.loop(1, planes)
            def _(k):
                for p in small:
                    spread(p, lax.rem(z + planes - k, planes))

        for d in range(1, planes) if large else ():

            @pl.when(z - d >= 0)
            def _():
                for p in large:
                    spread(p, z - d)

                    @pl.when(z < planes - 1)
                    def _():
                        chain(p, z - d, True).start()

            @pl.when(z + d < planes)
            def _():
                for p in large:
                    spread(p, z + d)

                    @pl.when(z > 0)
                    def _():
                        chain(p, z + d, False).start()

        for p in every:
            keep(p).wait()
            to_core(p, spot, side).start()
        if large:

            @pl.loop(0, planes)
            def _(k):
                plane = lax.rem(z + k, planes)
                for p in large:
                    to_first(p, plane, of_spot=first_spot(p)).wait_recv()
                    to_second(p, plane, of_spot=first_spot(p), shift=planes).start()

        if direct:

            @pl.loop(1, n)
            def _(k):
                for a in direct:
                    outgoing(a, k).start()

        for a in near:
            for k in range(1, outs[a].shape[0]):
                outgoing(a, k).start()
        for a in direct + near:
            own(a).start()
        for a in passing:
            passed(a, source(a, me), me, side).start()
        for a in single:
            crossing(a).start()

        for p in every:
            if p in small:

                @pl.loop(0, planes)
                def _(plane):
                    to_first(p, plane, of_spot=first_spot(p)).wait_recv()

                column_to_second(p, first_spot(p)).start()
            to_core(p, first_spot(p), side).start()
        for p in every:

            @pl.loop(0, planes)
            def _(plane):
                to_second(p, plane, of_spot=second_spot(p)).wait_recv()

            to_core(p, second_spot(p), side).start()
        for p in every:
            if p in small:
                column_to_second(p, across).wait_recv()
            else:

                @pl.loop(0, planes)
                def _(plane):
                    to_second(p, plane, of_spot=across, shift=planes).wait_recv()

            to_core(p, across, side).start()

        if direct:

            @pl.loop(1, n)
            def _(k):
                chip = lax.rem(me + n - k, n)
                for a in direct:
                    incoming(a, chip).wait_recv()
                    if plans[a][1]:
                        passed(a, slot(a, chip, side), chip, side).start()

        for a in near:
            for k in range(1, outs[a].shape[0]):
                incoming(a, peer_of(a, k)).wait_recv()
                outgoing(a, k).wait_send()
        for a in direct + near:
            own(a).wait()
        if direct:

            @pl.loop(1, n)
            def _(k):
                for a in direct:
                    outgoing(a, k).wait_send()

        if passing:

            @pl.loop(0, n)
            def _(k):
                for a in passing:
                    passed(a, slot(a, k, side), k, side).wait_send()
                    passed(a, slot(a, k, other), k, other).wait_recv()

        for a in single:
            crossing(a).wait()

        for p in every:
            if p in small:
                for k in range(1, planes):
                    along(p, k).wait_send()
                column_to_second(p, first_spot(p)).wait_send()
            else:
                for d in range(planes):

                    @pl.when(jnp.logical_and(z - d >= 0, z < planes - 1))
                    def _():
                        chain(p, z - d, True).wait_send()

                    @pl.when(jnp.logical_and(z + d < planes, z > 0))
                    def _():
                        chain(p, z + d, False).wait_send()

            @pl.loop(0, planes)
            def _(plane):
                to_first(p, plane).wait_send()
                to_second(p, plane).wait_send()
                if p in large:
                    to_second(p, plane, of_spot=first_spot(p), shift=planes).wait_send()

            @pl.loop(0, PLANE)
            def _(spot_now):
                to_core(p, spot_now, side).wait_send()
                to_core(p, spot_now, other).wait_recv()

    anywhere = pl.BlockSpec(memory_space=pl.ANY)
    relays = max(len(parts), 1)
    found = pl.pallas_call(
        body,
        out_shape=outs,
        in_specs=[anywhere] * count,
        out_specs=[anywhere] * count,
        scratch_shapes=[pltpu.SemaphoreType.DMA((count, n))] * 4
        + [pltpu.SemaphoreType.DMA((count,))]
        + [pltpu.SemaphoreType.DMA((relays, 2 * planes))] * 7
        + [pltpu.SemaphoreType.DMA((relays, PLANE))] * 2
        + [pltpu.SemaphoreType.DMA((relays,))],
        compiler_params=pltpu.CompilerParams(collective_id=ident, has_side_effects=True),
        cost_estimate=None if ident == 1 else NO_COST,
        name=f"exchange_{ident}",
    )(*arrays)
    return [
        x.reshape((n,) + x.shape[2:]) if kind == "relay" else x for kind, x in zip(kinds, found)
    ]


def share(ident, of_first, *of_second):
    arrays = (of_first, *of_second)
    count = len(arrays)

    def body(*refs):
        ins, results = refs[:count], refs[count : 2 * count]
        send, recv = refs[2 * count :]
        side = lax.axis_index("segment")
        other = 1 - side
        barrier = pltpu.get_barrier_semaphore()
        pl.semaphore_signal(barrier, inc=1, device_id={"segment": other}, device_id_type=MESH)
        pl.semaphore_wait(barrier, 1)

        def over(k):
            return pltpu.make_async_remote_copy(
                src_ref=ins[k],
                dst_ref=results[k],
                send_sem=send.at[k],
                recv_sem=recv.at[k],
                device_id={"segment": other},
                device_id_type=MESH,
            )

        for core, sent, found in ((0, [0], range(1, count)), (1, range(1, count), [0])):

            @pl.when(side == core)
            def _():
                for k in sent:
                    over(k).start()
                for k in found:
                    over(k).wait_recv()
                for k in sent:
                    over(k).wait_send()

    anywhere = pl.BlockSpec(memory_space=pl.ANY)
    arrived = pl.pallas_call(
        body,
        out_shape=[jax.ShapeDtypeStruct(x.shape, x.dtype) for x in arrays],
        in_specs=[anywhere] * count,
        out_specs=[anywhere] * count,
        scratch_shapes=[pltpu.SemaphoreType.DMA((count,))] * 2,
        compiler_params=pltpu.CompilerParams(collective_id=ident, has_side_effects=True),
        cost_estimate=NO_COST,
        name="share",
    )(*arrays)
    is_first = lax.axis_index("segment") == 0
    return [
        jnp.where(is_first == (k == 0), own, found) for k, (own, found) in enumerate(zip(arrays, arrived))
    ]


def local_call(kernel, name, out_shape, scratch, arguments, specs=None):
    return pl.pallas_call(
        kernel,
        out_shape=out_shape,
        in_specs=specs or [pl.BlockSpec(memory_space=pltpu.VMEM)] * len(arguments),
        scratch_shapes=scratch,
        compiler_params=pltpu.CompilerParams(vmem_limit_bytes=VMEM_BYTES),
        cost_estimate=None if name == "pack" else NO_COST,
        name=name,
    )(*arguments)


def split_two(value):
    top = value.astype(jnp.bfloat16)
    return top, (value - top.astype(jnp.float32)).astype(jnp.bfloat16)


def split_three(value):
    top = value.astype(jnp.bfloat16)
    rest = value - top.astype(jnp.float32)
    middle = rest.astype(jnp.bfloat16)
    bottom = (rest - middle.astype(jnp.float32)).astype(jnp.bfloat16)
    return top, middle, bottom


def exact_dot(value, low):
    rows = value.shape[0]
    product = low_dot(jnp.concatenate(split_three(value), axis=0), low)
    return product[:rows] + product[rows : 2 * rows] + product[2 * rows :]


def lane_of(shape):
    return lax.broadcasted_iota(jnp.int32, shape, len(shape) - 1)


def fold(value):
    axis = value.ndim - 1
    value = value + pltpu.roll(value, 64, axis)
    return value + pltpu.roll(value, 32, axis)


def turn(value, steps):
    steps = steps % LANES
    return pltpu.roll(value, steps, value.ndim - 1) if steps else value


def turn_back(value, steps):
    return pltpu.roll(value, lax.rem(LANES - steps, LANES), value.ndim - 1)


def row_pieces(rows, groups, taps, channels):
    depth = rows // groups
    pieces = []
    for chip in range(taps * channels // rows):
        for group in range(groups):
            first = chip * rows + group * depth
            at = first
            while at < first + depth:
                tap, channel = divmod(at, channels)
                take = min(first + depth - at, channels - channel)
                pieces.append((chip, group, at - first, tap, channel, take))
                at += take
    return pieces


def shift_rows(value, side, steps):
    parts = []
    empty = jnp.zeros((1,) + value.shape[1:], value.dtype)
    for first in range(0, value.shape[0], side):
        block = value[first : first + side]
        parts += [empty, block[:-1]] if steps > 0 else [block[1:], empty]
    return jnp.concatenate(parts, axis=0)


def per_micro(values, side):
    return jnp.concatenate(
        [jnp.broadcast_to(v[None], (side, SUBLANES, LANES)) for v in values], axis=0
    )


def pack_kernel(latent, noise, conv, squeeze, excite, critic, block, conv_out, noise_out, rows_f):
    side = lax.axis_index("segment")
    bf16 = jnp.bfloat16
    micros, _, edge, _, channels = latent.shape
    half_in = channels // 2
    rows_f[...] = jnp.zeros(rows_f.shape, jnp.float32)
    for m in range(micros):
        for i in range(edge):
            at = (m * edge + i) * SUBLANES
            rows_f[at : at + edge, :] = latent[m, 0, i].astype(jnp.float32)
    spread = rows_f.shape[0]
    block[:spread, :] = jnp.where(side == 0, rows_f[:, :half_in], rows_f[:, half_in:]).astype(bf16)
    at = spread
    for weight in (squeeze, excite, critic):
        rows = weight.shape[0] // 2
        block[at : at + rows, :] = jnp.where(side == 0, weight[:rows], weight[rows:]).astype(bf16)
        at += rows

    chips, depth, _ = conv_out.shape
    widths = conv.shape[1]
    half = widths // 2
    group = half // chips
    lane = lane_of((depth, LANES))
    for b in range(half // LANES):
        for c in range(LANES // group):
            value = jnp.zeros((depth, LANES), jnp.float32)
            for q in range(4):
                rows = slice(q * depth, (q + 1) * depth)
                first = conv[rows, b * LANES : (b + 1) * LANES]
                second = conv[rows, half + b * LANES : half + (b + 1) * LANES]
                to = q * group
                first = turn(first, to - c * group)
                second = turn(second, to - c * group)
                low = jnp.where(side == 0, first, turn(first, -group // 2))
                high = jnp.where(side == 0, turn(second, group // 2), second)
                both = jnp.where(lane % group < group // 2, low, high)
                value = jnp.where(lane // group == q, both, value)
            conv_out[b * (LANES // group) + c] = value.astype(bf16)

    pixels = noise.shape[2]
    parts = jnp.concatenate(
        [p.astype(jnp.float32) for p in split_three(noise[:, 0])]
        + [jnp.zeros((SUBLANES - 3 * micros, pixels), jnp.float32)],
        axis=0,
    ).astype(bf16)
    pixel = lax.broadcasted_iota(jnp.int32, (pixels, LANES), 0)
    spot = lane_of((pixels, LANES))
    within = spot % (4 * edge)
    lane_row = lane_of((1, LANES))
    lines = []
    for j in range(edge):
        wanted = 4 * edge * (within // 4) + 2 * edge * ((within % 4) // 2) + 2 * j + within % 2
        chosen = (pixel == wanted).astype(jnp.float32).astype(bf16)
        found = low_dot(parts, chosen)
        line = jnp.zeros((1, LANES), jnp.float32)
        for m in range(micros):
            total = found[m : m + 1] + found[micros + m : micros + m + 1]
            total = total + found[2 * micros + m : 2 * micros + m + 1]
            line = jnp.where(lane_row // (4 * edge) == m, total, line)
        lines.append(line)
    noise_out[...] = jnp.concatenate(
        lines + [jnp.zeros((SUBLANES - edge, LANES), jnp.float32)], axis=0
    )


def pack(n, latent, noise, conv_w, squeeze_w, excite_w, critic_w):
    micros, _, edge, _, channels = latent.shape
    spread = micros * edge * SUBLANES
    rows = spread + (squeeze_w.shape[0] + excite_w.shape[0] + critic_w.shape[0]) // 2
    return local_call(
        pack_kernel,
        "pack",
        [
            jax.ShapeDtypeStruct((rows, channels // 2), jnp.bfloat16),
            jax.ShapeDtypeStruct((n, conv_w.shape[0] // 4, LANES), jnp.bfloat16),
            jax.ShapeDtypeStruct((SUBLANES, LANES), jnp.float32),
        ],
        [pltpu.VMEM((spread, channels), jnp.float32)],
        [latent, noise, conv_w, squeeze_w, excite_w, critic_w],
    )


def own_columns(row_low, row_high, at, own):
    lane = lane_of((1, LANES))
    low = turn_back(row_low, at)
    high = turn(turn_back(row_high, at), own)
    value = jnp.where(lane < own, low, jnp.where(lane < 2 * own, high, 0.0))
    value = value + turn(value, 2 * own)
    return value + turn(value, 4 * own)


def front_kernel(side, micros, pixel_count, all_lat, conv, noise, vectors,
                 fake, xn, stats, opened_out, z1_out, pooled_out, consts, noise_rows,
                 weight, z, h, gate8):
    images = all_lat.shape[0]
    half_in = all_lat.shape[3]
    channels = 2 * half_in
    spread = micros * side * SUBLANES
    depth = conv.shape[1]
    taps = weight.shape[1] // LANES
    bf16, f32 = jnp.bfloat16, jnp.float32
    chip, core = lax.axis_index("dp"), lax.axis_index("segment")
    own = 16
    widths_rows = 2 * half_in // LANES
    at = 2 * own * lax.rem(chip, PLANE) + own * core
    base = chip // PLANE
    for k in range(3):
        consts[k : k + 1, :] = own_columns(
            vectors[pl.ds(k * widths_rows + base, 1), :],
            vectors[pl.ds(k * widths_rows + widths_rows // 2 + base, 1), :],
            at,
            own,
        )
    consts[3:, :] = jnp.zeros((SUBLANES - 3, LANES), f32)

    group = lane_of((depth, LANES)) // 32
    masks = [(group == g).astype(f32).astype(bf16) for g in range(4)]
    for owner, g, first, tap, channel, take in row_pieces(4 * depth, 4, taps, channels):
        weight[channel : channel + take, tap * LANES : (tap + 1) * LANES] = (
            conv[owner, first : first + take, :] * masks[g][:take]
        )
    lines = micros * side
    step = 4

    @pl.loop(0, images // step)
    def _(k):
        here = pl.ds(k * step, step)
        left = all_lat[here, 0, :spread].reshape(step * spread, half_in)
        right = all_lat[here, 1, :spread].reshape(step * spread, half_in)
        for tap in range(taps):
            cols = slice(tap * LANES, (tap + 1) * LANES)
            product = low_dot(left, weight[:half_in, cols]) + low_dot(right, weight[half_in:, cols])
            z[tap, here] = fold(product).reshape(step, lines, SUBLANES, LANES)

    from_lane = lax.broadcasted_iota(jnp.int32, (LANES, lines * LANES), 0)
    to_lane = lane_of((LANES, lines * LANES))
    chosen = from_lane == 4 * (to_lane // LANES) + (to_lane % LANES) // 32
    wide = exact_dot(
        noise[...].reshape(images * SUBLANES, LANES), chosen.astype(f32).astype(bf16)
    )
    for line in range(lines):
        noise_rows[:, line] = wide[:, line * LANES : (line + 1) * LANES].reshape(images, SUBLANES, LANES)

    shape3 = (lines, SUBLANES, LANES)
    lane = lane_of(shape3)
    row_first = (lane // 64) == 0
    col_first = ((lane // 32) % 2) == 0
    inside = lax.broadcasted_iota(jnp.int32, shape3, 1) < side
    first_half = (lane % 32) < 16
    gain_noise = consts[0:1, :][None]
    gain = consts[1:2, :][None]
    bias = consts[2:3, :][None]
    zero = jnp.zeros((SUBLANES, LANES), f32)

    def place(img, carry):
        lines_of = []
        for ky in range(3):
            z0, z1, z2 = z[3 * ky, img], z[3 * ky + 1, img], z[3 * ky + 2, img]
            lines_of.append(
                z1
                + jnp.where(col_first, pltpu.roll(z0, 1, 1), z0)
                + jnp.where(col_first, z2, pltpu.roll(z2, SUBLANES - 1, 1))
            )
        x0, x1, x2 = lines_of
        value = (
            x1
            + jnp.where(row_first, shift_rows(x0, side, 1), x0)
            + jnp.where(row_first, x2, shift_rows(x2, side, -1))
        )
        value = value + noise_rows[img] * gain_noise
        value = jnp.where(inside, value, 0.0)
        h[img] = value
        new = []
        for m in range(micros):
            part = value[m * side : (m + 1) * side]
            new.append(carry[2 * m] + jnp.sum(part, axis=0))
            new.append(carry[2 * m + 1] + jnp.sum(part * part, axis=0))
        return tuple(new)

    sums = lax.fori_loop(0, images, place, (zero,) * (2 * micros))
    means, stds = [], []
    for m in range(micros):
        mean_now = jnp.sum(fold(sums[2 * m]), axis=0, keepdims=True) / pixel_count
        square = jnp.sum(fold(sums[2 * m + 1]), axis=0, keepdims=True) / pixel_count
        means.append(mean_now)
        stds.append(lax.rsqrt(square - mean_now * mean_now + NORM_EPS))
        stats[m : m + 1, :] = stds[m]
    mean12, std12 = per_micro(means, side), per_micro(stds, side)

    count = images * micros
    rows_map = side * SUBLANES
    owner = lax.broadcasted_iota(jnp.int32, (count, count * rows_map), 1) // rows_map
    pool = (owner == lax.broadcasted_iota(jnp.int32, owner.shape, 0)).astype(f32).astype(bf16)
    area = 1.0 / (side * side)
    pooled = [
        low_dot(pool, all_lat[:, p, :spread].reshape(images * spread, half_in)) * area
        for p in range(2)
    ]
    rows_squeeze = channels // images // 2
    rows_excite = half_in // images // 2
    squeeze = all_lat[:, :, spread : spread + rows_squeeze].reshape(channels, half_in)
    excite = all_lat[:, :, spread + rows_squeeze : spread + rows_squeeze + rows_excite]
    excite = excite.reshape(half_in, half_in)
    z1 = exact_dot(pooled[0], squeeze[:half_in]) + exact_dot(pooled[1], squeeze[half_in:])
    z1_out[...] = z1
    pooled_out[:, :half_in] = pooled[0]
    pooled_out[:, half_in:] = pooled[1]
    wide = jax.nn.sigmoid(exact_dot(z1 * jax.nn.sigmoid(z1), excite))
    opened = wide[:, :LANES]
    for b in range(1, half_in // LANES):
        opened = jnp.where(base == b, wide[:, b * LANES : (b + 1) * LANES], opened)
    opened = jnp.where(lane_of(opened.shape) < own, turn_back(opened, at), 0.0)
    for steps in (own, 2 * own, 4 * own):
        opened = opened + turn(opened, steps)
    opened_out[...] = opened
    gate8[...] = jnp.broadcast_to(opened[:, None, :], gate8.shape)

    @pl.loop(0, images)
    def _(img):
        centred = (h[img] - mean12) * std12
        xn[img] = centred
        y = centred * gain + bias
        gated = y * turn(jax.nn.sigmoid(y), -16)
        pieces = []
        for m in range(micros):
            pieces.append(gated[m * side : (m + 1) * side] * gate8[img * micros + m][None])
        packed = jnp.where(first_half[:side], pieces[0], turn(pieces[1], 16))
        fake[img] = packed.reshape(side * SUBLANES, LANES).astype(bf16)


def front(side, micros, pixel_count, lat, conv, noise, vectors):
    images, _, _, half_in = lat.shape
    lines = micros * side
    count = images * micros
    f32 = jnp.float32
    return local_call(
        partial(front_kernel, side, micros, pixel_count),
        "front",
        [
            jax.ShapeDtypeStruct((images, side * SUBLANES, LANES), jnp.bfloat16),
            jax.ShapeDtypeStruct((images, lines, SUBLANES, LANES), f32),
            jax.ShapeDtypeStruct((SUBLANES, LANES), f32),
            jax.ShapeDtypeStruct((count, LANES), f32),
            jax.ShapeDtypeStruct((count, half_in), f32),
            jax.ShapeDtypeStruct((count, 2 * half_in), f32),
            jax.ShapeDtypeStruct((SUBLANES, LANES), f32),
            jax.ShapeDtypeStruct((images, lines, SUBLANES, LANES), f32),
        ],
        [
            pltpu.VMEM((2 * half_in, 9 * LANES), jnp.bfloat16),
            pltpu.VMEM((9, images, lines, SUBLANES, LANES), f32),
            pltpu.VMEM((images, lines, SUBLANES, LANES), f32),
            pltpu.VMEM((count, SUBLANES, LANES), f32),
        ],
        [lat, conv, noise, vectors],
    )


def critic_kernel(side, patches, spread, arrived, lat, real_bank, feat, proj, power, vectors, chosen,
                  dfake, dspec, tail, column_v, column_t, row_w, maps):
    bf16 = jnp.bfloat16
    core = lax.axis_index("segment")
    chips, _, rows_map, _ = arrived.shape
    size = feat.shape[0]
    at = 6 * size // LANES
    head = jnp.concatenate([vectors[at + k : at + k + 1, :] for k in range(size // LANES)], axis=1)
    offset = vectors[at + size // LANES : at + size // LANES + 1, 0:1]
    rows_before = spread + size // chips + size // chips // 2
    weight = lat[:, :, rows_before : rows_before + size // chips // 2]
    weight = weight.reshape(size, size).astype(jnp.float32)
    product = jnp.sum(weight * power[...], axis=1, keepdims=True)
    length = lax.rsqrt(jnp.sum(product * product))
    vec = product * length
    back = jnp.sum(weight * vec, axis=0, keepdims=True)
    sigma = jnp.sqrt(jnp.sum(back * back))
    unit = back / sigma
    turned = jnp.sum(weight * unit, axis=1, keepdims=True)
    turned = (turned - vec * jnp.sum(turned * vec)) * length
    column_v[...] = vec
    column_t[...] = turned
    row_w[...] = jnp.broadcast_to(unit, row_w.shape)
    spectral = (weight / sigma).astype(bf16)

    lane = lane_of((rows_map, LANES))
    per_block = LANES // 32
    for b in range(size // LANES):
        for q in range(4):
            value = None
            for c in range(per_block):
                chip = b * per_block + c
                low = arrived[chip, 0].astype(jnp.float32)
                high = arrived[chip, 1].astype(jnp.float32)
                low = jnp.where(core == 0, low, turn(low, -16))
                high = jnp.where(core == 0, turn(high, 16), high)
                both = turn(jnp.where(lane % 32 < 16, low, high), 32 * (c - q))
                value = both if value is None else jnp.where(lane // 32 == c, both, value)
            maps[q * rows_map : (q + 1) * rows_map, b * LANES : (b + 1) * LANES] = value.astype(bf16)
    fakes = 4 * rows_map
    maps[fakes:, :] = real_bank[chosen[core, 0]]
    rows = maps.shape[0]
    pre_act = low_dot(maps[...], feat[...])
    features = (pre_act * jax.nn.sigmoid(pre_act)).astype(bf16)
    projected = low_dot(features, proj[...]).astype(bf16)
    critic_act = low_dot(projected, spectral)
    opened = jax.nn.sigmoid(critic_act)
    activated = critic_act * opened
    logits = jnp.sum(activated * head, axis=1, keepdims=True) + offset
    row = lax.broadcasted_iota(jnp.int32, (rows, 1), 0)
    sign = jnp.where(row < fakes, 1.0, -1.0)
    valid = jnp.logical_or(row >= fakes, (row % SUBLANES) < side)
    margin = 1.0 + sign * logits
    soft = jnp.maximum(margin, 0.0) + jnp.log1p(jnp.exp(-jnp.abs(margin)))
    loss = jnp.sum(jnp.where(valid, soft, 0.0))
    dlogit = jnp.where(valid, sign * jax.nn.sigmoid(margin), 0.0) / patches
    slope = opened * (1.0 + critic_act * (1.0 - opened))
    dact = (dlogit * head * slope).astype(bf16)
    found = lax.dot_general(
        projected, dact, (((0,), (0,)), ((), ())), preferred_element_type=jnp.float32
    )
    dspec[...] = found.reshape(dspec.shape)
    dhead = jnp.sum(dlogit * activated, axis=0, keepdims=True)
    lane_row = lane_of((1, LANES))
    last = jnp.where(lane_row == 0, jnp.sum(dlogit), jnp.where(lane_row == 1, loss, 0.0))
    pieces = [dhead[:, k * LANES : (k + 1) * LANES] for k in range(size // LANES)] + [last]
    tail[...] = jnp.concatenate(
        pieces + [jnp.zeros((SUBLANES - len(pieces), LANES), jnp.float32)], axis=0
    )
    turned_dims = (((1,), (1,)), ((), ()))
    dproj = lax.dot_general(
        dact[:fakes], spectral, turned_dims, preferred_element_type=jnp.float32
    ).astype(bf16)
    dpre = lax.dot_general(dproj, proj[...], turned_dims, preferred_element_type=jnp.float32)
    dpre = (dpre * silu_slope(pre_act[:fakes])).astype(bf16)
    dmaps = lax.dot_general(dpre, feat[...], turned_dims, preferred_element_type=jnp.float32)
    for chip in range(chips):
        b, c = divmod(chip, per_block)
        value = None
        for q in range(4):
            part = dmaps[q * rows_map : (q + 1) * rows_map, b * LANES : (b + 1) * LANES]
            part = turn(part, 32 * (q - c))
            value = part if value is None else jnp.where(lane // 32 == q, part, value)
        dfake[chip] = value.astype(bf16)


def critic_step(side, patches, spread, arrived, lat, real_bank, feat, proj, power, vectors, chosen):
    f32 = jnp.float32
    chips, _, rows_map, _ = arrived.shape
    size = feat.shape[0]
    vmem = pl.BlockSpec(memory_space=pltpu.VMEM)
    smem = pl.BlockSpec(memory_space=pltpu.SMEM)
    return local_call(
        partial(critic_kernel, side, patches, spread),
        "critic_step",
        [
            jax.ShapeDtypeStruct((chips, rows_map, LANES), jnp.bfloat16),
            jax.ShapeDtypeStruct((chips, 2, size // chips // 2, size), f32),
            jax.ShapeDtypeStruct((SUBLANES, LANES), f32),
            jax.ShapeDtypeStruct((size, 1), f32),
            jax.ShapeDtypeStruct((size, 1), f32),
            jax.ShapeDtypeStruct((SUBLANES, size), f32),
        ],
        [pltpu.VMEM((4 * rows_map + real_bank.shape[1], size), jnp.bfloat16)],
        [arrived, lat, real_bank, feat, proj, power, vectors, chosen],
        [vmem] * 7 + [smem],
    )


def back_kernel(side, micros, pixel_count, grads, xn, all_lat, noise_rows, consts, stats, opened, tail,
                dspec_own, dspec_other, dconv, block, dspec, dy, packed, product, gate8, dze):
    images = all_lat.shape[0]
    half_in = all_lat.shape[3]
    channels = 2 * half_in
    lines = micros * side
    spread = lines * SUBLANES
    bf16 = jnp.bfloat16
    shape3 = (lines, SUBLANES, LANES)
    lane = lane_of(shape3)
    row_first = (lane // 64) == 0
    col_first = ((lane // 32) % 2) == 0
    first_half = (lane % 32) < 16
    inside = lax.broadcasted_iota(jnp.int32, shape3, 1) < side
    gain = consts[1:2, :][None]
    bias = consts[2:3, :][None]
    zero = jnp.zeros((SUBLANES, LANES), jnp.float32)
    core = lax.axis_index("segment")
    second = core == 1
    gate8[...] = jnp.broadcast_to(opened[...][:, None, :], gate8.shape)
    for plane in range(images // PLANE):
        for spot in range(PLANE):
            k = plane * PLANE + spot
            dspec[spot, plane] = jnp.where(second, dspec_own[k, 1], dspec_own[k, 0]) + dspec_other[k]

    def through_gate(img, carry):
        ascent = -grads[img].astype(jnp.float32).reshape(shape3)
        ascent = jnp.where(second, turn(ascent, -16), ascent)
        ascent = jnp.where(first_half, ascent, 0.0)
        centred = xn[img]
        y = centred * gain + bias
        gate = turn(jax.nn.sigmoid(y), -16)
        dopened = ascent * (y * gate)
        scale = jnp.concatenate(
            [jnp.broadcast_to(gate8[img * micros + m][None], (side, SUBLANES, LANES)) for m in range(micros)],
            axis=0,
        )
        dgated = ascent * scale
        dnormed = jnp.where(first_half, dgated * gate, turn(dgated * y * gate * (1.0 - gate), 16))
        dy[img] = dnormed
        new = []
        for m in range(micros):
            part = slice(m * side, (m + 1) * side)
            total = fold(jnp.sum(dopened[part], axis=0))
            total = total + turn(total, 16)
            gate_now = gate8[img * micros + m]
            dze[img * micros + m] = (
                jnp.broadcast_to(jnp.sum(total, axis=0, keepdims=True), (SUBLANES, LANES))
                * gate_now
                * (1.0 - gate_now)
            )
            new.append(carry[2 * m] + jnp.sum(dnormed[part] * centred[part], axis=0))
            new.append(carry[2 * m + 1] + jnp.sum(dnormed[part], axis=0))
        return tuple(new)

    sums = lax.fori_loop(0, images, through_gate, (zero,) * (2 * micros))
    sums = [jnp.sum(fold(s), axis=0, keepdims=True) for s in sums]
    gain_row = consts[1:2, :]
    mean_back = per_micro([gain_row * sums[2 * m + 1] / pixel_count for m in range(micros)], side)
    cross_back = per_micro([gain_row * sums[2 * m] / pixel_count for m in range(micros)], side)
    std12 = per_micro([stats[m : m + 1, :] for m in range(micros)], side)
    taps = 9
    groups = (taps + 3) // 4
    lane_flat = lane_of((spread, LANES)) // 32

    def through_norm(img, carry):
        centred = xn[img]
        dshift = (dy[img] * gain - mean_back - centred * cross_back) * std12
        dshift = jnp.where(inside, dshift, 0.0)
        carry = carry + jnp.sum(dshift * noise_rows[img], axis=0)
        dh = dshift.astype(bf16).astype(jnp.float32)
        swapped = jnp.where(col_first, turn(dh, -32), turn(dh, 32))
        col0 = jnp.where(col_first, dh, swapped)
        col1 = jnp.where(col_first, swapped, dh)
        by_col = [
            col1 + pltpu.roll(col0, SUBLANES - 1, 1),
            col0 + col1,
            col0 + pltpu.roll(col1, 1, 1),
        ]
        found = [None] * taps
        for kx in range(3):
            value = by_col[kx]
            turned = turn(value, 64)
            row0 = jnp.where(row_first, value, turned)
            row1 = jnp.where(row_first, turned, value)
            found[kx] = row1 + shift_rows(row0, side, -1)
            found[3 + kx] = row0 + row1
            found[6 + kx] = row0 + shift_rows(row1, side, 1)
        for g in range(groups):
            members = [f.reshape(spread, LANES) for f in found[4 * g : 4 * g + 4]]
            value = members[0]
            for k in range(1, len(members)):
                value = jnp.where(lane_flat == k, members[k], value)
            top, rest = split_two(value)
            packed[img, :, g * LANES : (g + 1) * LANES] = top
            packed[img, :, (groups + g) * LANES : (groups + g + 1) * LANES] = rest
        return carry

    dgain_noise = lax.fori_loop(0, images, through_norm, zero)
    dgain_noise = jnp.sum(fold(dgain_noise), axis=0, keepdims=True)
    lane_row = lane_of((1, LANES))
    for r in range(images * micros // 8):
        value = jnp.zeros((1, LANES), jnp.float32)
        for g in range(8):
            value = jnp.where(lane_row // 16 == g, dze[8 * r + g][0:1], value)
        block[r : r + 1, :] = value
    gains = jnp.where(
        lane_row // 32 == 0,
        dgain_noise,
        jnp.where(
            lane_row // 32 == 1,
            sum(sums[2 * m] for m in range(micros)),
            sum(sums[2 * m + 1] for m in range(micros)),
        ),
    )
    block[4:5, :] = gains
    block[5:8, :] = jnp.zeros((3, LANES), jnp.float32)
    block[8:16, :] = tail[...]

    width = groups * LANES
    flat = packed[...].reshape(images * spread, 2 * width)
    for p in range(2):
        side_rows = all_lat[:, p, :spread].reshape(images * spread, half_in)
        both = lax.dot_general(
            side_rows, flat, (((0,), (0,)), ((), ())), preferred_element_type=jnp.float32
        )
        product[p * half_in : (p + 1) * half_in, :] = both[:, :width] + both[:, width:]
    depth = dconv.shape[1]
    unit = 16
    lane_unit = lane_of((unit, LANES)) // 32
    for chip in range(dconv.shape[0]):
        for at in range(0, depth, unit):
            value = None
            for g in range(4):
                tap, channel = divmod((chip * 4 + g) * depth + at, channels)
                piece = product[channel : channel + unit, (tap // 4) * LANES : (tap // 4 + 1) * LANES]
                piece = turn(piece, 32 * (g - tap % 4))
                value = piece if value is None else jnp.where(lane_unit == g, piece, value)
            dconv[chip, at : at + unit, :] = value.astype(bf16)


def back(side, micros, pixel_count, depth, grads, xn, lat, noise_rows, consts, stats, opened, tail,
         dspec_own, dspec_other):
    images, _, _, half_in = lat.shape
    lines = micros * side
    count = images * micros
    f32 = jnp.float32
    return local_call(
        partial(back_kernel, side, micros, pixel_count),
        "back",
        [
            jax.ShapeDtypeStruct((images, depth, LANES), jnp.bfloat16),
            jax.ShapeDtypeStruct((2 * SUBLANES, LANES), f32),
            jax.ShapeDtypeStruct((PLANE, images // PLANE) + dspec_other.shape[1:], f32),
        ],
        [
            pltpu.VMEM((images, lines, SUBLANES, LANES), f32),
            pltpu.VMEM((images, lines * SUBLANES, 6 * LANES), jnp.bfloat16),
            pltpu.VMEM((2 * half_in, 3 * LANES), f32),
            pltpu.VMEM((count, SUBLANES, LANES), f32),
            pltpu.VMEM((count, SUBLANES, LANES), f32),
        ],
        [grads, xn, lat, noise_rows, consts, stats, opened, tail, dspec_own, dspec_other],
    )


def owner_kernel(dconv, mom, parts_in, mom_new, gram, parts, top, rest):
    chips, _, depth, _ = dconv.shape
    rows, widths = mom.shape
    half = widths // 2
    blocks = widths // LANES
    core = lax.axis_index("segment")
    lane = lane_of((depth, LANES))
    parts[...] = jnp.sum(parts_in[...], axis=0)
    for b in range(half // LANES):
        halves = []
        for c in range(PLANE):
            low = dconv[b * PLANE + c, 0].astype(jnp.float32)
            high = dconv[b * PLANE + c, 1].astype(jnp.float32)
            halves.append(
                (
                    jnp.where(lane % 32 < 16, low, turn(high, 16)),
                    jnp.where(lane % 32 < 16, turn(low, -16), high),
                )
            )
        for q in range(4):
            for k in range(2):
                value = None
                for c in range(PLANE):
                    piece = turn(halves[c][k], 32 * (c - q))
                    value = piece if value is None else jnp.where(lane // 32 == c, piece, value)
                at = (slice(q * depth, (q + 1) * depth), slice(k * half + b * LANES, k * half + (b + 1) * LANES))
                mom_new[at] = MOMENTUM * mom[at] + value
    for b in range(blocks):
        high, low = split_two(mom_new[:, b * LANES : (b + 1) * LANES])
        for at in (b, b + blocks) if b < PLANE else (b,):
            cols = slice(at * LANES, (at + 1) * LANES)
            top[:, cols] = high
            rest[:, cols] = low
    dims = (((0,), (0,)), ((), ()))
    share = LANES // 4
    span = gram.shape[2]

    @pl.loop(0, blocks)
    def _(b):
        own = pl.ds(pl.multiple_of(b * LANES, LANES), LANES)
        wide = pl.ds(pl.multiple_of(b * LANES, LANES), span)
        left_high, left_low = top[:, own], rest[:, own]
        right_high, right_low = top[:, wide], rest[:, wide]

        def times(left, right):
            return lax.dot_general(left, right, dims, preferred_element_type=jnp.float32)

        found = times(left_high, right_high) + (times(left_high, right_low) + times(left_low, right_high))
        for h in range(2):
            first = 2 * share * h
            gram[2 * b + h] = jnp.where(
                core == 0, found[first : first + share], found[first + share : first + 2 * share]
            )


def owner(dconv, mom, dspec):
    chips, _, depth, _ = dconv.shape
    rows, widths = mom.shape
    f32 = jnp.float32
    span = (widths // LANES // 2 + 1) * LANES
    return local_call(
        owner_kernel,
        "owner",
        [
            jax.ShapeDtypeStruct(mom.shape, f32),
            jax.ShapeDtypeStruct((chips, widths // chips // 2, span), f32),
            jax.ShapeDtypeStruct(dspec.shape[1:], f32),
        ],
        [pltpu.VMEM((rows, widths + PLANE * LANES), jnp.bfloat16)] * 2,
        [dconv, mom, dspec],
    )


def three(left_high, left_low, right_high, right_low, dims=(((1,), (0,)), ((), ()))):
    def times(left, right):
        return lax.dot_general(left, right, dims, preferred_element_type=jnp.float32)

    return times(left_high, right_high) + (times(left_high, right_low) + times(left_low, right_high))


def store_block(value, i, j, high, low):
    rows, cols = slice(i * BLOCK, (i + 1) * BLOCK), slice(j * BLOCK, (j + 1) * BLOCK)
    high[rows, cols], low[rows, cols] = split_two(value)
    if i < j:
        high[cols, rows], low[cols, rows] = split_two(value.T)


def polynomial(gram, gram_high, gram_low, high, low):
    for j in range(gram.shape[0] // BLOCK):
        cols, rows = slice(j * BLOCK, (j + 1) * BLOCK), slice(0, (j + 1) * BLOCK)
        found = three(gram_high[rows, :], gram_low[rows, :], gram_high[:, cols], gram_low[:, cols])
        for i in range(j + 1):
            here = slice(i * BLOCK, (i + 1) * BLOCK)
            store_block(NEWTON_B * gram[here, cols] + NEWTON_C * found[here], i, j, high, low)


def multiply(source, source_high, source_low, poly_high, poly_low, result, high, low):
    for j in range(source.shape[0] // BLOCK):
        cols, rows = slice(j * BLOCK, (j + 1) * BLOCK), slice(0, (j + 1) * BLOCK)
        found = three(source_high[rows, :], source_low[rows, :], poly_high[:, cols], poly_low[:, cols])
        for i in range(j + 1):
            here = slice(i * BLOCK, (i + 1) * BLOCK)
            value = NEWTON_A * source[here, cols] + found[here]
            result[here, cols] = value
            store_block(value, i, j, high, low)


def apply(x, x_high, x_low, poly_high, poly_low):
    for j in range(x.shape[1] // BLOCK):
        cols = slice(j * BLOCK, (j + 1) * BLOCK)
        found = three(x_high[...], x_low[...], poly_high[:, cols], poly_low[:, cols])
        x[:, cols] = NEWTON_A * x[:, cols] + found


def resplit(x, x_high, x_low):
    for j in range(x.shape[1] // BLOCK):
        cols = slice(j * BLOCK, (j + 1) * BLOCK)
        x_high[:, cols], x_low[:, cols] = split_two(x[:, cols])


def conv_ortho(packed, x, gram, high, low, p_high, p_low, x_high, x_low):
    size = gram.shape[1]
    blocks = size // LANES
    share = packed.shape[2] - 2 * SUBLANES
    span = packed.shape[3] // LANES
    chips_block = LANES // (2 * share)

    def block(b, k):
        pair = pl.ds(b * chips_block, chips_block)
        return packed[pair, :, :share, k * LANES : (k + 1) * LANES].reshape(LANES, LANES)

    eye = lax.broadcasted_iota(jnp.int32, (LANES, LANES), 0) == lane_of((LANES, LANES))

    def add_squares(b, total):
        return total + jnp.where(eye, block(b, 0), 0.0)

    total = lax.fori_loop(0, blocks, add_squares, jnp.zeros((LANES, LANES), jnp.float32))
    scale = 1.0 / (jnp.sqrt(jnp.sum(total)) + 1e-07)

    @pl.loop(0, blocks)
    def _(r):
        rows = pl.ds(pl.multiple_of(r * LANES, LANES), LANES)
        for ahead in range(span):
            cols = pl.ds(pl.multiple_of(lax.rem(r + ahead, blocks) * LANES, LANES), LANES)
            value = (block(r, ahead) * scale) * scale
            gram[0, rows, cols] = value
            high[0, rows, cols], low[0, rows, cols] = split_two(value)
            if ahead:
                value = value.T
                gram[0, cols, rows] = value
                high[0, cols, rows], low[0, cols, rows] = split_two(value)

    for j in range(size // BLOCK):
        cols = slice(j * BLOCK, (j + 1) * BLOCK)
        value = x[:, cols] * scale
        x[:, cols] = value
        x_high[:, cols], x_low[:, cols] = split_two(value)

    @pl.loop(0, NS_STEPS)
    def _(step):
        polynomial(gram.at[0], high.at[0], low.at[0], p_high, p_low)
        apply(x, x_high, x_low, p_high, p_low)

        @pl.when(step < NS_STEPS - 1)
        def _():
            resplit(x, x_high, x_low)
            for k in range(2):
                multiply(
                    gram.at[k], high.at[k], low.at[k], p_high, p_low,
                    gram.at[1 - k], high.at[1 - k], low.at[1 - k],
                )


def whole_ortho(chunks, x, x_high, x_low, gram, g_high, g_low, p_high, p_low):
    size = gram.shape[0]

    def rows_of(c):
        return pl.ds(pl.multiple_of(c * size, size), size)

    def add_squares(c, total):
        value = x[rows_of(c), :]
        return total + jnp.sum(value * value)

    scale = 1.0 / (jnp.sqrt(lax.fori_loop(0, chunks, add_squares, jnp.float32(0.0))) + 1e-07)

    @pl.loop(0, chunks)
    def _(c):
        rows = rows_of(c)
        value = x[rows, :] * scale
        x[rows, :] = value
        x_high[rows, :], x_low[rows, :] = split_two(value)

    @pl.loop(0, NS_STEPS)
    def _(_):
        gram[...] = jnp.zeros(gram.shape, jnp.float32)

        @pl.loop(0, chunks)
        def _(c):
            for j in range(size // BLOCK):
                cols, above = slice(j * BLOCK, (j + 1) * BLOCK), slice(0, (j + 1) * BLOCK)
                gram[above, cols] += three(
                    x_high[rows_of(c), above],
                    x_low[rows_of(c), above],
                    x_high[rows_of(c), cols],
                    x_low[rows_of(c), cols],
                    (((0,), (0,)), ((), ())),
                )

        for j in range(size // BLOCK):
            for i in range(j + 1):
                at = (slice(i * BLOCK, (i + 1) * BLOCK), slice(j * BLOCK, (j + 1) * BLOCK))
                store_block(gram[at], i, j, g_high, g_low)
        polynomial(gram, g_high, g_low, p_high, p_low)

        @pl.loop(0, chunks)
        def _(c):
            rows = rows_of(c)
            for j in range(size // BLOCK):
                cols = slice(j * BLOCK, (j + 1) * BLOCK)
                found = three(x_high[rows, :], x_low[rows, :], p_high[:, cols], p_low[:, cols])
                x[rows, cols] = NEWTON_A * x[rows, cols] + found
            x_high[rows, :], x_low[rows, :] = split_two(x[rows, :])


def outer_sum(left, right):
    a, b, c = split_three(left)
    d, e, f = split_three(right)
    return lax.dot_general(
        jnp.concatenate([a, a, b, a, b, c], axis=0),
        jnp.concatenate([d, e, d, f, e, d], axis=0),
        (((0,), (0,)), ((), ())),
        preferred_element_type=jnp.float32,
    )


def update_kernel(spread, size, summed, conv_mom, conv_w, lat, moms, squeeze_w, excite_w, critic_w, pooled, z1,
                  column_v, column_t, row_w, power, vectors, vec_m, vec_v,
                  conv_new, small, adam_out,
                  sems, x, gram, high, low, p_high, p_low, x_high, x_low, w,
                  whole, whole_high, whole_low, small_gram, sg_high, sg_low, sp_high, sp_low, weights, dze, moms_all):
    core = lax.axis_index("segment")
    chip = lax.axis_index("dp")
    keep = 1.0 - MUON_RATE * DECAY
    f32 = jnp.float32

    @pl.when(core == 0)
    def _():
        load_mom = pltpu.make_async_copy(conv_mom, x, sems.at[0])
        load_w = pltpu.make_async_copy(conv_w, w, sems.at[1])
        load_mom.start()
        load_w.start()
        load_mom.wait()
        conv_ortho(summed, x, gram, high, low, p_high, p_low, x_high, x_low)
        load_w.wait()
        conv_new[...] = w[...] * keep - MUON_RATE * x[...]

    @pl.when(core == 1)
    def _():
        chips = lat.shape[0]
        rows_each = [weight.shape[0] for weight in (squeeze_w, excite_w, critic_w)]
        lows = weights.shape[2]
        load_low = pltpu.make_async_copy(
            lat.at[:, :, pl.ds(spread + rows_each[0] // 2, lows)], weights, sems.at[0]
        )
        load_moms = pltpu.make_async_copy(moms, moms_all, sems.at[1])
        load_low.start()
        load_moms.start()
        own = size // chips // 2
        lane = lane_of((4 * (size // LANES), LANES)) // own
        groups = LANES // own
        held = []
        for e in range(groups):
            rows = []
            for b in range(size // LANES):
                device = b * groups + e
                rows.append(summed[device // 2, device % 2, -2 * SUBLANES : -SUBLANES, size:][:4])
            held.append(jnp.concatenate(rows, axis=0))
        for g in range(groups):
            value = jnp.zeros_like(held[0])
            for e in range(groups):
                value = jnp.where(lane == e, turn(held[e], own * (e - g)), value)
            for b in range(size // LANES):
                for r in range(4):
                    dze[groups * r + g : groups * r + g + 1, b * LANES : (b + 1) * LANES] = (
                        value[4 * b + r : 4 * b + r + 1]
                    )
        load_low.wait()
        load_moms.wait()
        excite_low = weights[:, :, : rows_each[1] // 2].reshape(size, size)
        critic = weights[:, :, rows_each[1] // 2 :].reshape(size, size).astype(f32)
        gate = z1[...]
        squeezed = gate * jax.nn.sigmoid(gate)
        back = lax.dot_general(
            jnp.concatenate(split_three(dze[...]), axis=0),
            excite_low,
            (((1,), (1,)), ((), ())),
            preferred_element_type=f32,
        )
        rows = dze.shape[0]
        back = back[:rows] + back[rows : 2 * rows] + back[2 * rows :]
        dz1 = back * silu_slope(gate)

        starts, firsts = [0], [0]
        for count in rows_each:
            starts.append(starts[-1] + count)
            firsts.append(firsts[-1] + chips * count)

        def fill(k, grad):
            count = rows_each[k]
            old = moms_all[:, starts[k] : starts[k + 1]].reshape(chips * count, size)
            whole[firsts[k] : firsts[k + 1], :] = MOMENTUM * old + grad

        fill(0, outer_sum(pooled[...], dz1))
        fill(1, outer_sum(squeezed, dze[...]))
        spec = summed[:, :, -2 * SUBLANES :, :size].reshape(size, size)
        vec = column_v[...]
        back_row = jnp.sum(critic * vec, axis=0, keepdims=True)
        square = jnp.sum(back_row * back_row)
        along = jnp.sum(spec * critic) / square
        direction = vec * row_w[0:1, :] + column_t[...] * power[...]
        fill(2, spec / jnp.sqrt(square) - along * direction)

        def own_rows(k):
            count = rows_each[k]
            return whole[pl.ds(pl.multiple_of(firsts[k] + chip * count, count), count), :]

        for k in range(3):
            small[starts[k] : starts[k + 1], :] = own_rows(k)

        @pl.loop(0, 3)
        def _(k):
            chunks = jnp.where(k == 0, firsts[1] // size, 1)
            first = jnp.where(k == 0, 0, firsts[1] + (k - 1) * size)
            view = whole.at[pl.ds(pl.multiple_of(first, size), firsts[1])]
            whole_ortho(
                chunks, view, whole_high, whole_low, small_gram, sg_high, sg_low, sp_high, sp_low
            )

        for k, weight in enumerate((squeeze_w, excite_w, critic_w)):
            small[starts[3] + starts[k] : starts[3] + starts[k + 1], :] = (
                weight[...] * keep - MUON_RATE * own_rows(k)
            )

        vec_rows = vectors.shape[0]
        lane_row = lane_of((1, LANES))
        lines = []
        for gain in range(3):
            for half in range(2):
                for b in range(size // LANES):
                    value = jnp.zeros((1, LANES), f32)
                    for e in range(groups):
                        device = b * groups + e
                        row = summed[device // 2, device % 2, -2 * SUBLANES : -SUBLANES, size:][4:5]
                        row = turn(row, own * (e - (2 * gain + half)))
                        value = jnp.where(lane_row // own == e, row, value)
                    lines.append(value)
        tails = jnp.sum(summed[:, :, -SUBLANES:, size:], axis=(0, 1))
        count = size // LANES
        last = tails[count : count + 1]
        lines += [tails[k : k + 1] for k in range(count)]
        lines.append(jnp.where(lane_row == 0, last, 0.0))
        lines.append(jnp.zeros((vec_rows - len(lines), LANES), f32))
        results = adam(vectors[...], vec_m[...], vec_v[...], jnp.concatenate(lines, axis=0))
        for k in range(3):
            adam_out[k * vec_rows : (k + 1) * vec_rows, :] = results[k]
        adam_out[3 * vec_rows :, :] = jnp.broadcast_to(jnp.sum(jnp.where(lane_row == 1, last, 0.0)), (SUBLANES, LANES))


def update(summed, conv_mom, conv_w, lat, moms, squeeze_w, excite_w, critic_w, pooled, z1, column_v, column_t,
           row_w, power, vectors, vec_m, vec_v, spread, size):
    f32, bf16 = jnp.float32, jnp.bfloat16
    widths = conv_w.shape[1]
    chips = lat.shape[0]
    small_rows = squeeze_w.shape[0] + excite_w.shape[0] + critic_w.shape[0]
    arguments = [summed, conv_mom, conv_w, lat, moms, squeeze_w, excite_w, critic_w, pooled, z1, column_v, column_t,
                 row_w, power, vectors, vec_m, vec_v]
    vmem, anywhere = pl.BlockSpec(memory_space=pltpu.VMEM), pl.BlockSpec(memory_space=pl.ANY)
    pair, square, small_square = (2, widths, widths), (widths, widths), (size, size)
    tall = chips * squeeze_w.shape[0]
    return local_call(
        partial(update_kernel, spread, size),
        "update",
        [
            jax.ShapeDtypeStruct(conv_w.shape, f32),
            jax.ShapeDtypeStruct((2 * small_rows, size), f32),
            jax.ShapeDtypeStruct((3 * vectors.shape[0] + SUBLANES, LANES), f32),
        ],
        [
            pltpu.SemaphoreType.DMA((2,)),
            pltpu.VMEM(conv_w.shape, f32),
            pltpu.VMEM(pair, f32),
            pltpu.VMEM(pair, bf16),
            pltpu.VMEM(pair, bf16),
            pltpu.VMEM(square, bf16),
            pltpu.VMEM(square, bf16),
            pltpu.VMEM(conv_w.shape, bf16),
            pltpu.VMEM(conv_w.shape, bf16),
            pltpu.VMEM(conv_w.shape, f32),
            pltpu.VMEM((chips * small_rows + size, size), f32),
            pltpu.VMEM((tall, size), bf16),
            pltpu.VMEM((tall, size), bf16),
            pltpu.VMEM(small_square, f32),
            pltpu.VMEM(small_square, bf16),
            pltpu.VMEM(small_square, bf16),
            pltpu.VMEM(small_square, bf16),
            pltpu.VMEM(small_square, bf16),
            pltpu.VMEM((chips, 2, (excite_w.shape[0] + critic_w.shape[0]) // 2, size), bf16),
            pltpu.VMEM(z1.shape, f32),
            pltpu.VMEM(moms.shape, f32),
        ],
        arguments,
        [vmem] + [anywhere] * 4 + [vmem] * 12,
    )


def by_channels(
    latent,
    noise,
    real_bank,
    real_index,
    frozen_feat,
    frozen_proj,
    power_vec,
    conv_w,
    conv_mom,
    squeeze_w,
    squeeze_mom,
    excite_w,
    excite_mom,
    critic_w,
    critic_mom,
    vectors,
    vec_m,
    vec_v,
):
    n = lax.axis_size("dp")
    chip, side = lax.axis_index("dp"), lax.axis_index("segment")
    f32 = jnp.float32
    micros, _, edge, _, channels = latent.shape
    pixels = noise.shape[2]
    rows, widths = conv_w.shape
    half = widths // 2
    own = half // n // 2
    depth = rows // 4
    proj_width = critic_w.shape[1]
    pixel_count = pixels * n
    patches = micros * pixel_count
    spread = micros * edge * SUBLANES

    def rows_of(vector):
        count = -(-vector.shape[0] // (SUBLANES * LANES)) * SUBLANES
        return jnp.pad(vector, (0, count * LANES - vector.shape[0])).reshape(count, LANES)

    vectors_rows = rows_of(vectors)
    power = power_vec.reshape(1, -1)
    block, conv_own, noise_own = pack(n, latent, noise, conv_w, squeeze_w, excite_w, critic_w)
    lat, conv, noise_all = exchange(
        n, 1, [("relay", True), ("a2a", False), ("relay", True)], [block, conv_own, noise_own]
    )

    moms = jnp.concatenate([squeeze_mom, excite_mom, critic_mom], axis=0)
    moms, lat = lax.optimization_barrier((moms, lat))
    moms = lax.all_gather(moms, "dp", axis=0)

    fake, xn, stats, opened, z1, pooled, consts, noise_rows = front(
        edge, micros, pixel_count, lat, conv, noise_all[:, 0], vectors_rows
    )
    (arrived,) = exchange(n, 2, [("a2a", True)], [fake])
    dfake, dspec, tail, column_v, column_t, row_w = critic_step(
        edge,
        patches,
        spread,
        arrived,
        lat,
        real_bank,
        frozen_feat,
        frozen_proj,
        power,
        vectors_rows,
        real_index,
    )

    returned, added = exchange(n, 3, [("a2a", True), ("cross", False)], [dfake, dspec])
    dconv, block, dspec = back(
        edge, micros, pixel_count, depth, returned, xn, lat, noise_rows, consts, stats, opened, tail,
        dspec, added,
    )

    dconv, dspec = exchange(n, 4, [("a2a", True), ("plane", False)], [dconv, dspec])
    conv_mom_new, gram, dspec = owner(dconv, conv_mom, dspec)
    grams, dspec = exchange(n, 5, [("a2a", False), ("line", False)], [gram, dspec])
    summed = jnp.concatenate(
        [
            jnp.sum(grams, axis=0),
            jnp.concatenate([jnp.sum(dspec, axis=0), block], axis=1),
        ],
        axis=0,
    )
    (summed,) = exchange(n, 6, [("relay", True)], [summed])

    conv_new, small, adam_new = update(
        summed, conv_mom_new, conv_w, lat, moms, squeeze_w, excite_w, critic_w, pooled, z1, column_v,
        column_t, row_w, power, vectors_rows, rows_of(vec_m), rows_of(vec_v), spread, proj_width,
    )
    conv_new, small, adam_new = share(7, conv_new, small, adam_new)
    pieces = []
    first = 0
    for weight in (squeeze_w, excite_w, critic_w) * 2:
        pieces.append(small[first : first + weight.shape[0]])
        first += weight.shape[0]
    size = vectors.shape[0]
    vec_rows = vectors_rows.shape[0]
    flat = adam_new[: 3 * vec_rows].reshape(3, vec_rows * LANES)[:, :size]
    return (
        adam_new[3 * vec_rows, 0],
        conv_mom_new,
        conv_new,
        pieces[0],
        pieces[3],
        pieces[1],
        pieces[4],
        pieces[2],
        pieces[5],
        flat[0],
        flat[1],
        flat[2],
    )


def shifted_2(value, axis, steps):
    count = lax.axis_size(axis)
    leading, last = (max(0, -steps), min(count, count - steps))
    return lax.ppermute(value, axis, [(source, source + steps) for source in range(leading, last)])


def for_sending(x):
    return jax.tree.map(lambda a: a.astype(jnp.bfloat16) if a.dtype == jnp.float32 else a, x)


def only_if(flag, compute):

    def empty_branch():
        return jax.tree.map(jnp.zeros_like, compute())

    return lax.cond(flag, compute, empty_branch)


def columns(latent_now):
    upsampled = jnp.repeat(jnp.repeat(latent_now, 2, axis=1), 2, axis=2)
    side_now = upsampled.shape[1]
    padded = jnp.pad(upsampled, ((0, 0), (1, 1), (1, 1), (0, 0)))
    taps = [
        padded[:, row_tap : row_tap + side_now, col_tap : col_tap + side_now, :]
        for row_tap in range(3)
        for col_tap in range(3)
    ]
    return jnp.concatenate(taps, axis=-1).reshape(-1, 9 * upsampled.shape[3])


def spectral_norm(weight, power):
    vector = high_dot(weight, power)
    vector = vector * lax.rsqrt(jnp.sum(vector * vector))
    product_one = high_dot(vector, weight)
    return weight / jnp.sqrt(jnp.sum(product_one * product_one))


def excite(pooled, squeeze_w, excite_w):
    return jax.nn.sigmoid(high_dot(jax.nn.silu(high_dot(pooled, squeeze_w)), excite_w))


def normalize(shifted, moments, pixel_count, bn_gain, bn_bias):
    mean_vec = moments[0] / pixel_count
    inv_std = lax.rsqrt(moments[1] / pixel_count - mean_vec * mean_vec + NORM_EPS)
    centred = (shifted - mean_vec) * inv_std
    return (centred, inv_std, centred * bn_gain + bn_bias)


def critic_pass(
    inputs, sign, patches, frozen_feat, frozen_proj, spectral, out_weight, out_bias, want_input
):
    pre_act = low_dot(inputs, frozen_feat)
    features = jax.nn.silu(pre_act).astype(jnp.bfloat16)
    projected = low_dot(features, frozen_proj).astype(jnp.bfloat16)
    critic_act = low_dot(projected, spectral)
    activated = jax.nn.silu(critic_act)
    logits = high_dot(activated, out_weight) + out_bias
    loss_part = jnp.sum(jax.nn.softplus(1.0 + sign * logits))
    dlogit = sign * jax.nn.sigmoid(1.0 + sign * logits) / patches
    dact = (dlogit[:, None] * out_weight * silu_slope(critic_act)).astype(jnp.bfloat16)
    result = [loss_part, low_dot(projected.T, dact), high_dot(dlogit, activated), jnp.sum(dlogit)]
    if want_input:
        dproj = low_dot(dact, spectral.T).astype(jnp.bfloat16)
        dpre = (low_dot(dproj, frozen_proj.T) * silu_slope(pre_act)).astype(jnp.bfloat16)
        result.append(low_dot(dpre, frozen_feat.T).astype(jnp.bfloat16))
    return result


def orthogonalize(momenta):
    squares = lax.psum(
        (
            jnp.sum(momenta[0] * momenta[0]),
            jnp.sum(momenta[1] * momenta[1]),
            jnp.sum(momenta[2] * momenta[2]),
            jnp.sum(momenta[3] * momenta[3]),
        ),
        "dp",
    )
    current = [
        matrix_now / (jnp.sqrt(square_now) + 1e-07)
        for matrix_now, square_now in zip(momenta, squares)
    ]

    def iterate(_, current):
        partials = [
            lax.psum_scatter(
                high_dot(matrix_now.T, matrix_now), "dp", scatter_dimension=0, tiled=True
            )
            for matrix_now in current
        ]
        full_grams = [lax.all_gather(part, "dp", axis=0, tiled=True) for part in partials]
        updated = []
        for matrix_now, gram in zip(current, full_grams):
            product_one = high_dot(matrix_now, gram)
            updated.append(
                NEWTON_A * matrix_now
                + NEWTON_B * product_one
                + NEWTON_C * high_dot(product_one, gram)
            )
        return updated

    return lax.fori_loop(0, NS_STEPS, iterate, current)


def by_images(
    latent,
    noise,
    real_bank,
    real_index,
    frozen_feat,
    frozen_proj,
    power_vec,
    conv_w,
    conv_mom,
    squeeze_w,
    squeeze_mom,
    excite_w,
    excite_mom,
    critic_w,
    critic_mom,
    vectors,
    vec_m,
    vec_v,
):
    gathered = (
        lax.all_gather(conv_w.astype(jnp.bfloat16), "dp", axis=0, tiled=True),
        lax.all_gather(squeeze_w.astype(jnp.bfloat16), "dp", axis=0, tiled=True),
        lax.all_gather(excite_w.astype(jnp.bfloat16), "dp", axis=0, tiled=True),
        lax.all_gather(critic_w.astype(jnp.bfloat16), "dp", axis=0, tiled=True),
    )
    conv_low, squeeze_low, excite_low, critic_low = gathered
    squeeze_full = squeeze_low.astype(jnp.float32)
    excite_full = excite_low.astype(jnp.float32)
    spectral_full, spectral_back = jax.vjp(
        partial(spectral_norm, power=power_vec), critic_low.astype(jnp.float32)
    )
    spectral = spectral_full.astype(jnp.bfloat16)
    micro_count, images, pixels = (noise.shape[0], noise.shape[1], noise.shape[2])
    widths = conv_low.shape[1]
    half_width = widths // 2
    proj_width = critic_low.shape[0]
    tokens = images * pixels
    pixel_count = tokens * lax.axis_size("dp")
    patches = micro_count * pixel_count
    noise_gain = vectors[:widths]
    bn_gain = vectors[widths : 2 * widths]
    bn_bias = vectors[2 * widths : 3 * widths]
    out_weight = vectors[3 * widths : 3 * widths + proj_width]
    out_bias = vectors[3 * widths + proj_width]
    generator = lax.axis_index("segment") == 0
    critic_side = jnp.logical_not(generator)
    pooled = jnp.mean(latent.astype(jnp.float32), axis=(2, 3))
    conv_acc = jnp.zeros(conv_low.shape, jnp.float32)
    squeeze_acc = jnp.zeros(squeeze_low.shape, jnp.float32)
    excite_acc = jnp.zeros(excite_low.shape, jnp.float32)
    spectral_acc = jnp.zeros(critic_low.shape, jnp.float32)
    vector_acc = jnp.zeros(vectors.shape, jnp.float32)
    loss_acc = jnp.zeros((), jnp.float32)
    for micro_step in range(micro_count):
        noise_now = noise[micro_step].reshape(-1)
        excitation, excite_back = jax.vjp(excite, pooled[micro_step], squeeze_full, excite_full)

        def gen_front():
            patches_in = columns(latent[micro_step])
            return (patches_in, low_dot(patches_in, conv_low) + noise_now[:, None] * noise_gain)

        patches_in, shifted = only_if(generator, gen_front)
        moments = lax.psum((jnp.sum(shifted, axis=0), jnp.sum(shifted * shifted, axis=0)), "dp")

        def gen_mid():
            centred, inv_std, normed = normalize(shifted, moments, pixel_count, bn_gain, bn_bias)
            gated = normed[:, :half_width] * jax.nn.sigmoid(normed[:, half_width:])
            fake_map = gated.reshape(images, pixels, half_width) * excitation[:, None, :]
            return fake_map.reshape(tokens, half_width).astype(jnp.bfloat16)

        fake_map = only_if(generator, gen_mid)
        arrived = shifted_2(fake_map, "segment", 1)

        def critic_work():
            real_map = real_bank[real_index[micro_step]].reshape(tokens, half_width)
            real_out = critic_pass(
                real_map,
                -1.0,
                patches,
                frozen_feat,
                frozen_proj,
                spectral,
                out_weight,
                out_bias,
                False,
            )
            fake_out = critic_pass(
                arrived,
                1.0,
                patches,
                frozen_feat,
                frozen_proj,
                spectral,
                out_weight,
                out_bias,
                True,
            )
            return (
                real_out[0] + fake_out[0],
                real_out[1] + fake_out[1],
                real_out[2] + fake_out[2],
                real_out[3] + fake_out[3],
                fake_out[4],
            )

        loss_part, dspec_part, dout_part, dbias_part, input_grad = only_if(critic_side, critic_work)
        returned = jax.tree.map(
            lambda part, own: part.astype(own.dtype),
            shifted_2(for_sending(input_grad), "segment", -1),
            input_grad,
        )

        def gen_back():
            dfake = -returned.astype(jnp.float32).reshape(images, pixels, half_width)
            centred, inv_std, normed = normalize(shifted, moments, pixel_count, bn_gain, bn_bias)
            opened = jax.nn.sigmoid(normed[:, half_width:])
            first_half = normed[:, :half_width]
            gated = (first_half * opened).reshape(images, pixels, half_width)
            unused, dsqueeze, dexcite = excite_back(jnp.sum(dfake * gated, axis=1))
            dgated = (dfake * excitation[:, None, :]).reshape(tokens, half_width)
            dnormed = jnp.concatenate(
                [dgated * opened, dgated * first_half * opened * (1.0 - opened)], axis=1
            )
            return (
                dnormed * bn_gain,
                centred,
                inv_std,
                dsqueeze,
                dexcite,
                jnp.sum(dnormed * centred, axis=0),
                jnp.sum(dnormed, axis=0),
            )

        dcentred, centred, inv_std, dsqueeze, dexcite, dgain, dbias = only_if(generator, gen_back)
        back_sums = lax.psum((jnp.sum(dcentred, axis=0), jnp.sum(dcentred * centred, axis=0)), "dp")

        def gen_grad():
            dshifted = inv_std * (
                dcentred - back_sums[0] / pixel_count - centred * back_sums[1] / pixel_count
            )
            return (dshifted.astype(jnp.bfloat16), jnp.sum(dshifted * noise_now[:, None], axis=0))

        dhidden, dnoise = only_if(generator, gen_grad)
        conv_acc = conv_acc + only_if(generator, lambda: low_dot(patches_in.T, dhidden))
        squeeze_acc = squeeze_acc + dsqueeze
        excite_acc = excite_acc + dexcite
        spectral_acc = spectral_acc + dspec_part
        vector_acc = vector_acc + jnp.concatenate(
            [dnoise, dgain, dbias, dout_part, dbias_part[None]]
        )
        loss_acc = loss_acc + loss_part
    critic_grad = spectral_back(spectral_acc)[0]
    conv_rows_sum, squeeze_rows, excite_rows, critic_rows = (
        lax.psum_scatter(conv_acc, "dp", scatter_dimension=0, tiled=True),
        lax.psum_scatter(squeeze_acc, "dp", scatter_dimension=0, tiled=True),
        lax.psum_scatter(excite_acc, "dp", scatter_dimension=0, tiled=True),
        lax.psum_scatter(critic_grad, "dp", scatter_dimension=0, tiled=True),
    )
    gradients = lax.psum((conv_rows_sum, squeeze_rows, excite_rows, critic_rows), "segment")
    vector_grad, loss_sum = lax.psum((vector_acc, loss_acc), ("segment", "dp"))
    weights = (conv_w, squeeze_w, excite_w, critic_w)
    new_moms = [
        MOMENTUM * old_mom + grad_now
        for old_mom, grad_now in zip((conv_mom, squeeze_mom, excite_mom, critic_mom), gradients)
    ]
    ortho = orthogonalize(new_moms)
    new_weights = [
        weight * (1.0 - MUON_RATE * DECAY) - MUON_RATE * step_dir
        for weight, step_dir in zip(weights, ortho)
    ]
    vec_m_new, vec_v_new, vectors_new = adam(vectors, vec_m, vec_v, vector_grad)
    return (
        loss_sum,
        new_moms[0],
        new_weights[0],
        new_moms[1],
        new_weights[1],
        new_moms[2],
        new_weights[2],
        new_moms[3],
        new_weights[3],
        vec_m_new,
        vec_v_new,
        vectors_new,
    )


def solution(mesh):
    placed = (
        P(None, "dp", None, None, None),
        P(None, "dp", None),
        P("dp", None, None),
        P(None, "dp"),
        P(),
        P(),
        P(),
        P("dp", None),
        P("dp", None),
        P("dp", None),
        P("dp", None),
        P("dp", None),
        P("dp", None),
        P("dp", None),
        P("dp", None),
        P(),
        P(),
        P(),
    )
    given = (
        P(),
        P("dp", None),
        P("dp", None),
        P("dp", None),
        P("dp", None),
        P("dp", None),
        P("dp", None),
        P("dp", None),
        P("dp", None),
        P(),
        P(),
        P(),
    )

    def step(latent, noise, *rest):
        n, sides = mesh.shape["dp"], mesh.shape["segment"]
        micros, images, edge = latent.shape[:3]
        fits = (
            n == 16
            and sides == 2
            and images == n
            and micros == 2
            and edge <= SUBLANES - 1
            and rest[5].shape[1] == 2 * n * sides * 16
        )
        plan = by_channels if fits else by_images
        return jax.shard_map(
            plan, mesh=mesh, in_specs=placed, out_specs=given, check_vma=False
        )(latent, noise, *rest)

    return step
```

```python
from functools import partial

import jax
import jax.numpy as jnp
from jax import lax
from jax.experimental import pallas as pl
from jax.experimental.pallas import tpu as pltpu
from jax.sharding import PartitionSpec as P

NS_STEPS = 5
STEP = 10


HIGHEST_PREC = lax.Precision.HIGHEST
HIGH_PREC = lax.Precision.HIGH
MESH = pl.DeviceIdType.MESH
NORM_EPS = 1e-05
NEWTON_A = 3.4445
NEWTON_B = -4.775
NEWTON_C = 2.0315
MOMENTUM = 0.95
MUON_RATE = 0.5
DECAY = 0.01
ADAM_RATE = 0.2
ADAM_BETA1 = 0.9
ADAM_BETA2 = 0.95
ADAM_EPS = 1e-08
LANES = 128
SUBLANES = 8
PLANE = 4
BLOCK = 256
FINE_BYTES = 64 * 1024
LONG = pl.CostEstimate(flops=10**12, bytes_accessed=0, transcendentals=0)
NO_COST = pl.CostEstimate(flops=0, bytes_accessed=0, transcendentals=0)
VMEM_BYTES = 56 * 1024 * 1024


def low_dot(left, right):
    return jnp.dot(left, right, preferred_element_type=jnp.float32)


def high_dot(left, right):
    return jnp.dot(left, right, precision=HIGHEST_PREC, preferred_element_type=jnp.float32)


def mid_dot(left, right):
    return jnp.dot(left, right, precision=HIGH_PREC, preferred_element_type=jnp.float32)


def silu_slope(value):
    opened = jax.nn.sigmoid(value)
    return opened * (1.0 + value * (1.0 - opened))


def adam(vectors, vec_m, vec_v, vector_grad):
    vec_m_new = ADAM_BETA1 * vec_m + (1.0 - ADAM_BETA1) * vector_grad
    vec_v_new = ADAM_BETA2 * vec_v + (1.0 - ADAM_BETA2) * vector_grad * vector_grad
    first_hat = vec_m_new / (1.0 - ADAM_BETA1**STEP)
    second_hat = vec_v_new / (1.0 - ADAM_BETA2**STEP)
    vectors_new = vectors * (1.0 - ADAM_RATE * DECAY) - ADAM_RATE * first_hat / (
        jnp.sqrt(second_hat) + ADAM_EPS
    )
    return vec_m_new, vec_v_new, vectors_new


def exchange(n, ident, plans, arrays):
    count = len(plans)
    kinds = [kind for kind, _ in plans]
    planes = n // PLANE

    def shape(kind, paired, x):
        if kind == "relay":
            lead, block = (planes, PLANE, 2), x.shape
        elif kind == "a2a":
            lead, block = ((n, 2) if paired else (n,)), x.shape[1:]
        elif kind == "plane":
            lead, block = (PLANE,), x.shape[1:]
        elif kind == "line":
            lead, block = (planes,), x.shape[1:]
        elif kind == "cross":
            lead, block = (), x.shape[:1] + x.shape[2:]
        else:
            lead, block = (), x.shape
        return jax.ShapeDtypeStruct(lead + block, x.dtype)

    outs = [shape(kind, paired, x) for (kind, paired), x in zip(plans, arrays)]
    direct = [a for a in range(count) if kinds[a] == "a2a"]
    near = [a for a in range(count) if kinds[a] in ("plane", "line")]
    single = [a for a in range(count) if kinds[a] in ("cross", "sib")]
    passing = [a for a in direct if plans[a][1]]
    parts = []
    for a in range(count):
        if kinds[a] == "relay":
            rows = arrays[a].shape[0]
            unit = 16 if arrays[a].dtype == jnp.bfloat16 else 8
            cut = -(-rows // (2 * unit)) * unit
            fine = arrays[a].size * arrays[a].dtype.itemsize > FINE_BYTES
            parts.append((a, 0, cut, 0, fine))
            if cut < rows:
                parts.append((a, cut, rows - cut, 1, fine))
    small = [p for p in range(len(parts)) if not parts[p][4]]
    large = [p for p in range(len(parts)) if parts[p][4]]

    def body(*refs):
        ins, results = refs[:count], refs[count : 2 * count]
        (send, recv, pass_send, pass_recv, here, up_send, z_send, z_recv, first_send, first_recv,
         second_send, second_recv, core_send, core_recv, part_here) = refs[2 * count :]
        me, side = lax.axis_index("dp"), lax.axis_index("segment")
        other = 1 - side
        z, spot = me // PLANE, me % PLANE
        beside = (spot + 1 - 2 * (spot % 2), (spot + 2) % PLANE)
        across = PLANE - 1 - spot
        barrier = pltpu.get_barrier_semaphore()

        def greet(where):
            pl.semaphore_signal(barrier, inc=1, device_id=where, device_id_type=MESH)

        greeted = 0
        if direct or near:

            @pl.loop(1, n)
            def _(k):
                greet({"dp": lax.rem(me + k, n)})

            greeted += n - 1
        elif parts:

            @pl.loop(1, planes)
            def _(k):
                greet({"dp": lax.rem(me + k * PLANE, n)})

            for spot_now in beside:
                greet({"dp": z * PLANE + spot_now})
            greeted += planes + 1
        if passing or single or parts:
            greet({"segment": other})
            greeted += 1
        pl.semaphore_wait(barrier, greeted)

        def remote(src, dst, send_sem, recv_sem, where):
            return pltpu.make_async_remote_copy(
                src_ref=src,
                dst_ref=dst,
                send_sem=send_sem,
                recv_sem=recv_sem,
                device_id=where,
                device_id_type=MESH,
            )

        every = range(len(parts))

        def cell(p, plane, spot_now):
            a, first, rows = parts[p][:3]
            return results[a].at[plane, spot_now, side, pl.ds(first, rows)]

        def column(p, spot_now, of_side):
            a, first, rows = parts[p][:3]
            return results[a].at[:, spot_now, of_side, pl.ds(first, rows)]

        def mine(p):
            a, first, rows = parts[p][:3]
            return ins[a].at[pl.ds(first, rows)]

        def first_spot(p):
            return beside[parts[p][3]]

        def second_spot(p):
            return beside[1 - parts[p][3]]

        def along(p, k):
            chip = lax.rem(z + k, planes) * PLANE + spot
            return remote(mine(p), cell(p, z, spot), z_send.at[p, k], z_recv.at[p, z], {"dp": chip})

        def chain(p, plane, up, src=None):
            held = cell(p, plane, spot)
            return remote(
                held if src is None else src,
                held,
                (up_send if up else z_send).at[p, plane],
                z_recv.at[p, plane],
                {"dp": me + PLANE if up else me - PLANE},
            )

        def from_plane(p, plane):
            held = cell(p, plane, spot)
            return remote(held, held, z_send.at[p, 0], z_recv.at[p, plane], {"dp": me})

        def to_first(p, plane, src=None, of_spot=None):
            held = cell(p, plane, spot if of_spot is None else of_spot)
            return remote(
                held if src is None else src,
                held,
                first_send.at[p, plane],
                first_recv.at[p, plane],
                {"dp": z * PLANE + first_spot(p)},
            )

        def to_second(p, plane, src=None, of_spot=None, shift=0):
            held = cell(p, plane, spot if of_spot is None else of_spot)
            return remote(
                held if src is None else src,
                held,
                second_send.at[p, plane + shift],
                second_recv.at[p, plane + shift],
                {"dp": z * PLANE + second_spot(p)},
            )

        def column_to_second(p, spot_now):
            held = column(p, spot_now, side)
            return remote(
                held,
                held,
                second_send.at[p, planes],
                second_recv.at[p, planes],
                {"dp": z * PLANE + second_spot(p)},
            )

        def to_core(p, spot_now, of_side):
            held = column(p, spot_now, of_side)
            return remote(
                held, held, core_send.at[p, spot_now], core_recv.at[p, spot_now], {"segment": other}
            )

        def keep(p):
            return pltpu.make_async_copy(mine(p), cell(p, z, spot), part_here.at[p])

        for p in every:
            to_first(p, z, mine(p)).start()
            to_second(p, z, mine(p)).start()
            if p in small:
                for k in range(1, planes):
                    along(p, k).start()
            else:

                @pl.when(z < planes - 1)
                def _():
                    chain(p, z, True, mine(p)).start()

                @pl.when(z > 0)
                def _():
                    chain(p, z, False, mine(p)).start()

            keep(p).start()

        def peer_of(a, k):
            if kinds[a] == "plane":
                return z * PLANE + lax.rem(spot + k, PLANE)
            if kinds[a] == "line":
                return lax.rem(z + k, planes) * PLANE + spot
            return lax.rem(me + k, n)

        def number(a, chip):
            if kinds[a] == "plane":
                return chip % PLANE
            if kinds[a] == "line":
                return chip // PLANE
            return chip

        def source(a, chip):
            return ins[a].at[number(a, chip)]

        def slot(a, chip, of_side):
            if plans[a][1]:
                return results[a].at[chip, of_side]
            return results[a].at[number(a, chip)]

        def outgoing(a, k):
            peer = peer_of(a, k)
            return remote(
                source(a, peer),
                slot(a, me, side),
                send.at[a, k],
                recv.at[a, number(a, me)],
                {"dp": peer},
            )

        def incoming(a, chip):
            return remote(
                source(a, chip), slot(a, chip, side), send.at[a, 0], recv.at[a, number(a, chip)], {"dp": chip}
            )

        def passed(a, src, chip, of_side):
            return remote(
                src,
                slot(a, chip, of_side),
                pass_send.at[a, chip],
                pass_recv.at[a, chip],
                {"segment": other},
            )

        def crossing(a):
            return remote(
                ins[a].at[:, other] if kinds[a] == "cross" else ins[a],
                results[a],
                pass_send.at[a, 0],
                pass_recv.at[a, 0],
                {"segment": other},
            )

        def own(a):
            return pltpu.make_async_copy(source(a, me), slot(a, me, side), here.at[a])

        def spread(p, plane):
            from_plane(p, plane).wait_recv()
            to_first(p, plane).start()
            to_second(p, plane).start()

        if small:

            @pl.loop(1, planes)
            def _(k):
                for p in small:
                    spread(p, lax.rem(z + planes - k, planes))

        for d in range(1, planes) if large else ():

            @pl.when(z - d >= 0)
            def _():
                for p in large:
                    spread(p, z - d)

                    @pl.when(z < planes - 1)
                    def _():
                        chain(p, z - d, True).start()

            @pl.when(z + d < planes)
            def _():
                for p in large:
                    spread(p, z + d)

                    @pl.when(z > 0)
                    def _():
                        chain(p, z + d, False).start()

        for p in every:
            keep(p).wait()
            to_core(p, spot, side).start()
        if large:

            @pl.loop(0, planes)
            def _(k):
                plane = lax.rem(z + k, planes)
                for p in large:
                    to_first(p, plane, of_spot=first_spot(p)).wait_recv()
                    to_second(p, plane, of_spot=first_spot(p), shift=planes).start()

        if direct:

            @pl.loop(1, n)
            def _(k):
                for a in direct:
                    outgoing(a, k).start()

        for a in near:
            for k in range(1, outs[a].shape[0]):
                outgoing(a, k).start()
        for a in direct + near:
            own(a).start()
        for a in passing:
            passed(a, source(a, me), me, side).start()
        for a in single:
            crossing(a).start()

        for p in every:
            if p in small:

                @pl.loop(0, planes)
                def _(plane):
                    to_first(p, plane, of_spot=first_spot(p)).wait_recv()

                column_to_second(p, first_spot(p)).start()
            to_core(p, first_spot(p), side).start()
        for p in every:

            @pl.loop(0, planes)
            def _(plane):
                to_second(p, plane, of_spot=second_spot(p)).wait_recv()

            to_core(p, second_spot(p), side).start()
        for p in every:
            if p in small:
                column_to_second(p, across).wait_recv()
            else:

                @pl.loop(0, planes)
                def _(plane):
                    to_second(p, plane, of_spot=across, shift=planes).wait_recv()

            to_core(p, across, side).start()

        if direct:

            @pl.loop(1, n)
            def _(k):
                chip = lax.rem(me + n - k, n)
                for a in direct:
                    incoming(a, chip).wait_recv()
                    if plans[a][1]:
                        passed(a, slot(a, chip, side), chip, side).start()

        for a in near:
            for k in range(1, outs[a].shape[0]):
                incoming(a, peer_of(a, k)).wait_recv()
                outgoing(a, k).wait_send()
        for a in direct + near:
            own(a).wait()
        if direct:

            @pl.loop(1, n)
            def _(k):
                for a in direct:
                    outgoing(a, k).wait_send()

        if passing:

            @pl.loop(0, n)
            def _(k):
                for a in passing:
                    passed(a, slot(a, k, side), k, side).wait_send()
                    passed(a, slot(a, k, other), k, other).wait_recv()

        for a in single:
            crossing(a).wait()

        for p in every:
            if p in small:
                for k in range(1, planes):
                    along(p, k).wait_send()
                column_to_second(p, first_spot(p)).wait_send()
            else:
                for d in range(planes):

                    @pl.when(jnp.logical_and(z - d >= 0, z < planes - 1))
                    def _():
                        chain(p, z - d, True).wait_send()

                    @pl.when(jnp.logical_and(z + d < planes, z > 0))
                    def _():
                        chain(p, z + d, False).wait_send()

            @pl.loop(0, planes)
            def _(plane):
                to_first(p, plane).wait_send()
                to_second(p, plane).wait_send()
                if p in large:
                    to_second(p, plane, of_spot=first_spot(p), shift=planes).wait_send()

            @pl.loop(0, PLANE)
            def _(spot_now):
                to_core(p, spot_now, side).wait_send()
                to_core(p, spot_now, other).wait_recv()

    anywhere = pl.BlockSpec(memory_space=pl.ANY)
    relays = max(len(parts), 1)
    found = pl.pallas_call(
        body,
        out_shape=outs,
        in_specs=[anywhere] * count,
        out_specs=[anywhere] * count,
        scratch_shapes=[pltpu.SemaphoreType.DMA((count, n))] * 4
        + [pltpu.SemaphoreType.DMA((count,))]
        + [pltpu.SemaphoreType.DMA((relays, 2 * planes))] * 7
        + [pltpu.SemaphoreType.DMA((relays, PLANE))] * 2
        + [pltpu.SemaphoreType.DMA((relays,))],
        compiler_params=pltpu.CompilerParams(collective_id=ident, has_side_effects=True),
        cost_estimate=NO_COST,
        name=f"exchange_{ident}",
    )(*arrays)
    return [
        x.reshape((n,) + x.shape[2:]) if kind == "relay" else x for kind, x in zip(kinds, found)
    ]


def share(ident, of_first, *of_second):
    arrays = (of_first, *of_second)
    count = len(arrays)

    def body(*refs):
        ins, results = refs[:count], refs[count : 2 * count]
        send, recv = refs[2 * count :]
        side = lax.axis_index("segment")
        other = 1 - side
        barrier = pltpu.get_barrier_semaphore()
        pl.semaphore_signal(barrier, inc=1, device_id={"segment": other}, device_id_type=MESH)
        pl.semaphore_wait(barrier, 1)

        def over(k):
            return pltpu.make_async_remote_copy(
                src_ref=ins[k],
                dst_ref=results[k],
                send_sem=send.at[k],
                recv_sem=recv.at[k],
                device_id={"segment": other},
                device_id_type=MESH,
            )

        for core, sent, found in ((0, [0], range(1, count)), (1, range(1, count), [0])):

            @pl.when(side == core)
            def _():
                for k in sent:
                    over(k).start()
                for k in found:
                    over(k).wait_recv()
                for k in sent:
                    over(k).wait_send()

    anywhere = pl.BlockSpec(memory_space=pl.ANY)
    arrived = pl.pallas_call(
        body,
        out_shape=[jax.ShapeDtypeStruct(x.shape, x.dtype) for x in arrays],
        in_specs=[anywhere] * count,
        out_specs=[anywhere] * count,
        scratch_shapes=[pltpu.SemaphoreType.DMA((count,))] * 2,
        compiler_params=pltpu.CompilerParams(collective_id=ident, has_side_effects=True),
        cost_estimate=NO_COST,
        name="share",
    )(*arrays)
    is_first = lax.axis_index("segment") == 0
    return [
        jnp.where(is_first == (k == 0), own, found) for k, (own, found) in enumerate(zip(arrays, arrived))
    ]


def local_call(kernel, name, out_shape, scratch, arguments, specs=None):
    return pl.pallas_call(
        kernel,
        out_shape=out_shape,
        in_specs=specs or [pl.BlockSpec(memory_space=pltpu.VMEM)] * len(arguments),
        scratch_shapes=scratch,
        compiler_params=pltpu.CompilerParams(vmem_limit_bytes=VMEM_BYTES),
        cost_estimate=LONG if name == "front" else NO_COST,
        name=name,
    )(*arguments)


def split_two(value):
    top = value.astype(jnp.bfloat16)
    return top, (value - top.astype(jnp.float32)).astype(jnp.bfloat16)


def split_three(value):
    top = value.astype(jnp.bfloat16)
    rest = value - top.astype(jnp.float32)
    middle = rest.astype(jnp.bfloat16)
    bottom = (rest - middle.astype(jnp.float32)).astype(jnp.bfloat16)
    return top, middle, bottom


def exact_dot(value, low):
    rows = value.shape[0]
    product = low_dot(jnp.concatenate(split_three(value), axis=0), low)
    return product[:rows] + product[rows : 2 * rows] + product[2 * rows :]


def lane_of(shape):
    return lax.broadcasted_iota(jnp.int32, shape, len(shape) - 1)


def fold(value):
    axis = value.ndim - 1
    value = value + pltpu.roll(value, 64, axis)
    return value + pltpu.roll(value, 32, axis)


def turn(value, steps):
    steps = steps % LANES
    return pltpu.roll(value, steps, value.ndim - 1) if steps else value


def turn_back(value, steps):
    return pltpu.roll(value, lax.rem(2 * LANES - steps, LANES), value.ndim - 1)


def row_pieces(rows, groups, taps, channels):
    depth = rows // groups
    pieces = []
    for chip in range(taps * channels // rows):
        for group in range(groups):
            first = chip * rows + group * depth
            at = first
            while at < first + depth:
                tap, channel = divmod(at, channels)
                take = min(first + depth - at, channels - channel)
                pieces.append((chip, group, at - first, tap, channel, take))
                at += take
    return pieces


def shift_rows(value, side, steps):
    parts = []
    empty = jnp.zeros((1,) + value.shape[1:], value.dtype)
    for first in range(0, value.shape[0], side):
        block = value[first : first + side]
        parts += [empty, block[:-1]] if steps > 0 else [block[1:], empty]
    return jnp.concatenate(parts, axis=0)


def per_micro(values, side):
    return jnp.concatenate(
        [jnp.broadcast_to(v[None], (side, SUBLANES, LANES)) for v in values], axis=0
    )


def pack_kernel(latent, noise, conv, squeeze, excite, critic, squeeze_mom, excite_mom, critic_mom,
                block, conv_out, noise_out, moms, rows_f):
    side = lax.axis_index("segment")
    bf16 = jnp.bfloat16
    micros, _, edge, _, channels = latent.shape
    half_in = channels // 2
    rows_f[...] = jnp.zeros(rows_f.shape, jnp.float32)
    for m in range(micros):
        for i in range(edge):
            at = (m * edge + i) * SUBLANES
            rows_f[at : at + edge, :] = latent[m, 0, i].astype(jnp.float32)
    spread = rows_f.shape[0]
    block[:spread, :] = jnp.where(side == 0, rows_f[:, :half_in], rows_f[:, half_in:]).astype(bf16)
    at = spread
    for weight in (squeeze, excite, critic):
        rows = weight.shape[0] // 2
        block[at : at + rows, :] = jnp.where(side == 0, weight[:rows], weight[rows:]).astype(bf16)
        at += rows
    at = 0
    for mom in (squeeze_mom, excite_mom, critic_mom):
        rows = mom.shape[0] // 2
        moms[at : at + rows, :] = jnp.where(side == 0, mom[:rows], mom[rows:])
        at += rows

    chips, depth, _ = conv_out.shape
    widths = conv.shape[1]
    half = widths // 2
    group = half // chips
    lane = lane_of((depth, LANES))
    @pl.loop(0, half // LANES)
    def _(b):
        low_cols = pl.ds(pl.multiple_of(b * LANES, LANES), LANES)
        high_cols = pl.ds(pl.multiple_of(half + b * LANES, LANES), LANES)
        for c in range(LANES // group):
            value = jnp.zeros((depth, LANES), jnp.float32)
            for q in range(4):
                rows = slice(q * depth, (q + 1) * depth)
                first = conv[rows, low_cols]
                second = conv[rows, high_cols]
                to = q * group
                steps = to - c * group + LANES - side * (group // 2)
                low = pltpu.roll(first, lax.rem(steps, LANES), 1)
                high = pltpu.roll(second, lax.rem(steps + group // 2, LANES), 1)
                both = jnp.where(lane % group < group // 2, low, high)
                value = jnp.where(lane // group == q, both, value)
            conv_out[b * (LANES // group) + c] = value.astype(bf16)

    pixels = noise.shape[2]
    parts = jnp.concatenate(
        [p.astype(jnp.float32) for p in split_three(noise[:, 0])]
        + [jnp.zeros((SUBLANES - 3 * micros, pixels), jnp.float32)],
        axis=0,
    ).astype(bf16)
    pixel = lax.broadcasted_iota(jnp.int32, (pixels, LANES), 0)
    spot = lane_of((pixels, LANES))
    within = spot % (4 * edge)
    lane_row = lane_of((1, LANES))
    lines = []
    for j in range(edge):
        wanted = 4 * edge * (within // 4) + 2 * edge * ((within % 4) // 2) + 2 * j + within % 2
        chosen = (pixel == wanted).astype(jnp.float32).astype(bf16)
        found = low_dot(parts, chosen)
        line = jnp.zeros((1, LANES), jnp.float32)
        for m in range(micros):
            total = found[m : m + 1] + found[micros + m : micros + m + 1]
            total = total + found[2 * micros + m : 2 * micros + m + 1]
            line = jnp.where(lane_row // (4 * edge) == m, total, line)
        lines.append(line)
    noise_out[...] = jnp.concatenate(
        lines + [jnp.zeros((SUBLANES - edge, LANES), jnp.float32)], axis=0
    )


def pack(n, latent, noise, conv_w, squeeze_w, excite_w, critic_w, squeeze_mom, excite_mom, critic_mom):
    micros, _, edge, _, channels = latent.shape
    spread = micros * edge * SUBLANES
    rows = spread + (squeeze_w.shape[0] + excite_w.shape[0] + critic_w.shape[0]) // 2
    return local_call(
        pack_kernel,
        "pack",
        [
            jax.ShapeDtypeStruct((rows, channels // 2), jnp.bfloat16),
            jax.ShapeDtypeStruct((n, conv_w.shape[0] // 4, LANES), jnp.bfloat16),
            jax.ShapeDtypeStruct((SUBLANES, LANES), jnp.float32),
            jax.ShapeDtypeStruct((rows - spread, squeeze_w.shape[1]), jnp.float32),
        ],
        [pltpu.VMEM((spread, channels), jnp.float32)],
        [latent, noise, conv_w, squeeze_w, excite_w, critic_w, squeeze_mom, excite_mom, critic_mom],
    )


def own_columns(row_low, row_high, at, own):
    lane = lane_of((1, LANES))
    low = turn_back(row_low, at)
    high = turn(turn_back(row_high, at), own)
    value = jnp.where(lane < own, low, jnp.where(lane < 2 * own, high, 0.0))
    value = value + turn(value, 2 * own)
    return value + turn(value, 4 * own)


def front_kernel(side, micros, pixel_count, all_lat, conv, noise, vectors,
                 fake, xn, stats, opened_out, z1_out, pooled_out, consts, noise_rows,
                 weight, z, h, gate8):
    images = all_lat.shape[0]
    half_in = all_lat.shape[3]
    channels = 2 * half_in
    spread = micros * side * SUBLANES
    depth = conv.shape[1]
    taps = weight.shape[1] // LANES
    bf16, f32 = jnp.bfloat16, jnp.float32
    chip, core = lax.axis_index("dp"), lax.axis_index("segment")
    own = 16
    widths_rows = 2 * half_in // LANES
    at = 2 * own * lax.rem(chip, PLANE) + own * core
    base = chip // PLANE
    for k in range(3):
        consts[k : k + 1, :] = own_columns(
            vectors[pl.ds(k * widths_rows + base, 1), :],
            vectors[pl.ds(k * widths_rows + widths_rows // 2 + base, 1), :],
            at,
            own,
        )
    consts[3:, :] = jnp.zeros((SUBLANES - 3, LANES), f32)

    group = lane_of((depth, LANES)) // 32
    masks = [(group == g).astype(f32).astype(bf16) for g in range(4)]
    for owner, g, first, tap, channel, take in row_pieces(4 * depth, 4, taps, channels):
        weight[channel : channel + take, tap * LANES : (tap + 1) * LANES] = (
            conv[owner, first : first + take, :] * masks[g][:take]
        )
    lines = micros * side
    step = 4

    @pl.loop(0, images // step)
    def _(k):
        here = pl.ds(k * step, step)
        left = all_lat[here, 0, :spread].reshape(step * spread, half_in)
        right = all_lat[here, 1, :spread].reshape(step * spread, half_in)
        for tap in range(0, taps, 2):
            cols = slice(tap * LANES, min(tap + 2, taps) * LANES)
            product = low_dot(left, weight[:half_in, cols]) + low_dot(right, weight[half_in:, cols])
            for k in range(product.shape[1] // LANES):
                value = fold(product[:, k * LANES : (k + 1) * LANES])
                z[tap + k, here] = value.reshape(step, lines, SUBLANES, LANES)

    from_lane = lax.broadcasted_iota(jnp.int32, (LANES, lines * LANES), 0)
    to_lane = lane_of((LANES, lines * LANES))
    chosen = from_lane == 4 * (to_lane // LANES) + (to_lane % LANES) // 32
    wide = exact_dot(
        noise[:, 0].reshape(images * SUBLANES, LANES), chosen.astype(f32).astype(bf16)
    )
    for line in range(lines):
        noise_rows[:, line] = wide[:, line * LANES : (line + 1) * LANES].reshape(images, SUBLANES, LANES)

    shape3 = (lines, SUBLANES, LANES)
    lane = lane_of(shape3)
    row_first = (lane // 64) == 0
    col_first = ((lane // 32) % 2) == 0
    inside = lax.broadcasted_iota(jnp.int32, shape3, 1) < side
    first_half = (lane % 32) < 16
    gain_noise = consts[0:1, :][None]
    gain = consts[1:2, :][None]
    bias = consts[2:3, :][None]
    zero = jnp.zeros((SUBLANES, LANES), f32)

    def place(img, carry):
        lines_of = []
        for ky in range(3):
            z0, z1, z2 = z[3 * ky, img], z[3 * ky + 1, img], z[3 * ky + 2, img]
            lines_of.append(
                z1
                + jnp.where(col_first, pltpu.roll(z0, 1, 1), z0)
                + jnp.where(col_first, z2, pltpu.roll(z2, SUBLANES - 1, 1))
            )
        x0, x1, x2 = lines_of
        value = (
            x1
            + jnp.where(row_first, shift_rows(x0, side, 1), x0)
            + jnp.where(row_first, x2, shift_rows(x2, side, -1))
        )
        value = value + noise_rows[img] * gain_noise
        value = jnp.where(inside, value, 0.0)
        h[img] = value
        new = []
        for m in range(micros):
            part = value[m * side : (m + 1) * side]
            new.append(carry[2 * m] + jnp.sum(part, axis=0))
            new.append(carry[2 * m + 1] + jnp.sum(part * part, axis=0))
        return tuple(new)

    sums = lax.fori_loop(0, images, place, (zero,) * (2 * micros))
    means, stds = [], []
    for m in range(micros):
        mean_now = jnp.sum(fold(sums[2 * m]), axis=0, keepdims=True) / pixel_count
        square = jnp.sum(fold(sums[2 * m + 1]), axis=0, keepdims=True) / pixel_count
        means.append(mean_now)
        stds.append(lax.rsqrt(square - mean_now * mean_now + NORM_EPS))
        stats[m : m + 1, :] = stds[m]
    mean12, std12 = per_micro(means, side), per_micro(stds, side)

    count = images * micros
    rows_map = side * SUBLANES
    owner = lax.broadcasted_iota(jnp.int32, (count, count * rows_map), 1) // rows_map
    pool = (owner == lax.broadcasted_iota(jnp.int32, owner.shape, 0)).astype(f32).astype(bf16)
    area = 1.0 / (side * side)
    pooled = [
        low_dot(pool, all_lat[:, p, :spread].reshape(images * spread, half_in)) * area
        for p in range(2)
    ]
    rows_squeeze = channels // images // 2
    rows_excite = half_in // images // 2
    squeeze = all_lat[:, :, spread : spread + rows_squeeze].reshape(channels, half_in)
    excite = all_lat[:, :, spread + rows_squeeze : spread + rows_squeeze + rows_excite]
    excite = excite.reshape(half_in, half_in)
    z1 = exact_dot(pooled[0], squeeze[:half_in]) + exact_dot(pooled[1], squeeze[half_in:])
    z1_out[...] = z1
    pooled_out[:, :half_in] = pooled[0]
    pooled_out[:, half_in:] = pooled[1]
    wide = jax.nn.sigmoid(exact_dot(z1 * jax.nn.sigmoid(z1), excite))
    opened = wide[:, :LANES]
    for b in range(1, half_in // LANES):
        opened = jnp.where(base == b, wide[:, b * LANES : (b + 1) * LANES], opened)
    opened = jnp.where(lane_of(opened.shape) < own, turn_back(opened, at), 0.0)
    for steps in (own, 2 * own, 4 * own):
        opened = opened + turn(opened, steps)
    opened_out[...] = opened
    gate8[...] = jnp.broadcast_to(opened[:, None, :], gate8.shape)

    @pl.loop(0, images)
    def _(img):
        centred = (h[img] - mean12) * std12
        xn[img] = centred
        y = centred * gain + bias
        gated = y * turn(jax.nn.sigmoid(y), -16)
        pieces = []
        for m in range(micros):
            pieces.append(gated[m * side : (m + 1) * side] * gate8[img * micros + m][None])
        packed = jnp.where(first_half[:side], pieces[0], turn(pieces[1], 16))
        fake[img] = packed.reshape(side * SUBLANES, LANES).astype(bf16)


def front(side, micros, pixel_count, lat, conv, noise, vectors):
    images, _, _, half_in = lat.shape
    lines = micros * side
    count = images * micros
    f32 = jnp.float32
    return local_call(
        partial(front_kernel, side, micros, pixel_count),
        "front",
        [
            jax.ShapeDtypeStruct((images, side * SUBLANES, LANES), jnp.bfloat16),
            jax.ShapeDtypeStruct((images, lines, SUBLANES, LANES), f32),
            jax.ShapeDtypeStruct((SUBLANES, LANES), f32),
            jax.ShapeDtypeStruct((count, LANES), f32),
            jax.ShapeDtypeStruct((count, half_in), f32),
            jax.ShapeDtypeStruct((count, 2 * half_in), f32),
            jax.ShapeDtypeStruct((SUBLANES, LANES), f32),
            jax.ShapeDtypeStruct((images, lines, SUBLANES, LANES), f32),
        ],
        [
            pltpu.VMEM((2 * half_in, 9 * LANES), jnp.bfloat16),
            pltpu.VMEM((9, images, lines, SUBLANES, LANES), f32),
            pltpu.VMEM((images, lines, SUBLANES, LANES), f32),
            pltpu.VMEM((count, SUBLANES, LANES), f32),
        ],
        [lat, conv, noise, vectors],
    )


def critic_kernel(side, patches, spread, arrived, lat, real_bank, feat, proj, power, vectors, chosen,
                  dfake, dspec, tail, column_v, column_t, row_w, maps, dmaps, weight_low, real_map, sem):
    bf16 = jnp.bfloat16
    core = lax.axis_index("segment")
    chips, _, rows_map, _ = arrived.shape
    size = feat.shape[0]
    at = 6 * size // LANES
    head = jnp.concatenate([vectors[at + k : at + k + 1, :] for k in range(size // LANES)], axis=1)
    offset = vectors[at + size // LANES : at + size // LANES + 1, 0:1]
    rows_before = spread + size // chips + size // chips // 2
    load = pltpu.make_async_copy(
        lat.at[:, :, pl.ds(rows_before, size // chips // 2)], weight_low, sem.at[0]
    )
    load_real = pltpu.make_async_copy(real_bank.at[chosen[core, 0]], real_map, sem.at[1])
    load.start()
    load_real.start()

    lane = lane_of((rows_map, LANES))
    per_block = LANES // 32

    @pl.loop(0, size // LANES)
    def _(b):
        both = []
        for c in range(per_block):
            low = turn_back(arrived[b * per_block + c, 0].astype(jnp.float32), 16 * core)
            high = turn_back(arrived[b * per_block + c, 1].astype(jnp.float32), 16 * core - 16)
            both.append(jnp.where(lane % 32 < 16, low, high))
        cols = pl.ds(pl.multiple_of(b * LANES, LANES), LANES)
        for q in range(4):
            value = turn(both[0], -32 * q)
            for c in range(1, per_block):
                value = jnp.where(lane // 32 == c, turn(both[c], 32 * (c - q)), value)
            maps[q * rows_map : (q + 1) * rows_map, cols] = value.astype(bf16)

    fakes = 4 * rows_map
    load_real.wait()
    maps[fakes:, :] = real_map[...]
    load.wait()
    weight = weight_low[...].reshape(size, size).astype(jnp.float32)
    product = jnp.sum(weight * power[...], axis=1, keepdims=True)
    length = lax.rsqrt(jnp.sum(product * product))
    vec = product * length
    back = jnp.sum(weight * vec, axis=0, keepdims=True)
    sigma = jnp.sqrt(jnp.sum(back * back))
    unit = back / sigma
    turned = jnp.sum(weight * unit, axis=1, keepdims=True)
    turned = (turned - vec * jnp.sum(turned * vec)) * length
    column_v[...] = vec
    column_t[...] = turned
    row_w[...] = jnp.broadcast_to(unit, row_w.shape)
    spectral = (weight / sigma).astype(bf16)
    rows = maps.shape[0]
    pre_act = low_dot(maps[...], feat[...])
    features = (pre_act * jax.nn.sigmoid(pre_act)).astype(bf16)
    projected = low_dot(features, proj[...]).astype(bf16)
    critic_act = low_dot(projected, spectral)
    opened = jax.nn.sigmoid(critic_act)
    activated = critic_act * opened
    logits = jnp.sum(activated * head, axis=1, keepdims=True) + offset
    row = lax.broadcasted_iota(jnp.int32, (rows, 1), 0)
    sign = jnp.where(row < fakes, 1.0, -1.0)
    valid = jnp.logical_or(row >= fakes, (row % SUBLANES) < side)
    margin = 1.0 + sign * logits
    soft = jnp.maximum(margin, 0.0) + jnp.log1p(jnp.exp(-jnp.abs(margin)))
    loss = jnp.sum(jnp.where(valid, soft, 0.0))
    dlogit = jnp.where(valid, sign * jax.nn.sigmoid(margin), 0.0) / patches
    slope = opened * (1.0 + critic_act * (1.0 - opened))
    dact = (dlogit * head * slope).astype(bf16)
    found = lax.dot_general(
        projected, dact, (((0,), (0,)), ((), ())), preferred_element_type=jnp.float32
    )
    dspec[...] = found.reshape(dspec.shape)
    dhead = jnp.sum(dlogit * activated, axis=0, keepdims=True)
    lane_row = lane_of((1, LANES))
    last = jnp.where(lane_row == 0, jnp.sum(dlogit), jnp.where(lane_row == 1, loss, 0.0))
    pieces = [dhead[:, k * LANES : (k + 1) * LANES] for k in range(size // LANES)] + [last]
    tail[...] = jnp.concatenate(
        pieces + [jnp.zeros((SUBLANES - len(pieces), LANES), jnp.float32)], axis=0
    )
    turned_dims = (((1,), (1,)), ((), ()))
    dproj = lax.dot_general(
        dact[:fakes], spectral, turned_dims, preferred_element_type=jnp.float32
    ).astype(bf16)
    dpre = lax.dot_general(dproj, proj[...], turned_dims, preferred_element_type=jnp.float32)
    dpre = (dpre * silu_slope(pre_act[:fakes])).astype(bf16)
    dmaps[...] = lax.dot_general(dpre, feat[...], turned_dims, preferred_element_type=jnp.float32)

    @pl.loop(0, size // LANES)
    def _(b):
        cols = pl.ds(pl.multiple_of(b * LANES, LANES), LANES)
        parts = [dmaps[q * rows_map : (q + 1) * rows_map, cols] for q in range(4)]
        for c in range(per_block):
            value = turn(parts[0], -32 * c)
            for q in range(1, 4):
                value = jnp.where(lane // 32 == q, turn(parts[q], 32 * (q - c)), value)
            dfake[b * per_block + c] = value.astype(bf16)


def critic_step(side, patches, spread, arrived, lat, real_bank, feat, proj, power, vectors, chosen):
    f32 = jnp.float32
    chips, _, rows_map, _ = arrived.shape
    size = feat.shape[0]
    vmem = pl.BlockSpec(memory_space=pltpu.VMEM)
    smem = pl.BlockSpec(memory_space=pltpu.SMEM)
    anywhere = pl.BlockSpec(memory_space=pl.ANY)
    return local_call(
        partial(critic_kernel, side, patches, spread),
        "critic_step",
        [
            jax.ShapeDtypeStruct((chips, rows_map, LANES), jnp.bfloat16),
            jax.ShapeDtypeStruct((chips, 2, size // chips // 2, size), f32),
            jax.ShapeDtypeStruct((SUBLANES, LANES), f32),
            jax.ShapeDtypeStruct((size, 1), f32),
            jax.ShapeDtypeStruct((size, 1), f32),
            jax.ShapeDtypeStruct((SUBLANES, size), f32),
        ],
        [
            pltpu.VMEM((4 * rows_map + real_bank.shape[1], size), jnp.bfloat16),
            pltpu.VMEM((4 * rows_map, size), f32),
            pltpu.VMEM((chips, 2, size // chips // 2, size), jnp.bfloat16),
            pltpu.VMEM(real_bank.shape[1:], jnp.bfloat16),
            pltpu.SemaphoreType.DMA((2,)),
        ],
        [arrived, lat, real_bank, feat, proj, power, vectors, chosen],
        [vmem, anywhere, anywhere] + [vmem] * 4 + [smem],
    )


def back_kernel(side, micros, pixel_count, grads, xn, lat, noise_rows, consts, stats, opened, tail,
                dspec_own, dspec_other, dconv, block, dspec, dy, packed, product, gate8, dze, all_lat, sem):
    images = all_lat.shape[0]
    half_in = all_lat.shape[3]
    channels = 2 * half_in
    lines = micros * side
    spread = lines * SUBLANES
    load = pltpu.make_async_copy(lat.at[:, :, pl.ds(0, spread)], all_lat, sem.at[0])
    load.start()
    bf16 = jnp.bfloat16
    shape3 = (lines, SUBLANES, LANES)
    lane = lane_of(shape3)
    row_first = (lane // 64) == 0
    col_first = ((lane // 32) % 2) == 0
    first_half = (lane % 32) < 16
    inside = lax.broadcasted_iota(jnp.int32, shape3, 1) < side
    gain = consts[1:2, :][None]
    bias = consts[2:3, :][None]
    zero = jnp.zeros((SUBLANES, LANES), jnp.float32)
    core = lax.axis_index("segment")
    second = core == 1
    gate8[...] = jnp.broadcast_to(opened[...][:, None, :], gate8.shape)
    for plane in range(images // PLANE):
        for spot in range(PLANE):
            k = plane * PLANE + spot
            dspec[spot, plane] = jnp.where(second, dspec_own[k, 1], dspec_own[k, 0]) + dspec_other[k]

    def through_gate(img, carry):
        ascent = -grads[img].astype(jnp.float32).reshape(shape3)
        ascent = jnp.where(second, turn(ascent, -16), ascent)
        ascent = jnp.where(first_half, ascent, 0.0)
        centred = xn[img]
        y = centred * gain + bias
        gate = turn(jax.nn.sigmoid(y), -16)
        dopened = ascent * (y * gate)
        scale = jnp.concatenate(
            [jnp.broadcast_to(gate8[img * micros + m][None], (side, SUBLANES, LANES)) for m in range(micros)],
            axis=0,
        )
        dgated = ascent * scale
        dnormed = jnp.where(first_half, dgated * gate, turn(dgated * y * gate * (1.0 - gate), 16))
        dy[img] = dnormed
        new = []
        for m in range(micros):
            part = slice(m * side, (m + 1) * side)
            total = fold(jnp.sum(dopened[part], axis=0))
            total = total + turn(total, 16)
            gate_now = gate8[img * micros + m]
            dze[img * micros + m] = (
                jnp.broadcast_to(jnp.sum(total, axis=0, keepdims=True), (SUBLANES, LANES))
                * gate_now
                * (1.0 - gate_now)
            )
            new.append(carry[2 * m] + jnp.sum(dnormed[part] * centred[part], axis=0))
            new.append(carry[2 * m + 1] + jnp.sum(dnormed[part], axis=0))
        return tuple(new)

    sums = lax.fori_loop(0, images, through_gate, (zero,) * (2 * micros))
    sums = [jnp.sum(fold(s), axis=0, keepdims=True) for s in sums]
    gain_row = consts[1:2, :]
    mean_back = per_micro([gain_row * sums[2 * m + 1] / pixel_count for m in range(micros)], side)
    cross_back = per_micro([gain_row * sums[2 * m] / pixel_count for m in range(micros)], side)
    std12 = per_micro([stats[m : m + 1, :] for m in range(micros)], side)
    taps = 9
    groups = (taps + 3) // 4
    lane_flat = lane_of((spread, LANES)) // 32

    def through_norm(img, carry):
        centred = xn[img]
        dshift = (dy[img] * gain - mean_back - centred * cross_back) * std12
        dshift = jnp.where(inside, dshift, 0.0)
        carry = carry + jnp.sum(dshift * noise_rows[img], axis=0)
        dh = dshift.astype(bf16).astype(jnp.float32)
        swapped = jnp.where(col_first, turn(dh, -32), turn(dh, 32))
        col0 = jnp.where(col_first, dh, swapped)
        col1 = jnp.where(col_first, swapped, dh)
        by_col = [
            col1 + pltpu.roll(col0, SUBLANES - 1, 1),
            col0 + col1,
            col0 + pltpu.roll(col1, 1, 1),
        ]
        found = [None] * taps
        for kx in range(3):
            value = by_col[kx]
            turned = turn(value, 64)
            row0 = jnp.where(row_first, value, turned)
            row1 = jnp.where(row_first, turned, value)
            found[kx] = row1 + shift_rows(row0, side, -1)
            found[3 + kx] = row0 + row1
            found[6 + kx] = row0 + shift_rows(row1, side, 1)
        for g in range(groups):
            members = [f.reshape(spread, LANES) for f in found[4 * g : 4 * g + 4]]
            value = members[0]
            for k in range(1, len(members)):
                value = jnp.where(lane_flat == k, members[k], value)
            top, rest = split_two(value)
            packed[img, :, g * LANES : (g + 1) * LANES] = top
            packed[img, :, (groups + g) * LANES : (groups + g + 1) * LANES] = rest
        return carry

    dgain_noise = lax.fori_loop(0, images, through_norm, zero)
    dgain_noise = jnp.sum(fold(dgain_noise), axis=0, keepdims=True)
    lane_row = lane_of((1, LANES))
    for r in range(images * micros // 8):
        value = jnp.zeros((1, LANES), jnp.float32)
        for g in range(8):
            value = jnp.where(lane_row // 16 == g, dze[8 * r + g][0:1], value)
        block[r : r + 1, :] = value
    gains = jnp.where(
        lane_row // 32 == 0,
        dgain_noise,
        jnp.where(
            lane_row // 32 == 1,
            sum(sums[2 * m] for m in range(micros)),
            sum(sums[2 * m + 1] for m in range(micros)),
        ),
    )
    block[4:5, :] = gains
    block[5:8, :] = jnp.zeros((3, LANES), jnp.float32)
    block[8:16, :] = tail[...]

    width = groups * LANES
    flat = packed[...].reshape(images * spread, 2 * width)
    load.wait()
    for p in range(2):
        side_rows = all_lat[:, p].reshape(images * spread, half_in)
        both = lax.dot_general(
            side_rows, flat, (((0,), (0,)), ((), ())), preferred_element_type=jnp.float32
        )
        product[p * half_in : (p + 1) * half_in, :] = both[:, :width] + both[:, width:]
    depth = dconv.shape[1]
    unit = 16
    lane_unit = lane_of((unit, LANES)) // 32
    for chip in range(dconv.shape[0]):
        for at in range(0, depth, unit):
            value = None
            for g in range(4):
                tap, channel = divmod((chip * 4 + g) * depth + at, channels)
                piece = product[channel : channel + unit, (tap // 4) * LANES : (tap // 4 + 1) * LANES]
                piece = turn(piece, 32 * (g - tap % 4))
                value = piece if value is None else jnp.where(lane_unit == g, piece, value)
            dconv[chip, at : at + unit, :] = value.astype(bf16)


def back(side, micros, pixel_count, depth, grads, xn, lat, noise_rows, consts, stats, opened, tail,
         dspec_own, dspec_other):
    images, _, _, half_in = lat.shape
    lines = micros * side
    count = images * micros
    f32 = jnp.float32
    return local_call(
        partial(back_kernel, side, micros, pixel_count),
        "back",
        [
            jax.ShapeDtypeStruct((images, depth, LANES), jnp.bfloat16),
            jax.ShapeDtypeStruct((2 * SUBLANES, LANES), f32),
            jax.ShapeDtypeStruct((PLANE, images // PLANE) + dspec_other.shape[1:], f32),
        ],
        [
            pltpu.VMEM((images, lines, SUBLANES, LANES), f32),
            pltpu.VMEM((images, lines * SUBLANES, 6 * LANES), jnp.bfloat16),
            pltpu.VMEM((2 * half_in, 3 * LANES), f32),
            pltpu.VMEM((count, SUBLANES, LANES), f32),
            pltpu.VMEM((count, SUBLANES, LANES), f32),
            pltpu.VMEM((images, 2, lines * SUBLANES, half_in), lat.dtype),
            pltpu.SemaphoreType.DMA((1,)),
        ],
        [grads, xn, lat, noise_rows, consts, stats, opened, tail, dspec_own, dspec_other],
        [pl.BlockSpec(memory_space=pltpu.VMEM)] * 2
        + [pl.BlockSpec(memory_space=pl.ANY)]
        + [pl.BlockSpec(memory_space=pltpu.VMEM)] * 7,
    )


def owner_kernel(dconv, mom, parts_in, mom_new, gram, parts, top, rest):
    chips, _, depth, _ = dconv.shape
    rows, widths = mom.shape
    half = widths // 2
    blocks = widths // LANES
    core = lax.axis_index("segment")
    lane = lane_of((depth, LANES))
    parts[...] = jnp.sum(parts_in[...], axis=0)
    @pl.loop(0, half // LANES)
    def _(b):
        halves = []
        for c in range(PLANE):
            low = dconv[b * PLANE + c, 0].astype(jnp.float32)
            high = dconv[b * PLANE + c, 1].astype(jnp.float32)
            halves.append(
                (
                    jnp.where(lane % 32 < 16, low, turn(high, 16)),
                    jnp.where(lane % 32 < 16, turn(low, -16), high),
                )
            )
        for q in range(4):
            for k in range(2):
                value = None
                for c in range(PLANE):
                    piece = turn(halves[c][k], 32 * (c - q))
                    value = piece if value is None else jnp.where(lane // 32 == c, piece, value)
                cols = pl.ds(pl.multiple_of(k * half + b * LANES, LANES), LANES)
                rows_now = slice(q * depth, (q + 1) * depth)
                mom_new[rows_now, cols] = MOMENTUM * mom[rows_now, cols] + value

    for b in range(blocks):
        high, low = split_two(mom_new[:, b * LANES : (b + 1) * LANES])
        for at in (b, b + blocks) if b < PLANE else (b,):
            cols = slice(at * LANES, (at + 1) * LANES)
            top[:, cols] = high
            rest[:, cols] = low
    dims = (((0,), (0,)), ((), ()))
    share = LANES // 4
    span = gram.shape[2]

    @pl.loop(0, blocks // 2)
    def _(pair):
        at = pl.multiple_of(2 * pair * LANES, LANES)
        own, wide = pl.ds(at, 2 * LANES), pl.ds(at, span + LANES)
        left_high, left_low = top[:, own], rest[:, own]
        right_high, right_low = top[:, wide], rest[:, wide]

        def times(left, right):
            return lax.dot_general(left, right, dims, preferred_element_type=jnp.float32)

        found = times(left_high, right_high) + (times(left_high, right_low) + times(left_low, right_high))
        for k in range(2):
            for h in range(2):
                first = k * LANES + 2 * share * h
                cols = slice(k * LANES, k * LANES + span)
                gram[4 * pair + 2 * k + h] = jnp.where(
                    core == 0,
                    found[first : first + share, cols],
                    found[first + share : first + 2 * share, cols],
                )


def owner(dconv, mom, dspec):
    chips, _, depth, _ = dconv.shape
    rows, widths = mom.shape
    f32 = jnp.float32
    span = (widths // LANES // 2 + 1) * LANES
    return local_call(
        owner_kernel,
        "owner",
        [
            jax.ShapeDtypeStruct(mom.shape, f32),
            jax.ShapeDtypeStruct((chips, widths // chips // 2, span), f32),
            jax.ShapeDtypeStruct(dspec.shape[1:], f32),
        ],
        [pltpu.VMEM((rows, widths + PLANE * LANES), jnp.bfloat16)] * 2,
        [dconv, mom, dspec],
    )


def collect_kernel(grams, dspec, block, summed):
    rows, span = grams.shape[1:]
    size = dspec.shape[2]
    summed[:rows, :] = jnp.sum(grams[...], axis=0)
    summed[rows:, :size] = jnp.sum(dspec[...], axis=0)
    summed[rows:, size:] = block[...]


def collect(grams, dspec, block):
    rows, span = grams.shape[1:]
    return local_call(
        collect_kernel,
        "collect",
        jax.ShapeDtypeStruct((rows + block.shape[0], span), jnp.float32),
        [],
        [grams, dspec, block],
    )


def three(left_high, left_low, right_high, right_low, dims=(((1,), (0,)), ((), ()))):
    def times(left, right):
        return lax.dot_general(left, right, dims, preferred_element_type=jnp.float32)

    return times(left_high, right_high) + (times(left_high, right_low) + times(left_low, right_high))


def store_block(value, i, j, high, low):
    rows, cols = slice(i * BLOCK, (i + 1) * BLOCK), slice(j * BLOCK, (j + 1) * BLOCK)
    high[rows, cols], low[rows, cols] = split_two(value)
    if i < j:
        high[cols, rows], low[cols, rows] = split_two(value.T)


def polynomial(gram, gram_high, gram_low, high, low):
    for j in range(gram.shape[0] // BLOCK):
        cols, rows = slice(j * BLOCK, (j + 1) * BLOCK), slice(0, (j + 1) * BLOCK)
        found = three(gram_high[rows, :], gram_low[rows, :], gram_high[:, cols], gram_low[:, cols])
        for i in range(j + 1):
            here = slice(i * BLOCK, (i + 1) * BLOCK)
            store_block(NEWTON_B * gram[here, cols] + NEWTON_C * found[here], i, j, high, low)


def multiply(source, source_high, source_low, poly_high, poly_low, result, high, low):
    for j in range(source.shape[0] // BLOCK):
        cols, rows = slice(j * BLOCK, (j + 1) * BLOCK), slice(0, (j + 1) * BLOCK)
        found = three(source_high[rows, :], source_low[rows, :], poly_high[:, cols], poly_low[:, cols])
        for i in range(j + 1):
            here = slice(i * BLOCK, (i + 1) * BLOCK)
            value = NEWTON_A * source[here, cols] + found[here]
            result[here, cols] = value
            store_block(value, i, j, high, low)


def apply(x, x_high, x_low, poly_high, poly_low):
    for j in range(x.shape[1] // BLOCK):
        cols = slice(j * BLOCK, (j + 1) * BLOCK)
        found = three(x_high[...], x_low[...], poly_high[:, cols], poly_low[:, cols])
        x[:, cols] = NEWTON_A * x[:, cols] + found


def resplit(x, x_high, x_low):
    for j in range(x.shape[1] // BLOCK):
        cols = slice(j * BLOCK, (j + 1) * BLOCK)
        x_high[:, cols], x_low[:, cols] = split_two(x[:, cols])


def conv_ortho(have_x, packed, x, gram, high, low, p_high, p_low, x_high, x_low):
    size = gram.shape[1]
    blocks = size // LANES
    share = packed.shape[2] - 2 * SUBLANES
    span = packed.shape[3] // LANES
    chips_block = LANES // (2 * share)

    def block(b, k):
        pair = pl.ds(b * chips_block, chips_block)
        return packed[pair, :, :share, k * LANES : (k + 1) * LANES].reshape(LANES, LANES)

    eye = lax.broadcasted_iota(jnp.int32, (LANES, LANES), 0) == lane_of((LANES, LANES))

    def add_squares(b, total):
        return total + jnp.where(eye, block(b, 0), 0.0)

    total = lax.fori_loop(0, blocks, add_squares, jnp.zeros((LANES, LANES), jnp.float32))
    scale = 1.0 / (jnp.sqrt(jnp.sum(total)) + 1e-07)

    @pl.loop(0, blocks)
    def _(r):
        rows = pl.ds(pl.multiple_of(r * LANES, LANES), LANES)
        for ahead in range(span):
            cols = pl.ds(pl.multiple_of(lax.rem(r + ahead, blocks) * LANES, LANES), LANES)
            value = (block(r, ahead) * scale) * scale
            gram[0, rows, cols] = value
            high[0, rows, cols], low[0, rows, cols] = split_two(value)
            if ahead:
                value = value.T
                gram[0, cols, rows] = value
                high[0, cols, rows], low[0, cols, rows] = split_two(value)

    have_x()
    for j in range(size // BLOCK):
        cols = slice(j * BLOCK, (j + 1) * BLOCK)
        value = x[:, cols] * scale
        x[:, cols] = value
        x_high[:, cols], x_low[:, cols] = split_two(value)

    @pl.loop(0, NS_STEPS)
    def _(step):
        polynomial(gram.at[0], high.at[0], low.at[0], p_high, p_low)
        apply(x, x_high, x_low, p_high, p_low)

        @pl.when(step < NS_STEPS - 1)
        def _():
            resplit(x, x_high, x_low)
            for k in range(2):
                multiply(
                    gram.at[k], high.at[k], low.at[k], p_high, p_low,
                    gram.at[1 - k], high.at[1 - k], low.at[1 - k],
                )


def whole_ortho(chunks, x, x_high, x_low, gram, g_high, g_low, p_high, p_low):
    size = gram.shape[0]

    def rows_of(c):
        return pl.ds(pl.multiple_of(c * size, size), size)

    def add_squares(c, total):
        value = x[rows_of(c), :]
        return total + jnp.sum(value * value)

    scale = 1.0 / (jnp.sqrt(lax.fori_loop(0, chunks, add_squares, jnp.float32(0.0))) + 1e-07)

    @pl.loop(0, chunks)
    def _(c):
        rows = rows_of(c)
        value = x[rows, :] * scale
        x[rows, :] = value
        x_high[rows, :], x_low[rows, :] = split_two(value)

    @pl.loop(0, NS_STEPS)
    def _(_):
        gram[...] = jnp.zeros(gram.shape, jnp.float32)

        @pl.loop(0, chunks)
        def _(c):
            for j in range(size // BLOCK):
                cols, above = slice(j * BLOCK, (j + 1) * BLOCK), slice(0, (j + 1) * BLOCK)
                gram[above, cols] += three(
                    x_high[rows_of(c), above],
                    x_low[rows_of(c), above],
                    x_high[rows_of(c), cols],
                    x_low[rows_of(c), cols],
                    (((0,), (0,)), ((), ())),
                )

        for j in range(size // BLOCK):
            for i in range(j + 1):
                at = (slice(i * BLOCK, (i + 1) * BLOCK), slice(j * BLOCK, (j + 1) * BLOCK))
                store_block(gram[at], i, j, g_high, g_low)
        polynomial(gram, g_high, g_low, p_high, p_low)

        @pl.loop(0, chunks)
        def _(c):
            rows = rows_of(c)
            for j in range(size // BLOCK):
                cols = slice(j * BLOCK, (j + 1) * BLOCK)
                found = three(x_high[rows, :], x_low[rows, :], p_high[:, cols], p_low[:, cols])
                x[rows, cols] = NEWTON_A * x[rows, cols] + found
            x_high[rows, :], x_low[rows, :] = split_two(x[rows, :])


def outer_sum(left, right):
    a, b, c = split_three(left)
    d, e, f = split_three(right)
    return lax.dot_general(
        jnp.concatenate([a, a, b, a, b, c], axis=0),
        jnp.concatenate([d, e, d, f, e, d], axis=0),
        (((0,), (0,)), ((), ())),
        preferred_element_type=jnp.float32,
    )


def update_kernel(spread, size, summed, conv_mom, conv_w, lat, moms, moms_other, squeeze_w, excite_w, critic_w, pooled, z1,
                  column_v, column_t, row_w, power, vectors, vec_m, vec_v,
                  conv_new, small, adam_out,
                  sems, x, gram, high, low, p_high, p_low, x_high, x_low, w,
                  whole, whole_high, whole_low, small_gram, sg_high, sg_low, sp_high, sp_low, weights, dze, moms_all):
    core = lax.axis_index("segment")
    chip = lax.axis_index("dp")
    keep = 1.0 - MUON_RATE * DECAY
    f32 = jnp.float32

    @pl.when(core == 0)
    def _():
        load_mom = pltpu.make_async_copy(conv_mom, x, sems.at[0])
        load_w = pltpu.make_async_copy(conv_w, w, sems.at[1])
        load_mom.start()
        load_w.start()
        conv_ortho(load_mom.wait, summed, x, gram, high, low, p_high, p_low, x_high, x_low)
        load_w.wait()
        conv_new[...] = w[...] * keep - MUON_RATE * x[...]

    @pl.when(core == 1)
    def _():
        chips = lat.shape[0]
        rows_each = [weight.shape[0] for weight in (squeeze_w, excite_w, critic_w)]
        lows = weights.shape[2]
        load_low = pltpu.make_async_copy(
            lat.at[:, :, pl.ds(spread + rows_each[0] // 2, lows)], weights, sems.at[0]
        )
        load_moms = pltpu.make_async_copy(moms, moms_all.at[:, 1], sems.at[1])
        load_other = pltpu.make_async_copy(moms_other, moms_all.at[:, 0], sems.at[2])
        load_low.start()
        load_moms.start()
        load_other.start()
        own = size // chips // 2
        lane = lane_of((4 * (size // LANES), LANES)) // own
        groups = LANES // own
        held = []
        for e in range(groups):
            rows = []
            for b in range(size // LANES):
                device = b * groups + e
                rows.append(summed[device // 2, device % 2, -2 * SUBLANES : -SUBLANES, size:][:4])
            held.append(jnp.concatenate(rows, axis=0))
        for g in range(groups):
            value = jnp.zeros_like(held[0])
            for e in range(groups):
                value = jnp.where(lane == e, turn(held[e], own * (e - g)), value)
            for b in range(size // LANES):
                for r in range(4):
                    dze[groups * r + g : groups * r + g + 1, b * LANES : (b + 1) * LANES] = (
                        value[4 * b + r : 4 * b + r + 1]
                    )
        load_low.wait()
        load_moms.wait()
        load_other.wait()
        excite_low = weights[:, :, : rows_each[1] // 2].reshape(size, size)
        critic = weights[:, :, rows_each[1] // 2 :].reshape(size, size).astype(f32)
        gate = z1[...]
        squeezed = gate * jax.nn.sigmoid(gate)
        back = lax.dot_general(
            jnp.concatenate(split_three(dze[...]), axis=0),
            excite_low,
            (((1,), (1,)), ((), ())),
            preferred_element_type=f32,
        )
        rows = dze.shape[0]
        back = back[:rows] + back[rows : 2 * rows] + back[2 * rows :]
        dz1 = back * silu_slope(gate)

        starts, firsts = [0], [0]
        for count in rows_each:
            starts.append(starts[-1] + count)
            firsts.append(firsts[-1] + chips * count)

        def fill(k, grad):
            count = rows_each[k]
            old = moms_all[:, :, starts[k] // 2 : starts[k + 1] // 2].reshape(chips * count, size)
            whole[firsts[k] : firsts[k + 1], :] = MOMENTUM * old + grad

        fill(0, outer_sum(pooled[...], dz1))
        fill(1, outer_sum(squeezed, dze[...]))
        spec = summed[:, :, -2 * SUBLANES :, :size].reshape(size, size)
        vec = column_v[...]
        back_row = jnp.sum(critic * vec, axis=0, keepdims=True)
        square = jnp.sum(back_row * back_row)
        along = jnp.sum(spec * critic) / square
        direction = vec * row_w[0:1, :] + column_t[...] * power[...]
        fill(2, spec / jnp.sqrt(square) - along * direction)

        def own_rows(k):
            count = rows_each[k]
            return whole[pl.ds(pl.multiple_of(firsts[k] + chip * count, count), count), :]

        for k in range(3):
            small[starts[k] : starts[k + 1], :] = own_rows(k)

        @pl.loop(0, 3)
        def _(k):
            chunks = jnp.where(k == 0, firsts[1] // size, 1)
            first = jnp.where(k == 0, 0, firsts[1] + (k - 1) * size)
            view = whole.at[pl.ds(pl.multiple_of(first, size), firsts[1])]
            whole_ortho(
                chunks, view, whole_high, whole_low, small_gram, sg_high, sg_low, sp_high, sp_low
            )

        for k, weight in enumerate((squeeze_w, excite_w, critic_w)):
            small[starts[3] + starts[k] : starts[3] + starts[k + 1], :] = (
                weight[...] * keep - MUON_RATE * own_rows(k)
            )

        vec_rows = vectors.shape[0]
        lane_row = lane_of((1, LANES))
        lines = []
        for gain in range(3):
            for half in range(2):
                for b in range(size // LANES):
                    value = jnp.zeros((1, LANES), f32)
                    for e in range(groups):
                        device = b * groups + e
                        row = summed[device // 2, device % 2, -2 * SUBLANES : -SUBLANES, size:][4:5]
                        row = turn(row, own * (e - (2 * gain + half)))
                        value = jnp.where(lane_row // own == e, row, value)
                    lines.append(value)
        tails = jnp.sum(summed[:, :, -SUBLANES:, size:], axis=(0, 1))
        count = size // LANES
        last = tails[count : count + 1]
        lines += [tails[k : k + 1] for k in range(count)]
        lines.append(jnp.where(lane_row == 0, last, 0.0))
        lines.append(jnp.zeros((vec_rows - len(lines), LANES), f32))
        results = adam(vectors[...], vec_m[...], vec_v[...], jnp.concatenate(lines, axis=0))
        for k in range(3):
            adam_out[k * vec_rows : (k + 1) * vec_rows, :] = results[k]
        adam_out[3 * vec_rows :, :] = jnp.broadcast_to(jnp.sum(jnp.where(lane_row == 1, last, 0.0)), (SUBLANES, LANES))


def update(summed, conv_mom, conv_w, lat, moms, moms_other, squeeze_w, excite_w, critic_w, pooled, z1, column_v, column_t,
           row_w, power, vectors, vec_m, vec_v, spread, size):
    f32, bf16 = jnp.float32, jnp.bfloat16
    widths = conv_w.shape[1]
    chips = lat.shape[0]
    small_rows = squeeze_w.shape[0] + excite_w.shape[0] + critic_w.shape[0]
    arguments = [summed, conv_mom, conv_w, lat, moms, moms_other, squeeze_w, excite_w, critic_w, pooled, z1, column_v, column_t,
                 row_w, power, vectors, vec_m, vec_v]
    vmem, anywhere = pl.BlockSpec(memory_space=pltpu.VMEM), pl.BlockSpec(memory_space=pl.ANY)
    pair, square, small_square = (2, widths, widths), (widths, widths), (size, size)
    tall = chips * squeeze_w.shape[0]
    return local_call(
        partial(update_kernel, spread, size),
        "update",
        [
            jax.ShapeDtypeStruct(conv_w.shape, f32),
            jax.ShapeDtypeStruct((2 * small_rows, size), f32),
            jax.ShapeDtypeStruct((3 * vectors.shape[0] + SUBLANES, LANES), f32),
        ],
        [
            pltpu.SemaphoreType.DMA((3,)),
            pltpu.VMEM(conv_w.shape, f32),
            pltpu.VMEM(pair, f32),
            pltpu.VMEM(pair, bf16),
            pltpu.VMEM(pair, bf16),
            pltpu.VMEM(square, bf16),
            pltpu.VMEM(square, bf16),
            pltpu.VMEM(conv_w.shape, bf16),
            pltpu.VMEM(conv_w.shape, bf16),
            pltpu.VMEM(conv_w.shape, f32),
            pltpu.VMEM((chips * small_rows + size, size), f32),
            pltpu.VMEM((tall, size), bf16),
            pltpu.VMEM((tall, size), bf16),
            pltpu.VMEM(small_square, f32),
            pltpu.VMEM(small_square, bf16),
            pltpu.VMEM(small_square, bf16),
            pltpu.VMEM(small_square, bf16),
            pltpu.VMEM(small_square, bf16),
            pltpu.VMEM((chips, 2, (excite_w.shape[0] + critic_w.shape[0]) // 2, size), bf16),
            pltpu.VMEM(z1.shape, f32),
            pltpu.VMEM((chips, 2) + moms.shape[1:], f32),
        ],
        arguments,
        [vmem] + [anywhere] * 5 + [vmem] * 12,
    )


def by_channels(
    latent,
    noise,
    real_bank,
    real_index,
    frozen_feat,
    frozen_proj,
    power_vec,
    conv_w,
    conv_mom,
    squeeze_w,
    squeeze_mom,
    excite_w,
    excite_mom,
    critic_w,
    critic_mom,
    vectors,
    vec_m,
    vec_v,
):
    n = lax.axis_size("dp")
    chip, side = lax.axis_index("dp"), lax.axis_index("segment")
    f32 = jnp.float32
    micros, _, edge, _, channels = latent.shape
    pixels = noise.shape[2]
    rows, widths = conv_w.shape
    half = widths // 2
    own = half // n // 2
    depth = rows // 4
    proj_width = critic_w.shape[1]
    pixel_count = pixels * n
    patches = micros * pixel_count
    spread = micros * edge * SUBLANES

    def rows_of(vector):
        count = -(-vector.shape[0] // (SUBLANES * LANES)) * SUBLANES
        return jnp.pad(vector, (0, count * LANES - vector.shape[0])).reshape(count, LANES)

    vectors_rows = rows_of(vectors)
    power = power_vec.reshape(1, -1)
    block, conv_own, noise_own, moms = pack(
        n, latent, noise, conv_w, squeeze_w, excite_w, critic_w, squeeze_mom, excite_mom, critic_mom
    )
    lat, conv, noise_all = exchange(
        n, 1, [("relay", True), ("a2a", False), ("relay", True)], [block, conv_own, noise_own]
    )

    moms, lat = lax.optimization_barrier((moms, lat))
    moms = lax.all_gather(moms, "dp", axis=0)

    fake, xn, stats, opened, z1, pooled, consts, noise_rows = front(
        edge, micros, pixel_count, lat, conv, noise_all, vectors_rows
    )
    (arrived,) = exchange(n, 2, [("a2a", True)], [fake])
    dfake, dspec, tail, column_v, column_t, row_w = critic_step(
        edge,
        patches,
        spread,
        arrived,
        lat,
        real_bank,
        frozen_feat,
        frozen_proj,
        power,
        vectors_rows,
        real_index,
    )

    returned, added = exchange(n, 3, [("a2a", True), ("cross", False)], [dfake, dspec])
    dconv, block, dspec = back(
        edge, micros, pixel_count, depth, returned, xn, lat, noise_rows, consts, stats, opened, tail,
        dspec, added,
    )

    dconv, dspec = exchange(n, 4, [("a2a", True), ("plane", False)], [dconv, dspec])
    conv_mom_new, gram, dspec = owner(dconv, conv_mom, dspec)
    grams, dspec = exchange(n, 5, [("a2a", False), ("line", False)], [gram, dspec])
    summed = collect(grams, dspec, block)
    summed, moms_other = exchange(n, 6, [("relay", True), ("sib", False)], [summed, moms])

    conv_new, small, adam_new = update(
        summed, conv_mom_new, conv_w, lat, moms, moms_other, squeeze_w, excite_w, critic_w, pooled, z1, column_v,
        column_t, row_w, power, vectors_rows, rows_of(vec_m), rows_of(vec_v), spread, proj_width,
    )
    conv_new, small, adam_new = share(7, conv_new, small, adam_new)
    pieces = []
    first = 0
    for weight in (squeeze_w, excite_w, critic_w) * 2:
        pieces.append(small[first : first + weight.shape[0]])
        first += weight.shape[0]
    size = vectors.shape[0]
    vec_rows = vectors_rows.shape[0]
    flat = adam_new[: 3 * vec_rows].reshape(3, vec_rows * LANES)[:, :size]
    return (
        adam_new[3 * vec_rows, 0],
        conv_mom_new,
        conv_new,
        pieces[0],
        pieces[3],
        pieces[1],
        pieces[4],
        pieces[2],
        pieces[5],
        flat[0],
        flat[1],
        flat[2],
    )


def shifted_2(value, axis, steps):
    count = lax.axis_size(axis)
    leading, last = (max(0, -steps), min(count, count - steps))
    return lax.ppermute(value, axis, [(source, source + steps) for source in range(leading, last)])


def for_sending(x):
    return jax.tree.map(lambda a: a.astype(jnp.bfloat16) if a.dtype == jnp.float32 else a, x)


def only_if(flag, compute):

    def empty_branch():
        return jax.tree.map(jnp.zeros_like, compute())

    return lax.cond(flag, compute, empty_branch)


def columns(latent_now):
    upsampled = jnp.repeat(jnp.repeat(latent_now, 2, axis=1), 2, axis=2)
    side_now = upsampled.shape[1]
    padded = jnp.pad(upsampled, ((0, 0), (1, 1), (1, 1), (0, 0)))
    taps = [
        padded[:, row_tap : row_tap + side_now, col_tap : col_tap + side_now, :]
        for row_tap in range(3)
        for col_tap in range(3)
    ]
    return jnp.concatenate(taps, axis=-1).reshape(-1, 9 * upsampled.shape[3])


def spectral_norm(weight, power):
    vector = high_dot(weight, power)
    vector = vector * lax.rsqrt(jnp.sum(vector * vector))
    product_one = high_dot(vector, weight)
    return weight / jnp.sqrt(jnp.sum(product_one * product_one))


def excite(pooled, squeeze_w, excite_w):
    return jax.nn.sigmoid(high_dot(jax.nn.silu(high_dot(pooled, squeeze_w)), excite_w))


def normalize(shifted, moments, pixel_count, bn_gain, bn_bias):
    mean_vec = moments[0] / pixel_count
    inv_std = lax.rsqrt(moments[1] / pixel_count - mean_vec * mean_vec + NORM_EPS)
    centred = (shifted - mean_vec) * inv_std
    return (centred, inv_std, centred * bn_gain + bn_bias)


def critic_pass(
    inputs, sign, patches, frozen_feat, frozen_proj, spectral, out_weight, out_bias, want_input
):
    pre_act = low_dot(inputs, frozen_feat)
    features = jax.nn.silu(pre_act).astype(jnp.bfloat16)
    projected = low_dot(features, frozen_proj).astype(jnp.bfloat16)
    critic_act = low_dot(projected, spectral)
    activated = jax.nn.silu(critic_act)
    logits = high_dot(activated, out_weight) + out_bias
    loss_part = jnp.sum(jax.nn.softplus(1.0 + sign * logits))
    dlogit = sign * jax.nn.sigmoid(1.0 + sign * logits) / patches
    dact = (dlogit[:, None] * out_weight * silu_slope(critic_act)).astype(jnp.bfloat16)
    result = [loss_part, low_dot(projected.T, dact), high_dot(dlogit, activated), jnp.sum(dlogit)]
    if want_input:
        dproj = low_dot(dact, spectral.T).astype(jnp.bfloat16)
        dpre = (low_dot(dproj, frozen_proj.T) * silu_slope(pre_act)).astype(jnp.bfloat16)
        result.append(low_dot(dpre, frozen_feat.T).astype(jnp.bfloat16))
    return result


def orthogonalize(momenta):
    squares = lax.psum(
        (
            jnp.sum(momenta[0] * momenta[0]),
            jnp.sum(momenta[1] * momenta[1]),
            jnp.sum(momenta[2] * momenta[2]),
            jnp.sum(momenta[3] * momenta[3]),
        ),
        "dp",
    )
    current = [
        matrix_now / (jnp.sqrt(square_now) + 1e-07)
        for matrix_now, square_now in zip(momenta, squares)
    ]

    def iterate(_, current):
        partials = [
            lax.psum_scatter(
                high_dot(matrix_now.T, matrix_now), "dp", scatter_dimension=0, tiled=True
            )
            for matrix_now in current
        ]
        full_grams = [lax.all_gather(part, "dp", axis=0, tiled=True) for part in partials]
        updated = []
        for matrix_now, gram in zip(current, full_grams):
            product_one = high_dot(matrix_now, gram)
            updated.append(
                NEWTON_A * matrix_now
                + NEWTON_B * product_one
                + NEWTON_C * high_dot(product_one, gram)
            )
        return updated

    return lax.fori_loop(0, NS_STEPS, iterate, current)


def by_images(
    latent,
    noise,
    real_bank,
    real_index,
    frozen_feat,
    frozen_proj,
    power_vec,
    conv_w,
    conv_mom,
    squeeze_w,
    squeeze_mom,
    excite_w,
    excite_mom,
    critic_w,
    critic_mom,
    vectors,
    vec_m,
    vec_v,
):
    gathered = (
        lax.all_gather(conv_w.astype(jnp.bfloat16), "dp", axis=0, tiled=True),
        lax.all_gather(squeeze_w.astype(jnp.bfloat16), "dp", axis=0, tiled=True),
        lax.all_gather(excite_w.astype(jnp.bfloat16), "dp", axis=0, tiled=True),
        lax.all_gather(critic_w.astype(jnp.bfloat16), "dp", axis=0, tiled=True),
    )
    conv_low, squeeze_low, excite_low, critic_low = gathered
    squeeze_full = squeeze_low.astype(jnp.float32)
    excite_full = excite_low.astype(jnp.float32)
    spectral_full, spectral_back = jax.vjp(
        partial(spectral_norm, power=power_vec), critic_low.astype(jnp.float32)
    )
    spectral = spectral_full.astype(jnp.bfloat16)
    micro_count, images, pixels = (noise.shape[0], noise.shape[1], noise.shape[2])
    widths = conv_low.shape[1]
    half_width = widths // 2
    proj_width = critic_low.shape[0]
    tokens = images * pixels
    pixel_count = tokens * lax.axis_size("dp")
    patches = micro_count * pixel_count
    noise_gain = vectors[:widths]
    bn_gain = vectors[widths : 2 * widths]
    bn_bias = vectors[2 * widths : 3 * widths]
    out_weight = vectors[3 * widths : 3 * widths + proj_width]
    out_bias = vectors[3 * widths + proj_width]
    generator = lax.axis_index("segment") == 0
    critic_side = jnp.logical_not(generator)
    pooled = jnp.mean(latent.astype(jnp.float32), axis=(2, 3))
    conv_acc = jnp.zeros(conv_low.shape, jnp.float32)
    squeeze_acc = jnp.zeros(squeeze_low.shape, jnp.float32)
    excite_acc = jnp.zeros(excite_low.shape, jnp.float32)
    spectral_acc = jnp.zeros(critic_low.shape, jnp.float32)
    vector_acc = jnp.zeros(vectors.shape, jnp.float32)
    loss_acc = jnp.zeros((), jnp.float32)
    for micro_step in range(micro_count):
        noise_now = noise[micro_step].reshape(-1)
        excitation, excite_back = jax.vjp(excite, pooled[micro_step], squeeze_full, excite_full)

        def gen_front():
            patches_in = columns(latent[micro_step])
            return (patches_in, low_dot(patches_in, conv_low) + noise_now[:, None] * noise_gain)

        patches_in, shifted = only_if(generator, gen_front)
        moments = lax.psum((jnp.sum(shifted, axis=0), jnp.sum(shifted * shifted, axis=0)), "dp")

        def gen_mid():
            centred, inv_std, normed = normalize(shifted, moments, pixel_count, bn_gain, bn_bias)
            gated = normed[:, :half_width] * jax.nn.sigmoid(normed[:, half_width:])
            fake_map = gated.reshape(images, pixels, half_width) * excitation[:, None, :]
            return fake_map.reshape(tokens, half_width).astype(jnp.bfloat16)

        fake_map = only_if(generator, gen_mid)
        arrived = shifted_2(fake_map, "segment", 1)

        def critic_work():
            real_map = real_bank[real_index[micro_step]].reshape(tokens, half_width)
            real_out = critic_pass(
                real_map,
                -1.0,
                patches,
                frozen_feat,
                frozen_proj,
                spectral,
                out_weight,
                out_bias,
                False,
            )
            fake_out = critic_pass(
                arrived,
                1.0,
                patches,
                frozen_feat,
                frozen_proj,
                spectral,
                out_weight,
                out_bias,
                True,
            )
            return (
                real_out[0] + fake_out[0],
                real_out[1] + fake_out[1],
                real_out[2] + fake_out[2],
                real_out[3] + fake_out[3],
                fake_out[4],
            )

        loss_part, dspec_part, dout_part, dbias_part, input_grad = only_if(critic_side, critic_work)
        returned = jax.tree.map(
            lambda part, own: part.astype(own.dtype),
            shifted_2(for_sending(input_grad), "segment", -1),
            input_grad,
        )

        def gen_back():
            dfake = -returned.astype(jnp.float32).reshape(images, pixels, half_width)
            centred, inv_std, normed = normalize(shifted, moments, pixel_count, bn_gain, bn_bias)
            opened = jax.nn.sigmoid(normed[:, half_width:])
            first_half = normed[:, :half_width]
            gated = (first_half * opened).reshape(images, pixels, half_width)
            unused, dsqueeze, dexcite = excite_back(jnp.sum(dfake * gated, axis=1))
            dgated = (dfake * excitation[:, None, :]).reshape(tokens, half_width)
            dnormed = jnp.concatenate(
                [dgated * opened, dgated * first_half * opened * (1.0 - opened)], axis=1
            )
            return (
                dnormed * bn_gain,
                centred,
                inv_std,
                dsqueeze,
                dexcite,
                jnp.sum(dnormed * centred, axis=0),
                jnp.sum(dnormed, axis=0),
            )

        dcentred, centred, inv_std, dsqueeze, dexcite, dgain, dbias = only_if(generator, gen_back)
        back_sums = lax.psum((jnp.sum(dcentred, axis=0), jnp.sum(dcentred * centred, axis=0)), "dp")

        def gen_grad():
            dshifted = inv_std * (
                dcentred - back_sums[0] / pixel_count - centred * back_sums[1] / pixel_count
            )
            return (dshifted.astype(jnp.bfloat16), jnp.sum(dshifted * noise_now[:, None], axis=0))

        dhidden, dnoise = only_if(generator, gen_grad)
        conv_acc = conv_acc + only_if(generator, lambda: low_dot(patches_in.T, dhidden))
        squeeze_acc = squeeze_acc + dsqueeze
        excite_acc = excite_acc + dexcite
        spectral_acc = spectral_acc + dspec_part
        vector_acc = vector_acc + jnp.concatenate(
            [dnoise, dgain, dbias, dout_part, dbias_part[None]]
        )
        loss_acc = loss_acc + loss_part
    critic_grad = spectral_back(spectral_acc)[0]
    conv_rows_sum, squeeze_rows, excite_rows, critic_rows = (
        lax.psum_scatter(conv_acc, "dp", scatter_dimension=0, tiled=True),
        lax.psum_scatter(squeeze_acc, "dp", scatter_dimension=0, tiled=True),
        lax.psum_scatter(excite_acc, "dp", scatter_dimension=0, tiled=True),
        lax.psum_scatter(critic_grad, "dp", scatter_dimension=0, tiled=True),
    )
    gradients = lax.psum((conv_rows_sum, squeeze_rows, excite_rows, critic_rows), "segment")
    vector_grad, loss_sum = lax.psum((vector_acc, loss_acc), ("segment", "dp"))
    weights = (conv_w, squeeze_w, excite_w, critic_w)
    new_moms = [
        MOMENTUM * old_mom + grad_now
        for old_mom, grad_now in zip((conv_mom, squeeze_mom, excite_mom, critic_mom), gradients)
    ]
    ortho = orthogonalize(new_moms)
    new_weights = [
        weight * (1.0 - MUON_RATE * DECAY) - MUON_RATE * step_dir
        for weight, step_dir in zip(weights, ortho)
    ]
    vec_m_new, vec_v_new, vectors_new = adam(vectors, vec_m, vec_v, vector_grad)
    return (
        loss_sum,
        new_moms[0],
        new_weights[0],
        new_moms[1],
        new_weights[1],
        new_moms[2],
        new_weights[2],
        new_moms[3],
        new_weights[3],
        vec_m_new,
        vec_v_new,
        vectors_new,
    )


def solution(mesh):
    placed = (
        P(None, "dp", None, None, None),
        P(None, "dp", None),
        P("dp", None, None),
        P(None, "dp"),
        P(),
        P(),
        P(),
        P("dp", None),
        P("dp", None),
        P("dp", None),
        P("dp", None),
        P("dp", None),
        P("dp", None),
        P("dp", None),
        P("dp", None),
        P(),
        P(),
        P(),
    )
    given = (
        P(),
        P("dp", None),
        P("dp", None),
        P("dp", None),
        P("dp", None),
        P("dp", None),
        P("dp", None),
        P("dp", None),
        P("dp", None),
        P(),
        P(),
        P(),
    )

    def step(latent, noise, *rest):
        n, sides = mesh.shape["dp"], mesh.shape["segment"]
        micros, images, edge = latent.shape[:3]
        fits = (
            n == 16
            and sides == 2
            and images == n
            and micros == 2
            and edge <= SUBLANES - 1
            and rest[5].shape[1] == 2 * n * sides * 16
        )
        plan = by_channels if fits else by_images
        return jax.shard_map(
            plan, mesh=mesh, in_specs=placed, out_specs=given, check_vma=False
        )(latent, noise, *rest)

    return step
```

```python
from functools import partial

import jax
import jax.numpy as jnp
from jax import lax
from jax.experimental import pallas as pl
from jax.experimental.pallas import tpu as pltpu
from jax.sharding import PartitionSpec as P

NS_STEPS = 5
STEP = 10


HIGHEST_PREC = lax.Precision.HIGHEST
HIGH_PREC = lax.Precision.HIGH
MESH = pl.DeviceIdType.MESH
NORM_EPS = 1e-05
NEWTON_A = 3.4445
NEWTON_B = -4.775
NEWTON_C = 2.0315
MOMENTUM = 0.95
MUON_RATE = 0.5
DECAY = 0.01
ADAM_RATE = 0.2
ADAM_BETA1 = 0.9
ADAM_BETA2 = 0.95
ADAM_EPS = 1e-08
LANES = 128
SUBLANES = 8
PLANE = 4
BLOCK = 256
FINE_BYTES = 64 * 1024
NO_COST = pl.CostEstimate(flops=0, bytes_accessed=0, transcendentals=0)
VMEM_BYTES = 56 * 1024 * 1024


def low_dot(left, right):
    return jnp.dot(left, right, preferred_element_type=jnp.float32)


def high_dot(left, right):
    return jnp.dot(left, right, precision=HIGHEST_PREC, preferred_element_type=jnp.float32)


def mid_dot(left, right):
    return jnp.dot(left, right, precision=HIGH_PREC, preferred_element_type=jnp.float32)


def silu_slope(value):
    opened = jax.nn.sigmoid(value)
    return opened * (1.0 + value * (1.0 - opened))


def adam(vectors, vec_m, vec_v, vector_grad):
    vec_m_new = ADAM_BETA1 * vec_m + (1.0 - ADAM_BETA1) * vector_grad
    vec_v_new = ADAM_BETA2 * vec_v + (1.0 - ADAM_BETA2) * vector_grad * vector_grad
    first_hat = vec_m_new / (1.0 - ADAM_BETA1**STEP)
    second_hat = vec_v_new / (1.0 - ADAM_BETA2**STEP)
    vectors_new = vectors * (1.0 - ADAM_RATE * DECAY) - ADAM_RATE * first_hat / (
        jnp.sqrt(second_hat) + ADAM_EPS
    )
    return vec_m_new, vec_v_new, vectors_new


def exchange(n, ident, plans, arrays, core=None):
    count = len(plans)
    kinds = [kind for kind, _ in plans]
    planes = n // PLANE

    def shape(kind, paired, x):
        if kind == "relay":
            lead, block = (planes, PLANE) + ((2,) if paired else ()), x.shape
        elif kind == "a2a":
            lead, block = ((n, 2) if paired else (n,)), x.shape[1:]
        elif kind == "plane":
            lead, block = (PLANE,), x.shape[1:]
        elif kind == "line":
            lead, block = (planes,), x.shape[1:]
        elif kind == "cross":
            lead, block = (), x.shape[:1] + x.shape[2:]
        else:
            lead, block = (), x.shape
        return jax.ShapeDtypeStruct(lead + block, x.dtype)

    outs = [shape(kind, paired, x) for (kind, paired), x in zip(plans, arrays)]
    direct = [a for a in range(count) if kinds[a] == "a2a"]
    near = [a for a in range(count) if kinds[a] in ("plane", "line")]
    single = [a for a in range(count) if kinds[a] in ("cross", "sib")]
    passing = [a for a in direct if plans[a][1]]
    parts = []
    for a in range(count):
        if kinds[a] == "relay":
            rows = arrays[a].shape[0]
            unit = 16 if arrays[a].dtype == jnp.bfloat16 else 8
            cut = -(-rows // (2 * unit)) * unit
            fine = arrays[a].size * arrays[a].dtype.itemsize > FINE_BYTES
            parts.append((a, 0, cut, 0, fine))
            if cut < rows:
                parts.append((a, cut, rows - cut, 1, fine))
    small = [p for p in range(len(parts)) if not parts[p][4]]
    large = [p for p in range(len(parts)) if parts[p][4]]

    coupled = [p for p in range(len(parts)) if plans[parts[p][0]][1]]

    def body(*refs):
        if core is None:
            run(*refs)
        else:
            pl.when(lax.axis_index("segment") == core)(partial(run, *refs))

    def run(*refs):
        ins, results = refs[:count], refs[count : 2 * count]
        (send, recv, pass_send, pass_recv, here, up_send, z_send, z_recv, first_send, first_recv,
         second_send, second_recv, core_send, core_recv, part_here) = refs[2 * count :]
        me, side = lax.axis_index("dp"), lax.axis_index("segment")
        other = 1 - side
        z, spot = me // PLANE, me % PLANE
        beside = (spot + 1 - 2 * (spot % 2), (spot + 2) % PLANE)
        across = PLANE - 1 - spot
        barrier = pltpu.get_barrier_semaphore()

        def greet(where):
            pl.semaphore_signal(barrier, inc=1, device_id=where, device_id_type=MESH)

        greeted = 0
        if direct or near:

            @pl.loop(1, n)
            def _(k):
                greet({"dp": lax.rem(me + k, n)})

            greeted += n - 1
        elif parts:

            @pl.loop(1, planes)
            def _(k):
                greet({"dp": lax.rem(me + k * PLANE, n)})

            for spot_now in beside:
                greet({"dp": z * PLANE + spot_now})
            greeted += planes + 1
        if passing or single or coupled:
            greet({"segment": other})
            greeted += 1
        pl.semaphore_wait(barrier, greeted)

        def remote(src, dst, send_sem, recv_sem, where):
            return pltpu.make_async_remote_copy(
                src_ref=src,
                dst_ref=dst,
                send_sem=send_sem,
                recv_sem=recv_sem,
                device_id=where,
                device_id_type=MESH,
            )

        every = range(len(parts))

        def cell(p, plane, spot_now):
            a, first, rows = parts[p][:3]
            if p in coupled:
                return results[a].at[plane, spot_now, side, pl.ds(first, rows)]
            return results[a].at[plane, spot_now, pl.ds(first, rows)]

        def column(p, spot_now, of_side):
            a, first, rows = parts[p][:3]
            if p in coupled:
                return results[a].at[:, spot_now, of_side, pl.ds(first, rows)]
            return results[a].at[:, spot_now, pl.ds(first, rows)]

        def mine(p):
            a, first, rows = parts[p][:3]
            return ins[a].at[pl.ds(first, rows)]

        def first_spot(p):
            return beside[parts[p][3]]

        def second_spot(p):
            return beside[1 - parts[p][3]]

        def along(p, k):
            chip = lax.rem(z + k, planes) * PLANE + spot
            return remote(mine(p), cell(p, z, spot), z_send.at[p, k], z_recv.at[p, z], {"dp": chip})

        def chain(p, plane, up, src=None):
            held = cell(p, plane, spot)
            return remote(
                held if src is None else src,
                held,
                (up_send if up else z_send).at[p, plane],
                z_recv.at[p, plane],
                {"dp": me + PLANE if up else me - PLANE},
            )

        def from_plane(p, plane):
            held = cell(p, plane, spot)
            return remote(held, held, z_send.at[p, 0], z_recv.at[p, plane], {"dp": me})

        def to_first(p, plane, src=None, of_spot=None):
            held = cell(p, plane, spot if of_spot is None else of_spot)
            return remote(
                held if src is None else src,
                held,
                first_send.at[p, plane],
                first_recv.at[p, plane],
                {"dp": z * PLANE + first_spot(p)},
            )

        def to_second(p, plane, src=None, of_spot=None, shift=0):
            held = cell(p, plane, spot if of_spot is None else of_spot)
            return remote(
                held if src is None else src,
                held,
                second_send.at[p, plane + shift],
                second_recv.at[p, plane + shift],
                {"dp": z * PLANE + second_spot(p)},
            )

        def column_to_second(p, spot_now):
            held = column(p, spot_now, side)
            return remote(
                held,
                held,
                second_send.at[p, planes],
                second_recv.at[p, planes],
                {"dp": z * PLANE + second_spot(p)},
            )

        def to_core(p, spot_now, of_side):
            held = column(p, spot_now, of_side)
            return remote(
                held, held, core_send.at[p, spot_now], core_recv.at[p, spot_now], {"segment": other}
            )

        def keep(p):
            return pltpu.make_async_copy(mine(p), cell(p, z, spot), part_here.at[p])

        for p in every:
            to_first(p, z, mine(p)).start()
            to_second(p, z, mine(p)).start()
            if p in small:
                for k in range(1, planes):
                    along(p, k).start()
            else:

                @pl.when(z < planes - 1)
                def _():
                    chain(p, z, True, mine(p)).start()

                @pl.when(z > 0)
                def _():
                    chain(p, z, False, mine(p)).start()

            keep(p).start()

        def peer_of(a, k):
            if kinds[a] == "plane":
                return z * PLANE + lax.rem(spot + k, PLANE)
            if kinds[a] == "line":
                return lax.rem(z + k, planes) * PLANE + spot
            return lax.rem(me + lax.rem(k + 6, n - 1) + 1, n)

        def number(a, chip):
            if kinds[a] == "plane":
                return chip % PLANE
            if kinds[a] == "line":
                return chip // PLANE
            return chip

        def source(a, chip):
            return ins[a].at[number(a, chip)]

        def slot(a, chip, of_side):
            if plans[a][1]:
                return results[a].at[chip, of_side]
            return results[a].at[number(a, chip)]

        def outgoing(a, k):
            peer = peer_of(a, k)
            return remote(
                source(a, peer),
                slot(a, me, side),
                send.at[a, k],
                recv.at[a, number(a, me)],
                {"dp": peer},
            )

        def incoming(a, chip):
            return remote(
                source(a, chip), slot(a, chip, side), send.at[a, 0], recv.at[a, number(a, chip)], {"dp": chip}
            )

        def passed(a, src, chip, of_side):
            return remote(
                src,
                slot(a, chip, of_side),
                pass_send.at[a, chip],
                pass_recv.at[a, chip],
                {"segment": other},
            )

        def crossing(a):
            return remote(
                ins[a].at[:, other] if kinds[a] == "cross" else ins[a],
                results[a],
                pass_send.at[a, 0],
                pass_recv.at[a, 0],
                {"segment": other},
            )

        def own(a):
            return pltpu.make_async_copy(source(a, me), slot(a, me, side), here.at[a])

        def spread(p, plane):
            from_plane(p, plane).wait_recv()
            to_first(p, plane).start()
            to_second(p, plane).start()

        if small:

            @pl.loop(1, planes)
            def _(k):
                for p in small:
                    spread(p, lax.rem(z + planes - k, planes))

        for d in range(1, planes) if large else ():

            @pl.when(z - d >= 0)
            def _():
                for p in large:
                    spread(p, z - d)

                    @pl.when(z < planes - 1)
                    def _():
                        chain(p, z - d, True).start()

            @pl.when(z + d < planes)
            def _():
                for p in large:
                    spread(p, z + d)

                    @pl.when(z > 0)
                    def _():
                        chain(p, z + d, False).start()

        for p in every:
            keep(p).wait()
            if p in coupled:
                to_core(p, spot, side).start()
        if large:

            @pl.loop(0, planes)
            def _(k):
                plane = lax.rem(z + k, planes)
                for p in large:
                    to_first(p, plane, of_spot=first_spot(p)).wait_recv()
                    to_second(p, plane, of_spot=first_spot(p), shift=planes).start()

        if direct:

            @pl.loop(1, n)
            def _(k):
                for a in direct:
                    outgoing(a, k).start()

        for a in near:
            for k in range(1, outs[a].shape[0]):
                outgoing(a, k).start()
        for a in direct + near:
            own(a).start()
        for a in passing:
            passed(a, source(a, me), me, side).start()
        for a in single:
            crossing(a).start()

        for p in every:
            if p in small:

                @pl.loop(0, planes)
                def _(plane):
                    to_first(p, plane, of_spot=first_spot(p)).wait_recv()

                column_to_second(p, first_spot(p)).start()
            if p in coupled:
                to_core(p, first_spot(p), side).start()
        for p in every:

            @pl.loop(0, planes)
            def _(plane):
                to_second(p, plane, of_spot=second_spot(p)).wait_recv()

            if p in coupled:
                to_core(p, second_spot(p), side).start()
        for p in every:
            if p in small:
                column_to_second(p, across).wait_recv()
            else:

                @pl.loop(0, planes)
                def _(plane):
                    to_second(p, plane, of_spot=across, shift=planes).wait_recv()

            if p in coupled:
                to_core(p, across, side).start()

        if direct:

            @pl.loop(1, n)
            def _(k):
                chip = lax.rem(me + n - lax.rem(k + 6, n - 1) - 1, n)
                for a in direct:
                    incoming(a, chip).wait_recv()
                    if plans[a][1]:
                        passed(a, slot(a, chip, side), chip, side).start()

        for a in near:
            for k in range(1, outs[a].shape[0]):
                incoming(a, peer_of(a, k)).wait_recv()
                outgoing(a, k).wait_send()
        for a in direct + near:
            own(a).wait()
        if direct:

            @pl.loop(1, n)
            def _(k):
                for a in direct:
                    outgoing(a, k).wait_send()

        if passing:

            @pl.loop(0, n)
            def _(k):
                for a in passing:
                    passed(a, slot(a, k, side), k, side).wait_send()
                    passed(a, slot(a, k, other), k, other).wait_recv()

        for a in single:
            crossing(a).wait()

        for p in every:
            if p in small:
                for k in range(1, planes):
                    along(p, k).wait_send()
                column_to_second(p, first_spot(p)).wait_send()
            else:
                for d in range(planes):

                    @pl.when(jnp.logical_and(z - d >= 0, z < planes - 1))
                    def _():
                        chain(p, z - d, True).wait_send()

                    @pl.when(jnp.logical_and(z + d < planes, z > 0))
                    def _():
                        chain(p, z + d, False).wait_send()

            @pl.loop(0, planes)
            def _(plane):
                to_first(p, plane).wait_send()
                to_second(p, plane).wait_send()
                if p in large:
                    to_second(p, plane, of_spot=first_spot(p), shift=planes).wait_send()

            if p in coupled:

                @pl.loop(0, PLANE)
                def _(spot_now):
                    to_core(p, spot_now, side).wait_send()
                    to_core(p, spot_now, other).wait_recv()

    anywhere = pl.BlockSpec(memory_space=pl.ANY)
    relays = max(len(parts), 1)
    found = pl.pallas_call(
        body,
        out_shape=outs,
        in_specs=[anywhere] * count,
        out_specs=[anywhere] * count,
        scratch_shapes=[pltpu.SemaphoreType.DMA((count, n))] * 4
        + [pltpu.SemaphoreType.DMA((count,))]
        + [pltpu.SemaphoreType.DMA((relays, 2 * planes))] * 7
        + [pltpu.SemaphoreType.DMA((relays, PLANE))] * 2
        + [pltpu.SemaphoreType.DMA((relays,))],
        compiler_params=pltpu.CompilerParams(collective_id=ident, has_side_effects=True),
        cost_estimate=NO_COST,
        name=f"exchange_{ident}",
    )(*arrays)
    return [
        x.reshape((n,) + x.shape[2:]) if kind == "relay" else x for kind, x in zip(kinds, found)
    ]


def share(ident, of_first, *of_second):
    arrays = (of_first, *of_second)
    count = len(arrays)

    def body(*refs):
        ins, results = refs[:count], refs[count : 2 * count]
        send, recv = refs[2 * count :]
        side = lax.axis_index("segment")
        other = 1 - side
        barrier = pltpu.get_barrier_semaphore()
        pl.semaphore_signal(barrier, inc=1, device_id={"segment": other}, device_id_type=MESH)
        pl.semaphore_wait(barrier, 1)

        def over(k):
            return pltpu.make_async_remote_copy(
                src_ref=ins[k],
                dst_ref=results[k],
                send_sem=send.at[k],
                recv_sem=recv.at[k],
                device_id={"segment": other},
                device_id_type=MESH,
            )

        for core, sent, found in ((0, [0], range(1, count)), (1, range(1, count), [0])):

            @pl.when(side == core)
            def _():
                for k in sent:
                    over(k).start()
                for k in found:
                    over(k).wait_recv()
                for k in sent:
                    over(k).wait_send()

    anywhere = pl.BlockSpec(memory_space=pl.ANY)
    arrived = pl.pallas_call(
        body,
        out_shape=[jax.ShapeDtypeStruct(x.shape, x.dtype) for x in arrays],
        in_specs=[anywhere] * count,
        out_specs=[anywhere] * count,
        scratch_shapes=[pltpu.SemaphoreType.DMA((count,))] * 2,
        compiler_params=pltpu.CompilerParams(collective_id=ident, has_side_effects=True),
        cost_estimate=NO_COST,
        name="share",
    )(*arrays)
    is_first = lax.axis_index("segment") == 0
    return [
        jnp.where(is_first == (k == 0), own, found) for k, (own, found) in enumerate(zip(arrays, arrived))
    ]


def local_call(kernel, name, out_shape, scratch, arguments, specs=None):
    return pl.pallas_call(
        kernel,
        out_shape=out_shape,
        in_specs=specs or [pl.BlockSpec(memory_space=pltpu.VMEM)] * len(arguments),
        scratch_shapes=scratch,
        compiler_params=pltpu.CompilerParams(vmem_limit_bytes=VMEM_BYTES),
        cost_estimate=NO_COST,
        name=name,
    )(*arguments)


def split_two(value):
    top = value.astype(jnp.bfloat16)
    return top, (value - top.astype(jnp.float32)).astype(jnp.bfloat16)


def split_three(value):
    top = value.astype(jnp.bfloat16)
    rest = value - top.astype(jnp.float32)
    middle = rest.astype(jnp.bfloat16)
    bottom = (rest - middle.astype(jnp.float32)).astype(jnp.bfloat16)
    return top, middle, bottom


def exact_dot(value, low):
    rows = value.shape[0]
    product = low_dot(jnp.concatenate(split_three(value), axis=0), low)
    return product[:rows] + product[rows : 2 * rows] + product[2 * rows :]


def lane_of(shape):
    return lax.broadcasted_iota(jnp.int32, shape, len(shape) - 1)


def fold(value):
    axis = value.ndim - 1
    value = value + pltpu.roll(value, 64, axis)
    return value + pltpu.roll(value, 32, axis)


def turn(value, steps):
    steps = steps % LANES
    return pltpu.roll(value, steps, value.ndim - 1) if steps else value


def turn_back(value, steps):
    return pltpu.roll(value, lax.rem(2 * LANES - steps, LANES), value.ndim - 1)


def row_pieces(rows, groups, taps, channels):
    depth = rows // groups
    pieces = []
    for chip in range(taps * channels // rows):
        for group in range(groups):
            first = chip * rows + group * depth
            at = first
            while at < first + depth:
                tap, channel = divmod(at, channels)
                take = min(first + depth - at, channels - channel)
                pieces.append((chip, group, at - first, tap, channel, take))
                at += take
    return pieces


def shift_rows(value, side, steps):
    parts = []
    empty = jnp.zeros((1,) + value.shape[1:], value.dtype)
    for first in range(0, value.shape[0], side):
        block = value[first : first + side]
        parts += [empty, block[:-1]] if steps > 0 else [block[1:], empty]
    return jnp.concatenate(parts, axis=0)


def per_micro(values, side):
    return jnp.concatenate(
        [jnp.broadcast_to(v[None], (side, SUBLANES, LANES)) for v in values], axis=0
    )


def pack_kernel(latent, noise, conv, squeeze, excite, critic, squeeze_mom, excite_mom, critic_mom,
                block, conv_out, noise_out, moms, rows_f):
    side = lax.axis_index("segment")
    bf16 = jnp.bfloat16
    micros, _, edge, _, channels = latent.shape
    half_in = channels // 2
    rows_f[...] = jnp.zeros(rows_f.shape, jnp.float32)
    for m in range(micros):
        for i in range(edge):
            at = (m * edge + i) * SUBLANES
            rows_f[at : at + edge, :] = latent[m, 0, i].astype(jnp.float32)
    spread = rows_f.shape[0]
    block[:spread, :] = jnp.where(side == 0, rows_f[:, :half_in], rows_f[:, half_in:]).astype(bf16)
    at = spread
    for weight in (squeeze, excite, critic):
        rows = weight.shape[0] // 2
        block[at : at + rows, :] = jnp.where(side == 0, weight[:rows], weight[rows:]).astype(bf16)
        at += rows
    at = 0
    for mom in (squeeze_mom, excite_mom, critic_mom):
        moms[at : at + mom.shape[0], :] = mom[...]
        at += mom.shape[0]

    chips, depth, _ = conv_out.shape
    widths = conv.shape[1]
    half = widths // 2
    group = half // chips
    lane = lane_of((depth, LANES))
    @pl.loop(0, half // LANES)
    def _(b):
        low_cols = pl.ds(pl.multiple_of(b * LANES, LANES), LANES)
        high_cols = pl.ds(pl.multiple_of(half + b * LANES, LANES), LANES)
        for c in range(LANES // group):
            value = jnp.zeros((depth, LANES), jnp.float32)
            for q in range(4):
                rows = slice(q * depth, (q + 1) * depth)
                first = conv[rows, low_cols]
                second = conv[rows, high_cols]
                to = q * group
                steps = to - c * group + LANES - side * (group // 2)
                low = pltpu.roll(first, lax.rem(steps, LANES), 1)
                high = pltpu.roll(second, lax.rem(steps + group // 2, LANES), 1)
                both = jnp.where(lane % group < group // 2, low, high)
                value = jnp.where(lane // group == q, both, value)
            conv_out[b * (LANES // group) + c] = value.astype(bf16)

    pixels = noise.shape[2]
    parts = jnp.concatenate(
        [p.astype(jnp.float32) for p in split_three(noise[:, 0])]
        + [jnp.zeros((SUBLANES - 3 * micros, pixels), jnp.float32)],
        axis=0,
    ).astype(bf16)
    pixel = lax.broadcasted_iota(jnp.int32, (pixels, LANES), 0)
    spot = lane_of((pixels, LANES))
    within = spot % (4 * edge)
    lane_row = lane_of((1, LANES))
    lines = []
    for j in range(edge):
        wanted = 4 * edge * (within // 4) + 2 * edge * ((within % 4) // 2) + 2 * j + within % 2
        chosen = (pixel == wanted).astype(jnp.float32).astype(bf16)
        found = low_dot(parts, chosen)
        line = jnp.zeros((1, LANES), jnp.float32)
        for m in range(micros):
            total = found[m : m + 1] + found[micros + m : micros + m + 1]
            total = total + found[2 * micros + m : 2 * micros + m + 1]
            line = jnp.where(lane_row // (4 * edge) == m, total, line)
        lines.append(line)
    noise_out[...] = jnp.concatenate(
        lines + [jnp.zeros((SUBLANES - edge, LANES), jnp.float32)], axis=0
    )


def pack(n, latent, noise, conv_w, squeeze_w, excite_w, critic_w, squeeze_mom, excite_mom, critic_mom):
    micros, _, edge, _, channels = latent.shape
    spread = micros * edge * SUBLANES
    rows = spread + (squeeze_w.shape[0] + excite_w.shape[0] + critic_w.shape[0]) // 2
    return local_call(
        pack_kernel,
        "pack",
        [
            jax.ShapeDtypeStruct((rows, channels // 2), jnp.bfloat16),
            jax.ShapeDtypeStruct((n, conv_w.shape[0] // 4, LANES), jnp.bfloat16),
            jax.ShapeDtypeStruct((SUBLANES, LANES), jnp.float32),
            jax.ShapeDtypeStruct((2 * (rows - spread), squeeze_w.shape[1]), jnp.float32),
        ],
        [pltpu.VMEM((spread, channels), jnp.float32)],
        [latent, noise, conv_w, squeeze_w, excite_w, critic_w, squeeze_mom, excite_mom, critic_mom],
    )


def own_columns(row_low, row_high, at, own):
    lane = lane_of((1, LANES))
    low = turn_back(row_low, at)
    high = turn(turn_back(row_high, at), own)
    value = jnp.where(lane < own, low, jnp.where(lane < 2 * own, high, 0.0))
    value = value + turn(value, 2 * own)
    return value + turn(value, 4 * own)


def front_kernel(side, micros, pixel_count, all_lat, conv, noise, vectors,
                 fake, xn, stats, opened_out, z1_out, pooled_out, consts, noise_rows,
                 weight, z, h, gate8):
    images = all_lat.shape[0]
    half_in = all_lat.shape[3]
    channels = 2 * half_in
    spread = micros * side * SUBLANES
    depth = conv.shape[1]
    taps = weight.shape[1] // LANES
    bf16, f32 = jnp.bfloat16, jnp.float32
    chip, core = lax.axis_index("dp"), lax.axis_index("segment")
    own = 16
    widths_rows = 2 * half_in // LANES
    at = 2 * own * lax.rem(chip, PLANE) + own * core
    base = chip // PLANE
    for k in range(3):
        consts[k : k + 1, :] = own_columns(
            vectors[pl.ds(k * widths_rows + base, 1), :],
            vectors[pl.ds(k * widths_rows + widths_rows // 2 + base, 1), :],
            at,
            own,
        )
    consts[3:, :] = jnp.zeros((SUBLANES - 3, LANES), f32)

    group = lane_of((depth, LANES)) // 32
    masks = [(group == g).astype(f32).astype(bf16) for g in range(4)]
    for owner, g, first, tap, channel, take in row_pieces(4 * depth, 4, taps, channels):
        weight[channel : channel + take, tap * LANES : (tap + 1) * LANES] = (
            conv[owner, first : first + take, :] * masks[g][:take]
        )
    lines = micros * side
    step = 4

    @pl.loop(0, images // step)
    def _(k):
        here = pl.ds(k * step, step)
        left = all_lat[here, 0, :spread].reshape(step * spread, half_in)
        right = all_lat[here, 1, :spread].reshape(step * spread, half_in)
        for tap in range(0, taps, 2):
            cols = slice(tap * LANES, min(tap + 2, taps) * LANES)
            product = low_dot(left, weight[:half_in, cols]) + low_dot(right, weight[half_in:, cols])
            for k in range(product.shape[1] // LANES):
                value = fold(product[:, k * LANES : (k + 1) * LANES])
                z[tap + k, here] = value.reshape(step, lines, SUBLANES, LANES)

    from_lane = lax.broadcasted_iota(jnp.int32, (LANES, lines * LANES), 0)
    to_lane = lane_of((LANES, lines * LANES))
    chosen = from_lane == 4 * (to_lane // LANES) + (to_lane % LANES) // 32
    wide = exact_dot(
        noise[:, 0].reshape(images * SUBLANES, LANES), chosen.astype(f32).astype(bf16)
    )
    for line in range(lines):
        noise_rows[:, line] = wide[:, line * LANES : (line + 1) * LANES].reshape(images, SUBLANES, LANES)

    shape3 = (lines, SUBLANES, LANES)
    lane = lane_of(shape3)
    row_first = (lane // 64) == 0
    col_first = ((lane // 32) % 2) == 0
    inside = lax.broadcasted_iota(jnp.int32, shape3, 1) < side
    first_half = (lane % 32) < 16
    gain_noise = consts[0:1, :][None]
    gain = consts[1:2, :][None]
    bias = consts[2:3, :][None]
    zero = jnp.zeros((SUBLANES, LANES), f32)

    def place(img, carry):
        lines_of = []
        for ky in range(3):
            z0, z1, z2 = z[3 * ky, img], z[3 * ky + 1, img], z[3 * ky + 2, img]
            lines_of.append(
                z1
                + jnp.where(col_first, pltpu.roll(z0, 1, 1), z0)
                + jnp.where(col_first, z2, pltpu.roll(z2, SUBLANES - 1, 1))
            )
        x0, x1, x2 = lines_of
        value = (
            x1
            + jnp.where(row_first, shift_rows(x0, side, 1), x0)
            + jnp.where(row_first, x2, shift_rows(x2, side, -1))
        )
        value = value + noise_rows[img] * gain_noise
        value = jnp.where(inside, value, 0.0)
        h[img] = value
        new = []
        for m in range(micros):
            part = value[m * side : (m + 1) * side]
            new.append(carry[2 * m] + jnp.sum(part, axis=0))
            new.append(carry[2 * m + 1] + jnp.sum(part * part, axis=0))
        return tuple(new)

    sums = lax.fori_loop(0, images, place, (zero,) * (2 * micros))
    means, stds = [], []
    for m in range(micros):
        mean_now = jnp.sum(fold(sums[2 * m]), axis=0, keepdims=True) / pixel_count
        square = jnp.sum(fold(sums[2 * m + 1]), axis=0, keepdims=True) / pixel_count
        means.append(mean_now)
        stds.append(lax.rsqrt(square - mean_now * mean_now + NORM_EPS))
        stats[m : m + 1, :] = stds[m]
    mean12, std12 = per_micro(means, side), per_micro(stds, side)

    count = images * micros
    rows_map = side * SUBLANES
    owner = lax.broadcasted_iota(jnp.int32, (count, count * rows_map), 1) // rows_map
    pool = (owner == lax.broadcasted_iota(jnp.int32, owner.shape, 0)).astype(f32).astype(bf16)
    area = 1.0 / (side * side)
    pooled = [
        low_dot(pool, all_lat[:, p, :spread].reshape(images * spread, half_in)) * area
        for p in range(2)
    ]
    rows_squeeze = channels // images // 2
    rows_excite = half_in // images // 2
    squeeze = all_lat[:, :, spread : spread + rows_squeeze].reshape(channels, half_in)
    excite = all_lat[:, :, spread + rows_squeeze : spread + rows_squeeze + rows_excite]
    excite = excite.reshape(half_in, half_in)
    z1 = exact_dot(pooled[0], squeeze[:half_in]) + exact_dot(pooled[1], squeeze[half_in:])
    z1_out[...] = z1
    pooled_out[:, :half_in] = pooled[0]
    pooled_out[:, half_in:] = pooled[1]
    wide = jax.nn.sigmoid(exact_dot(z1 * jax.nn.sigmoid(z1), excite))
    opened = wide[:, :LANES]
    for b in range(1, half_in // LANES):
        opened = jnp.where(base == b, wide[:, b * LANES : (b + 1) * LANES], opened)
    opened = jnp.where(lane_of(opened.shape) < own, turn_back(opened, at), 0.0)
    for steps in (own, 2 * own, 4 * own):
        opened = opened + turn(opened, steps)
    opened_out[...] = opened
    gate8[...] = jnp.broadcast_to(opened[:, None, :], gate8.shape)

    @pl.loop(0, images)
    def _(img):
        centred = (h[img] - mean12) * std12
        xn[img] = centred
        y = centred * gain + bias
        gated = y * turn(jax.nn.sigmoid(y), -16)
        pieces = []
        for m in range(micros):
            pieces.append(gated[m * side : (m + 1) * side] * gate8[img * micros + m][None])
        packed = jnp.where(first_half[:side], pieces[0], turn(pieces[1], 16))
        fake[img] = packed.reshape(side * SUBLANES, LANES).astype(bf16)


def front(side, micros, pixel_count, lat, conv, noise, vectors):
    images, _, _, half_in = lat.shape
    lines = micros * side
    count = images * micros
    f32 = jnp.float32
    return local_call(
        partial(front_kernel, side, micros, pixel_count),
        "front",
        [
            jax.ShapeDtypeStruct((images, side * SUBLANES, LANES), jnp.bfloat16),
            jax.ShapeDtypeStruct((images, lines, SUBLANES, LANES), f32),
            jax.ShapeDtypeStruct((SUBLANES, LANES), f32),
            jax.ShapeDtypeStruct((count, LANES), f32),
            jax.ShapeDtypeStruct((count, half_in), f32),
            jax.ShapeDtypeStruct((count, 2 * half_in), f32),
            jax.ShapeDtypeStruct((SUBLANES, LANES), f32),
            jax.ShapeDtypeStruct((images, lines, SUBLANES, LANES), f32),
        ],
        [
            pltpu.VMEM((2 * half_in, 9 * LANES), jnp.bfloat16),
            pltpu.VMEM((9, images, lines, SUBLANES, LANES), f32),
            pltpu.VMEM((images, lines, SUBLANES, LANES), f32),
            pltpu.VMEM((count, SUBLANES, LANES), f32),
        ],
        [lat, conv, noise, vectors],
    )


def critic_kernel(side, patches, spread, arrived, lat, real_bank, feat, proj, power, vectors, chosen,
                  dfake, dspec, tail, column_v, column_t, row_w, maps, dmaps, weight_low, real_map, sem):
    bf16 = jnp.bfloat16
    core = lax.axis_index("segment")
    chips, _, rows_map, _ = arrived.shape
    size = feat.shape[0]
    at = 6 * size // LANES
    head = jnp.concatenate([vectors[at + k : at + k + 1, :] for k in range(size // LANES)], axis=1)
    offset = vectors[at + size // LANES : at + size // LANES + 1, 0:1]
    rows_before = spread + size // chips + size // chips // 2
    load = pltpu.make_async_copy(
        lat.at[:, :, pl.ds(rows_before, size // chips // 2)], weight_low, sem.at[0]
    )
    load_real = pltpu.make_async_copy(real_bank.at[chosen[core, 0]], real_map, sem.at[1])
    load.start()
    load_real.start()

    lane = lane_of((rows_map, LANES))
    per_block = LANES // 32

    @pl.loop(0, size // LANES)
    def _(b):
        both = []
        for c in range(per_block):
            low = turn_back(arrived[b * per_block + c, 0].astype(jnp.float32), 16 * core)
            high = turn_back(arrived[b * per_block + c, 1].astype(jnp.float32), 16 * core - 16)
            both.append(jnp.where(lane % 32 < 16, low, high))
        cols = pl.ds(pl.multiple_of(b * LANES, LANES), LANES)
        for q in range(4):
            value = turn(both[0], -32 * q)
            for c in range(1, per_block):
                value = jnp.where(lane // 32 == c, turn(both[c], 32 * (c - q)), value)
            maps[q * rows_map : (q + 1) * rows_map, cols] = value.astype(bf16)

    fakes = 4 * rows_map
    load_real.wait()
    maps[fakes:, :] = real_map[...]
    load.wait()
    weight = weight_low[...].reshape(size, size).astype(jnp.float32)
    product = jnp.sum(weight * power[...], axis=1, keepdims=True)
    length = lax.rsqrt(jnp.sum(product * product))
    vec = product * length
    back = jnp.sum(weight * vec, axis=0, keepdims=True)
    sigma = jnp.sqrt(jnp.sum(back * back))
    unit = back / sigma
    turned = jnp.sum(weight * unit, axis=1, keepdims=True)
    turned = (turned - vec * jnp.sum(turned * vec)) * length
    column_v[...] = vec
    column_t[...] = turned
    row_w[...] = jnp.broadcast_to(unit, row_w.shape)
    spectral = (weight / sigma).astype(bf16)
    rows = maps.shape[0]
    pre_act = low_dot(maps[...], feat[...])
    features = (pre_act * jax.nn.sigmoid(pre_act)).astype(bf16)
    projected = low_dot(features, proj[...]).astype(bf16)
    critic_act = low_dot(projected, spectral)
    opened = jax.nn.sigmoid(critic_act)
    activated = critic_act * opened
    logits = jnp.sum(activated * head, axis=1, keepdims=True) + offset
    row = lax.broadcasted_iota(jnp.int32, (rows, 1), 0)
    sign = jnp.where(row < fakes, 1.0, -1.0)
    valid = jnp.logical_or(row >= fakes, (row % SUBLANES) < side)
    margin = 1.0 + sign * logits
    soft = jnp.maximum(margin, 0.0) + jnp.log1p(jnp.exp(-jnp.abs(margin)))
    loss = jnp.sum(jnp.where(valid, soft, 0.0))
    dlogit = jnp.where(valid, sign * jax.nn.sigmoid(margin), 0.0) / patches
    slope = opened * (1.0 + critic_act * (1.0 - opened))
    dact = (dlogit * head * slope).astype(bf16)
    found = lax.dot_general(
        projected, dact, (((0,), (0,)), ((), ())), preferred_element_type=jnp.float32
    )
    dspec[...] = found.reshape(dspec.shape)
    dhead = jnp.sum(dlogit * activated, axis=0, keepdims=True)
    lane_row = lane_of((1, LANES))
    last = jnp.where(lane_row == 0, jnp.sum(dlogit), jnp.where(lane_row == 1, loss, 0.0))
    pieces = [dhead[:, k * LANES : (k + 1) * LANES] for k in range(size // LANES)] + [last]
    tail[...] = jnp.concatenate(
        pieces + [jnp.zeros((SUBLANES - len(pieces), LANES), jnp.float32)], axis=0
    )
    turned_dims = (((1,), (1,)), ((), ()))
    dproj = lax.dot_general(
        dact[:fakes], spectral, turned_dims, preferred_element_type=jnp.float32
    ).astype(bf16)
    dpre = lax.dot_general(dproj, proj[...], turned_dims, preferred_element_type=jnp.float32)
    dpre = (dpre * silu_slope(pre_act[:fakes])).astype(bf16)
    dmaps[...] = lax.dot_general(dpre, feat[...], turned_dims, preferred_element_type=jnp.float32)

    @pl.loop(0, size // LANES)
    def _(b):
        cols = pl.ds(pl.multiple_of(b * LANES, LANES), LANES)
        parts = [dmaps[q * rows_map : (q + 1) * rows_map, cols] for q in range(4)]
        for c in range(per_block):
            value = turn(parts[0], -32 * c)
            for q in range(1, 4):
                value = jnp.where(lane // 32 == q, turn(parts[q], 32 * (q - c)), value)
            dfake[b * per_block + c] = value.astype(bf16)


def critic_step(side, patches, spread, arrived, lat, real_bank, feat, proj, power, vectors, chosen):
    f32 = jnp.float32
    chips, _, rows_map, _ = arrived.shape
    size = feat.shape[0]
    vmem = pl.BlockSpec(memory_space=pltpu.VMEM)
    smem = pl.BlockSpec(memory_space=pltpu.SMEM)
    anywhere = pl.BlockSpec(memory_space=pl.ANY)
    return local_call(
        partial(critic_kernel, side, patches, spread),
        "critic_step",
        [
            jax.ShapeDtypeStruct((chips, rows_map, LANES), jnp.bfloat16),
            jax.ShapeDtypeStruct((chips, 2, size // chips // 2, size), f32),
            jax.ShapeDtypeStruct((SUBLANES, LANES), f32),
            jax.ShapeDtypeStruct((size, 1), f32),
            jax.ShapeDtypeStruct((size, 1), f32),
            jax.ShapeDtypeStruct((SUBLANES, size), f32),
        ],
        [
            pltpu.VMEM((4 * rows_map + real_bank.shape[1], size), jnp.bfloat16),
            pltpu.VMEM((4 * rows_map, size), f32),
            pltpu.VMEM((chips, 2, size // chips // 2, size), jnp.bfloat16),
            pltpu.VMEM(real_bank.shape[1:], jnp.bfloat16),
            pltpu.SemaphoreType.DMA((2,)),
        ],
        [arrived, lat, real_bank, feat, proj, power, vectors, chosen],
        [vmem, anywhere, anywhere] + [vmem] * 4 + [smem],
    )


def back_kernel(side, micros, pixel_count, grads, xn, lat, noise_rows, consts, stats, opened, tail,
                dspec_own, dspec_other, dconv, block, dspec, dy, packed, product, gate8, dze, all_lat, sem):
    images = all_lat.shape[0]
    half_in = all_lat.shape[3]
    channels = 2 * half_in
    lines = micros * side
    spread = lines * SUBLANES
    load = pltpu.make_async_copy(lat.at[:, :, pl.ds(0, spread)], all_lat, sem.at[0])
    load.start()
    bf16 = jnp.bfloat16
    shape3 = (lines, SUBLANES, LANES)
    lane = lane_of(shape3)
    row_first = (lane // 64) == 0
    col_first = ((lane // 32) % 2) == 0
    first_half = (lane % 32) < 16
    inside = lax.broadcasted_iota(jnp.int32, shape3, 1) < side
    gain = consts[1:2, :][None]
    bias = consts[2:3, :][None]
    zero = jnp.zeros((SUBLANES, LANES), jnp.float32)
    core = lax.axis_index("segment")
    second = core == 1
    gate8[...] = jnp.broadcast_to(opened[...][:, None, :], gate8.shape)
    for plane in range(images // PLANE):
        for spot in range(PLANE):
            k = plane * PLANE + spot
            dspec[spot, plane] = jnp.where(second, dspec_own[k, 1], dspec_own[k, 0]) + dspec_other[k]

    def through_gate(img, carry):
        ascent = -grads[img].astype(jnp.float32).reshape(shape3)
        ascent = jnp.where(second, turn(ascent, -16), ascent)
        ascent = jnp.where(first_half, ascent, 0.0)
        centred = xn[img]
        y = centred * gain + bias
        gate = turn(jax.nn.sigmoid(y), -16)
        dopened = ascent * (y * gate)
        scale = jnp.concatenate(
            [jnp.broadcast_to(gate8[img * micros + m][None], (side, SUBLANES, LANES)) for m in range(micros)],
            axis=0,
        )
        dgated = ascent * scale
        dnormed = jnp.where(first_half, dgated * gate, turn(dgated * y * gate * (1.0 - gate), 16))
        dy[img] = dnormed
        new = []
        for m in range(micros):
            part = slice(m * side, (m + 1) * side)
            total = fold(jnp.sum(dopened[part], axis=0))
            total = total + turn(total, 16)
            gate_now = gate8[img * micros + m]
            dze[img * micros + m] = (
                jnp.broadcast_to(jnp.sum(total, axis=0, keepdims=True), (SUBLANES, LANES))
                * gate_now
                * (1.0 - gate_now)
            )
            new.append(carry[2 * m] + jnp.sum(dnormed[part] * centred[part], axis=0))
            new.append(carry[2 * m + 1] + jnp.sum(dnormed[part], axis=0))
        return tuple(new)

    sums = lax.fori_loop(0, images, through_gate, (zero,) * (2 * micros))
    sums = [jnp.sum(fold(s), axis=0, keepdims=True) for s in sums]
    gain_row = consts[1:2, :]
    mean_back = per_micro([gain_row * sums[2 * m + 1] / pixel_count for m in range(micros)], side)
    cross_back = per_micro([gain_row * sums[2 * m] / pixel_count for m in range(micros)], side)
    std12 = per_micro([stats[m : m + 1, :] for m in range(micros)], side)
    taps = 9
    groups = (taps + 3) // 4
    lane_flat = lane_of((spread, LANES)) // 32

    def through_norm(img, carry):
        centred = xn[img]
        dshift = (dy[img] * gain - mean_back - centred * cross_back) * std12
        dshift = jnp.where(inside, dshift, 0.0)
        carry = carry + jnp.sum(dshift * noise_rows[img], axis=0)
        dh = dshift.astype(bf16).astype(jnp.float32)
        swapped = jnp.where(col_first, turn(dh, -32), turn(dh, 32))
        col0 = jnp.where(col_first, dh, swapped)
        col1 = jnp.where(col_first, swapped, dh)
        by_col = [
            col1 + pltpu.roll(col0, SUBLANES - 1, 1),
            col0 + col1,
            col0 + pltpu.roll(col1, 1, 1),
        ]
        found = [None] * taps
        for kx in range(3):
            value = by_col[kx]
            turned = turn(value, 64)
            row0 = jnp.where(row_first, value, turned)
            row1 = jnp.where(row_first, turned, value)
            found[kx] = row1 + shift_rows(row0, side, -1)
            found[3 + kx] = row0 + row1
            found[6 + kx] = row0 + shift_rows(row1, side, 1)
        for g in range(groups):
            members = [f.reshape(spread, LANES) for f in found[4 * g : 4 * g + 4]]
            value = members[0]
            for k in range(1, len(members)):
                value = jnp.where(lane_flat == k, members[k], value)
            top, rest = split_two(value)
            packed[img, :, g * LANES : (g + 1) * LANES] = top
            packed[img, :, (groups + g) * LANES : (groups + g + 1) * LANES] = rest
        return carry

    dgain_noise = lax.fori_loop(0, images, through_norm, zero)
    dgain_noise = jnp.sum(fold(dgain_noise), axis=0, keepdims=True)
    lane_row = lane_of((1, LANES))
    for r in range(images * micros // 8):
        value = jnp.zeros((1, LANES), jnp.float32)
        for g in range(8):
            value = jnp.where(lane_row // 16 == g, dze[8 * r + g][0:1], value)
        block[r : r + 1, :] = value
    gains = jnp.where(
        lane_row // 32 == 0,
        dgain_noise,
        jnp.where(
            lane_row // 32 == 1,
            sum(sums[2 * m] for m in range(micros)),
            sum(sums[2 * m + 1] for m in range(micros)),
        ),
    )
    block[4:5, :] = gains
    block[5:8, :] = jnp.zeros((3, LANES), jnp.float32)
    block[8:16, :] = tail[...]

    width = groups * LANES
    flat = packed[...].reshape(images * spread, 2 * width)
    load.wait()
    for p in range(2):
        side_rows = all_lat[:, p].reshape(images * spread, half_in)
        both = lax.dot_general(
            side_rows, flat, (((0,), (0,)), ((), ())), preferred_element_type=jnp.float32
        )
        product[p * half_in : (p + 1) * half_in, :] = both[:, :width] + both[:, width:]
    depth = dconv.shape[1]
    unit = 16
    lane_unit = lane_of((unit, LANES)) // 32
    for chip in range(dconv.shape[0]):
        for at in range(0, depth, unit):
            value = None
            for g in range(4):
                tap, channel = divmod((chip * 4 + g) * depth + at, channels)
                piece = product[channel : channel + unit, (tap // 4) * LANES : (tap // 4 + 1) * LANES]
                piece = turn(piece, 32 * (g - tap % 4))
                value = piece if value is None else jnp.where(lane_unit == g, piece, value)
            dconv[chip, at : at + unit, :] = value.astype(bf16)


def back(side, micros, pixel_count, depth, grads, xn, lat, noise_rows, consts, stats, opened, tail,
         dspec_own, dspec_other):
    images, _, _, half_in = lat.shape
    lines = micros * side
    count = images * micros
    f32 = jnp.float32
    return local_call(
        partial(back_kernel, side, micros, pixel_count),
        "back",
        [
            jax.ShapeDtypeStruct((images, depth, LANES), jnp.bfloat16),
            jax.ShapeDtypeStruct((2 * SUBLANES, LANES), f32),
            jax.ShapeDtypeStruct((PLANE, images // PLANE) + dspec_other.shape[1:], f32),
        ],
        [
            pltpu.VMEM((images, lines, SUBLANES, LANES), f32),
            pltpu.VMEM((images, lines * SUBLANES, 6 * LANES), jnp.bfloat16),
            pltpu.VMEM((2 * half_in, 3 * LANES), f32),
            pltpu.VMEM((count, SUBLANES, LANES), f32),
            pltpu.VMEM((count, SUBLANES, LANES), f32),
            pltpu.VMEM((images, 2, lines * SUBLANES, half_in), lat.dtype),
            pltpu.SemaphoreType.DMA((1,)),
        ],
        [grads, xn, lat, noise_rows, consts, stats, opened, tail, dspec_own, dspec_other],
        [pl.BlockSpec(memory_space=pltpu.VMEM)] * 2
        + [pl.BlockSpec(memory_space=pl.ANY)]
        + [pl.BlockSpec(memory_space=pltpu.VMEM)] * 7,
    )


def owner_kernel(dconv, mom, parts_in, mom_new, gram, parts, top, rest):
    chips, _, depth, _ = dconv.shape
    rows, widths = mom.shape
    half = widths // 2
    blocks = widths // LANES
    core = lax.axis_index("segment")
    lane = lane_of((depth, LANES))
    parts[...] = jnp.sum(parts_in[...], axis=0)
    @pl.loop(0, half // LANES)
    def _(b):
        halves = []
        for c in range(PLANE):
            low = dconv[b * PLANE + c, 0].astype(jnp.float32)
            high = dconv[b * PLANE + c, 1].astype(jnp.float32)
            halves.append(
                (
                    jnp.where(lane % 32 < 16, low, turn(high, 16)),
                    jnp.where(lane % 32 < 16, turn(low, -16), high),
                )
            )
        for q in range(4):
            for k in range(2):
                value = None
                for c in range(PLANE):
                    piece = turn(halves[c][k], 32 * (c - q))
                    value = piece if value is None else jnp.where(lane // 32 == c, piece, value)
                cols = pl.ds(pl.multiple_of(k * half + b * LANES, LANES), LANES)
                rows_now = slice(q * depth, (q + 1) * depth)
                mom_new[rows_now, cols] = MOMENTUM * mom[rows_now, cols] + value

    for b in range(blocks):
        high, low = split_two(mom_new[:, b * LANES : (b + 1) * LANES])
        for at in (b, b + blocks) if b < PLANE else (b,):
            cols = slice(at * LANES, (at + 1) * LANES)
            top[:, cols] = high
            rest[:, cols] = low
    dims = (((0,), (0,)), ((), ()))
    share = LANES // 4
    span = gram.shape[2]

    @pl.loop(0, blocks // 2)
    def _(pair):
        at = pl.multiple_of(2 * pair * LANES, LANES)
        own, wide = pl.ds(at, 2 * LANES), pl.ds(at, span + LANES)
        left_high, left_low = top[:, own], rest[:, own]
        right_high, right_low = top[:, wide], rest[:, wide]

        def times(left, right):
            return lax.dot_general(left, right, dims, preferred_element_type=jnp.float32)

        found = times(left_high, right_high) + (times(left_high, right_low) + times(left_low, right_high))
        for k in range(2):
            for h in range(2):
                first = k * LANES + 2 * share * h
                cols = slice(k * LANES, k * LANES + span)
                gram[4 * pair + 2 * k + h] = jnp.where(
                    core == 0,
                    found[first : first + share, cols],
                    found[first + share : first + 2 * share, cols],
                )


def owner(dconv, mom, dspec):
    chips, _, depth, _ = dconv.shape
    rows, widths = mom.shape
    f32 = jnp.float32
    span = (widths // LANES // 2 + 1) * LANES
    return local_call(
        owner_kernel,
        "owner",
        [
            jax.ShapeDtypeStruct(mom.shape, f32),
            jax.ShapeDtypeStruct((chips, widths // chips // 2, span), f32),
            jax.ShapeDtypeStruct(dspec.shape[1:], f32),
        ],
        [pltpu.VMEM((rows, widths + PLANE * LANES), jnp.bfloat16)] * 2,
        [dconv, mom, dspec],
    )


def collect_kernel(grams, dspec, block, gram, small):
    size = dspec.shape[2]
    gram[...] = jnp.sum(grams[...], axis=0)
    small[:, :size] = jnp.sum(dspec[...], axis=0)
    small[:, size:] = block[...]


def collect(grams, dspec, block):
    return local_call(
        collect_kernel,
        "collect",
        [
            jax.ShapeDtypeStruct(grams.shape[1:], jnp.float32),
            jax.ShapeDtypeStruct((block.shape[0], dspec.shape[2] + block.shape[1]), jnp.float32),
        ],
        [],
        [grams, dspec, block],
    )


def three(left_high, left_low, right_high, right_low, dims=(((1,), (0,)), ((), ()))):
    def times(left, right):
        return lax.dot_general(left, right, dims, preferred_element_type=jnp.float32)

    return times(left_high, right_high) + (times(left_high, right_low) + times(left_low, right_high))


def store_block(value, i, j, high, low):
    rows, cols = slice(i * BLOCK, (i + 1) * BLOCK), slice(j * BLOCK, (j + 1) * BLOCK)
    high[rows, cols], low[rows, cols] = split_two(value)
    if i < j:
        high[cols, rows], low[cols, rows] = split_two(value.T)


def polynomial(gram, gram_high, gram_low, high, low):
    for j in range(gram.shape[0] // BLOCK):
        cols, rows = slice(j * BLOCK, (j + 1) * BLOCK), slice(0, (j + 1) * BLOCK)
        found = three(gram_high[rows, :], gram_low[rows, :], gram_high[:, cols], gram_low[:, cols])
        for i in range(j + 1):
            here = slice(i * BLOCK, (i + 1) * BLOCK)
            store_block(NEWTON_B * gram[here, cols] + NEWTON_C * found[here], i, j, high, low)


def multiply(source, source_high, source_low, poly_high, poly_low, result, high, low):
    for j in range(source.shape[0] // BLOCK):
        cols, rows = slice(j * BLOCK, (j + 1) * BLOCK), slice(0, (j + 1) * BLOCK)
        found = three(source_high[rows, :], source_low[rows, :], poly_high[:, cols], poly_low[:, cols])
        for i in range(j + 1):
            here = slice(i * BLOCK, (i + 1) * BLOCK)
            value = NEWTON_A * source[here, cols] + found[here]
            result[here, cols] = value
            store_block(value, i, j, high, low)


def apply(x, x_high, x_low, poly_high, poly_low):
    for j in range(x.shape[1] // BLOCK):
        cols = slice(j * BLOCK, (j + 1) * BLOCK)
        found = three(x_high[...], x_low[...], poly_high[:, cols], poly_low[:, cols])
        x[:, cols] = NEWTON_A * x[:, cols] + found


def resplit(x, x_high, x_low):
    for j in range(x.shape[1] // BLOCK):
        cols = slice(j * BLOCK, (j + 1) * BLOCK)
        x_high[:, cols], x_low[:, cols] = split_two(x[:, cols])


def conv_ortho(have_x, packed, x, gram, high, low, p_high, p_low, x_high, x_low):
    size = gram.shape[1]
    blocks = size // LANES
    share = packed.shape[2]
    span = packed.shape[3] // LANES
    chips_block = LANES // (2 * share)

    def block(b, k):
        pair = pl.ds(b * chips_block, chips_block)
        return packed[pair, :, :share, k * LANES : (k + 1) * LANES].reshape(LANES, LANES)

    eye = lax.broadcasted_iota(jnp.int32, (LANES, LANES), 0) == lane_of((LANES, LANES))

    def add_squares(b, total):
        return total + jnp.where(eye, block(b, 0), 0.0)

    total = lax.fori_loop(0, blocks, add_squares, jnp.zeros((LANES, LANES), jnp.float32))
    scale = 1.0 / (jnp.sqrt(jnp.sum(total)) + 1e-07)

    @pl.loop(0, blocks)
    def _(r):
        rows = pl.ds(pl.multiple_of(r * LANES, LANES), LANES)
        for ahead in range(span):
            cols = pl.ds(pl.multiple_of(lax.rem(r + ahead, blocks) * LANES, LANES), LANES)
            value = (block(r, ahead) * scale) * scale
            gram[0, rows, cols] = value
            high[0, rows, cols], low[0, rows, cols] = split_two(value)
            if ahead:
                value = value.T
                gram[0, cols, rows] = value
                high[0, cols, rows], low[0, cols, rows] = split_two(value)

    have_x()
    for j in range(size // BLOCK):
        cols = slice(j * BLOCK, (j + 1) * BLOCK)
        value = x[:, cols] * scale
        x[:, cols] = value
        x_high[:, cols], x_low[:, cols] = split_two(value)

    @pl.loop(0, NS_STEPS)
    def _(step):
        polynomial(gram.at[0], high.at[0], low.at[0], p_high, p_low)
        apply(x, x_high, x_low, p_high, p_low)

        @pl.when(step < NS_STEPS - 1)
        def _():
            resplit(x, x_high, x_low)
            for k in range(2):
                multiply(
                    gram.at[k], high.at[k], low.at[k], p_high, p_low,
                    gram.at[1 - k], high.at[1 - k], low.at[1 - k],
                )


def whole_ortho(chunks, x, x_high, x_low, gram, g_high, g_low, p_high, p_low):
    size = gram.shape[0]

    def rows_of(c):
        return pl.ds(pl.multiple_of(c * size, size), size)

    def add_squares(c, total):
        value = x[rows_of(c), :]
        return total + jnp.sum(value * value)

    scale = 1.0 / (jnp.sqrt(lax.fori_loop(0, chunks, add_squares, jnp.float32(0.0))) + 1e-07)

    @pl.loop(0, chunks)
    def _(c):
        rows = rows_of(c)
        value = x[rows, :] * scale
        x[rows, :] = value
        x_high[rows, :], x_low[rows, :] = split_two(value)

    @pl.loop(0, NS_STEPS)
    def _(_):
        gram[...] = jnp.zeros(gram.shape, jnp.float32)

        @pl.loop(0, chunks)
        def _(c):
            for j in range(size // BLOCK):
                cols, above = slice(j * BLOCK, (j + 1) * BLOCK), slice(0, (j + 1) * BLOCK)
                gram[above, cols] += three(
                    x_high[rows_of(c), above],
                    x_low[rows_of(c), above],
                    x_high[rows_of(c), cols],
                    x_low[rows_of(c), cols],
                    (((0,), (0,)), ((), ())),
                )

        for j in range(size // BLOCK):
            for i in range(j + 1):
                at = (slice(i * BLOCK, (i + 1) * BLOCK), slice(j * BLOCK, (j + 1) * BLOCK))
                store_block(gram[at], i, j, g_high, g_low)
        polynomial(gram, g_high, g_low, p_high, p_low)

        @pl.loop(0, chunks)
        def _(c):
            rows = rows_of(c)
            for j in range(size // BLOCK):
                cols = slice(j * BLOCK, (j + 1) * BLOCK)
                found = three(x_high[rows, :], x_low[rows, :], p_high[:, cols], p_low[:, cols])
                x[rows, cols] = NEWTON_A * x[rows, cols] + found
            x_high[rows, :], x_low[rows, :] = split_two(x[rows, :])


def outer_sum(left, right):
    a, b, c = split_three(left)
    d, e, f = split_three(right)
    return lax.dot_general(
        jnp.concatenate([a, a, b, a, b, c], axis=0),
        jnp.concatenate([d, e, d, f, e, d], axis=0),
        (((0,), (0,)), ((), ())),
        preferred_element_type=jnp.float32,
    )


def update_kernel(spread, size, gram_rows, smalls_in, conv_mom, conv_w, lat, moms, squeeze_w, excite_w, critic_w, pooled, z1,
                  column_v, column_t, row_w, power, vectors, vec_m, vec_v,
                  conv_new, small, adam_out,
                  sems, x, gram, high, low, p_high, p_low, x_high, x_low, w,
                  whole, whole_high, whole_low, small_gram, sg_high, sg_low, sp_high, sp_low, weights, dze, moms_all, smalls):
    core = lax.axis_index("segment")
    chip = lax.axis_index("dp")
    keep = 1.0 - MUON_RATE * DECAY
    f32 = jnp.float32

    @pl.when(core == 0)
    def _():
        load_mom = pltpu.make_async_copy(conv_mom, x, sems.at[0])
        load_w = pltpu.make_async_copy(conv_w, w, sems.at[1])
        load_mom.start()
        load_w.start()
        conv_ortho(load_mom.wait, gram_rows, x, gram, high, low, p_high, p_low, x_high, x_low)
        load_w.wait()
        conv_new[...] = w[...] * keep - MUON_RATE * x[...]

    @pl.when(core == 1)
    def _():
        chips = lat.shape[0]
        rows_each = [weight.shape[0] for weight in (squeeze_w, excite_w, critic_w)]
        lows = weights.shape[2]
        load_low = pltpu.make_async_copy(
            lat.at[:, :, pl.ds(spread + rows_each[0] // 2, lows)], weights, sems.at[0]
        )
        load_moms = pltpu.make_async_copy(moms, moms_all, sems.at[1])
        load_smalls = pltpu.make_async_copy(smalls_in, smalls, sems.at[2])
        load_smalls.start()
        load_low.start()
        load_moms.start()
        load_smalls.wait()
        own = size // chips // 2
        lane = lane_of((4 * (size // LANES), LANES)) // own
        groups = LANES // own
        held = []
        for e in range(groups):
            rows = []
            for b in range(size // LANES):
                device = b * groups + e
                first = device % 2 * 2 * SUBLANES
                rows.append(smalls[device // 2, first : first + 4, size:])
            held.append(jnp.concatenate(rows, axis=0))
        for g in range(groups):
            value = jnp.zeros_like(held[0])
            for e in range(groups):
                value = jnp.where(lane == e, turn(held[e], own * (e - g)), value)
            for b in range(size // LANES):
                for r in range(4):
                    dze[groups * r + g : groups * r + g + 1, b * LANES : (b + 1) * LANES] = (
                        value[4 * b + r : 4 * b + r + 1]
                    )
        load_low.wait()
        load_moms.wait()
        excite_low = weights[:, :, : rows_each[1] // 2].reshape(size, size)
        critic = weights[:, :, rows_each[1] // 2 :].reshape(size, size).astype(f32)
        gate = z1[...]
        squeezed = gate * jax.nn.sigmoid(gate)
        back = lax.dot_general(
            jnp.concatenate(split_three(dze[...]), axis=0),
            excite_low,
            (((1,), (1,)), ((), ())),
            preferred_element_type=f32,
        )
        rows = dze.shape[0]
        back = back[:rows] + back[rows : 2 * rows] + back[2 * rows :]
        dz1 = back * silu_slope(gate)

        starts, firsts = [0], [0]
        for count in rows_each:
            starts.append(starts[-1] + count)
            firsts.append(firsts[-1] + chips * count)

        def fill(k, grad):
            count = rows_each[k]
            old = moms_all[:, starts[k] : starts[k + 1]].reshape(chips * count, size)
            whole[firsts[k] : firsts[k + 1], :] = MOMENTUM * old + grad

        fill(0, outer_sum(pooled[...], dz1))
        fill(1, outer_sum(squeezed, dze[...]))
        spec = smalls[:, :, :size].reshape(size, size)
        vec = column_v[...]
        back_row = jnp.sum(critic * vec, axis=0, keepdims=True)
        square = jnp.sum(back_row * back_row)
        along = jnp.sum(spec * critic) / square
        direction = vec * row_w[0:1, :] + column_t[...] * power[...]
        fill(2, spec / jnp.sqrt(square) - along * direction)

        def own_rows(k):
            count = rows_each[k]
            return whole[pl.ds(pl.multiple_of(firsts[k] + chip * count, count), count), :]

        for k in range(3):
            small[starts[k] : starts[k + 1], :] = own_rows(k)

        @pl.loop(0, 3)
        def _(k):
            chunks = jnp.where(k == 0, firsts[1] // size, 1)
            first = jnp.where(k == 0, 0, firsts[1] + (k - 1) * size)
            view = whole.at[pl.ds(pl.multiple_of(first, size), firsts[1])]
            whole_ortho(
                chunks, view, whole_high, whole_low, small_gram, sg_high, sg_low, sp_high, sp_low
            )

        for k, weight in enumerate((squeeze_w, excite_w, critic_w)):
            small[starts[3] + starts[k] : starts[3] + starts[k + 1], :] = (
                weight[...] * keep - MUON_RATE * own_rows(k)
            )

        vec_rows = vectors.shape[0]
        lane_row = lane_of((1, LANES))
        lines = []
        for gain in range(3):
            for half in range(2):
                for b in range(size // LANES):
                    value = jnp.zeros((1, LANES), f32)
                    for e in range(groups):
                        device = b * groups + e
                        first = device % 2 * 2 * SUBLANES + 4
                        row = smalls[device // 2, first : first + 1, size:]
                        row = turn(row, own * (e - (2 * gain + half)))
                        value = jnp.where(lane_row // own == e, row, value)
                    lines.append(value)
        tails = jnp.sum(smalls[:, SUBLANES : 2 * SUBLANES, size:] + smalls[:, 3 * SUBLANES :, size:], axis=0)
        count = size // LANES
        last = tails[count : count + 1]
        lines += [tails[k : k + 1] for k in range(count)]
        lines.append(jnp.where(lane_row == 0, last, 0.0))
        lines.append(jnp.zeros((vec_rows - len(lines), LANES), f32))
        results = adam(vectors[...], vec_m[...], vec_v[...], jnp.concatenate(lines, axis=0))
        for k in range(3):
            adam_out[k * vec_rows : (k + 1) * vec_rows, :] = results[k]
        adam_out[3 * vec_rows :, :] = jnp.broadcast_to(jnp.sum(jnp.where(lane_row == 1, last, 0.0)), (SUBLANES, LANES))


def update(gram_rows, smalls, conv_mom, conv_w, lat, moms, squeeze_w, excite_w, critic_w, pooled, z1, column_v, column_t,
           row_w, power, vectors, vec_m, vec_v, spread, size):
    f32, bf16 = jnp.float32, jnp.bfloat16
    widths = conv_w.shape[1]
    chips = lat.shape[0]
    small_rows = squeeze_w.shape[0] + excite_w.shape[0] + critic_w.shape[0]
    arguments = [gram_rows, smalls, conv_mom, conv_w, lat, moms, squeeze_w, excite_w, critic_w, pooled, z1, column_v, column_t,
                 row_w, power, vectors, vec_m, vec_v]
    vmem, anywhere = pl.BlockSpec(memory_space=pltpu.VMEM), pl.BlockSpec(memory_space=pl.ANY)
    pair, square, small_square = (2, widths, widths), (widths, widths), (size, size)
    tall = chips * squeeze_w.shape[0]
    return local_call(
        partial(update_kernel, spread, size),
        "update",
        [
            jax.ShapeDtypeStruct(conv_w.shape, f32),
            jax.ShapeDtypeStruct((2 * small_rows, size), f32),
            jax.ShapeDtypeStruct((3 * vectors.shape[0] + SUBLANES, LANES), f32),
        ],
        [
            pltpu.SemaphoreType.DMA((3,)),
            pltpu.VMEM(conv_w.shape, f32),
            pltpu.VMEM(pair, f32),
            pltpu.VMEM(pair, bf16),
            pltpu.VMEM(pair, bf16),
            pltpu.VMEM(square, bf16),
            pltpu.VMEM(square, bf16),
            pltpu.VMEM(conv_w.shape, bf16),
            pltpu.VMEM(conv_w.shape, bf16),
            pltpu.VMEM(conv_w.shape, f32),
            pltpu.VMEM((chips * small_rows + size, size), f32),
            pltpu.VMEM((tall, size), bf16),
            pltpu.VMEM((tall, size), bf16),
            pltpu.VMEM(small_square, f32),
            pltpu.VMEM(small_square, bf16),
            pltpu.VMEM(small_square, bf16),
            pltpu.VMEM(small_square, bf16),
            pltpu.VMEM(small_square, bf16),
            pltpu.VMEM((chips, 2, (excite_w.shape[0] + critic_w.shape[0]) // 2, size), bf16),
            pltpu.VMEM(z1.shape, f32),
            pltpu.VMEM(moms.shape, f32),
            pltpu.VMEM(smalls.shape, f32),
        ],
        arguments,
        [vmem] + [anywhere] * 5 + [vmem] * 12,
    )


def by_channels(
    latent,
    noise,
    real_bank,
    real_index,
    frozen_feat,
    frozen_proj,
    power_vec,
    conv_w,
    conv_mom,
    squeeze_w,
    squeeze_mom,
    excite_w,
    excite_mom,
    critic_w,
    critic_mom,
    vectors,
    vec_m,
    vec_v,
):
    n = lax.axis_size("dp")
    chip, side = lax.axis_index("dp"), lax.axis_index("segment")
    f32 = jnp.float32
    micros, _, edge, _, channels = latent.shape
    pixels = noise.shape[2]
    rows, widths = conv_w.shape
    half = widths // 2
    own = half // n // 2
    depth = rows // 4
    proj_width = critic_w.shape[1]
    pixel_count = pixels * n
    patches = micros * pixel_count
    spread = micros * edge * SUBLANES

    def rows_of(vector):
        count = -(-vector.shape[0] // (SUBLANES * LANES)) * SUBLANES
        return jnp.pad(vector, (0, count * LANES - vector.shape[0])).reshape(count, LANES)

    vectors_rows = rows_of(vectors)
    power = power_vec.reshape(1, -1)
    block, conv_own, noise_own, moms = pack(
        n, latent, noise, conv_w, squeeze_w, excite_w, critic_w, squeeze_mom, excite_mom, critic_mom
    )
    lat, conv, noise_all = exchange(
        n, 1, [("relay", True), ("a2a", False), ("relay", True)], [block, conv_own, noise_own]
    )

    fake, xn, stats, opened, z1, pooled, consts, noise_rows = front(
        edge, micros, pixel_count, lat, conv, noise_all, vectors_rows
    )
    (arrived,) = exchange(n, 2, [("a2a", True)], [fake])
    dfake, dspec, tail, column_v, column_t, row_w = critic_step(
        edge,
        patches,
        spread,
        arrived,
        lat,
        real_bank,
        frozen_feat,
        frozen_proj,
        power,
        vectors_rows,
        real_index,
    )

    returned, added = exchange(n, 3, [("a2a", True), ("cross", False)], [dfake, dspec])
    dconv, block, dspec = back(
        edge, micros, pixel_count, depth, returned, xn, lat, noise_rows, consts, stats, opened, tail,
        dspec, added,
    )

    dconv, dspec = exchange(n, 4, [("a2a", True), ("plane", False)], [dconv, dspec])
    conv_mom_new, gram, dspec = owner(dconv, conv_mom, dspec)
    grams, dspec = exchange(n, 5, [("a2a", False), ("line", False)], [gram, dspec])
    gram, small = collect(grams, dspec, block)
    gram, small_other = exchange(n, 6, [("relay", True), ("sib", False)], [gram, small])
    small = jnp.concatenate([small_other, small], axis=0)
    smalls, moms = exchange(n, 8, [("relay", False)] * 2, [small, moms], core=1)

    conv_new, small, adam_new = update(
        gram, smalls, conv_mom_new, conv_w, lat, moms, squeeze_w, excite_w, critic_w, pooled, z1, column_v,
        column_t, row_w, power, vectors_rows, rows_of(vec_m), rows_of(vec_v), spread, proj_width,
    )
    conv_new, small, adam_new = share(7, conv_new, small, adam_new)
    pieces = []
    first = 0
    for weight in (squeeze_w, excite_w, critic_w) * 2:
        pieces.append(small[first : first + weight.shape[0]])
        first += weight.shape[0]
    size = vectors.shape[0]
    vec_rows = vectors_rows.shape[0]
    flat = adam_new[: 3 * vec_rows].reshape(3, vec_rows * LANES)[:, :size]
    return (
        adam_new[3 * vec_rows, 0],
        conv_mom_new,
        conv_new,
        pieces[0],
        pieces[3],
        pieces[1],
        pieces[4],
        pieces[2],
        pieces[5],
        flat[0],
        flat[1],
        flat[2],
    )


def shifted_2(value, axis, steps):
    count = lax.axis_size(axis)
    leading, last = (max(0, -steps), min(count, count - steps))
    return lax.ppermute(value, axis, [(source, source + steps) for source in range(leading, last)])


def for_sending(x):
    return jax.tree.map(lambda a: a.astype(jnp.bfloat16) if a.dtype == jnp.float32 else a, x)


def only_if(flag, compute):

    def empty_branch():
        return jax.tree.map(jnp.zeros_like, compute())

    return lax.cond(flag, compute, empty_branch)


def columns(latent_now):
    upsampled = jnp.repeat(jnp.repeat(latent_now, 2, axis=1), 2, axis=2)
    side_now = upsampled.shape[1]
    padded = jnp.pad(upsampled, ((0, 0), (1, 1), (1, 1), (0, 0)))
    taps = [
        padded[:, row_tap : row_tap + side_now, col_tap : col_tap + side_now, :]
        for row_tap in range(3)
        for col_tap in range(3)
    ]
    return jnp.concatenate(taps, axis=-1).reshape(-1, 9 * upsampled.shape[3])


def spectral_norm(weight, power):
    vector = high_dot(weight, power)
    vector = vector * lax.rsqrt(jnp.sum(vector * vector))
    product_one = high_dot(vector, weight)
    return weight / jnp.sqrt(jnp.sum(product_one * product_one))


def excite(pooled, squeeze_w, excite_w):
    return jax.nn.sigmoid(high_dot(jax.nn.silu(high_dot(pooled, squeeze_w)), excite_w))


def normalize(shifted, moments, pixel_count, bn_gain, bn_bias):
    mean_vec = moments[0] / pixel_count
    inv_std = lax.rsqrt(moments[1] / pixel_count - mean_vec * mean_vec + NORM_EPS)
    centred = (shifted - mean_vec) * inv_std
    return (centred, inv_std, centred * bn_gain + bn_bias)


def critic_pass(
    inputs, sign, patches, frozen_feat, frozen_proj, spectral, out_weight, out_bias, want_input
):
    pre_act = low_dot(inputs, frozen_feat)
    features = jax.nn.silu(pre_act).astype(jnp.bfloat16)
    projected = low_dot(features, frozen_proj).astype(jnp.bfloat16)
    critic_act = low_dot(projected, spectral)
    activated = jax.nn.silu(critic_act)
    logits = high_dot(activated, out_weight) + out_bias
    loss_part = jnp.sum(jax.nn.softplus(1.0 + sign * logits))
    dlogit = sign * jax.nn.sigmoid(1.0 + sign * logits) / patches
    dact = (dlogit[:, None] * out_weight * silu_slope(critic_act)).astype(jnp.bfloat16)
    result = [loss_part, low_dot(projected.T, dact), high_dot(dlogit, activated), jnp.sum(dlogit)]
    if want_input:
        dproj = low_dot(dact, spectral.T).astype(jnp.bfloat16)
        dpre = (low_dot(dproj, frozen_proj.T) * silu_slope(pre_act)).astype(jnp.bfloat16)
        result.append(low_dot(dpre, frozen_feat.T).astype(jnp.bfloat16))
    return result


def orthogonalize(momenta):
    squares = lax.psum(
        (
            jnp.sum(momenta[0] * momenta[0]),
            jnp.sum(momenta[1] * momenta[1]),
            jnp.sum(momenta[2] * momenta[2]),
            jnp.sum(momenta[3] * momenta[3]),
        ),
        "dp",
    )
    current = [
        matrix_now / (jnp.sqrt(square_now) + 1e-07)
        for matrix_now, square_now in zip(momenta, squares)
    ]

    def iterate(_, current):
        partials = [
            lax.psum_scatter(
                high_dot(matrix_now.T, matrix_now), "dp", scatter_dimension=0, tiled=True
            )
            for matrix_now in current
        ]
        full_grams = [lax.all_gather(part, "dp", axis=0, tiled=True) for part in partials]
        updated = []
        for matrix_now, gram in zip(current, full_grams):
            product_one = high_dot(matrix_now, gram)
            updated.append(
                NEWTON_A * matrix_now
                + NEWTON_B * product_one
                + NEWTON_C * high_dot(product_one, gram)
            )
        return updated

    return lax.fori_loop(0, NS_STEPS, iterate, current)


def by_images(
    latent,
    noise,
    real_bank,
    real_index,
    frozen_feat,
    frozen_proj,
    power_vec,
    conv_w,
    conv_mom,
    squeeze_w,
    squeeze_mom,
    excite_w,
    excite_mom,
    critic_w,
    critic_mom,
    vectors,
    vec_m,
    vec_v,
):
    gathered = (
        lax.all_gather(conv_w.astype(jnp.bfloat16), "dp", axis=0, tiled=True),
        lax.all_gather(squeeze_w.astype(jnp.bfloat16), "dp", axis=0, tiled=True),
        lax.all_gather(excite_w.astype(jnp.bfloat16), "dp", axis=0, tiled=True),
        lax.all_gather(critic_w.astype(jnp.bfloat16), "dp", axis=0, tiled=True),
    )
    conv_low, squeeze_low, excite_low, critic_low = gathered
    squeeze_full = squeeze_low.astype(jnp.float32)
    excite_full = excite_low.astype(jnp.float32)
    spectral_full, spectral_back = jax.vjp(
        partial(spectral_norm, power=power_vec), critic_low.astype(jnp.float32)
    )
    spectral = spectral_full.astype(jnp.bfloat16)
    micro_count, images, pixels = (noise.shape[0], noise.shape[1], noise.shape[2])
    widths = conv_low.shape[1]
    half_width = widths // 2
    proj_width = critic_low.shape[0]
    tokens = images * pixels
    pixel_count = tokens * lax.axis_size("dp")
    patches = micro_count * pixel_count
    noise_gain = vectors[:widths]
    bn_gain = vectors[widths : 2 * widths]
    bn_bias = vectors[2 * widths : 3 * widths]
    out_weight = vectors[3 * widths : 3 * widths + proj_width]
    out_bias = vectors[3 * widths + proj_width]
    generator = lax.axis_index("segment") == 0
    critic_side = jnp.logical_not(generator)
    pooled = jnp.mean(latent.astype(jnp.float32), axis=(2, 3))
    conv_acc = jnp.zeros(conv_low.shape, jnp.float32)
    squeeze_acc = jnp.zeros(squeeze_low.shape, jnp.float32)
    excite_acc = jnp.zeros(excite_low.shape, jnp.float32)
    spectral_acc = jnp.zeros(critic_low.shape, jnp.float32)
    vector_acc = jnp.zeros(vectors.shape, jnp.float32)
    loss_acc = jnp.zeros((), jnp.float32)
    for micro_step in range(micro_count):
        noise_now = noise[micro_step].reshape(-1)
        excitation, excite_back = jax.vjp(excite, pooled[micro_step], squeeze_full, excite_full)

        def gen_front():
            patches_in = columns(latent[micro_step])
            return (patches_in, low_dot(patches_in, conv_low) + noise_now[:, None] * noise_gain)

        patches_in, shifted = only_if(generator, gen_front)
        moments = lax.psum((jnp.sum(shifted, axis=0), jnp.sum(shifted * shifted, axis=0)), "dp")

        def gen_mid():
            centred, inv_std, normed = normalize(shifted, moments, pixel_count, bn_gain, bn_bias)
            gated = normed[:, :half_width] * jax.nn.sigmoid(normed[:, half_width:])
            fake_map = gated.reshape(images, pixels, half_width) * excitation[:, None, :]
            return fake_map.reshape(tokens, half_width).astype(jnp.bfloat16)

        fake_map = only_if(generator, gen_mid)
        arrived = shifted_2(fake_map, "segment", 1)

        def critic_work():
            real_map = real_bank[real_index[micro_step]].reshape(tokens, half_width)
            real_out = critic_pass(
                real_map,
                -1.0,
                patches,
                frozen_feat,
                frozen_proj,
                spectral,
                out_weight,
                out_bias,
                False,
            )
            fake_out = critic_pass(
                arrived,
                1.0,
                patches,
                frozen_feat,
                frozen_proj,
                spectral,
                out_weight,
                out_bias,
                True,
            )
            return (
                real_out[0] + fake_out[0],
                real_out[1] + fake_out[1],
                real_out[2] + fake_out[2],
                real_out[3] + fake_out[3],
                fake_out[4],
            )

        loss_part, dspec_part, dout_part, dbias_part, input_grad = only_if(critic_side, critic_work)
        returned = jax.tree.map(
            lambda part, own: part.astype(own.dtype),
            shifted_2(for_sending(input_grad), "segment", -1),
            input_grad,
        )

        def gen_back():
            dfake = -returned.astype(jnp.float32).reshape(images, pixels, half_width)
            centred, inv_std, normed = normalize(shifted, moments, pixel_count, bn_gain, bn_bias)
            opened = jax.nn.sigmoid(normed[:, half_width:])
            first_half = normed[:, :half_width]
            gated = (first_half * opened).reshape(images, pixels, half_width)
            unused, dsqueeze, dexcite = excite_back(jnp.sum(dfake * gated, axis=1))
            dgated = (dfake * excitation[:, None, :]).reshape(tokens, half_width)
            dnormed = jnp.concatenate(
                [dgated * opened, dgated * first_half * opened * (1.0 - opened)], axis=1
            )
            return (
                dnormed * bn_gain,
                centred,
                inv_std,
                dsqueeze,
                dexcite,
                jnp.sum(dnormed * centred, axis=0),
                jnp.sum(dnormed, axis=0),
            )

        dcentred, centred, inv_std, dsqueeze, dexcite, dgain, dbias = only_if(generator, gen_back)
        back_sums = lax.psum((jnp.sum(dcentred, axis=0), jnp.sum(dcentred * centred, axis=0)), "dp")

        def gen_grad():
            dshifted = inv_std * (
                dcentred - back_sums[0] / pixel_count - centred * back_sums[1] / pixel_count
            )
            return (dshifted.astype(jnp.bfloat16), jnp.sum(dshifted * noise_now[:, None], axis=0))

        dhidden, dnoise = only_if(generator, gen_grad)
        conv_acc = conv_acc + only_if(generator, lambda: low_dot(patches_in.T, dhidden))
        squeeze_acc = squeeze_acc + dsqueeze
        excite_acc = excite_acc + dexcite
        spectral_acc = spectral_acc + dspec_part
        vector_acc = vector_acc + jnp.concatenate(
            [dnoise, dgain, dbias, dout_part, dbias_part[None]]
        )
        loss_acc = loss_acc + loss_part
    critic_grad = spectral_back(spectral_acc)[0]
    conv_rows_sum, squeeze_rows, excite_rows, critic_rows = (
        lax.psum_scatter(conv_acc, "dp", scatter_dimension=0, tiled=True),
        lax.psum_scatter(squeeze_acc, "dp", scatter_dimension=0, tiled=True),
        lax.psum_scatter(excite_acc, "dp", scatter_dimension=0, tiled=True),
        lax.psum_scatter(critic_grad, "dp", scatter_dimension=0, tiled=True),
    )
    gradients = lax.psum((conv_rows_sum, squeeze_rows, excite_rows, critic_rows), "segment")
    vector_grad, loss_sum = lax.psum((vector_acc, loss_acc), ("segment", "dp"))
    weights = (conv_w, squeeze_w, excite_w, critic_w)
    new_moms = [
        MOMENTUM * old_mom + grad_now
        for old_mom, grad_now in zip((conv_mom, squeeze_mom, excite_mom, critic_mom), gradients)
    ]
    ortho = orthogonalize(new_moms)
    new_weights = [
        weight * (1.0 - MUON_RATE * DECAY) - MUON_RATE * step_dir
        for weight, step_dir in zip(weights, ortho)
    ]
    vec_m_new, vec_v_new, vectors_new = adam(vectors, vec_m, vec_v, vector_grad)
    return (
        loss_sum,
        new_moms[0],
        new_weights[0],
        new_moms[1],
        new_weights[1],
        new_moms[2],
        new_weights[2],
        new_moms[3],
        new_weights[3],
        vec_m_new,
        vec_v_new,
        vectors_new,
    )


def solution(mesh):
    placed = (
        P(None, "dp", None, None, None),
        P(None, "dp", None),
        P("dp", None, None),
        P(None, "dp"),
        P(),
        P(),
        P(),
        P("dp", None),
        P("dp", None),
        P("dp", None),
        P("dp", None),
        P("dp", None),
        P("dp", None),
        P("dp", None),
        P("dp", None),
        P(),
        P(),
        P(),
    )
    given = (
        P(),
        P("dp", None),
        P("dp", None),
        P("dp", None),
        P("dp", None),
        P("dp", None),
        P("dp", None),
        P("dp", None),
        P("dp", None),
        P(),
        P(),
        P(),
    )

    def step(latent, noise, *rest):
        n, sides = mesh.shape["dp"], mesh.shape["segment"]
        micros, images, edge = latent.shape[:3]
        fits = (
            n == 16
            and sides == 2
            and images == n
            and micros == 2
            and edge <= SUBLANES - 1
            and rest[5].shape[1] == 2 * n * sides * 16
        )
        plan = by_channels if fits else by_images
        return jax.shard_map(
            plan, mesh=mesh, in_specs=placed, out_specs=given, check_vma=False
        )(latent, noise, *rest)

    return step
```

```python
from functools import partial

import jax
import jax.numpy as jnp
from jax import lax
from jax.experimental import pallas as pl
from jax.experimental.pallas import tpu as pltpu
from jax.sharding import PartitionSpec as P

NS_STEPS = 5
STEP = 10


HIGHEST_PREC = lax.Precision.HIGHEST
HIGH_PREC = lax.Precision.HIGH
MESH = pl.DeviceIdType.MESH
NORM_EPS = 1e-05
NEWTON_A = 3.4445
NEWTON_B = -4.775
NEWTON_C = 2.0315
MOMENTUM = 0.95
MUON_RATE = 0.5
DECAY = 0.01
ADAM_RATE = 0.2
ADAM_BETA1 = 0.9
ADAM_BETA2 = 0.95
ADAM_EPS = 1e-08
LANES = 128
SUBLANES = 8
PLANE = 4
BLOCK = 256
FINE_BYTES = 64 * 1024
NO_COST = pl.CostEstimate(flops=0, bytes_accessed=0, transcendentals=0)
VMEM_BYTES = 56 * 1024 * 1024


def low_dot(left, right):
    return jnp.dot(left, right, preferred_element_type=jnp.float32)


def high_dot(left, right):
    return jnp.dot(left, right, precision=HIGHEST_PREC, preferred_element_type=jnp.float32)


def mid_dot(left, right):
    return jnp.dot(left, right, precision=HIGH_PREC, preferred_element_type=jnp.float32)


def silu_slope(value):
    opened = jax.nn.sigmoid(value)
    return opened * (1.0 + value * (1.0 - opened))


def adam(vectors, vec_m, vec_v, vector_grad):
    vec_m_new = ADAM_BETA1 * vec_m + (1.0 - ADAM_BETA1) * vector_grad
    vec_v_new = ADAM_BETA2 * vec_v + (1.0 - ADAM_BETA2) * vector_grad * vector_grad
    first_hat = vec_m_new / (1.0 - ADAM_BETA1**STEP)
    second_hat = vec_v_new / (1.0 - ADAM_BETA2**STEP)
    vectors_new = vectors * (1.0 - ADAM_RATE * DECAY) - ADAM_RATE * first_hat / (
        jnp.sqrt(second_hat) + ADAM_EPS
    )
    return vec_m_new, vec_v_new, vectors_new


def exchange(n, ident, plans, arrays, core=None):
    count = len(plans)
    kinds = [kind for kind, _ in plans]
    planes = n // PLANE

    def shape(kind, paired, x):
        if kind == "relay":
            lead, block = (planes, PLANE) + ((2,) if paired else ()), x.shape
        elif kind == "a2a":
            lead, block = ((n, 2) if paired else (n,)), x.shape[1:]
        elif kind == "plane":
            lead, block = (PLANE,), x.shape[1:]
        elif kind == "line":
            lead, block = (planes,), x.shape[1:]
        elif kind == "cross":
            lead, block = (), x.shape[:1] + x.shape[2:]
        else:
            lead, block = (), x.shape
        return jax.ShapeDtypeStruct(lead + block, x.dtype)

    outs = [shape(kind, paired, x) for (kind, paired), x in zip(plans, arrays)]
    direct = [a for a in range(count) if kinds[a] == "a2a"]
    near = [a for a in range(count) if kinds[a] in ("plane", "line")]
    single = [a for a in range(count) if kinds[a] in ("cross", "sib")]
    passing = [a for a in direct if plans[a][1]]
    parts = []
    for a in range(count):
        if kinds[a] == "relay":
            rows = arrays[a].shape[0]
            unit = 16 if arrays[a].dtype == jnp.bfloat16 else 8
            cut = -(-rows // (2 * unit)) * unit
            fine = arrays[a].size * arrays[a].dtype.itemsize > FINE_BYTES
            parts.append((a, 0, cut, 0, fine))
            if cut < rows:
                parts.append((a, cut, rows - cut, 1, fine))
    small = [p for p in range(len(parts)) if not parts[p][4]]
    large = [p for p in range(len(parts)) if parts[p][4]]

    coupled = [p for p in range(len(parts)) if plans[parts[p][0]][1]]

    def body(*refs):
        if core is None:
            run(*refs)
        else:
            pl.when(lax.axis_index("segment") == core)(partial(run, *refs))

    def run(*refs):
        ins, results = refs[:count], refs[count : 2 * count]
        (send, recv, pass_send, pass_recv, here, up_send, z_send, z_recv, first_send, first_recv,
         second_send, second_recv, core_send, core_recv, part_here) = refs[2 * count :]
        me, side = lax.axis_index("dp"), lax.axis_index("segment")
        other = 1 - side
        z, spot = me // PLANE, me % PLANE
        beside = (spot + 1 - 2 * (spot % 2), (spot + 2) % PLANE)
        across = PLANE - 1 - spot
        barrier = pltpu.get_barrier_semaphore()

        def greet(where):
            pl.semaphore_signal(barrier, inc=1, device_id=where, device_id_type=MESH)

        greeted = 0
        if direct or near:

            @pl.loop(1, n)
            def _(k):
                greet({"dp": lax.rem(me + k, n)})

            greeted += n - 1
        elif parts:

            @pl.loop(1, planes)
            def _(k):
                greet({"dp": lax.rem(me + k * PLANE, n)})

            for spot_now in beside:
                greet({"dp": z * PLANE + spot_now})
            greeted += planes + 1
        if passing or single or coupled:
            greet({"segment": other})
            greeted += 1
        pl.semaphore_wait(barrier, greeted)

        def remote(src, dst, send_sem, recv_sem, where):
            return pltpu.make_async_remote_copy(
                src_ref=src,
                dst_ref=dst,
                send_sem=send_sem,
                recv_sem=recv_sem,
                device_id=where,
                device_id_type=MESH,
            )

        every = range(len(parts))

        def cell(p, plane, spot_now):
            a, first, rows = parts[p][:3]
            if p in coupled:
                return results[a].at[plane, spot_now, side, pl.ds(first, rows)]
            return results[a].at[plane, spot_now, pl.ds(first, rows)]

        def column(p, spot_now, of_side):
            a, first, rows = parts[p][:3]
            if p in coupled:
                return results[a].at[:, spot_now, of_side, pl.ds(first, rows)]
            return results[a].at[:, spot_now, pl.ds(first, rows)]

        def mine(p):
            a, first, rows = parts[p][:3]
            return ins[a].at[pl.ds(first, rows)]

        def first_spot(p):
            return beside[parts[p][3]]

        def second_spot(p):
            return beside[1 - parts[p][3]]

        def along(p, k):
            chip = lax.rem(z + k, planes) * PLANE + spot
            return remote(mine(p), cell(p, z, spot), z_send.at[p, k], z_recv.at[p, z], {"dp": chip})

        def chain(p, plane, up, src=None):
            held = cell(p, plane, spot)
            return remote(
                held if src is None else src,
                held,
                (up_send if up else z_send).at[p, plane],
                z_recv.at[p, plane],
                {"dp": me + PLANE if up else me - PLANE},
            )

        def from_plane(p, plane):
            held = cell(p, plane, spot)
            return remote(held, held, z_send.at[p, 0], z_recv.at[p, plane], {"dp": me})

        def to_first(p, plane, src=None, of_spot=None):
            held = cell(p, plane, spot if of_spot is None else of_spot)
            return remote(
                held if src is None else src,
                held,
                first_send.at[p, plane],
                first_recv.at[p, plane],
                {"dp": z * PLANE + first_spot(p)},
            )

        def to_second(p, plane, src=None, of_spot=None, shift=0):
            held = cell(p, plane, spot if of_spot is None else of_spot)
            return remote(
                held if src is None else src,
                held,
                second_send.at[p, plane + shift],
                second_recv.at[p, plane + shift],
                {"dp": z * PLANE + second_spot(p)},
            )

        def column_to_second(p, spot_now):
            held = column(p, spot_now, side)
            return remote(
                held,
                held,
                second_send.at[p, planes],
                second_recv.at[p, planes],
                {"dp": z * PLANE + second_spot(p)},
            )

        def to_core(p, spot_now, of_side):
            held = column(p, spot_now, of_side)
            return remote(
                held, held, core_send.at[p, spot_now], core_recv.at[p, spot_now], {"segment": other}
            )

        def keep(p):
            return pltpu.make_async_copy(mine(p), cell(p, z, spot), part_here.at[p])

        for p in every:
            to_first(p, z, mine(p)).start()
            to_second(p, z, mine(p)).start()
            if p in small:
                for k in range(1, planes):
                    along(p, k).start()
            else:

                @pl.when(z < planes - 1)
                def _():
                    chain(p, z, True, mine(p)).start()

                @pl.when(z > 0)
                def _():
                    chain(p, z, False, mine(p)).start()

            keep(p).start()

        def peer_of(a, k):
            if kinds[a] == "plane":
                return z * PLANE + lax.rem(spot + k, PLANE)
            if kinds[a] == "line":
                return lax.rem(z + k, planes) * PLANE + spot
            return lax.rem(me + lax.rem(k + 6, n - 1) + 1, n)

        def number(a, chip):
            if kinds[a] == "plane":
                return chip % PLANE
            if kinds[a] == "line":
                return chip // PLANE
            return chip

        def source(a, chip):
            return ins[a].at[number(a, chip)]

        def slot(a, chip, of_side):
            if plans[a][1]:
                return results[a].at[chip, of_side]
            return results[a].at[number(a, chip)]

        def outgoing(a, k):
            peer = peer_of(a, k)
            return remote(
                source(a, peer),
                slot(a, me, side),
                send.at[a, k],
                recv.at[a, number(a, me)],
                {"dp": peer},
            )

        def incoming(a, chip):
            return remote(
                source(a, chip), slot(a, chip, side), send.at[a, 0], recv.at[a, number(a, chip)], {"dp": chip}
            )

        def passed(a, src, chip, of_side):
            return remote(
                src,
                slot(a, chip, of_side),
                pass_send.at[a, chip],
                pass_recv.at[a, chip],
                {"segment": other},
            )

        def crossing(a):
            return remote(
                ins[a].at[:, other] if kinds[a] == "cross" else ins[a],
                results[a],
                pass_send.at[a, 0],
                pass_recv.at[a, 0],
                {"segment": other},
            )

        def own(a):
            return pltpu.make_async_copy(source(a, me), slot(a, me, side), here.at[a])

        def spread(p, plane):
            from_plane(p, plane).wait_recv()
            to_first(p, plane).start()
            to_second(p, plane).start()

        if small:

            @pl.loop(1, planes)
            def _(k):
                for p in small:
                    spread(p, lax.rem(z + planes - k, planes))

        for d in range(1, planes) if large else ():

            @pl.when(z - d >= 0)
            def _():
                for p in large:
                    spread(p, z - d)

                    @pl.when(z < planes - 1)
                    def _():
                        chain(p, z - d, True).start()

            @pl.when(z + d < planes)
            def _():
                for p in large:
                    spread(p, z + d)

                    @pl.when(z > 0)
                    def _():
                        chain(p, z + d, False).start()

        for p in every:
            keep(p).wait()
            if p in coupled:
                to_core(p, spot, side).start()
        if large:

            @pl.loop(0, planes)
            def _(k):
                plane = lax.rem(z + k, planes)
                for p in large:
                    to_first(p, plane, of_spot=first_spot(p)).wait_recv()
                    to_second(p, plane, of_spot=first_spot(p), shift=planes).start()

        if direct:

            @pl.loop(1, n)
            def _(k):
                for a in direct:
                    outgoing(a, k).start()

        for a in near:
            for k in range(1, outs[a].shape[0]):
                outgoing(a, k).start()
        for a in direct + near:
            own(a).start()
        for a in passing:
            passed(a, source(a, me), me, side).start()
        for a in single:
            crossing(a).start()

        for p in every:
            if p in small:

                @pl.loop(0, planes)
                def _(plane):
                    to_first(p, plane, of_spot=first_spot(p)).wait_recv()

                column_to_second(p, first_spot(p)).start()
            if p in coupled:
                to_core(p, first_spot(p), side).start()
        for p in every:

            @pl.loop(0, planes)
            def _(plane):
                to_second(p, plane, of_spot=second_spot(p)).wait_recv()

            if p in coupled:
                to_core(p, second_spot(p), side).start()
        for p in every:
            if p in small:
                column_to_second(p, across).wait_recv()
            else:

                @pl.loop(0, planes)
                def _(plane):
                    to_second(p, plane, of_spot=across, shift=planes).wait_recv()

            if p in coupled:
                to_core(p, across, side).start()

        if direct:

            @pl.loop(1, n)
            def _(k):
                chip = lax.rem(me + n - lax.rem(k + 6, n - 1) - 1, n)
                for a in direct:
                    incoming(a, chip).wait_recv()
                    if plans[a][1]:
                        passed(a, slot(a, chip, side), chip, side).start()

        for a in near:
            for k in range(1, outs[a].shape[0]):
                incoming(a, peer_of(a, k)).wait_recv()
                outgoing(a, k).wait_send()
        for a in direct + near:
            own(a).wait()
        if direct:

            @pl.loop(1, n)
            def _(k):
                for a in direct:
                    outgoing(a, k).wait_send()

        if passing:

            @pl.loop(0, n)
            def _(k):
                for a in passing:
                    passed(a, slot(a, k, side), k, side).wait_send()
                    passed(a, slot(a, k, other), k, other).wait_recv()

        for a in single:
            crossing(a).wait()

        for p in every:
            if p in small:
                for k in range(1, planes):
                    along(p, k).wait_send()
                column_to_second(p, first_spot(p)).wait_send()
            else:
                for d in range(planes):

                    @pl.when(jnp.logical_and(z - d >= 0, z < planes - 1))
                    def _():
                        chain(p, z - d, True).wait_send()

                    @pl.when(jnp.logical_and(z + d < planes, z > 0))
                    def _():
                        chain(p, z + d, False).wait_send()

            @pl.loop(0, planes)
            def _(plane):
                to_first(p, plane).wait_send()
                to_second(p, plane).wait_send()
                if p in large:
                    to_second(p, plane, of_spot=first_spot(p), shift=planes).wait_send()

            if p in coupled:

                @pl.loop(0, PLANE)
                def _(spot_now):
                    to_core(p, spot_now, side).wait_send()
                    to_core(p, spot_now, other).wait_recv()

    anywhere = pl.BlockSpec(memory_space=pl.ANY)
    relays = max(len(parts), 1)
    found = pl.pallas_call(
        body,
        out_shape=outs,
        in_specs=[anywhere] * count,
        out_specs=[anywhere] * count,
        scratch_shapes=[pltpu.SemaphoreType.DMA((count, n))] * 4
        + [pltpu.SemaphoreType.DMA((count,))]
        + [pltpu.SemaphoreType.DMA((relays, 2 * planes))] * 7
        + [pltpu.SemaphoreType.DMA((relays, PLANE))] * 2
        + [pltpu.SemaphoreType.DMA((relays,))],
        compiler_params=pltpu.CompilerParams(collective_id=ident, has_side_effects=True),
        cost_estimate=NO_COST,
        name=f"exchange_{ident}",
    )(*arrays)
    return [
        x.reshape((n,) + x.shape[2:]) if kind == "relay" else x for kind, x in zip(kinds, found)
    ]


def share(ident, of_first, *of_second):
    arrays = (of_first, *of_second)
    count = len(arrays)

    def body(*refs):
        ins, results = refs[:count], refs[count : 2 * count]
        send, recv = refs[2 * count :]
        side = lax.axis_index("segment")
        other = 1 - side
        barrier = pltpu.get_barrier_semaphore()
        pl.semaphore_signal(barrier, inc=1, device_id={"segment": other}, device_id_type=MESH)
        pl.semaphore_wait(barrier, 1)

        def over(k):
            return pltpu.make_async_remote_copy(
                src_ref=ins[k],
                dst_ref=results[k],
                send_sem=send.at[k],
                recv_sem=recv.at[k],
                device_id={"segment": other},
                device_id_type=MESH,
            )

        for core, sent, found in ((0, [0], range(1, count)), (1, range(1, count), [0])):

            @pl.when(side == core)
            def _():
                for k in sent:
                    over(k).start()
                for k in found:
                    over(k).wait_recv()
                for k in sent:
                    over(k).wait_send()

    anywhere = pl.BlockSpec(memory_space=pl.ANY)
    arrived = pl.pallas_call(
        body,
        out_shape=[jax.ShapeDtypeStruct(x.shape, x.dtype) for x in arrays],
        in_specs=[anywhere] * count,
        out_specs=[anywhere] * count,
        scratch_shapes=[pltpu.SemaphoreType.DMA((count,))] * 2,
        compiler_params=pltpu.CompilerParams(collective_id=ident, has_side_effects=True),
        cost_estimate=NO_COST,
        name="share",
    )(*arrays)
    is_first = lax.axis_index("segment") == 0
    return [
        jnp.where(is_first == (k == 0), own, found) for k, (own, found) in enumerate(zip(arrays, arrived))
    ]


def local_call(kernel, name, out_shape, scratch, arguments, specs=None):
    return pl.pallas_call(
        kernel,
        out_shape=out_shape,
        in_specs=specs or [pl.BlockSpec(memory_space=pltpu.VMEM)] * len(arguments),
        scratch_shapes=scratch,
        compiler_params=pltpu.CompilerParams(vmem_limit_bytes=VMEM_BYTES),
        cost_estimate=NO_COST,
        name=name,
    )(*arguments)


def split_two(value):
    top = value.astype(jnp.bfloat16)
    return top, (value - top.astype(jnp.float32)).astype(jnp.bfloat16)


def split_three(value):
    top = value.astype(jnp.bfloat16)
    rest = value - top.astype(jnp.float32)
    middle = rest.astype(jnp.bfloat16)
    bottom = (rest - middle.astype(jnp.float32)).astype(jnp.bfloat16)
    return top, middle, bottom


def exact_dot(value, low):
    rows = value.shape[0]
    product = low_dot(jnp.concatenate(split_three(value), axis=0), low)
    return product[:rows] + product[rows : 2 * rows] + product[2 * rows :]


def lane_of(shape):
    return lax.broadcasted_iota(jnp.int32, shape, len(shape) - 1)


def fold(value):
    axis = value.ndim - 1
    value = value + pltpu.roll(value, 64, axis)
    return value + pltpu.roll(value, 32, axis)


def turn(value, steps):
    steps = steps % LANES
    return pltpu.roll(value, steps, value.ndim - 1) if steps else value


def turn_back(value, steps):
    return pltpu.roll(value, lax.rem(2 * LANES - steps, LANES), value.ndim - 1)


def row_pieces(rows, groups, taps, channels):
    depth = rows // groups
    pieces = []
    for chip in range(taps * channels // rows):
        for group in range(groups):
            first = chip * rows + group * depth
            at = first
            while at < first + depth:
                tap, channel = divmod(at, channels)
                take = min(first + depth - at, channels - channel)
                pieces.append((chip, group, at - first, tap, channel, take))
                at += take
    return pieces


def shift_rows(value, side, steps):
    parts = []
    empty = jnp.zeros((1,) + value.shape[1:], value.dtype)
    for first in range(0, value.shape[0], side):
        block = value[first : first + side]
        parts += [empty, block[:-1]] if steps > 0 else [block[1:], empty]
    return jnp.concatenate(parts, axis=0)


def per_micro(values, side):
    return jnp.concatenate(
        [jnp.broadcast_to(v[None], (side, SUBLANES, LANES)) for v in values], axis=0
    )


def pack_kernel(latent, noise, conv, squeeze, excite, critic, squeeze_mom, excite_mom, critic_mom,
                block, conv_out, noise_out, moms, rows_f):
    side = lax.axis_index("segment")
    bf16 = jnp.bfloat16
    micros, _, edge, _, channels = latent.shape
    half_in = channels // 2
    rows_f[...] = jnp.zeros(rows_f.shape, jnp.float32)
    for m in range(micros):
        for i in range(edge):
            at = (m * edge + i) * SUBLANES
            rows_f[at : at + edge, :] = latent[m, 0, i].astype(jnp.float32)
    spread = rows_f.shape[0]
    block[:spread, :] = jnp.where(side == 0, rows_f[:, :half_in], rows_f[:, half_in:]).astype(bf16)
    at = spread
    for weight in (squeeze, excite, critic):
        rows = weight.shape[0] // 2
        block[at : at + rows, :] = jnp.where(side == 0, weight[:rows], weight[rows:]).astype(bf16)
        at += rows
    at = 0
    for mom in (squeeze_mom, excite_mom, critic_mom):
        moms[at : at + mom.shape[0], :] = mom[...]
        at += mom.shape[0]

    chips, depth, _ = conv_out.shape
    widths = conv.shape[1]
    half = widths // 2
    group = half // chips
    lane = lane_of((depth, LANES))
    @pl.loop(0, half // LANES)
    def _(b):
        low_cols = pl.ds(pl.multiple_of(b * LANES, LANES), LANES)
        high_cols = pl.ds(pl.multiple_of(half + b * LANES, LANES), LANES)
        for c in range(LANES // group):
            value = jnp.zeros((depth, LANES), jnp.float32)
            for q in range(4):
                rows = slice(q * depth, (q + 1) * depth)
                first = conv[rows, low_cols]
                second = conv[rows, high_cols]
                to = q * group
                steps = to - c * group + LANES - side * (group // 2)
                low = pltpu.roll(first, lax.rem(steps, LANES), 1)
                high = pltpu.roll(second, lax.rem(steps + group // 2, LANES), 1)
                both = jnp.where(lane % group < group // 2, low, high)
                value = jnp.where(lane // group == q, both, value)
            conv_out[b * (LANES // group) + c] = value.astype(bf16)

    pixels = noise.shape[2]
    parts = jnp.concatenate(
        [p.astype(jnp.float32) for p in split_three(noise[:, 0])]
        + [jnp.zeros((SUBLANES - 3 * micros, pixels), jnp.float32)],
        axis=0,
    ).astype(bf16)
    pixel = lax.broadcasted_iota(jnp.int32, (pixels, LANES), 0)
    spot = lane_of((pixels, LANES))
    within = spot % (4 * edge)
    lane_row = lane_of((1, LANES))
    lines = []
    for j in range(edge):
        wanted = 4 * edge * (within // 4) + 2 * edge * ((within % 4) // 2) + 2 * j + within % 2
        chosen = (pixel == wanted).astype(jnp.float32).astype(bf16)
        found = low_dot(parts, chosen)
        line = jnp.zeros((1, LANES), jnp.float32)
        for m in range(micros):
            total = found[m : m + 1] + found[micros + m : micros + m + 1]
            total = total + found[2 * micros + m : 2 * micros + m + 1]
            line = jnp.where(lane_row // (4 * edge) == m, total, line)
        lines.append(line)
    noise_out[...] = jnp.concatenate(
        lines + [jnp.zeros((SUBLANES - edge, LANES), jnp.float32)], axis=0
    )


def pack(n, latent, noise, conv_w, squeeze_w, excite_w, critic_w, squeeze_mom, excite_mom, critic_mom):
    micros, _, edge, _, channels = latent.shape
    spread = micros * edge * SUBLANES
    rows = spread + (squeeze_w.shape[0] + excite_w.shape[0] + critic_w.shape[0]) // 2
    return local_call(
        pack_kernel,
        "pack",
        [
            jax.ShapeDtypeStruct((rows, channels // 2), jnp.bfloat16),
            jax.ShapeDtypeStruct((n, conv_w.shape[0] // 4, LANES), jnp.bfloat16),
            jax.ShapeDtypeStruct((SUBLANES, LANES), jnp.float32),
            jax.ShapeDtypeStruct((2 * (rows - spread), squeeze_w.shape[1]), jnp.float32),
        ],
        [pltpu.VMEM((spread, channels), jnp.float32)],
        [latent, noise, conv_w, squeeze_w, excite_w, critic_w, squeeze_mom, excite_mom, critic_mom],
    )


def own_columns(row_low, row_high, at, own):
    lane = lane_of((1, LANES))
    low = turn_back(row_low, at)
    high = turn(turn_back(row_high, at), own)
    value = jnp.where(lane < own, low, jnp.where(lane < 2 * own, high, 0.0))
    value = value + turn(value, 2 * own)
    return value + turn(value, 4 * own)


def front_kernel(side, micros, pixel_count, all_lat, conv, noise, vectors,
                 fake, xn, stats, opened_out, z1_out, pooled_out, consts, noise_rows,
                 weight, z, h, gate8):
    images = all_lat.shape[0]
    half_in = all_lat.shape[3]
    channels = 2 * half_in
    spread = micros * side * SUBLANES
    depth = conv.shape[1]
    taps = weight.shape[1] // LANES
    bf16, f32 = jnp.bfloat16, jnp.float32
    chip, core = lax.axis_index("dp"), lax.axis_index("segment")
    own = 16
    widths_rows = 2 * half_in // LANES
    at = 2 * own * lax.rem(chip, PLANE) + own * core
    base = chip // PLANE
    for k in range(3):
        consts[k : k + 1, :] = own_columns(
            vectors[pl.ds(k * widths_rows + base, 1), :],
            vectors[pl.ds(k * widths_rows + widths_rows // 2 + base, 1), :],
            at,
            own,
        )
    consts[3:, :] = jnp.zeros((SUBLANES - 3, LANES), f32)

    group = lane_of((depth, LANES)) // 32
    masks = [(group == g).astype(f32).astype(bf16) for g in range(4)]
    for owner, g, first, tap, channel, take in row_pieces(4 * depth, 4, taps, channels):
        weight[channel : channel + take, tap * LANES : (tap + 1) * LANES] = (
            conv[owner, first : first + take, :] * masks[g][:take]
        )
    lines = micros * side
    step = 4

    @pl.loop(0, images // step)
    def _(k):
        here = pl.ds(k * step, step)
        left = all_lat[here, 0, :spread].reshape(step * spread, half_in)
        right = all_lat[here, 1, :spread].reshape(step * spread, half_in)
        for tap in range(0, taps, 2):
            cols = slice(tap * LANES, min(tap + 2, taps) * LANES)
            product = low_dot(left, weight[:half_in, cols]) + low_dot(right, weight[half_in:, cols])
            for k in range(product.shape[1] // LANES):
                value = fold(product[:, k * LANES : (k + 1) * LANES])
                z[tap + k, here] = value.reshape(step, lines, SUBLANES, LANES)

    from_lane = lax.broadcasted_iota(jnp.int32, (LANES, lines * LANES), 0)
    to_lane = lane_of((LANES, lines * LANES))
    chosen = from_lane == 4 * (to_lane // LANES) + (to_lane % LANES) // 32
    wide = exact_dot(
        noise[:, 0].reshape(images * SUBLANES, LANES), chosen.astype(f32).astype(bf16)
    )
    for line in range(lines):
        noise_rows[:, line] = wide[:, line * LANES : (line + 1) * LANES].reshape(images, SUBLANES, LANES)

    shape3 = (lines, SUBLANES, LANES)
    lane = lane_of(shape3)
    row_first = (lane // 64) == 0
    col_first = ((lane // 32) % 2) == 0
    inside = lax.broadcasted_iota(jnp.int32, shape3, 1) < side
    first_half = (lane % 32) < 16
    gain_noise = consts[0:1, :][None]
    gain = consts[1:2, :][None]
    bias = consts[2:3, :][None]
    zero = jnp.zeros((SUBLANES, LANES), f32)

    def place(img, carry):
        lines_of = []
        for ky in range(3):
            z0, z1, z2 = z[3 * ky, img], z[3 * ky + 1, img], z[3 * ky + 2, img]
            lines_of.append(
                z1
                + jnp.where(col_first, pltpu.roll(z0, 1, 1), z0)
                + jnp.where(col_first, z2, pltpu.roll(z2, SUBLANES - 1, 1))
            )
        x0, x1, x2 = lines_of
        value = (
            x1
            + jnp.where(row_first, shift_rows(x0, side, 1), x0)
            + jnp.where(row_first, x2, shift_rows(x2, side, -1))
        )
        value = value + noise_rows[img] * gain_noise
        value = jnp.where(inside, value, 0.0)
        h[img] = value
        new = []
        for m in range(micros):
            part = value[m * side : (m + 1) * side]
            new.append(carry[2 * m] + jnp.sum(part, axis=0))
            new.append(carry[2 * m + 1] + jnp.sum(part * part, axis=0))
        return tuple(new)

    sums = lax.fori_loop(0, images, place, (zero,) * (2 * micros))
    means, stds = [], []
    for m in range(micros):
        mean_now = jnp.sum(fold(sums[2 * m]), axis=0, keepdims=True) / pixel_count
        square = jnp.sum(fold(sums[2 * m + 1]), axis=0, keepdims=True) / pixel_count
        means.append(mean_now)
        stds.append(lax.rsqrt(square - mean_now * mean_now + NORM_EPS))
        stats[m : m + 1, :] = stds[m]
    mean12, std12 = per_micro(means, side), per_micro(stds, side)

    count = images * micros
    rows_map = side * SUBLANES
    owner = lax.broadcasted_iota(jnp.int32, (count, count * rows_map), 1) // rows_map
    pool = (owner == lax.broadcasted_iota(jnp.int32, owner.shape, 0)).astype(f32).astype(bf16)
    area = 1.0 / (side * side)
    pooled = [
        low_dot(pool, all_lat[:, p, :spread].reshape(images * spread, half_in)) * area
        for p in range(2)
    ]
    rows_squeeze = channels // images // 2
    rows_excite = half_in // images // 2
    squeeze = all_lat[:, :, spread : spread + rows_squeeze].reshape(channels, half_in)
    excite = all_lat[:, :, spread + rows_squeeze : spread + rows_squeeze + rows_excite]
    excite = excite.reshape(half_in, half_in)
    z1 = exact_dot(pooled[0], squeeze[:half_in]) + exact_dot(pooled[1], squeeze[half_in:])
    z1_out[...] = z1
    pooled_out[:, :half_in] = pooled[0]
    pooled_out[:, half_in:] = pooled[1]
    wide = jax.nn.sigmoid(exact_dot(z1 * jax.nn.sigmoid(z1), excite))
    opened = wide[:, :LANES]
    for b in range(1, half_in // LANES):
        opened = jnp.where(base == b, wide[:, b * LANES : (b + 1) * LANES], opened)
    opened = jnp.where(lane_of(opened.shape) < own, turn_back(opened, at), 0.0)
    for steps in (own, 2 * own, 4 * own):
        opened = opened + turn(opened, steps)
    opened_out[...] = opened
    gate8[...] = jnp.broadcast_to(opened[:, None, :], gate8.shape)

    @pl.loop(0, images)
    def _(img):
        centred = (h[img] - mean12) * std12
        xn[img] = centred
        y = centred * gain + bias
        gated = y * turn(jax.nn.sigmoid(y), -16)
        pieces = []
        for m in range(micros):
            pieces.append(gated[m * side : (m + 1) * side] * gate8[img * micros + m][None])
        packed = jnp.where(first_half[:side], pieces[0], turn(pieces[1], 16))
        fake[img] = packed.reshape(side * SUBLANES, LANES).astype(bf16)


def front(side, micros, pixel_count, lat, conv, noise, vectors):
    images, _, _, half_in = lat.shape
    lines = micros * side
    count = images * micros
    f32 = jnp.float32
    return local_call(
        partial(front_kernel, side, micros, pixel_count),
        "front",
        [
            jax.ShapeDtypeStruct((images, side * SUBLANES, LANES), jnp.bfloat16),
            jax.ShapeDtypeStruct((images, lines, SUBLANES, LANES), f32),
            jax.ShapeDtypeStruct((SUBLANES, LANES), f32),
            jax.ShapeDtypeStruct((count, LANES), f32),
            jax.ShapeDtypeStruct((count, half_in), f32),
            jax.ShapeDtypeStruct((count, 2 * half_in), f32),
            jax.ShapeDtypeStruct((SUBLANES, LANES), f32),
            jax.ShapeDtypeStruct((images, lines, SUBLANES, LANES), f32),
        ],
        [
            pltpu.VMEM((2 * half_in, 9 * LANES), jnp.bfloat16),
            pltpu.VMEM((9, images, lines, SUBLANES, LANES), f32),
            pltpu.VMEM((images, lines, SUBLANES, LANES), f32),
            pltpu.VMEM((count, SUBLANES, LANES), f32),
        ],
        [lat, conv, noise, vectors],
    )


def critic_kernel(side, patches, spread, arrived, lat, real_bank, feat, proj, power, vectors, chosen,
                  dfake, dspec, tail, column_v, column_t, row_w, maps, dmaps, weight_low, real_map, sem):
    bf16 = jnp.bfloat16
    core = lax.axis_index("segment")
    chips, _, rows_map, _ = arrived.shape
    size = feat.shape[0]
    at = 6 * size // LANES
    head = jnp.concatenate([vectors[at + k : at + k + 1, :] for k in range(size // LANES)], axis=1)
    offset = vectors[at + size // LANES : at + size // LANES + 1, 0:1]
    rows_before = spread + size // chips + size // chips // 2
    load = pltpu.make_async_copy(
        lat.at[:, :, pl.ds(rows_before, size // chips // 2)], weight_low, sem.at[0]
    )
    load_real = pltpu.make_async_copy(real_bank.at[chosen[core, 0]], real_map, sem.at[1])
    load.start()
    load_real.start()

    lane = lane_of((rows_map, LANES))
    per_block = LANES // 32

    @pl.loop(0, size // LANES)
    def _(b):
        both = []
        for c in range(per_block):
            low = turn_back(arrived[b * per_block + c, 0].astype(jnp.float32), 16 * core)
            high = turn_back(arrived[b * per_block + c, 1].astype(jnp.float32), 16 * core - 16)
            both.append(jnp.where(lane % 32 < 16, low, high))
        cols = pl.ds(pl.multiple_of(b * LANES, LANES), LANES)
        for q in range(4):
            value = turn(both[0], -32 * q)
            for c in range(1, per_block):
                value = jnp.where(lane // 32 == c, turn(both[c], 32 * (c - q)), value)
            maps[q * rows_map : (q + 1) * rows_map, cols] = value.astype(bf16)

    fakes = 4 * rows_map
    load_real.wait()
    maps[fakes:, :] = real_map[...]
    load.wait()
    weight = weight_low[...].reshape(size, size).astype(jnp.float32)
    product = jnp.sum(weight * power[...], axis=1, keepdims=True)
    length = lax.rsqrt(jnp.sum(product * product))
    vec = product * length
    back = jnp.sum(weight * vec, axis=0, keepdims=True)
    sigma = jnp.sqrt(jnp.sum(back * back))
    unit = back / sigma
    turned = jnp.sum(weight * unit, axis=1, keepdims=True)
    turned = (turned - vec * jnp.sum(turned * vec)) * length
    column_v[...] = vec
    column_t[...] = turned
    row_w[...] = jnp.broadcast_to(unit, row_w.shape)
    spectral = (weight / sigma).astype(bf16)
    rows = maps.shape[0]
    pre_act = low_dot(maps[...], feat[...])
    features = (pre_act * jax.nn.sigmoid(pre_act)).astype(bf16)
    projected = low_dot(features, proj[...]).astype(bf16)
    critic_act = low_dot(projected, spectral)
    opened = jax.nn.sigmoid(critic_act)
    activated = critic_act * opened
    logits = jnp.sum(activated * head, axis=1, keepdims=True) + offset
    row = lax.broadcasted_iota(jnp.int32, (rows, 1), 0)
    sign = jnp.where(row < fakes, 1.0, -1.0)
    valid = jnp.logical_or(row >= fakes, (row % SUBLANES) < side)
    margin = 1.0 + sign * logits
    soft = jnp.maximum(margin, 0.0) + jnp.log1p(jnp.exp(-jnp.abs(margin)))
    loss = jnp.sum(jnp.where(valid, soft, 0.0))
    dlogit = jnp.where(valid, sign * jax.nn.sigmoid(margin), 0.0) / patches
    slope = opened * (1.0 + critic_act * (1.0 - opened))
    dact = (dlogit * head * slope).astype(bf16)
    found = lax.dot_general(
        projected, dact, (((0,), (0,)), ((), ())), preferred_element_type=jnp.float32
    )
    dspec[...] = found.reshape(dspec.shape)
    dhead = jnp.sum(dlogit * activated, axis=0, keepdims=True)
    lane_row = lane_of((1, LANES))
    last = jnp.where(lane_row == 0, jnp.sum(dlogit), jnp.where(lane_row == 1, loss, 0.0))
    pieces = [dhead[:, k * LANES : (k + 1) * LANES] for k in range(size // LANES)] + [last]
    tail[...] = jnp.concatenate(
        pieces + [jnp.zeros((SUBLANES - len(pieces), LANES), jnp.float32)], axis=0
    )
    turned_dims = (((1,), (1,)), ((), ()))
    dproj = lax.dot_general(
        dact[:fakes], spectral, turned_dims, preferred_element_type=jnp.float32
    ).astype(bf16)
    dpre = lax.dot_general(dproj, proj[...], turned_dims, preferred_element_type=jnp.float32)
    dpre = (dpre * silu_slope(pre_act[:fakes])).astype(bf16)
    dmaps[...] = lax.dot_general(dpre, feat[...], turned_dims, preferred_element_type=jnp.float32)

    @pl.loop(0, size // LANES)
    def _(b):
        cols = pl.ds(pl.multiple_of(b * LANES, LANES), LANES)
        parts = [dmaps[q * rows_map : (q + 1) * rows_map, cols] for q in range(4)]
        for c in range(per_block):
            value = turn(parts[0], -32 * c)
            for q in range(1, 4):
                value = jnp.where(lane // 32 == q, turn(parts[q], 32 * (q - c)), value)
            dfake[b * per_block + c] = value.astype(bf16)


def critic_step(side, patches, spread, arrived, lat, real_bank, feat, proj, power, vectors, chosen):
    f32 = jnp.float32
    chips, _, rows_map, _ = arrived.shape
    size = feat.shape[0]
    vmem = pl.BlockSpec(memory_space=pltpu.VMEM)
    smem = pl.BlockSpec(memory_space=pltpu.SMEM)
    anywhere = pl.BlockSpec(memory_space=pl.ANY)
    return local_call(
        partial(critic_kernel, side, patches, spread),
        "critic_step",
        [
            jax.ShapeDtypeStruct((chips, rows_map, LANES), jnp.bfloat16),
            jax.ShapeDtypeStruct((chips, 2, size // chips // 2, size), f32),
            jax.ShapeDtypeStruct((SUBLANES, LANES), f32),
            jax.ShapeDtypeStruct((size, 1), f32),
            jax.ShapeDtypeStruct((size, 1), f32),
            jax.ShapeDtypeStruct((SUBLANES, size), f32),
        ],
        [
            pltpu.VMEM((4 * rows_map + real_bank.shape[1], size), jnp.bfloat16),
            pltpu.VMEM((4 * rows_map, size), f32),
            pltpu.VMEM((chips, 2, size // chips // 2, size), jnp.bfloat16),
            pltpu.VMEM(real_bank.shape[1:], jnp.bfloat16),
            pltpu.SemaphoreType.DMA((2,)),
        ],
        [arrived, lat, real_bank, feat, proj, power, vectors, chosen],
        [vmem, anywhere, anywhere] + [vmem] * 4 + [smem],
    )


def back_kernel(side, micros, pixel_count, grads, xn, lat, noise_rows, consts, stats, opened, tail,
                dspec_own, dspec_other, dconv, block, dspec, dy, packed, product, gate8, dze, all_lat, sem):
    images = all_lat.shape[0]
    half_in = all_lat.shape[3]
    channels = 2 * half_in
    lines = micros * side
    spread = lines * SUBLANES
    load = pltpu.make_async_copy(lat.at[:, :, pl.ds(0, spread)], all_lat, sem.at[0])
    load.start()
    bf16 = jnp.bfloat16
    shape3 = (lines, SUBLANES, LANES)
    lane = lane_of(shape3)
    row_first = (lane // 64) == 0
    col_first = ((lane // 32) % 2) == 0
    first_half = (lane % 32) < 16
    inside = lax.broadcasted_iota(jnp.int32, shape3, 1) < side
    gain = consts[1:2, :][None]
    bias = consts[2:3, :][None]
    zero = jnp.zeros((SUBLANES, LANES), jnp.float32)
    core = lax.axis_index("segment")
    second = core == 1
    gate8[...] = jnp.broadcast_to(opened[...][:, None, :], gate8.shape)
    for plane in range(images // PLANE):
        for spot in range(PLANE):
            k = plane * PLANE + spot
            dspec[spot, plane] = jnp.where(second, dspec_own[k, 1], dspec_own[k, 0]) + dspec_other[k]

    def through_gate(img, carry):
        ascent = -grads[img].astype(jnp.float32).reshape(shape3)
        ascent = jnp.where(second, turn(ascent, -16), ascent)
        ascent = jnp.where(first_half, ascent, 0.0)
        centred = xn[img]
        y = centred * gain + bias
        gate = turn(jax.nn.sigmoid(y), -16)
        dopened = ascent * (y * gate)
        scale = jnp.concatenate(
            [jnp.broadcast_to(gate8[img * micros + m][None], (side, SUBLANES, LANES)) for m in range(micros)],
            axis=0,
        )
        dgated = ascent * scale
        dnormed = jnp.where(first_half, dgated * gate, turn(dgated * y * gate * (1.0 - gate), 16))
        dy[img] = dnormed
        new = []
        for m in range(micros):
            part = slice(m * side, (m + 1) * side)
            total = fold(jnp.sum(dopened[part], axis=0))
            total = total + turn(total, 16)
            gate_now = gate8[img * micros + m]
            dze[img * micros + m] = (
                jnp.broadcast_to(jnp.sum(total, axis=0, keepdims=True), (SUBLANES, LANES))
                * gate_now
                * (1.0 - gate_now)
            )
            new.append(carry[2 * m] + jnp.sum(dnormed[part] * centred[part], axis=0))
            new.append(carry[2 * m + 1] + jnp.sum(dnormed[part], axis=0))
        return tuple(new)

    sums = lax.fori_loop(0, images, through_gate, (zero,) * (2 * micros))
    sums = [jnp.sum(fold(s), axis=0, keepdims=True) for s in sums]
    gain_row = consts[1:2, :]
    mean_back = per_micro([gain_row * sums[2 * m + 1] / pixel_count for m in range(micros)], side)
    cross_back = per_micro([gain_row * sums[2 * m] / pixel_count for m in range(micros)], side)
    std12 = per_micro([stats[m : m + 1, :] for m in range(micros)], side)
    taps = 9
    groups = (taps + 3) // 4
    lane_flat = lane_of((spread, LANES)) // 32

    def through_norm(img, carry):
        centred = xn[img]
        dshift = (dy[img] * gain - mean_back - centred * cross_back) * std12
        dshift = jnp.where(inside, dshift, 0.0)
        carry = carry + jnp.sum(dshift * noise_rows[img], axis=0)
        dh = dshift.astype(bf16).astype(jnp.float32)
        swapped = jnp.where(col_first, turn(dh, -32), turn(dh, 32))
        col0 = jnp.where(col_first, dh, swapped)
        col1 = jnp.where(col_first, swapped, dh)
        by_col = [
            col1 + pltpu.roll(col0, SUBLANES - 1, 1),
            col0 + col1,
            col0 + pltpu.roll(col1, 1, 1),
        ]
        found = [None] * taps
        for kx in range(3):
            value = by_col[kx]
            turned = turn(value, 64)
            row0 = jnp.where(row_first, value, turned)
            row1 = jnp.where(row_first, turned, value)
            found[kx] = row1 + shift_rows(row0, side, -1)
            found[3 + kx] = row0 + row1
            found[6 + kx] = row0 + shift_rows(row1, side, 1)
        for g in range(groups):
            members = [f.reshape(spread, LANES) for f in found[4 * g : 4 * g + 4]]
            value = members[0]
            for k in range(1, len(members)):
                value = jnp.where(lane_flat == k, members[k], value)
            top, rest = split_two(value)
            packed[img, :, g * LANES : (g + 1) * LANES] = top
            packed[img, :, (groups + g) * LANES : (groups + g + 1) * LANES] = rest
        return carry

    dgain_noise = lax.fori_loop(0, images, through_norm, zero)
    dgain_noise = jnp.sum(fold(dgain_noise), axis=0, keepdims=True)
    lane_row = lane_of((1, LANES))
    for r in range(images * micros // 8):
        value = jnp.zeros((1, LANES), jnp.float32)
        for g in range(8):
            value = jnp.where(lane_row // 16 == g, dze[8 * r + g][0:1], value)
        block[r : r + 1, :] = value
    gains = jnp.where(
        lane_row // 32 == 0,
        dgain_noise,
        jnp.where(
            lane_row // 32 == 1,
            sum(sums[2 * m] for m in range(micros)),
            sum(sums[2 * m + 1] for m in range(micros)),
        ),
    )
    block[4:5, :] = gains
    block[5:8, :] = jnp.zeros((3, LANES), jnp.float32)
    block[8:16, :] = tail[...]

    width = groups * LANES
    flat = packed[...].reshape(images * spread, 2 * width)
    load.wait()
    for p in range(2):
        side_rows = all_lat[:, p].reshape(images * spread, half_in)
        both = lax.dot_general(
            side_rows, flat, (((0,), (0,)), ((), ())), preferred_element_type=jnp.float32
        )
        product[p * half_in : (p + 1) * half_in, :] = both[:, :width] + both[:, width:]
    depth = dconv.shape[1]
    unit = 16
    lane_unit = lane_of((unit, LANES)) // 32
    for chip in range(dconv.shape[0]):
        for at in range(0, depth, unit):
            value = None
            for g in range(4):
                tap, channel = divmod((chip * 4 + g) * depth + at, channels)
                piece = product[channel : channel + unit, (tap // 4) * LANES : (tap // 4 + 1) * LANES]
                piece = turn(piece, 32 * (g - tap % 4))
                value = piece if value is None else jnp.where(lane_unit == g, piece, value)
            dconv[chip, at : at + unit, :] = value.astype(bf16)


def back(side, micros, pixel_count, depth, grads, xn, lat, noise_rows, consts, stats, opened, tail,
         dspec_own, dspec_other):
    images, _, _, half_in = lat.shape
    lines = micros * side
    count = images * micros
    f32 = jnp.float32
    return local_call(
        partial(back_kernel, side, micros, pixel_count),
        "back",
        [
            jax.ShapeDtypeStruct((images, depth, LANES), jnp.bfloat16),
            jax.ShapeDtypeStruct((2 * SUBLANES, LANES), f32),
            jax.ShapeDtypeStruct((PLANE, images // PLANE) + dspec_other.shape[1:], f32),
        ],
        [
            pltpu.VMEM((images, lines, SUBLANES, LANES), f32),
            pltpu.VMEM((images, lines * SUBLANES, 6 * LANES), jnp.bfloat16),
            pltpu.VMEM((2 * half_in, 3 * LANES), f32),
            pltpu.VMEM((count, SUBLANES, LANES), f32),
            pltpu.VMEM((count, SUBLANES, LANES), f32),
            pltpu.VMEM((images, 2, lines * SUBLANES, half_in), lat.dtype),
            pltpu.SemaphoreType.DMA((1,)),
        ],
        [grads, xn, lat, noise_rows, consts, stats, opened, tail, dspec_own, dspec_other],
        [pl.BlockSpec(memory_space=pltpu.VMEM)] * 2
        + [pl.BlockSpec(memory_space=pl.ANY)]
        + [pl.BlockSpec(memory_space=pltpu.VMEM)] * 7,
    )


def owner_kernel(dconv, mom, parts_in, mom_new, gram, parts, top, rest):
    chips, _, depth, _ = dconv.shape
    rows, widths = mom.shape
    half = widths // 2
    blocks = widths // LANES
    core = lax.axis_index("segment")
    lane = lane_of((depth, LANES))
    parts[...] = jnp.sum(parts_in[...], axis=0)
    @pl.loop(0, half // LANES)
    def _(b):
        halves = []
        for c in range(PLANE):
            low = dconv[b * PLANE + c, 0].astype(jnp.float32)
            high = dconv[b * PLANE + c, 1].astype(jnp.float32)
            halves.append(
                (
                    jnp.where(lane % 32 < 16, low, turn(high, 16)),
                    jnp.where(lane % 32 < 16, turn(low, -16), high),
                )
            )
        for q in range(4):
            for k in range(2):
                value = None
                for c in range(PLANE):
                    piece = turn(halves[c][k], 32 * (c - q))
                    value = piece if value is None else jnp.where(lane // 32 == c, piece, value)
                cols = pl.ds(pl.multiple_of(k * half + b * LANES, LANES), LANES)
                rows_now = slice(q * depth, (q + 1) * depth)
                mom_new[rows_now, cols] = MOMENTUM * mom[rows_now, cols] + value

    for b in range(blocks):
        high, low = split_two(mom_new[:, b * LANES : (b + 1) * LANES])
        for at in (b, b + blocks) if b < PLANE else (b,):
            cols = slice(at * LANES, (at + 1) * LANES)
            top[:, cols] = high
            rest[:, cols] = low
    dims = (((0,), (0,)), ((), ()))
    share = LANES // 4
    span = gram.shape[2]

    @pl.loop(0, blocks // 2)
    def _(pair):
        at = pl.multiple_of(2 * pair * LANES, LANES)
        own, wide = pl.ds(at, 2 * LANES), pl.ds(at, span + LANES)
        left_high, left_low = top[:, own], rest[:, own]
        right_high, right_low = top[:, wide], rest[:, wide]

        def times(left, right):
            return lax.dot_general(left, right, dims, preferred_element_type=jnp.float32)

        found = times(left_high, right_high) + (times(left_high, right_low) + times(left_low, right_high))
        for k in range(2):
            for h in range(2):
                first = k * LANES + 2 * share * h
                cols = slice(k * LANES, k * LANES + span)
                gram[4 * pair + 2 * k + h] = jnp.where(
                    core == 0,
                    found[first : first + share, cols],
                    found[first + share : first + 2 * share, cols],
                )


def owner(dconv, mom, dspec):
    chips, _, depth, _ = dconv.shape
    rows, widths = mom.shape
    f32 = jnp.float32
    span = (widths // LANES // 2 + 1) * LANES
    return local_call(
        owner_kernel,
        "owner",
        [
            jax.ShapeDtypeStruct(mom.shape, f32),
            jax.ShapeDtypeStruct((chips, widths // chips // 2, span), f32),
            jax.ShapeDtypeStruct(dspec.shape[1:], f32),
        ],
        [pltpu.VMEM((rows, widths + PLANE * LANES), jnp.bfloat16)] * 2,
        [dconv, mom, dspec],
    )


def collect_kernel(grams, dspec, block, gram, small):
    size = dspec.shape[2]
    gram[...] = jnp.sum(grams[...], axis=0)
    small[:, :size] = jnp.sum(dspec[...], axis=0)
    small[:, size:] = block[...]


def collect(grams, dspec, block):
    return local_call(
        collect_kernel,
        "collect",
        [
            jax.ShapeDtypeStruct(grams.shape[1:], jnp.float32),
            jax.ShapeDtypeStruct((block.shape[0], dspec.shape[2] + block.shape[1]), jnp.float32),
        ],
        [],
        [grams, dspec, block],
    )


def three(left_high, left_low, right_high, right_low, dims=(((1,), (0,)), ((), ()))):
    def times(left, right):
        return lax.dot_general(left, right, dims, preferred_element_type=jnp.float32)

    return times(left_high, right_high) + (times(left_high, right_low) + times(left_low, right_high))


def store_block(value, i, j, high, low):
    rows, cols = slice(i * BLOCK, (i + 1) * BLOCK), slice(j * BLOCK, (j + 1) * BLOCK)
    high[rows, cols], low[rows, cols] = split_two(value)
    if i < j:
        high[cols, rows], low[cols, rows] = split_two(value.T)


def polynomial(gram, gram_high, gram_low, high, low):
    for j in range(gram.shape[0] // BLOCK):
        cols, rows = slice(j * BLOCK, (j + 1) * BLOCK), slice(0, (j + 1) * BLOCK)
        found = three(gram_high[rows, :], gram_low[rows, :], gram_high[:, cols], gram_low[:, cols])
        for i in range(j + 1):
            here = slice(i * BLOCK, (i + 1) * BLOCK)
            store_block(NEWTON_B * gram[here, cols] + NEWTON_C * found[here], i, j, high, low)


def multiply(source, source_high, source_low, poly_high, poly_low, result, high, low):
    for j in range(source.shape[0] // BLOCK):
        cols, rows = slice(j * BLOCK, (j + 1) * BLOCK), slice(0, (j + 1) * BLOCK)
        found = three(source_high[rows, :], source_low[rows, :], poly_high[:, cols], poly_low[:, cols])
        for i in range(j + 1):
            here = slice(i * BLOCK, (i + 1) * BLOCK)
            value = NEWTON_A * source[here, cols] + found[here]
            result[here, cols] = value
            store_block(value, i, j, high, low)


def apply(x, x_high, x_low, poly_high, poly_low):

    @pl.loop(0, x.shape[1] // BLOCK)
    def _(j):
        cols = pl.ds(pl.multiple_of(j * BLOCK, BLOCK), BLOCK)
        found = three(x_high[...], x_low[...], poly_high[:, cols], poly_low[:, cols])
        x[:, cols] = NEWTON_A * x[:, cols] + found


def resplit(x, x_high, x_low):
    for j in range(x.shape[1] // BLOCK):
        cols = slice(j * BLOCK, (j + 1) * BLOCK)
        x_high[:, cols], x_low[:, cols] = split_two(x[:, cols])


def conv_ortho(have_x, packed, x, gram, high, low, p_high, p_low, x_high, x_low):
    size = gram.shape[1]
    blocks = size // LANES
    share = packed.shape[2]
    span = packed.shape[3] // LANES
    chips_block = LANES // (2 * share)

    def block(b, k):
        pair = pl.ds(b * chips_block, chips_block)
        return packed[pair, :, :share, k * LANES : (k + 1) * LANES].reshape(LANES, LANES)

    eye = lax.broadcasted_iota(jnp.int32, (LANES, LANES), 0) == lane_of((LANES, LANES))

    def add_squares(b, total):
        return total + jnp.where(eye, block(b, 0), 0.0)

    total = lax.fori_loop(0, blocks, add_squares, jnp.zeros((LANES, LANES), jnp.float32))
    scale = 1.0 / (jnp.sqrt(jnp.sum(total)) + 1e-07)

    @pl.loop(0, blocks)
    def _(r):
        rows = pl.ds(pl.multiple_of(r * LANES, LANES), LANES)
        for ahead in range(span):
            cols = pl.ds(pl.multiple_of(lax.rem(r + ahead, blocks) * LANES, LANES), LANES)
            value = (block(r, ahead) * scale) * scale
            gram[0, rows, cols] = value
            high[0, rows, cols], low[0, rows, cols] = split_two(value)
            if ahead:
                value = value.T
                gram[0, cols, rows] = value
                high[0, cols, rows], low[0, cols, rows] = split_two(value)

    have_x()
    for j in range(size // BLOCK):
        cols = slice(j * BLOCK, (j + 1) * BLOCK)
        value = x[:, cols] * scale
        x[:, cols] = value
        x_high[:, cols], x_low[:, cols] = split_two(value)

    @pl.loop(0, NS_STEPS)
    def _(step):
        polynomial(gram.at[0], high.at[0], low.at[0], p_high, p_low)
        apply(x, x_high, x_low, p_high, p_low)

        @pl.when(step < NS_STEPS - 1)
        def _():
            resplit(x, x_high, x_low)
            for k in range(2):
                multiply(
                    gram.at[k], high.at[k], low.at[k], p_high, p_low,
                    gram.at[1 - k], high.at[1 - k], low.at[1 - k],
                )


def whole_ortho(chunks, x, x_high, x_low, gram, g_high, g_low, p_high, p_low):
    size = gram.shape[0]

    def rows_of(c):
        return pl.ds(pl.multiple_of(c * size, size), size)

    def add_squares(c, total):
        value = x[rows_of(c), :]
        return total + jnp.sum(value * value)

    scale = 1.0 / (jnp.sqrt(lax.fori_loop(0, chunks, add_squares, jnp.float32(0.0))) + 1e-07)

    @pl.loop(0, chunks)
    def _(c):
        rows = rows_of(c)
        value = x[rows, :] * scale
        x[rows, :] = value
        x_high[rows, :], x_low[rows, :] = split_two(value)

    @pl.loop(0, NS_STEPS)
    def _(_):
        gram[...] = jnp.zeros(gram.shape, jnp.float32)

        @pl.loop(0, chunks)
        def _(c):
            for j in range(size // BLOCK):
                cols, above = slice(j * BLOCK, (j + 1) * BLOCK), slice(0, (j + 1) * BLOCK)
                gram[above, cols] += three(
                    x_high[rows_of(c), above],
                    x_low[rows_of(c), above],
                    x_high[rows_of(c), cols],
                    x_low[rows_of(c), cols],
                    (((0,), (0,)), ((), ())),
                )

        for j in range(size // BLOCK):
            for i in range(j + 1):
                at = (slice(i * BLOCK, (i + 1) * BLOCK), slice(j * BLOCK, (j + 1) * BLOCK))
                store_block(gram[at], i, j, g_high, g_low)
        polynomial(gram, g_high, g_low, p_high, p_low)

        @pl.loop(0, chunks)
        def _(c):
            rows = rows_of(c)
            for j in range(size // BLOCK):
                cols = slice(j * BLOCK, (j + 1) * BLOCK)
                found = three(x_high[rows, :], x_low[rows, :], p_high[:, cols], p_low[:, cols])
                x[rows, cols] = NEWTON_A * x[rows, cols] + found
            x_high[rows, :], x_low[rows, :] = split_two(x[rows, :])


def outer_sum(left, right):
    a, b, c = split_three(left)
    d, e, f = split_three(right)
    return lax.dot_general(
        jnp.concatenate([a, a, b, a, b, c], axis=0),
        jnp.concatenate([d, e, d, f, e, d], axis=0),
        (((0,), (0,)), ((), ())),
        preferred_element_type=jnp.float32,
    )


def update_kernel(spread, size, gram_rows, smalls_in, conv_mom, conv_w, lat, moms, squeeze_w, excite_w, critic_w, pooled, z1,
                  column_v, column_t, row_w, power, vectors, vec_m, vec_v,
                  conv_new, small, adam_out,
                  sems, x, gram, high, low, p_high, p_low, x_high, x_low, w,
                  whole, whole_high, whole_low, small_gram, sg_high, sg_low, sp_high, sp_low, weights, dze, moms_all, smalls):
    core = lax.axis_index("segment")
    chip = lax.axis_index("dp")
    keep = 1.0 - MUON_RATE * DECAY
    f32 = jnp.float32

    @pl.when(core == 0)
    def _():
        load_mom = pltpu.make_async_copy(conv_mom, x, sems.at[0])
        load_w = pltpu.make_async_copy(conv_w, w, sems.at[1])
        load_mom.start()
        load_w.start()
        conv_ortho(load_mom.wait, gram_rows, x, gram, high, low, p_high, p_low, x_high, x_low)
        load_w.wait()
        conv_new[...] = w[...] * keep - MUON_RATE * x[...]

    @pl.when(core == 1)
    def _():
        chips = lat.shape[0]
        rows_each = [weight.shape[0] for weight in (squeeze_w, excite_w, critic_w)]
        lows = weights.shape[2]
        load_low = pltpu.make_async_copy(
            lat.at[:, :, pl.ds(spread + rows_each[0] // 2, lows)], weights, sems.at[0]
        )
        load_moms = pltpu.make_async_copy(moms, moms_all, sems.at[1])
        load_smalls = pltpu.make_async_copy(smalls_in, smalls, sems.at[2])
        load_smalls.start()
        load_low.start()
        load_moms.start()
        load_smalls.wait()
        own = size // chips // 2
        lane = lane_of((4 * (size // LANES), LANES)) // own
        groups = LANES // own
        held = []
        for e in range(groups):
            rows = []
            for b in range(size // LANES):
                device = b * groups + e
                first = device % 2 * 2 * SUBLANES
                rows.append(smalls[device // 2, first : first + 4, size:])
            held.append(jnp.concatenate(rows, axis=0))
        for g in range(groups):
            value = jnp.zeros_like(held[0])
            for e in range(groups):
                value = jnp.where(lane == e, turn(held[e], own * (e - g)), value)
            for b in range(size // LANES):
                for r in range(4):
                    dze[groups * r + g : groups * r + g + 1, b * LANES : (b + 1) * LANES] = (
                        value[4 * b + r : 4 * b + r + 1]
                    )
        load_low.wait()
        load_moms.wait()
        excite_low = weights[:, :, : rows_each[1] // 2].reshape(size, size)
        critic = weights[:, :, rows_each[1] // 2 :].reshape(size, size).astype(f32)
        gate = z1[...]
        squeezed = gate * jax.nn.sigmoid(gate)
        back = lax.dot_general(
            jnp.concatenate(split_three(dze[...]), axis=0),
            excite_low,
            (((1,), (1,)), ((), ())),
            preferred_element_type=f32,
        )
        rows = dze.shape[0]
        back = back[:rows] + back[rows : 2 * rows] + back[2 * rows :]
        dz1 = back * silu_slope(gate)

        starts, firsts = [0], [0]
        for count in rows_each:
            starts.append(starts[-1] + count)
            firsts.append(firsts[-1] + chips * count)

        def fill(k, grad):
            count = rows_each[k]
            old = moms_all[:, starts[k] : starts[k + 1]].reshape(chips * count, size)
            whole[firsts[k] : firsts[k + 1], :] = MOMENTUM * old + grad

        fill(0, outer_sum(pooled[...], dz1))
        fill(1, outer_sum(squeezed, dze[...]))
        spec = smalls[:, :, :size].reshape(size, size)
        vec = column_v[...]
        back_row = jnp.sum(critic * vec, axis=0, keepdims=True)
        square = jnp.sum(back_row * back_row)
        along = jnp.sum(spec * critic) / square
        direction = vec * row_w[0:1, :] + column_t[...] * power[...]
        fill(2, spec / jnp.sqrt(square) - along * direction)

        def own_rows(k):
            count = rows_each[k]
            return whole[pl.ds(pl.multiple_of(firsts[k] + chip * count, count), count), :]

        for k in range(3):
            small[starts[k] : starts[k + 1], :] = own_rows(k)

        @pl.loop(0, 3)
        def _(k):
            chunks = jnp.where(k == 0, firsts[1] // size, 1)
            first = jnp.where(k == 0, 0, firsts[1] + (k - 1) * size)
            view = whole.at[pl.ds(pl.multiple_of(first, size), firsts[1])]
            whole_ortho(
                chunks, view, whole_high, whole_low, small_gram, sg_high, sg_low, sp_high, sp_low
            )

        for k, weight in enumerate((squeeze_w, excite_w, critic_w)):
            small[starts[3] + starts[k] : starts[3] + starts[k + 1], :] = (
                weight[...] * keep - MUON_RATE * own_rows(k)
            )

        vec_rows = vectors.shape[0]
        lane_row = lane_of((1, LANES))
        lines = []
        for gain in range(3):
            for half in range(2):
                for b in range(size // LANES):
                    value = jnp.zeros((1, LANES), f32)
                    for e in range(groups):
                        device = b * groups + e
                        first = device % 2 * 2 * SUBLANES + 4
                        row = smalls[device // 2, first : first + 1, size:]
                        row = turn(row, own * (e - (2 * gain + half)))
                        value = jnp.where(lane_row // own == e, row, value)
                    lines.append(value)
        tails = jnp.sum(smalls[:, SUBLANES : 2 * SUBLANES, size:] + smalls[:, 3 * SUBLANES :, size:], axis=0)
        count = size // LANES
        last = tails[count : count + 1]
        lines += [tails[k : k + 1] for k in range(count)]
        lines.append(jnp.where(lane_row == 0, last, 0.0))
        lines.append(jnp.zeros((vec_rows - len(lines), LANES), f32))
        results = adam(vectors[...], vec_m[...], vec_v[...], jnp.concatenate(lines, axis=0))
        for k in range(3):
            adam_out[k * vec_rows : (k + 1) * vec_rows, :] = results[k]
        adam_out[3 * vec_rows :, :] = jnp.broadcast_to(jnp.sum(jnp.where(lane_row == 1, last, 0.0)), (SUBLANES, LANES))


def update(gram_rows, smalls, conv_mom, conv_w, lat, moms, squeeze_w, excite_w, critic_w, pooled, z1, column_v, column_t,
           row_w, power, vectors, vec_m, vec_v, spread, size):
    f32, bf16 = jnp.float32, jnp.bfloat16
    widths = conv_w.shape[1]
    chips = lat.shape[0]
    small_rows = squeeze_w.shape[0] + excite_w.shape[0] + critic_w.shape[0]
    arguments = [gram_rows, smalls, conv_mom, conv_w, lat, moms, squeeze_w, excite_w, critic_w, pooled, z1, column_v, column_t,
                 row_w, power, vectors, vec_m, vec_v]
    vmem, anywhere = pl.BlockSpec(memory_space=pltpu.VMEM), pl.BlockSpec(memory_space=pl.ANY)
    pair, square, small_square = (2, widths, widths), (widths, widths), (size, size)
    tall = chips * squeeze_w.shape[0]
    return local_call(
        partial(update_kernel, spread, size),
        "update",
        [
            jax.ShapeDtypeStruct(conv_w.shape, f32),
            jax.ShapeDtypeStruct((2 * small_rows, size), f32),
            jax.ShapeDtypeStruct((3 * vectors.shape[0] + SUBLANES, LANES), f32),
        ],
        [
            pltpu.SemaphoreType.DMA((3,)),
            pltpu.VMEM(conv_w.shape, f32),
            pltpu.VMEM(pair, f32),
            pltpu.VMEM(pair, bf16),
            pltpu.VMEM(pair, bf16),
            pltpu.VMEM(square, bf16),
            pltpu.VMEM(square, bf16),
            pltpu.VMEM(conv_w.shape, bf16),
            pltpu.VMEM(conv_w.shape, bf16),
            pltpu.VMEM(conv_w.shape, f32),
            pltpu.VMEM((chips * small_rows + size, size), f32),
            pltpu.VMEM((tall, size), bf16),
            pltpu.VMEM((tall, size), bf16),
            pltpu.VMEM(small_square, f32),
            pltpu.VMEM(small_square, bf16),
            pltpu.VMEM(small_square, bf16),
            pltpu.VMEM(small_square, bf16),
            pltpu.VMEM(small_square, bf16),
            pltpu.VMEM((chips, 2, (excite_w.shape[0] + critic_w.shape[0]) // 2, size), bf16),
            pltpu.VMEM(z1.shape, f32),
            pltpu.VMEM(moms.shape, f32),
            pltpu.VMEM(smalls.shape, f32),
        ],
        arguments,
        [vmem] + [anywhere] * 5 + [vmem] * 12,
    )


def by_channels(
    latent,
    noise,
    real_bank,
    real_index,
    frozen_feat,
    frozen_proj,
    power_vec,
    conv_w,
    conv_mom,
    squeeze_w,
    squeeze_mom,
    excite_w,
    excite_mom,
    critic_w,
    critic_mom,
    vectors,
    vec_m,
    vec_v,
):
    n = lax.axis_size("dp")
    chip, side = lax.axis_index("dp"), lax.axis_index("segment")
    f32 = jnp.float32
    micros, _, edge, _, channels = latent.shape
    pixels = noise.shape[2]
    rows, widths = conv_w.shape
    half = widths // 2
    own = half // n // 2
    depth = rows // 4
    proj_width = critic_w.shape[1]
    pixel_count = pixels * n
    patches = micros * pixel_count
    spread = micros * edge * SUBLANES

    def rows_of(vector):
        count = -(-vector.shape[0] // (SUBLANES * LANES)) * SUBLANES
        return jnp.pad(vector, (0, count * LANES - vector.shape[0])).reshape(count, LANES)

    vectors_rows = rows_of(vectors)
    power = power_vec.reshape(1, -1)
    block, conv_own, noise_own, moms = pack(
        n, latent, noise, conv_w, squeeze_w, excite_w, critic_w, squeeze_mom, excite_mom, critic_mom
    )
    lat, conv, noise_all = exchange(
        n, 1, [("relay", True), ("a2a", False), ("relay", True)], [block, conv_own, noise_own]
    )

    fake, xn, stats, opened, z1, pooled, consts, noise_rows = front(
        edge, micros, pixel_count, lat, conv, noise_all, vectors_rows
    )
    (arrived,) = exchange(n, 2, [("a2a", True)], [fake])
    dfake, dspec, tail, column_v, column_t, row_w = critic_step(
        edge,
        patches,
        spread,
        arrived,
        lat,
        real_bank,
        frozen_feat,
        frozen_proj,
        power,
        vectors_rows,
        real_index,
    )

    returned, added = exchange(n, 3, [("a2a", True), ("cross", False)], [dfake, dspec])
    dconv, block, dspec = back(
        edge, micros, pixel_count, depth, returned, xn, lat, noise_rows, consts, stats, opened, tail,
        dspec, added,
    )

    dconv, dspec = exchange(n, 4, [("a2a", True), ("plane", False)], [dconv, dspec])
    conv_mom_new, gram, dspec = owner(dconv, conv_mom, dspec)
    grams, dspec = exchange(n, 5, [("a2a", False), ("line", False)], [gram, dspec])
    gram, small = collect(grams, dspec, block)
    gram, small_other = exchange(n, 6, [("relay", True), ("sib", False)], [gram, small])
    small = jnp.concatenate([small_other, small], axis=0)
    smalls, moms = exchange(n, 8, [("relay", False)] * 2, [small, moms], core=1)

    conv_new, small, adam_new = update(
        gram, smalls, conv_mom_new, conv_w, lat, moms, squeeze_w, excite_w, critic_w, pooled, z1, column_v,
        column_t, row_w, power, vectors_rows, rows_of(vec_m), rows_of(vec_v), spread, proj_width,
    )
    conv_new, small, adam_new = share(7, conv_new, small, adam_new)
    pieces = []
    first = 0
    for weight in (squeeze_w, excite_w, critic_w) * 2:
        pieces.append(small[first : first + weight.shape[0]])
        first += weight.shape[0]
    size = vectors.shape[0]
    vec_rows = vectors_rows.shape[0]
    flat = adam_new[: 3 * vec_rows].reshape(3, vec_rows * LANES)[:, :size]
    return (
        adam_new[3 * vec_rows, 0],
        conv_mom_new,
        conv_new,
        pieces[0],
        pieces[3],
        pieces[1],
        pieces[4],
        pieces[2],
        pieces[5],
        flat[0],
        flat[1],
        flat[2],
    )


def shifted_2(value, axis, steps):
    count = lax.axis_size(axis)
    leading, last = (max(0, -steps), min(count, count - steps))
    return lax.ppermute(value, axis, [(source, source + steps) for source in range(leading, last)])


def for_sending(x):
    return jax.tree.map(lambda a: a.astype(jnp.bfloat16) if a.dtype == jnp.float32 else a, x)


def only_if(flag, compute):

    def empty_branch():
        return jax.tree.map(jnp.zeros_like, compute())

    return lax.cond(flag, compute, empty_branch)


def columns(latent_now):
    upsampled = jnp.repeat(jnp.repeat(latent_now, 2, axis=1), 2, axis=2)
    side_now = upsampled.shape[1]
    padded = jnp.pad(upsampled, ((0, 0), (1, 1), (1, 1), (0, 0)))
    taps = [
        padded[:, row_tap : row_tap + side_now, col_tap : col_tap + side_now, :]
        for row_tap in range(3)
        for col_tap in range(3)
    ]
    return jnp.concatenate(taps, axis=-1).reshape(-1, 9 * upsampled.shape[3])


def spectral_norm(weight, power):
    vector = high_dot(weight, power)
    vector = vector * lax.rsqrt(jnp.sum(vector * vector))
    product_one = high_dot(vector, weight)
    return weight / jnp.sqrt(jnp.sum(product_one * product_one))


def excite(pooled, squeeze_w, excite_w):
    return jax.nn.sigmoid(high_dot(jax.nn.silu(high_dot(pooled, squeeze_w)), excite_w))


def normalize(shifted, moments, pixel_count, bn_gain, bn_bias):
    mean_vec = moments[0] / pixel_count
    inv_std = lax.rsqrt(moments[1] / pixel_count - mean_vec * mean_vec + NORM_EPS)
    centred = (shifted - mean_vec) * inv_std
    return (centred, inv_std, centred * bn_gain + bn_bias)


def critic_pass(
    inputs, sign, patches, frozen_feat, frozen_proj, spectral, out_weight, out_bias, want_input
):
    pre_act = low_dot(inputs, frozen_feat)
    features = jax.nn.silu(pre_act).astype(jnp.bfloat16)
    projected = low_dot(features, frozen_proj).astype(jnp.bfloat16)
    critic_act = low_dot(projected, spectral)
    activated = jax.nn.silu(critic_act)
    logits = high_dot(activated, out_weight) + out_bias
    loss_part = jnp.sum(jax.nn.softplus(1.0 + sign * logits))
    dlogit = sign * jax.nn.sigmoid(1.0 + sign * logits) / patches
    dact = (dlogit[:, None] * out_weight * silu_slope(critic_act)).astype(jnp.bfloat16)
    result = [loss_part, low_dot(projected.T, dact), high_dot(dlogit, activated), jnp.sum(dlogit)]
    if want_input:
        dproj = low_dot(dact, spectral.T).astype(jnp.bfloat16)
        dpre = (low_dot(dproj, frozen_proj.T) * silu_slope(pre_act)).astype(jnp.bfloat16)
        result.append(low_dot(dpre, frozen_feat.T).astype(jnp.bfloat16))
    return result


def orthogonalize(momenta):
    squares = lax.psum(
        (
            jnp.sum(momenta[0] * momenta[0]),
            jnp.sum(momenta[1] * momenta[1]),
            jnp.sum(momenta[2] * momenta[2]),
            jnp.sum(momenta[3] * momenta[3]),
        ),
        "dp",
    )
    current = [
        matrix_now / (jnp.sqrt(square_now) + 1e-07)
        for matrix_now, square_now in zip(momenta, squares)
    ]

    def iterate(_, current):
        partials = [
            lax.psum_scatter(
                high_dot(matrix_now.T, matrix_now), "dp", scatter_dimension=0, tiled=True
            )
            for matrix_now in current
        ]
        full_grams = [lax.all_gather(part, "dp", axis=0, tiled=True) for part in partials]
        updated = []
        for matrix_now, gram in zip(current, full_grams):
            product_one = high_dot(matrix_now, gram)
            updated.append(
                NEWTON_A * matrix_now
                + NEWTON_B * product_one
                + NEWTON_C * high_dot(product_one, gram)
            )
        return updated

    return lax.fori_loop(0, NS_STEPS, iterate, current)


def by_images(
    latent,
    noise,
    real_bank,
    real_index,
    frozen_feat,
    frozen_proj,
    power_vec,
    conv_w,
    conv_mom,
    squeeze_w,
    squeeze_mom,
    excite_w,
    excite_mom,
    critic_w,
    critic_mom,
    vectors,
    vec_m,
    vec_v,
):
    gathered = (
        lax.all_gather(conv_w.astype(jnp.bfloat16), "dp", axis=0, tiled=True),
        lax.all_gather(squeeze_w.astype(jnp.bfloat16), "dp", axis=0, tiled=True),
        lax.all_gather(excite_w.astype(jnp.bfloat16), "dp", axis=0, tiled=True),
        lax.all_gather(critic_w.astype(jnp.bfloat16), "dp", axis=0, tiled=True),
    )
    conv_low, squeeze_low, excite_low, critic_low = gathered
    squeeze_full = squeeze_low.astype(jnp.float32)
    excite_full = excite_low.astype(jnp.float32)
    spectral_full, spectral_back = jax.vjp(
        partial(spectral_norm, power=power_vec), critic_low.astype(jnp.float32)
    )
    spectral = spectral_full.astype(jnp.bfloat16)
    micro_count, images, pixels = (noise.shape[0], noise.shape[1], noise.shape[2])
    widths = conv_low.shape[1]
    half_width = widths // 2
    proj_width = critic_low.shape[0]
    tokens = images * pixels
    pixel_count = tokens * lax.axis_size("dp")
    patches = micro_count * pixel_count
    noise_gain = vectors[:widths]
    bn_gain = vectors[widths : 2 * widths]
    bn_bias = vectors[2 * widths : 3 * widths]
    out_weight = vectors[3 * widths : 3 * widths + proj_width]
    out_bias = vectors[3 * widths + proj_width]
    generator = lax.axis_index("segment") == 0
    critic_side = jnp.logical_not(generator)
    pooled = jnp.mean(latent.astype(jnp.float32), axis=(2, 3))
    conv_acc = jnp.zeros(conv_low.shape, jnp.float32)
    squeeze_acc = jnp.zeros(squeeze_low.shape, jnp.float32)
    excite_acc = jnp.zeros(excite_low.shape, jnp.float32)
    spectral_acc = jnp.zeros(critic_low.shape, jnp.float32)
    vector_acc = jnp.zeros(vectors.shape, jnp.float32)
    loss_acc = jnp.zeros((), jnp.float32)
    for micro_step in range(micro_count):
        noise_now = noise[micro_step].reshape(-1)
        excitation, excite_back = jax.vjp(excite, pooled[micro_step], squeeze_full, excite_full)

        def gen_front():
            patches_in = columns(latent[micro_step])
            return (patches_in, low_dot(patches_in, conv_low) + noise_now[:, None] * noise_gain)

        patches_in, shifted = only_if(generator, gen_front)
        moments = lax.psum((jnp.sum(shifted, axis=0), jnp.sum(shifted * shifted, axis=0)), "dp")

        def gen_mid():
            centred, inv_std, normed = normalize(shifted, moments, pixel_count, bn_gain, bn_bias)
            gated = normed[:, :half_width] * jax.nn.sigmoid(normed[:, half_width:])
            fake_map = gated.reshape(images, pixels, half_width) * excitation[:, None, :]
            return fake_map.reshape(tokens, half_width).astype(jnp.bfloat16)

        fake_map = only_if(generator, gen_mid)
        arrived = shifted_2(fake_map, "segment", 1)

        def critic_work():
            real_map = real_bank[real_index[micro_step]].reshape(tokens, half_width)
            real_out = critic_pass(
                real_map,
                -1.0,
                patches,
                frozen_feat,
                frozen_proj,
                spectral,
                out_weight,
                out_bias,
                False,
            )
            fake_out = critic_pass(
                arrived,
                1.0,
                patches,
                frozen_feat,
                frozen_proj,
                spectral,
                out_weight,
                out_bias,
                True,
            )
            return (
                real_out[0] + fake_out[0],
                real_out[1] + fake_out[1],
                real_out[2] + fake_out[2],
                real_out[3] + fake_out[3],
                fake_out[4],
            )

        loss_part, dspec_part, dout_part, dbias_part, input_grad = only_if(critic_side, critic_work)
        returned = jax.tree.map(
            lambda part, own: part.astype(own.dtype),
            shifted_2(for_sending(input_grad), "segment", -1),
            input_grad,
        )

        def gen_back():
            dfake = -returned.astype(jnp.float32).reshape(images, pixels, half_width)
            centred, inv_std, normed = normalize(shifted, moments, pixel_count, bn_gain, bn_bias)
            opened = jax.nn.sigmoid(normed[:, half_width:])
            first_half = normed[:, :half_width]
            gated = (first_half * opened).reshape(images, pixels, half_width)
            unused, dsqueeze, dexcite = excite_back(jnp.sum(dfake * gated, axis=1))
            dgated = (dfake * excitation[:, None, :]).reshape(tokens, half_width)
            dnormed = jnp.concatenate(
                [dgated * opened, dgated * first_half * opened * (1.0 - opened)], axis=1
            )
            return (
                dnormed * bn_gain,
                centred,
                inv_std,
                dsqueeze,
                dexcite,
                jnp.sum(dnormed * centred, axis=0),
                jnp.sum(dnormed, axis=0),
            )

        dcentred, centred, inv_std, dsqueeze, dexcite, dgain, dbias = only_if(generator, gen_back)
        back_sums = lax.psum((jnp.sum(dcentred, axis=0), jnp.sum(dcentred * centred, axis=0)), "dp")

        def gen_grad():
            dshifted = inv_std * (
                dcentred - back_sums[0] / pixel_count - centred * back_sums[1] / pixel_count
            )
            return (dshifted.astype(jnp.bfloat16), jnp.sum(dshifted * noise_now[:, None], axis=0))

        dhidden, dnoise = only_if(generator, gen_grad)
        conv_acc = conv_acc + only_if(generator, lambda: low_dot(patches_in.T, dhidden))
        squeeze_acc = squeeze_acc + dsqueeze
        excite_acc = excite_acc + dexcite
        spectral_acc = spectral_acc + dspec_part
        vector_acc = vector_acc + jnp.concatenate(
            [dnoise, dgain, dbias, dout_part, dbias_part[None]]
        )
        loss_acc = loss_acc + loss_part
    critic_grad = spectral_back(spectral_acc)[0]
    conv_rows_sum, squeeze_rows, excite_rows, critic_rows = (
        lax.psum_scatter(conv_acc, "dp", scatter_dimension=0, tiled=True),
        lax.psum_scatter(squeeze_acc, "dp", scatter_dimension=0, tiled=True),
        lax.psum_scatter(excite_acc, "dp", scatter_dimension=0, tiled=True),
        lax.psum_scatter(critic_grad, "dp", scatter_dimension=0, tiled=True),
    )
    gradients = lax.psum((conv_rows_sum, squeeze_rows, excite_rows, critic_rows), "segment")
    vector_grad, loss_sum = lax.psum((vector_acc, loss_acc), ("segment", "dp"))
    weights = (conv_w, squeeze_w, excite_w, critic_w)
    new_moms = [
        MOMENTUM * old_mom + grad_now
        for old_mom, grad_now in zip((conv_mom, squeeze_mom, excite_mom, critic_mom), gradients)
    ]
    ortho = orthogonalize(new_moms)
    new_weights = [
        weight * (1.0 - MUON_RATE * DECAY) - MUON_RATE * step_dir
        for weight, step_dir in zip(weights, ortho)
    ]
    vec_m_new, vec_v_new, vectors_new = adam(vectors, vec_m, vec_v, vector_grad)
    return (
        loss_sum,
        new_moms[0],
        new_weights[0],
        new_moms[1],
        new_weights[1],
        new_moms[2],
        new_weights[2],
        new_moms[3],
        new_weights[3],
        vec_m_new,
        vec_v_new,
        vectors_new,
    )


def solution(mesh):
    placed = (
        P(None, "dp", None, None, None),
        P(None, "dp", None),
        P("dp", None, None),
        P(None, "dp"),
        P(),
        P(),
        P(),
        P("dp", None),
        P("dp", None),
        P("dp", None),
        P("dp", None),
        P("dp", None),
        P("dp", None),
        P("dp", None),
        P("dp", None),
        P(),
        P(),
        P(),
    )
    given = (
        P(),
        P("dp", None),
        P("dp", None),
        P("dp", None),
        P("dp", None),
        P("dp", None),
        P("dp", None),
        P("dp", None),
        P("dp", None),
        P(),
        P(),
        P(),
    )

    def step(latent, noise, *rest):
        n, sides = mesh.shape["dp"], mesh.shape["segment"]
        micros, images, edge = latent.shape[:3]
        fits = (
            n == 16
            and sides == 2
            and images == n
            and micros == 2
            and edge <= SUBLANES - 1
            and rest[5].shape[1] == 2 * n * sides * 16
        )
        plan = by_channels if fits else by_images
        return jax.shard_map(
            plan, mesh=mesh, in_specs=placed, out_specs=given, check_vma=False
        )(latent, noise, *rest)

    return step
```
